32 devices in a mesh: dp: 2 (over core), tm: 4 (over z), space: 4 (over y, x).
Axes of the slice: x: 2, y: 2, z: 4, core: 2. Of those that a mesh axis runs over, the one named last changes fastest.
Arguments:
- patches: bfloat16 [2, 8, 256, 1152], P('dp', 'tm', 'space'), may hold values from -4 to 4
- query_s: bfloat16 [2, 8, 256, 1152], P('dp', 'tm', 'space'), may hold values from -8 to 8
- key_s: bfloat16 [2, 8, 256, 1152], P('dp', 'tm', 'space'), may hold values from -8 to 8
- value_s: bfloat16 [2, 8, 256, 1152], P('dp', 'tm', 'space'), may hold values from -6 to 6
- query_t: bfloat16 [2, 8, 256, 1152], P('dp', 'tm', 'space'), may hold values from -8 to 8
- key_t: bfloat16 [2, 8, 256, 1152], P('dp', 'tm', 'space'), may hold values from -8 to 8
- value_t: bfloat16 [2, 8, 256, 1152], P('dp', 'tm', 'space'), may hold values from -6 to 6
- adapters_a: bfloat16 [4, 1152, 16], replicated, may hold values from -0.1875 to 0.1875
- adapters_b: bfloat16 [4, 16, 1152], replicated, may hold values from -1.5 to 1.5
- cotangent: bfloat16 [2, 8, 256, 1152], P('dp', 'tm', 'space'), may hold values from -6 to 6
Outputs:
- mixed: bfloat16 [2, 8, 256, 1152], P('dp', 'tm', 'space')
- grads_a: float32 [4, 1152, 16], replicated
- grads_b: float32 [4, 16, 1152], replicated
The draws below stay inside these ranges and needn't reach their ends.
All inputs are finite; a program needn't handle non-finite values.
Results may differ from the reference program's by a relative error of at most 0.018.
The reference program's roundings to bfloat16 on the way (of `probs_low`, `o_s`, `hidden`, `o_t`, `dscore` and `dhidden`) count: a program that leaves them out, or rounds other values in their place, can miss the bound.
Values may be sent and summed in bfloat16 or wider, within the bound.
No kernel may reach another device: no remote copies, remote signals or barrier semaphores. Data moves between devices by JAX's collectives and lax.ppermute only.
A program may use at most 64 MiB of HBM per device.

```python
import jax
import jax.numpy as jnp
from jax import lax

D = 1152
HEADS = 16
RANK = 16
HEAD_DIM = 72
CLIPS = 2
FRAMES = 8
PATCHES = 256


def paired(key):
    shape = (CLIPS, FRAMES, PATCHES, D)
    first, second = jax.random.split(key, 2)
    keys = 1.4 * jnp.clip(jax.random.normal(first, shape, jnp.float32), -4.0, 4.0)
    query = 1.4 * jnp.clip(jax.random.normal(second, shape, jnp.float32), -4.0, 4.0)
    return (query.astype(jnp.bfloat16), keys.astype(jnp.bfloat16))


def draw_query_s(key, part):
    return paired(jax.random.fold_in(key, 11))[0]


def draw_key_s(key, part):
    return paired(jax.random.fold_in(key, 11))[1]


def draw_query_t(key, part):
    return paired(jax.random.fold_in(key, 12))[0]


def draw_key_t(key, part):
    return paired(jax.random.fold_in(key, 12))[1]


def shard_levels(own_key, dims, cuts, least, high):
    def one(dim, shards_of):
        draws = jax.random.uniform(jax.random.fold_in(jax.random.fold_in(own_key, 6), dim), (shards_of,), jnp.float32, least / len(cuts), high / len(cuts))
        return jnp.repeat(jnp.exp(draws), dims[dim] // shards_of).reshape((-1,) + (1,) * (len(dims) - dim - 1))

    factor_of = one(*cuts[0])
    for cut in cuts[1:]:
        factor_of = factor_of * one(*cut)
    return factor_of


def normal_values(rng, extent, width, reach, cuts=(), kind=jnp.bfloat16):
    level = shard_levels(rng, extent, cuts, -0.22, 0.18) if cuts else 1.0
    drawn = jax.random.normal(rng, extent, jnp.float32) * width * level
    return jnp.minimum(jnp.maximum(drawn, -reach), reach).astype(kind)


def setup_inputs(seed: int = 0) -> dict:
    key_of = jax.random.split(jax.random.key(seed), 11)
    return {
        "patches": normal_values(key_of[0], (CLIPS, FRAMES, PATCHES, D), 0.5, 4.0, ((0, 2), (1, 4), (2, 4))),
        "query_s": draw_query_s(jax.random.fold_in(key_of[10], 71), 0),
        "key_s": draw_key_s(jax.random.fold_in(key_of[10], 71), 0),
        "value_s": normal_values(key_of[3], (CLIPS, FRAMES, PATCHES, D), 1.0, 6.0, ((0, 2), (1, 4), (2, 4))),
        "query_t": draw_query_t(jax.random.fold_in(key_of[10], 71), 0),
        "key_t": draw_key_t(jax.random.fold_in(key_of[10], 71), 0),
        "value_t": normal_values(key_of[6], (CLIPS, FRAMES, PATCHES, D), 1.0, 6.0, ((0, 2), (1, 4), (2, 4))),
        "adapters_a": normal_values(key_of[7], (4, D, RANK), D ** -0.5, 0.1875),
        "adapters_b": normal_values(key_of[8], (4, RANK, D), RANK ** -0.5, 1.5),
        "cotangent": normal_values(key_of[9], (CLIPS, FRAMES, PATCHES, D), 1.0, 6.0, ((0, 2), (1, 4), (2, 4))),
    }


def softmax_probs(query, keys):
    length = query.shape[0]
    count = keys.shape[0]
    heads_q = query.astype(jnp.float32).reshape(length, HEADS, HEAD_DIM)
    heads_k = keys.astype(jnp.float32).reshape(count, HEADS, HEAD_DIM)
    scores = jnp.einsum("qhd,khd->hqk", heads_q, heads_k) * (HEAD_DIM ** -0.5)
    peak = jnp.max(scores, axis=-1, keepdims=True)
    weights = jnp.exp(scores - peak)
    return weights / jnp.sum(weights, axis=-1, keepdims=True)


def attend_forward(query, keys, values):
    length = query.shape[0]
    probs = softmax_probs(query, keys)
    probs_low = lax.optimization_barrier(probs.astype(jnp.bfloat16)).astype(jnp.float32)
    heads_v = values.astype(jnp.float32).reshape(values.shape[0], HEADS, HEAD_DIM)
    output = jnp.einsum("hqk,khd->qhd", probs_low, heads_v)
    return output.reshape(length, D).astype(jnp.bfloat16)


def attend_backward(query, keys, values, grad):
    length = query.shape[0]
    count = keys.shape[0]
    probs = softmax_probs(query, keys)
    probs_low = lax.optimization_barrier(probs.astype(jnp.bfloat16)).astype(jnp.float32)
    heads_g = grad.astype(jnp.float32).reshape(length, HEADS, HEAD_DIM)
    heads_v = values.astype(jnp.float32).reshape(count, HEADS, HEAD_DIM)
    heads_k = keys.astype(jnp.float32).reshape(count, HEADS, HEAD_DIM)
    dvals = jnp.einsum("hqk,qhd->khd", probs_low, heads_g).reshape(count, D).astype(jnp.bfloat16)
    dprob = jnp.einsum("qhd,khd->hqk", heads_g, heads_v)
    inner = jnp.sum(probs * dprob, axis=-1, keepdims=True)
    dscore = (probs * (dprob - inner) * (HEAD_DIM ** -0.5)).astype(jnp.bfloat16)
    dscore = lax.optimization_barrier(dscore).astype(jnp.float32)
    dquery = jnp.einsum("hqk,khd->qhd", dscore, heads_k).reshape(length, D).astype(jnp.bfloat16)
    return dquery, dvals


def reference(patches, query_s, key_s, value_s, query_t, key_t, value_t, adapters_a, adapters_b, cotangent):
    def flat(array):
        return array.reshape(-1, D)

    def encode(inputs, index):
        return jnp.dot(flat(inputs), adapters_a[index], preferred_element_type=jnp.float32).astype(jnp.bfloat16)

    def adapted(base, codes, index):
        lifted = flat(base).astype(jnp.float32) + jnp.dot(codes, adapters_b[index], preferred_element_type=jnp.float32)
        return lifted.astype(jnp.bfloat16)

    def to_frames(array):
        return array.reshape(CLIPS * FRAMES, PATCHES, D)

    def to_time(array):
        return array.reshape(CLIPS, FRAMES, PATCHES, D).transpose(0, 2, 1, 3).reshape(CLIPS * PATCHES, FRAMES, D)

    def from_time(array):
        return array.reshape(CLIPS, PATCHES, FRAMES, D).transpose(0, 2, 1, 3).reshape(-1, D)

    codes_sq = encode(patches, 0)
    codes_sv = encode(patches, 1)
    q_s = to_frames(adapted(query_s, codes_sq, 0))
    v_s = to_frames(adapted(value_s, codes_sv, 1))
    k_s = to_frames(key_s)
    o_s = lax.map(lambda trio: attend_forward(trio[0], trio[1], trio[2]), (q_s, k_s, v_s))
    hidden = (flat(patches).astype(jnp.float32) + flat(o_s).astype(jnp.float32)).astype(jnp.bfloat16)
    codes_tq = encode(hidden, 2)
    codes_tv = encode(hidden, 3)
    q_t = to_time(adapted(query_t, codes_tq, 2))
    v_t = to_time(adapted(value_t, codes_tv, 3))
    k_t = to_time(key_t)
    o_t = from_time(jax.vmap(attend_forward)(q_t, k_t, v_t))
    mixed = (hidden.astype(jnp.float32) + o_t.astype(jnp.float32)).astype(jnp.bfloat16)

    dq_t, dv_t = jax.vmap(attend_backward)(q_t, k_t, v_t, to_time(cotangent))
    dq_t = from_time(dq_t)
    dv_t = from_time(dv_t)

    def adapter_grads(codes, inputs, dproj, index):
        grad_b = jnp.dot(codes.T, dproj, preferred_element_type=jnp.float32)
        dcodes = jnp.dot(dproj, adapters_b[index].T, preferred_element_type=jnp.float32).astype(jnp.bfloat16)
        grad_a = jnp.dot(flat(inputs).T, dcodes, preferred_element_type=jnp.float32)
        return grad_a, grad_b, dcodes

    ga_tq, gb_tq, dcodes_tq = adapter_grads(codes_tq, hidden, dq_t, 2)
    ga_tv, gb_tv, dcodes_tv = adapter_grads(codes_tv, hidden, dv_t, 3)
    dhidden = flat(cotangent).astype(jnp.float32)
    dhidden = dhidden + jnp.dot(dcodes_tq, adapters_a[2].T, preferred_element_type=jnp.float32)
    dhidden = (dhidden + jnp.dot(dcodes_tv, adapters_a[3].T, preferred_element_type=jnp.float32)).astype(jnp.bfloat16)

    dq_s, dv_s = lax.map(lambda quad: attend_backward(quad[0], quad[1], quad[2], quad[3]), (q_s, k_s, v_s, to_frames(dhidden)))
    ga_sq, gb_sq, dcodes_sq = adapter_grads(codes_sq, patches, flat(dq_s), 0)
    ga_sv, gb_sv, dcodes_sv = adapter_grads(codes_sv, patches, flat(dv_s), 1)
    factor = (CLIPS * FRAMES * PATCHES) ** -0.5
    grads_a = jnp.stack([ga_sq, ga_sv, ga_tq, ga_tv]) * factor
    grads_b = jnp.stack([gb_sq, gb_sv, gb_tq, gb_tv]) * factor
    return mixed.reshape(CLIPS, FRAMES, PATCHES, D), grads_a, grads_b
```

```python
import functools

import jax
import jax.numpy as jnp
from jax import lax
from jax.experimental import pallas as pl
from jax.experimental.pallas import tpu as pltpu
from jax.sharding import PartitionSpec as P

HEAD_DIM = 72
RANK = 16
SCALE = HEAD_DIM ** (-0.5)
F32 = jnp.float32
BF16 = jnp.bfloat16
NN = (((1,), (0,)), ((), ()))
NT = (((1,), (1,)), ((), ()))
TN = (((0,), (0,)), ((), ()))


def mm(a, b, dims=NN):
    return lax.dot_general(a, b, dims, preferred_element_type=F32)


def call(kernel, out_shape, *args, flops=0):
    vmem = pl.BlockSpec(memory_space=pltpu.VMEM)
    single = not isinstance(out_shape, (tuple, list))
    outs = (out_shape,) if single else tuple(out_shape)
    moved = sum(a.size * a.dtype.itemsize for a in args)
    moved += sum(o.size * o.dtype.itemsize for o in outs)
    result = pl.pallas_call(
        kernel,
        out_shape=outs,
        in_specs=[vmem] * len(args),
        out_specs=tuple(vmem for _ in outs),
        compiler_params=pltpu.CompilerParams(vmem_limit_bytes=48 * 1024 * 1024),
        cost_estimate=pl.CostEstimate(flops=flops, bytes_accessed=moved, transcendentals=0),
    )(*args)
    return result[0] if single else result


def shape(dims, dtype):
    return jax.ShapeDtypeStruct(tuple(dims), dtype)


def probs_of(keys, q_t, mask):
    scores = mm(keys, q_t) * SCALE
    if mask is not None:
        scores = jnp.where(mask, scores, -1e30)
    peak = jnp.max(scores, axis=0, keepdims=True)
    weights = jnp.exp(scores - peak)
    return weights / jnp.sum(weights, axis=0, keepdims=True)


def head_forward(q_t, k_t, v_t, mask=None):
    probs = probs_of(k_t.T, q_t, mask)
    return mm(v_t, probs.astype(BF16))


def head_backward(q_t, k_t, v_t, g_t, mask=None, forward=False):
    probs = probs_of(k_t.T, q_t, mask)
    low = probs.astype(BF16)
    dvals = mm(g_t, low, NT)
    dprob = mm(v_t.T, g_t)
    inner = jnp.sum(probs * dprob, axis=0, keepdims=True)
    dscore = (probs * (dprob - inner) * SCALE).astype(BF16)
    dquery = mm(k_t, dscore)
    out = mm(v_t, low) if forward else None
    return dquery, dvals, out


def rows_of(array, head):
    return array[head * HEAD_DIM : (head + 1) * HEAD_DIM]


def pack_time_kernel(n_t, sub, q_ref, k_ref, v_ref, g_ref, out_ref):
    for index, ref in enumerate((q_ref, k_ref, v_ref, g_ref)):
        frames = ref.shape[1]
        for i in range(n_t):
            for f in range(frames):
                out_ref[i, index, f * sub : (f + 1) * sub] = ref[0, f, i * sub : (i + 1) * sub]


def pack_space_kernel(n_s, p_ref, q_ref, k_ref, v_ref, g_ref, at_ref, b_ref, first_ref, second_ref):
    tokens, width = first_ref.shape[3], p_ref.shape[3]
    d_s = width // n_s

    def flat(ref):
        return ref[0].reshape(tokens, width)

    patches = flat(p_ref)
    downs = jnp.concatenate([at_ref[0], at_ref[1]], axis=0)
    codes_q = mm(patches, at_ref[0], NT).astype(BF16)
    codes_v = mm(patches, at_ref[1], NT).astype(BF16)
    codes_t = mm(downs, patches, NT).astype(BF16)
    query = (flat(q_ref).astype(F32) + mm(codes_q, b_ref[0])).astype(BF16)
    value = (flat(v_ref).astype(F32) + mm(codes_v, b_ref[1])).astype(BF16)
    for index, array in enumerate((query, flat(k_ref), value)):
        turned = array.T
        for j in range(n_s):
            first_ref[j, index] = turned[j * d_s : (j + 1) * d_s]
    for index, array in enumerate((patches, flat(g_ref))):
        turned = array.T
        for j in range(n_s):
            second_ref[j, index * d_s : (index + 1) * d_s] = turned[j * d_s : (j + 1) * d_s]
    for j in range(n_s):
        second_ref[j, 2 * d_s :] = codes_t


def frame_rows(pieces, f, patch_dev):
    return jnp.concatenate([x[:, f * patch_dev : (f + 1) * patch_dev] for x in pieces], axis=1)


def space_forward_kernel(frames, first_ref, qkv_ref, out_ref):
    n_s, _, d_s, tokens = first_ref.shape
    patch_dev = tokens // frames
    total = n_s * patch_dev
    step = min(total, 256)
    for index in range(3):
        pieces = [first_ref[j, index] for j in range(n_s)]
        for f in range(frames):
            qkv_ref[index, f] = frame_rows(pieces, f, patch_dev)
    for f in range(frames):
        query = qkv_ref[0, f].astype(F32)
        keys = qkv_ref[1, f].astype(F32)
        vals = qkv_ref[2, f].astype(F32)
        heads = []
        for h in range(d_s // HEAD_DIM):
            k_h = rows_of(keys, h).astype(BF16)
            v_h = rows_of(vals, h).astype(BF16)
            q_h = rows_of(query, h).astype(BF16)
            parts = [
                head_forward(q_h[:, s : s + step], k_h, v_h) for s in range(0, total, step)
            ]
            heads.append(parts[0] if len(parts) == 1 else jnp.concatenate(parts, axis=1))
        out = jnp.concatenate(heads, axis=0).astype(BF16)
        for j in range(n_s):
            out_ref[j, :, f * patch_dev : (f + 1) * patch_dev] = out[
                :, j * patch_dev : (j + 1) * patch_dev
            ]


def lane_block(rows):
    return lax.broadcasted_iota(jnp.int32, (rows, 128), 1) // (2 * RANK)


def fold(token_rows):
    block = lane_block(8)
    result = token_rows[0:8]
    for k in range(1, 4):
        result = jnp.where(block == k, token_rows[8 * k : 8 * k + 8], result)
    return result


def unfold(folded):
    pieces = [folded]
    for k in range(1, 4):
        pieces.append(pltpu.roll(folded, 128 - 2 * RANK * k, 1))
    return jnp.concatenate(pieces, axis=0)


def hidden_kernel(n_t, frames, out_ref, second_ref, at_ref, hidden_ref, send_ref):
    n_s, d_s, tokens = out_ref.shape
    patch_dev = tokens // frames
    sub = patch_dev // n_t
    downs = jnp.concatenate([at_ref[2], at_ref[3]] * 4, axis=0)
    for j in range(n_s):
        hidden = (second_ref[j, :d_s].astype(F32) + out_ref[j].astype(F32)).astype(BF16)
        hidden_ref[j] = hidden
        codes = mm(downs, hidden).T
        for i in range(n_t):
            rows = jnp.concatenate(
                [
                    codes[f * patch_dev + i * sub : f * patch_dev + (i + 1) * sub]
                    for f in range(frames)
                ],
                axis=0,
            )
            send_ref[i * n_s + j] = fold(rows)


def turn_kernel(time_ref, out_ref):
    n_t = time_ref.shape[0]
    for index in range(4):
        rows = jnp.concatenate([time_ref[i, index] for i in range(n_t)], axis=0)
        out_ref[index] = rows.T


def time_kernel(n_s, sub, x_ref, codes_ref, b_ref, out_ref, send_ref, grad_b_ref):
    _, width, tokens = x_ref.shape
    n_t = codes_ref.shape[0] // n_s
    pieces = []
    for i in range(n_t):
        total = codes_ref[i * n_s]
        for j in range(1, n_s):
            total = total + codes_ref[i * n_s + j]
        pieces.append(unfold(total))
    codes = jnp.concatenate(pieces, axis=0).T
    codes_q = codes[:RANK].astype(BF16)
    codes_v = codes[RANK : 2 * RANK].astype(BF16)
    query = (x_ref[0].astype(F32) + mm(b_ref[2], codes_q, TN)).astype(BF16).astype(F32)
    vals = (x_ref[2].astype(F32) + mm(b_ref[3], codes_v, TN)).astype(BF16).astype(F32)
    keys = x_ref[1].astype(F32)
    grad = x_ref[3].astype(F32)
    row = lax.broadcasted_iota(jnp.int32, (tokens, tokens), 0)
    col = lax.broadcasted_iota(jnp.int32, (tokens, tokens), 1)
    mask = lax.rem(row, sub) == lax.rem(col, sub)
    outs, d_query, d_vals = [], [], []
    for h in range(width // HEAD_DIM):
        dq, dv, out = head_backward(
            rows_of(query, h).astype(BF16),
            rows_of(keys, h).astype(BF16),
            rows_of(vals, h).astype(BF16),
            rows_of(grad, h).astype(BF16),
            mask,
            True,
        )
        outs.append(out)
        d_query.append(dq)
        d_vals.append(dv)
    out = jnp.concatenate(outs, axis=0).astype(BF16).T
    per = tokens // n_t
    for i in range(n_t):
        out_ref[i] = out[i * per : (i + 1) * per]
    d_query = jnp.concatenate(d_query, axis=0).astype(BF16)
    d_vals = jnp.concatenate(d_vals, axis=0).astype(BF16)
    grad_b_ref[:RANK] = mm(codes_q, d_query, NT)
    grad_b_ref[RANK:] = mm(codes_v, d_vals, NT)
    d_codes = jnp.concatenate([mm(b_ref[2], d_query), mm(b_ref[3], d_vals)] * 4, axis=0)
    d_codes = d_codes.astype(BF16).astype(F32).T
    for i in range(n_t):
        folded = fold(d_codes[i * per : (i + 1) * per])
        for j in range(n_s):
            send_ref[i * n_s + j] = folded


def space_backward_kernel(
    frames, qkv_ref, hidden_ref, second_ref, codes_ref, grad_b_ref, at_ref, b_ref, send_ref, part_ref
):
    n_s, d_s, tokens = hidden_ref.shape
    n_t = codes_ref.shape[0] // n_s
    patch_dev = tokens // frames
    sub = patch_dev // n_t
    total = n_s * patch_dev
    step = min(total, 256)
    ups = jnp.concatenate([at_ref[2], at_ref[3]], axis=0).T
    grads, grad_a = [], None
    for j in range(n_s):
        chunks = [unfold(codes_ref[i * n_s + j]) for i in range(n_t)]
        rows = jnp.concatenate(
            [chunks[i][f * sub : (f + 1) * sub] for f in range(frames) for i in range(n_t)], axis=0
        )
        d_codes = rows.T[: 2 * RANK].astype(BF16)
        term = mm(d_codes, hidden_ref[j], NT)
        grad_a = term if grad_a is None else grad_a + term
        cot = second_ref[j, d_s : 2 * d_s].astype(F32)
        grads.append((cot + mm(ups, d_codes)).astype(BF16))
    part_ref[: 2 * RANK] = grad_a
    grad_b_q = grad_b_v = None
    codes = [second_ref[j, 2 * d_s :] for j in range(n_s)]
    for f in range(frames):
        query = qkv_ref[0, f].astype(F32)
        keys = qkv_ref[1, f].astype(F32)
        vals = qkv_ref[2, f].astype(F32)
        grad = frame_rows(grads, f, patch_dev).astype(F32)
        d_query, d_vals = [], []
        for h in range(d_s // HEAD_DIM):
            k_h = rows_of(keys, h).astype(BF16)
            v_h = rows_of(vals, h).astype(BF16)
            q_h = rows_of(query, h).astype(BF16)
            g_h = rows_of(grad, h).astype(BF16)
            dq_parts, dv_sum = [], None
            for s in range(0, total, step):
                dq, dv, _ = head_backward(q_h[:, s : s + step], k_h, v_h, g_h[:, s : s + step])
                dq_parts.append(dq)
                dv_sum = dv if dv_sum is None else dv_sum + dv
            d_query.append(
                dq_parts[0] if len(dq_parts) == 1 else jnp.concatenate(dq_parts, axis=1)
            )
            d_vals.append(dv_sum)
        d_query = jnp.concatenate(d_query, axis=0).astype(BF16)
        d_vals = jnp.concatenate(d_vals, axis=0).astype(BF16)
        partial = jnp.concatenate([mm(b_ref[0], d_query), mm(b_ref[1], d_vals)], axis=0)
        for j in range(n_s):
            send_ref[j, :, f * total : (f + 1) * total] = partial.astype(BF16)
        frame_codes = frame_rows(codes, f, patch_dev)
        term_q = mm(frame_codes[:RANK], d_query, NT)
        term_v = mm(frame_codes[RANK:], d_vals, NT)
        grad_b_q = term_q if grad_b_q is None else grad_b_q + term_q
        grad_b_v = term_v if grad_b_v is None else grad_b_v + term_v
    part_ref[2 * RANK : 3 * RANK] = grad_b_q
    part_ref[3 * RANK :] = grad_b_v
    time_grad = grad_b_ref[...].astype(BF16)
    for j in range(n_s):
        send_ref[j, :, frames * total : frames * total + d_s] = time_grad[
            :, j * d_s : (j + 1) * d_s
        ]


def merge_kernel(frames, n_out, second_ref, recv_ref, part_ref, send_ref):
    n_s, _, tokens = second_ref.shape
    d_s = part_ref.shape[1]
    patch_dev = tokens // frames
    total = n_s * patch_dev
    patches = [second_ref[j, :d_s] for j in range(n_s)]
    grad_a = None
    for f in range(frames):
        codes = None
        for j in range(n_s):
            term = recv_ref[j, :, f * total : (f + 1) * total].astype(F32)
            codes = term if codes is None else codes + term
        term = mm(codes.astype(BF16), frame_rows(patches, f, patch_dev), NT)
        grad_a = term if grad_a is None else grad_a + term
    time_grad = None
    for j in range(n_s):
        term = recv_ref[j, :, frames * total : frames * total + d_s].astype(F32)
        time_grad = term if time_grad is None else time_grad + term
    rows = jnp.concatenate([grad_a, part_ref[...], time_grad], axis=0)
    per = rows.shape[0] // n_out
    for i in range(n_out):
        send_ref[i] = rows[i * per : (i + 1) * per].astype(send_ref.dtype)


def total_kernel(recv_ref, send_ref):
    total = recv_ref[0].astype(F32)
    for i in range(1, recv_ref.shape[0]):
        total = total + recv_ref[i].astype(F32)
    for i in range(send_ref.shape[0]):
        send_ref[i] = total.astype(send_ref.dtype)


def final_kernel(factor, n_s, recv_ref, a_ref, b_ref):
    count, per, d_s = recv_ref.shape
    blocks = count // n_s
    half = blocks // 2
    for block in range(blocks):
        rows = jnp.concatenate([recv_ref[block * n_s + j] for j in range(n_s)], axis=1)
        rows = rows.astype(F32) * factor
        target = a_ref if block < half else b_ref
        start = (block % half) * per
        target[start // RANK, start % RANK : start % RANK + per] = rows


def mixed_kernel(frames, hidden_ref, out_ref, mixed_ref):
    n_s, d_s, tokens = hidden_ref.shape
    n_t = out_ref.shape[0]
    patch_dev = tokens // frames
    sub = patch_dev // n_t
    hidden = hidden_ref[...].reshape(n_s * d_s, tokens).T
    for f in range(frames):
        for i in range(n_t):
            start = f * patch_dev + i * sub
            total = hidden[start : start + sub].astype(F32)
            total = total + out_ref[i, f * sub : (f + 1) * sub].astype(F32)
            mixed_ref[0, f, i * sub : (i + 1) * sub] = total.astype(BF16)


def swap(array, axes):
    return lax.all_to_all(array, axes, split_axis=0, concat_axis=0, tiled=True)


def per_device(
    patches, query_s, key_s, value_s, query_t, key_t, value_t, adapters_a, adapters_b, cotangent
):
    _, frames, patch_dev, width = patches.shape
    n_d, n_t, n_s = (lax.axis_size(name) for name in ("dp", "tm", "space"))
    tokens = frames * patch_dev
    sub = patch_dev // n_t
    d_s = width // n_s
    n_out = n_d * n_t
    total = n_s * patch_dev
    factor = (tokens * n_d * n_t * n_s) ** (-0.5)
    here = lax.axis_index("space") * d_s
    downs = jnp.swapaxes(adapters_a, 1, 2)
    downs_here = lax.dynamic_slice_in_dim(downs, here, d_s, 2)
    ups_here = lax.dynamic_slice_in_dim(adapters_b, here, d_s, 2)

    time_send = call(
        functools.partial(pack_time_kernel, n_t, sub),
        shape((n_t, 4, frames * sub, width), BF16),
        query_t, key_t, value_t, cotangent,
    )
    time_recv = swap(time_send, "tm")
    first, second = call(
        functools.partial(pack_space_kernel, n_s),
        (shape((n_s, 3, d_s, tokens), BF16), shape((n_s, 2 * d_s + 2 * RANK, tokens), BF16)),
        patches, query_s, key_s, value_s, cotangent, downs, adapters_b,
    )
    first = swap(first, "space")
    second = swap(second, "space")
    qkv, out_s = call(
        functools.partial(space_forward_kernel, frames),
        (shape((3, frames, d_s, total), BF16), shape((n_s, d_s, tokens), BF16)),
        first,
    )
    hidden, codes_send = call(
        functools.partial(hidden_kernel, n_t, frames),
        (shape((n_s, d_s, tokens), BF16), shape((n_t * n_s, 8, 128), F32)),
        out_s, second, downs_here,
    )
    codes_recv = swap(codes_send, ("tm", "space"))
    turned = call(turn_kernel, shape((4, width, n_t * frames * sub), BF16), time_recv)
    out_t, dcodes_send, time_grad_b = call(
        functools.partial(time_kernel, n_s, sub),
        (
            shape((n_t, frames * sub, width), BF16),
            shape((n_t * n_s, 8, 128), F32),
            shape((2 * RANK, width), F32),
        ),
        turned, codes_recv, adapters_b,
    )
    dcodes_recv = swap(dcodes_send, ("tm", "space"))
    part_lanes = frames * total + -(-d_s // 128) * 128
    partial_send, part = call(
        functools.partial(space_backward_kernel, frames),
        (shape((n_s, 2 * RANK, part_lanes), BF16), shape((4 * RANK, d_s), F32)),
        qkv, hidden, second, dcodes_recv, time_grad_b, downs_here, ups_here,
    )
    partial_recv = swap(partial_send, "space")
    sums_send = call(
        functools.partial(merge_kernel, frames, n_out),
        shape((n_out, 8 * RANK // n_out, d_s), F32),
        second, partial_recv, part,
    )
    sums_recv = swap(sums_send, ("dp", "tm"))
    all_send = call(total_kernel, shape((n_out * n_s, 8 * RANK // n_out, d_s), F32), sums_recv)
    all_recv = swap(all_send, ("dp", "tm", "space"))
    grads_a, grads_b = call(
        functools.partial(final_kernel, factor, n_s),
        (shape((4, RANK, width), F32), shape((4, RANK, width), F32)),
        all_recv,
    )
    mixed = call(
        functools.partial(mixed_kernel, frames),
        shape(patches.shape, BF16),
        swap(hidden, "space"), swap(out_t, "tm"),
    )
    return (mixed, jnp.swapaxes(grads_a, 1, 2), grads_b)


def solution(mesh):
    token = P("dp", "tm", "space", None)
    return jax.shard_map(
        per_device,
        mesh=mesh,
        in_specs=(token,) * 7 + (P(), P(), token),
        out_specs=(token, P(), P()),
        check_vma=False,
    )
```

```python
import functools

import jax
import jax.numpy as jnp
from jax import lax
from jax.experimental import pallas as pl
from jax.experimental.pallas import tpu as pltpu
from jax.sharding import PartitionSpec as P

HEAD_DIM = 72
RANK = 16
SCALE = HEAD_DIM ** (-0.5)
F32 = jnp.float32
BF16 = jnp.bfloat16
NN = (((1,), (0,)), ((), ()))
NT = (((1,), (1,)), ((), ()))
TN = (((0,), (0,)), ((), ()))


def mm(a, b, dims=NN):
    return lax.dot_general(a, b, dims, preferred_element_type=F32)


def call(kernel, out_shape, *args, scratch=(), anywhere=False):
    vmem = pl.BlockSpec(memory_space=pltpu.VMEM)
    single = not isinstance(out_shape, (tuple, list))
    outs = (out_shape,) if single else tuple(out_shape)
    result = pl.pallas_call(
        kernel,
        out_shape=outs,
        in_specs=[pl.BlockSpec(memory_space=pl.ANY) if anywhere else vmem] * len(args),
        out_specs=tuple(vmem for _ in outs),
        scratch_shapes=list(scratch),
        compiler_params=pltpu.CompilerParams(vmem_limit_bytes=48 * 1024 * 1024),
    )(*args)
    return result[0] if single else list(result)


def shape(dims, dtype):
    return jax.ShapeDtypeStruct(tuple(dims), dtype)


def probs_of(keys, q_t, mask):
    scores = mm(keys, q_t) * SCALE
    if mask is not None:
        scores = jnp.where(mask, scores, -1e30)
    peak = jnp.max(scores, axis=0, keepdims=True)
    weights = jnp.exp(scores - peak)
    return weights / jnp.sum(weights, axis=0, keepdims=True)


def head_forward(q_t, k_t, v_t, mask=None):
    probs = probs_of(k_t.T, q_t, mask)
    return mm(v_t, probs.astype(BF16))


def head_backward(q_t, k_t, v_t, g_t, mask=None, forward=False):
    probs = probs_of(k_t.T, q_t, mask)
    low = probs.astype(BF16)
    dvals = mm(g_t, low, NT)
    dprob = mm(v_t.T, g_t)
    inner = jnp.sum(probs * dprob, axis=0, keepdims=True)
    dscore = (probs * (dprob - inner) * SCALE).astype(BF16)
    dquery = mm(k_t, dscore)
    out = mm(v_t, low) if forward else None
    return dquery, dvals, out


def rows_of(array, head):
    return array[head * HEAD_DIM : (head + 1) * HEAD_DIM]


def peer(axis, distance):
    return lax.axis_index(axis) ^ distance


def load_all(refs, buffers, sems):
    copies = [
        pltpu.make_async_copy(ref, buffer, sems.at[index])
        for index, (ref, buffer) in enumerate(zip(refs, buffers))
    ]
    for copy in copies:
        copy.start()
    return copies


def pack_time_kernel(n_t, sub, q_ref, k_ref, v_ref, g_ref, *rest):
    outs, sems = rest[:n_t], rest[n_t]
    frames = q_ref.shape[1]
    copies = []
    for k in range(n_t):
        start = pl.multiple_of(peer("tm", k) * sub, sub)
        for index, ref in enumerate((q_ref, k_ref, v_ref, g_ref)):
            for f in range(frames):
                copy = pltpu.make_async_copy(
                    ref.at[0, f, pl.ds(start, sub)],
                    outs[k].at[index, f * sub : (f + 1) * sub],
                    sems.at[len(copies)],
                )
                copy.start()
                copies.append(copy)
    for copy in copies:
        copy.wait()


def pack_space_kernel(n_s, *refs):
    ins, refs = refs[:7], refs[7:]
    firsts, seconds, buffers = refs[:n_s], refs[n_s : 2 * n_s], refs[2 * n_s : 2 * n_s + 7]
    turned_ref, sems = refs[2 * n_s + 7 :]
    p_buf, at_buf, b_buf, q_buf, v_buf, k_buf, g_buf = buffers
    copies = load_all(ins, buffers, sems)
    d_s, tokens = firsts[0].shape[1:]

    def flat(ref):
        return ref[0].reshape(tokens, ref.shape[3])

    def send(array, targets, index):
        turned = array.T
        for j in range(n_s):
            turned_ref[index, j] = turned[j * d_s : (j + 1) * d_s]
        for k in range(n_s):
            targets(k)[...] = turned_ref[index, peer("space", k)]

    copies[0].wait()
    copies[1].wait()
    copies[2].wait()
    patches = flat(p_buf)
    codes_q = mm(patches, at_buf[0], NT).astype(BF16)
    codes_v = mm(patches, at_buf[1], NT).astype(BF16)
    codes_t = jnp.concatenate([codes_q, codes_v], axis=1).T
    copies[3].wait()
    query = (flat(q_buf).astype(F32) + mm(codes_q, b_buf[0])).astype(BF16)
    send(query, lambda k: firsts[k].at[0], 0)
    copies[4].wait()
    value = (flat(v_buf).astype(F32) + mm(codes_v, b_buf[1])).astype(BF16)
    send(value, lambda k: firsts[k].at[2], 1)
    copies[5].wait()
    send(flat(k_buf), lambda k: firsts[k].at[1], 2)
    send(patches, lambda k: seconds[k].at[:d_s], 3)
    copies[6].wait()
    send(flat(g_buf), lambda k: seconds[k].at[d_s : 2 * d_s], 4)
    for k in range(n_s):
        seconds[k][2 * d_s :] = codes_t


def frame_rows(pieces, f, patch_dev):
    return jnp.concatenate([x[:, f * patch_dev : (f + 1) * patch_dev] for x in pieces], axis=1)


def space_forward_kernel(frames, n_s, *refs):
    firsts, qkv_ref, outs = refs[:n_s], refs[n_s], refs[n_s + 1 :]
    _, d_s, tokens = firsts[0].shape
    patch_dev = tokens // frames
    total = n_s * patch_dev
    step = min(total, 256)
    for index in range(3):
        pieces = [first[index] for first in firsts]
        for f in range(frames):
            qkv_ref[index, f] = frame_rows(pieces, f, patch_dev)
    for f in range(frames):
        query = qkv_ref[0, f].astype(F32)
        keys = qkv_ref[1, f].astype(F32)
        vals = qkv_ref[2, f].astype(F32)
        heads = []
        for h in range(d_s // HEAD_DIM):
            k_h = rows_of(keys, h).astype(BF16)
            v_h = rows_of(vals, h).astype(BF16)
            q_h = rows_of(query, h).astype(BF16)
            parts = [
                head_forward(q_h[:, s : s + step], k_h, v_h) for s in range(0, total, step)
            ]
            heads.append(parts[0] if len(parts) == 1 else jnp.concatenate(parts, axis=1))
        out = jnp.concatenate(heads, axis=0).astype(BF16)
        for k in range(n_s):
            outs[k][:, f * patch_dev : (f + 1) * patch_dev] = out[
                :, k * patch_dev : (k + 1) * patch_dev
            ]


def lane_block(rows):
    return lax.broadcasted_iota(jnp.int32, (rows, 128), 1) // (2 * RANK)


def fold(token_rows):
    block = lane_block(8)
    result = token_rows[0:8]
    for k in range(1, 4):
        result = jnp.where(block == k, token_rows[8 * k : 8 * k + 8], result)
    return result


def unfold(folded):
    pieces = [folded]
    for k in range(1, 4):
        pieces.append(pltpu.roll(folded, 128 - 2 * RANK * k, 1))
    return jnp.concatenate(pieces, axis=0)


def hidden_kernel(n_t, n_s, *refs):
    pieces, refs = refs[:n_s], refs[n_s:]
    p_ref, at_ref, hidden_ref = refs[:3]
    sends = refs[3 : 3 + n_t]
    out_buf, codes_buf = refs[3 + n_t :]
    _, frames, patch_dev, width = p_ref.shape
    tokens = frames * patch_dev
    sub = patch_dev // n_t
    for k in range(n_s):
        out_buf[peer("space", k)] = pieces[k][...]
    out = out_buf[...].reshape(width, tokens).T
    hidden = (p_ref[0].reshape(tokens, width).astype(F32) + out.astype(F32)).astype(BF16)
    hidden_ref[...] = hidden
    downs = jnp.concatenate([at_ref[2], at_ref[3]] * 4, axis=0)
    codes_buf[...] = mm(hidden, downs, NT).astype(BF16).astype(F32)
    for k in range(n_t):
        rows = [
            codes_buf[pl.ds(pl.multiple_of(f * patch_dev + peer("tm", k) * sub, sub), sub)]
            for f in range(frames)
        ]
        sends[k][...] = fold(jnp.concatenate(rows, axis=0))


def turn_kernel(*refs):
    pieces, out_ref = refs[:-1], refs[-1]
    for index in range(4):
        rows = jnp.concatenate([piece[index] for piece in pieces], axis=0)
        out_ref[index] = rows.T


def time_kernel(n_t, sub, x_ref, b_ref, *refs):
    codes_refs, refs = refs[:n_t], refs[n_t:]
    outs, sends, grad_b_ref = refs[:n_t], refs[n_t : 2 * n_t], refs[2 * n_t]
    _, width, tokens = x_ref.shape
    codes = jnp.concatenate([unfold(ref[...]) for ref in codes_refs], axis=0).T
    codes_q = codes[:RANK].astype(BF16)
    codes_v = codes[RANK : 2 * RANK].astype(BF16)
    query = (x_ref[0].astype(F32) + mm(b_ref[2], codes_q, TN)).astype(BF16).astype(F32)
    vals = (x_ref[2].astype(F32) + mm(b_ref[3], codes_v, TN)).astype(BF16).astype(F32)
    keys = x_ref[1].astype(F32)
    grad = x_ref[3].astype(F32)
    row = lax.broadcasted_iota(jnp.int32, (tokens, tokens), 0)
    col = lax.broadcasted_iota(jnp.int32, (tokens, tokens), 1)
    mask = lax.rem(row, sub) == lax.rem(col, sub)
    outs_h, d_query, d_vals = [], [], []
    for h in range(width // HEAD_DIM):
        dq, dv, out = head_backward(
            rows_of(query, h).astype(BF16),
            rows_of(keys, h).astype(BF16),
            rows_of(vals, h).astype(BF16),
            rows_of(grad, h).astype(BF16),
            mask,
            True,
        )
        outs_h.append(out)
        d_query.append(dq)
        d_vals.append(dv)
    d_query = jnp.concatenate(d_query, axis=0).astype(BF16)
    d_vals = jnp.concatenate(d_vals, axis=0).astype(BF16)
    d_codes = jnp.concatenate([mm(b_ref[2], d_query), mm(b_ref[3], d_vals)] * 4, axis=0)
    d_codes = d_codes.astype(BF16).astype(F32).T
    per = tokens // n_t
    for k in range(n_t):
        sends[k][...] = fold(d_codes[k * per : (k + 1) * per])
    out = jnp.concatenate(outs_h, axis=0).astype(BF16).T
    for k in range(n_t):
        outs[k][...] = out[k * per : (k + 1) * per]
    grad_b_ref[:RANK] = mm(codes_q, d_query, NT)
    grad_b_ref[RANK:] = mm(codes_v, d_vals, NT)


def place_codes_kernel(frames, sub, *refs):
    pieces, (out_ref, buf) = refs[:-2], refs[-2:]
    patch_dev = sub * len(pieces)
    for k, piece in enumerate(pieces):
        rows = unfold(piece[...])
        for f in range(frames):
            start = pl.multiple_of(f * patch_dev + peer("tm", k) * sub, sub)
            buf[pl.ds(start, sub)] = rows[f * sub : (f + 1) * sub]
    out_ref[...] = buf[...].T[: 2 * RANK].astype(BF16)


def space_backward_kernel(frames, n_s, qkv_ref, hidden_ref, grad_b_ref, at_ref, at_here_ref, b_here_ref, *refs):
    seconds, dcodes, sends = refs[:n_s], refs[n_s : 2 * n_s], refs[2 * n_s : 3 * n_s]
    part_ref, cut_buf = refs[3 * n_s :]
    d_s = part_ref.shape[1]
    tokens = hidden_ref.shape[0]
    patch_dev = tokens // frames
    total = n_s * patch_dev
    step = min(total, 256)
    ups = jnp.concatenate([at_here_ref[2], at_here_ref[3]], axis=0).T
    grads = []
    for k in range(n_s):
        cot = seconds[k][d_s : 2 * d_s].astype(F32)
        grads.append((cot + mm(ups, dcodes[k][...])).astype(BF16))
    grad_b_q = grad_b_v = None
    codes = [second[2 * d_s :] for second in seconds]
    for f in range(frames):
        query = qkv_ref[0, f].astype(F32)
        keys = qkv_ref[1, f].astype(F32)
        vals = qkv_ref[2, f].astype(F32)
        grad = frame_rows(grads, f, patch_dev).astype(F32)
        d_query, d_vals = [], []
        for h in range(d_s // HEAD_DIM):
            k_h = rows_of(keys, h).astype(BF16)
            v_h = rows_of(vals, h).astype(BF16)
            q_h = rows_of(query, h).astype(BF16)
            g_h = rows_of(grad, h).astype(BF16)
            dq_parts, dv_sum = [], None
            for s in range(0, total, step):
                dq, dv, _ = head_backward(q_h[:, s : s + step], k_h, v_h, g_h[:, s : s + step])
                dq_parts.append(dq)
                dv_sum = dv if dv_sum is None else dv_sum + dv
            d_query.append(
                dq_parts[0] if len(dq_parts) == 1 else jnp.concatenate(dq_parts, axis=1)
            )
            d_vals.append(dv_sum)
        d_query = jnp.concatenate(d_query, axis=0).astype(BF16)
        d_vals = jnp.concatenate(d_vals, axis=0).astype(BF16)
        partial = jnp.concatenate([mm(b_here_ref[0], d_query), mm(b_here_ref[1], d_vals)], axis=0)
        partial = partial.astype(BF16)
        blocks = [partial[:, m * patch_dev : (m + 1) * patch_dev] for m in range(n_s)]
        for k in range(n_s):
            turned = jnp.concatenate([blocks[m ^ k] for m in range(n_s)], axis=1)
            sends[k][:, f * total : (f + 1) * total] = turned
        frame_codes = frame_rows(codes, f, patch_dev)
        term_q = mm(frame_codes[:RANK], d_query, NT)
        term_v = mm(frame_codes[RANK:], d_vals, NT)
        grad_b_q = term_q if grad_b_q is None else grad_b_q + term_q
        grad_b_v = term_v if grad_b_v is None else grad_b_v + term_v
    part_ref[:RANK] = grad_b_q
    part_ref[RANK:] = grad_b_v
    grad_a = mm(dcodes[0][...], hidden_ref[...])
    pad = -(-d_s // 128) * 128
    for j in range(n_s):
        cut_buf[j, 0, :, :d_s] = grad_a[:, j * d_s : (j + 1) * d_s].astype(BF16)
        cut_buf[j, 1, :, :d_s] = grad_b_ref[:, j * d_s : (j + 1) * d_s].astype(BF16)
    for k in range(n_s):
        for index in range(2):
            start = frames * total + index * pad
            sends[k][:, start : start + pad] = cut_buf[peer("space", k), index]


def add_up(terms):
    result = None
    for term in terms:
        result = term if result is None else result + term
    return result


def merge_kernel(frames, n_s, n_d, part_ref, *refs):
    seconds, recvs, refs = refs[:n_s], refs[n_s : 2 * n_s], refs[2 * n_s :]
    sends, buf = refs[:n_d], refs[n_d]
    d_s = part_ref.shape[1]
    tokens = seconds[0].shape[1]
    patch_dev = tokens // frames
    total = n_s * patch_dev
    pad = -(-d_s // 128) * 128
    patches = [second[:d_s] for second in seconds]
    terms = []
    for f in range(frames):
        codes = [recv[:, f * total : (f + 1) * total].astype(F32) for recv in recvs]
        terms.append(mm(add_up(codes).astype(BF16), frame_rows(patches, f, patch_dev), NT))
    start = frames * total
    time_a = add_up([recv[:, start : start + d_s].astype(F32) for recv in recvs])
    time_b = add_up([recv[:, start + pad : start + pad + d_s].astype(F32) for recv in recvs])
    rows = jnp.concatenate([add_up(terms), time_a, part_ref[...], time_b], axis=0)
    per = rows.shape[0] // n_d
    for d in range(n_d):
        buf[d] = rows[d * per : (d + 1) * per]
    for k in range(n_d):
        sends[k][...] = buf[peer("dp", k)]


def total_kernel(*refs):
    refs[-1][...] = add_up([ref[...].astype(F32) for ref in refs[:-1]]).astype(refs[-1].dtype)


def join_kernel(*refs):
    pieces, (out_ref, buf) = refs[:-2], refs[-2:]
    for k, piece in enumerate(pieces):
        buf[peer("space", k)] = piece[...]
    out_ref[...] = jnp.concatenate([buf[j] for j in range(len(pieces))], axis=1)


def final_kernel(factor, n_d, *refs):
    pieces, (a_ref, b_ref, buf) = refs[:n_d], refs[n_d:]
    for k, piece in enumerate(pieces):
        buf[peer("dp", k)] = piece[...]
    per = pieces[0].shape[0]
    half = n_d // 2
    for d in range(n_d):
        rows = buf[d].astype(F32) * factor
        target = a_ref if d < half else b_ref
        for r in range(0, per, min(per, RANK)):
            start = (d % half) * per + r
            size = min(per, RANK)
            target[start // RANK, start % RANK : start % RANK + size] = rows[r : r + size]


def mixed_kernel(frames, hidden_ref, *refs):
    pieces, (mixed_ref, buf) = refs[:-2], refs[-2:]
    n_t = len(pieces)
    tokens, width = hidden_ref.shape
    patch_dev = tokens // frames
    sub = patch_dev // n_t
    for k, piece in enumerate(pieces):
        for f in range(frames):
            start = pl.multiple_of(f * patch_dev + peer("tm", k) * sub, sub)
            buf[pl.ds(start, sub)] = piece[f * sub : (f + 1) * sub]
    total = hidden_ref[...].astype(F32) + buf[...].astype(F32)
    mixed_ref[0] = total.astype(BF16).reshape(frames, patch_dev, width)


def exchange(pieces, axis):
    size = lax.axis_size(axis)
    return [pieces[0]] + [
        lax.ppermute(pieces[k], axis, [(i, i ^ k) for i in range(size)]) for k in range(1, size)
    ]


def share(array, axis):
    return exchange([array] * lax.axis_size(axis), axis)


def per_device(
    patches, query_s, key_s, value_s, query_t, key_t, value_t, adapters_a, adapters_b, cotangent
):
    _, frames, patch_dev, width = patches.shape
    n_d, n_t, n_s = (lax.axis_size(name) for name in ("dp", "tm", "space"))
    tokens = frames * patch_dev
    sub = patch_dev // n_t
    d_s = width // n_s
    total = n_s * patch_dev
    factor = (tokens * n_d * n_t * n_s) ** (-0.5)
    here = lax.axis_index("space") * d_s
    downs = jnp.swapaxes(adapters_a, 1, 2)
    downs_here = lax.dynamic_slice_in_dim(downs, here, d_s, 2)
    ups_here = lax.dynamic_slice_in_dim(adapters_b, here, d_s, 2)
    dma = pltpu.SemaphoreType.DMA
    pad = -(-d_s // 128) * 128

    time_pieces = exchange(
        call(
            functools.partial(pack_time_kernel, n_t, sub),
            [shape((4, frames * sub, width), BF16)] * n_t,
            query_t, key_t, value_t, cotangent,
            scratch=[dma((4 * frames * n_t,))],
            anywhere=True,
        ),
        "tm",
    )
    packed = call(
        functools.partial(pack_space_kernel, n_s),
        [shape((3, d_s, tokens), BF16)] * n_s + [shape((2 * d_s + 2 * RANK, tokens), BF16)] * n_s,
        patches, downs, adapters_b, query_s, value_s, key_s, cotangent,
        scratch=[
            pltpu.VMEM(x.shape, BF16)
            for x in (patches, downs, adapters_b, query_s, value_s, key_s, cotangent)
        ]
        + [pltpu.VMEM((5, n_s, d_s, tokens), BF16), dma((7,))],
        anywhere=True,
    )
    firsts = exchange(packed[:n_s], "space")
    seconds = exchange(packed[n_s:], "space")
    qkv, *out_s = call(
        functools.partial(space_forward_kernel, frames, n_s),
        [shape((3, frames, d_s, total), BF16)] + [shape((d_s, tokens), BF16)] * n_s,
        *firsts,
    )
    out_s = exchange(out_s, "space")
    hidden, *codes = call(
        functools.partial(hidden_kernel, n_t, n_s),
        [shape((tokens, width), BF16)] + [shape((8, 128), F32)] * n_t,
        *out_s, patches, downs,
        scratch=[pltpu.VMEM((n_s, d_s, tokens), BF16), pltpu.VMEM((tokens, 128), F32)],
    )
    codes = exchange(codes, "tm")
    turned = call(turn_kernel, shape((4, width, n_t * frames * sub), BF16), *time_pieces)
    timed = call(
        functools.partial(time_kernel, n_t, sub),
        [shape((frames * sub, width), BF16)] * n_t
        + [shape((8, 128), F32)] * n_t
        + [shape((2 * RANK, width), F32)],
        turned, adapters_b, *codes,
    )
    out_t, dcodes, time_grad_b = timed[:n_t], timed[n_t : 2 * n_t], timed[2 * n_t]
    dcodes = exchange(dcodes, "tm")
    dcodes = call(
        functools.partial(place_codes_kernel, frames, sub),
        shape((2 * RANK, tokens), BF16),
        *dcodes,
        scratch=[pltpu.VMEM((tokens, 128), F32)],
    )
    dcodes = share(dcodes, "space")
    *partial, part = call(
        functools.partial(space_backward_kernel, frames, n_s),
        [shape((2 * RANK, frames * total + 2 * pad), BF16)] * n_s + [shape((2 * RANK, d_s), F32)],
        qkv, hidden, time_grad_b, downs, downs_here, ups_here, *seconds, *dcodes,
        scratch=[pltpu.VMEM((n_s, 2, 2 * RANK, pad), BF16)],
    )
    partial = exchange(partial, "space")
    rows = 8 * RANK // n_d
    sums = call(
        functools.partial(merge_kernel, frames, n_s, n_d),
        [shape((rows, d_s), F32)] * n_d,
        part, *seconds, *partial,
        scratch=[pltpu.VMEM((n_d, rows, d_s), F32)],
    )
    sums = call(total_kernel, shape((rows, d_s), BF16), *exchange(sums, "dp"))
    sums = call(total_kernel, shape((rows, d_s), BF16), *share(sums, "tm"))
    sums = call(
        join_kernel,
        shape((rows, width), BF16),
        *share(sums, "space"),
        scratch=[pltpu.VMEM((n_s, rows, d_s), BF16)],
    )
    grads_a, grads_b = call(
        functools.partial(final_kernel, factor, n_d),
        [shape((4, RANK, width), F32)] * 2,
        *share(sums, "dp"),
        scratch=[pltpu.VMEM((n_d, rows, width), BF16)],
    )
    mixed = call(
        functools.partial(mixed_kernel, frames),
        shape(patches.shape, BF16),
        hidden, *exchange(out_t, "tm"),
        scratch=[pltpu.VMEM((tokens, width), BF16)],
    )
    return (mixed, jnp.swapaxes(grads_a, 1, 2), grads_b)


def solution(mesh):
    token = P("dp", "tm", "space", None)
    return jax.shard_map(
        per_device,
        mesh=mesh,
        in_specs=(token,) * 7 + (P(), P(), token),
        out_specs=(token, P(), P()),
        check_vma=False,
    )
```

```python
import functools

import jax
import jax.numpy as jnp
from jax import lax
from jax.experimental import pallas as pl
from jax.experimental.pallas import tpu as pltpu
from jax.sharding import PartitionSpec as P

HEAD_DIM = 72
RANK = 16
SCALE = HEAD_DIM ** (-0.5)
F32 = jnp.float32
BF16 = jnp.bfloat16
NN = (((1,), (0,)), ((), ()))
NT = (((1,), (1,)), ((), ()))
TN = (((0,), (0,)), ((), ()))


def mm(a, b, dims=NN):
    return lax.dot_general(a, b, dims, preferred_element_type=F32)


def call(kernel, out_shape, *args, scratch=(), hbm=False, limit=48, after=(), carry=()):
    vmem = pl.BlockSpec(memory_space=pltpu.VMEM)
    anywhere = pl.BlockSpec(memory_space=pl.ANY)
    main = pl.BlockSpec(memory_space=pltpu.HBM) if hbm else vmem
    single = not isinstance(out_shape, (tuple, list))
    outs = (out_shape,) if single else tuple(out_shape)
    used, extra = len(args), len(after) + len(carry)

    def body(*refs):
        inside = refs[:used] + refs[used + extra : used + extra + len(outs)]
        kernel(*inside, *refs[used + extra + len(outs) + len(carry) :])

    result = pl.pallas_call(
        body,
        out_shape=outs + tuple(shape(x.shape, x.dtype) for x in carry),
        in_specs=[main] * used + [anywhere] * extra,
        out_specs=(vmem,) * len(outs) + (anywhere,) * len(carry),
        scratch_shapes=list(scratch),
        input_output_aliases={used + len(after) + i: len(outs) + i for i in range(len(carry))},
        compiler_params=pltpu.CompilerParams(vmem_limit_bytes=limit * 1024 * 1024),
    )(*args, *after, *carry)
    return result[0] if single and not carry else list(result)


def shape(dims, dtype):
    return jax.ShapeDtypeStruct(tuple(dims), dtype)


def probs_of(keys, q_t, mask):
    scores = mm(keys, q_t) * SCALE
    if mask is not None:
        scores = jnp.where(mask, scores, -1e30)
    peak = jnp.max(scores, axis=0, keepdims=True)
    weights = jnp.exp(scores - peak)
    return weights / jnp.sum(weights, axis=0, keepdims=True)


def head_forward(q_t, k_t, v_t, mask=None):
    probs = probs_of(k_t.T, q_t, mask)
    return mm(v_t, probs.astype(BF16))


def head_backward(q_t, k_t, v_t, g_t, mask=None, forward=False):
    probs = probs_of(k_t.T, q_t, mask)
    low = probs.astype(BF16)
    dvals = mm(g_t, low, NT)
    dprob = mm(v_t.T, g_t)
    inner = jnp.sum(probs * dprob, axis=0, keepdims=True)
    dscore = (probs * (dprob - inner) * SCALE).astype(BF16)
    dquery = mm(k_t, dscore)
    out = mm(v_t, low) if forward else None
    return dquery, dvals, out


def rows_of(array, head):
    return array[head * HEAD_DIM : (head + 1) * HEAD_DIM]


def peer(axis, distance):
    return lax.axis_index(axis) ^ distance


def load_all(refs, buffers, sems):
    copies = [
        pltpu.make_async_copy(ref, buffer, sems.at[index])
        for index, (ref, buffer) in enumerate(zip(refs, buffers))
    ]
    for copy in copies:
        copy.start()
    return copies


def pack_time_kernel(n_t, sub, q_ref, k_ref, v_ref, g_ref, *rest):
    outs, sems = rest[:n_t], rest[n_t]
    frames = q_ref.shape[1]
    copies = []
    for k in range(n_t):
        start = pl.multiple_of(peer("tm", k) * sub, sub)
        for index, ref in enumerate((q_ref, k_ref, v_ref, g_ref)):
            for f in range(frames):
                copy = pltpu.make_async_copy(
                    ref.at[0, f, pl.ds(start, sub)],
                    outs[k].at[index, f * sub : (f + 1) * sub],
                    sems.at[len(copies)],
                )
                copy.start()
                copies.append(copy)
    for copy in copies:
        copy.wait()


def pack_space_kernel(n_s, *refs):
    ins, refs = refs[:7], refs[7:]
    outs, buffers, (turned_ref, sems) = refs[:n_s], refs[n_s : n_s + 7], refs[n_s + 7 :]
    p_buf, at_buf, b_buf, q_buf, v_buf, k_buf, g_buf = buffers
    copies = load_all(ins, buffers, sems)
    d_s, tokens = turned_ref.shape[2:]

    def flat(ref):
        return ref[0].reshape(tokens, ref.shape[3])

    def send(array, index):
        turned = array.T
        for j in range(n_s):
            turned_ref[index, j] = turned[j * d_s : (j + 1) * d_s]
        for k in range(n_s):
            outs[k][index * d_s : (index + 1) * d_s] = turned_ref[index, peer("space", k)]

    copies[0].wait()
    copies[1].wait()
    copies[2].wait()
    patches = flat(p_buf)
    codes_q = mm(patches, at_buf[0], NT).astype(BF16)
    codes_v = mm(patches, at_buf[1], NT).astype(BF16)
    codes_t = jnp.concatenate([codes_q, codes_v], axis=1).T
    copies[3].wait()
    query = (flat(q_buf).astype(F32) + mm(codes_q, b_buf[0])).astype(BF16)
    send(query, 0)
    copies[4].wait()
    value = (flat(v_buf).astype(F32) + mm(codes_v, b_buf[1])).astype(BF16)
    send(value, 2)
    copies[5].wait()
    send(flat(k_buf), 1)
    send(patches, 3)
    copies[6].wait()
    send(flat(g_buf), 4)
    for k in range(n_s):
        outs[k][5 * d_s :] = codes_t


def frame_rows(pieces, f, patch_dev):
    return jnp.concatenate([x[:, f * patch_dev : (f + 1) * patch_dev] for x in pieces], axis=1)


def space_forward_kernel(frames, n_s, *refs):
    packed, qkv_ref, outs = refs[:n_s], refs[n_s], refs[n_s + 1 :]
    d_s, tokens = outs[0].shape
    patch_dev = tokens // frames
    total = n_s * patch_dev
    step = min(total, 256)
    for index in range(3):
        pieces = [x[index * d_s : (index + 1) * d_s] for x in packed]
        for f in range(frames):
            qkv_ref[index, f] = frame_rows(pieces, f, patch_dev)
    for f in range(frames):
        query = qkv_ref[0, f].astype(F32)
        keys = qkv_ref[1, f].astype(F32)
        vals = qkv_ref[2, f].astype(F32)
        heads = []
        for h in range(d_s // HEAD_DIM):
            k_h = rows_of(keys, h).astype(BF16)
            v_h = rows_of(vals, h).astype(BF16)
            q_h = rows_of(query, h).astype(BF16)
            parts = [
                head_forward(q_h[:, s : s + step], k_h, v_h) for s in range(0, total, step)
            ]
            heads.append(parts[0] if len(parts) == 1 else jnp.concatenate(parts, axis=1))
        out = jnp.concatenate(heads, axis=0).astype(BF16)
        for k in range(n_s):
            outs[k][:, f * patch_dev : (f + 1) * patch_dev] = out[
                :, k * patch_dev : (k + 1) * patch_dev
            ]


def lane_block(rows):
    return lax.broadcasted_iota(jnp.int32, (rows, 128), 1) // (2 * RANK)


def fold(token_rows):
    block = lane_block(8)
    result = token_rows[0:8]
    for k in range(1, 4):
        result = jnp.where(block == k, token_rows[8 * k : 8 * k + 8], result)
    return result


def unfold(folded):
    pieces = [folded]
    for k in range(1, 4):
        pieces.append(pltpu.roll(folded, 128 - 2 * RANK * k, 1))
    return jnp.concatenate(pieces, axis=0)


def hidden_kernel(n_t, n_s, *refs):
    pieces, refs = refs[:n_s], refs[n_s:]
    p_ref, at_ref, hidden_ref = refs[:3]
    sends = refs[3 : 3 + n_t]
    out_buf, codes_buf = refs[3 + n_t :]
    _, frames, patch_dev, width = p_ref.shape
    tokens = frames * patch_dev
    sub = patch_dev // n_t
    for k in range(n_s):
        out_buf[peer("space", k)] = pieces[k][...]
    out = out_buf[...].reshape(width, tokens).T
    hidden = (p_ref[0].reshape(tokens, width).astype(F32) + out.astype(F32)).astype(BF16)
    hidden_ref[...] = hidden
    downs = jnp.concatenate([at_ref[2], at_ref[3]] * 4, axis=0)
    codes_buf[...] = mm(hidden, downs, NT).astype(BF16).astype(F32)
    for k in range(n_t):
        rows = [
            codes_buf[pl.ds(pl.multiple_of(f * patch_dev + peer("tm", k) * sub, sub), sub)]
            for f in range(frames)
        ]
        sends[k][...] = fold(jnp.concatenate(rows, axis=0))


def turn_kernel(*refs):
    pieces, out_ref = refs[:-1], refs[-1]
    for index in range(4):
        rows = jnp.concatenate([piece[index] for piece in pieces], axis=0)
        out_ref[index] = rows.T


def time_kernel(n_t, sub, x_ref, b_ref, *refs):
    codes_refs, refs = refs[:n_t], refs[n_t:]
    outs, sends, grad_b_ref = refs[:n_t], refs[n_t : 2 * n_t], refs[2 * n_t]
    _, width, tokens = x_ref.shape
    codes = jnp.concatenate([unfold(ref[...]) for ref in codes_refs], axis=0).T
    codes_q = codes[:RANK].astype(BF16)
    codes_v = codes[RANK : 2 * RANK].astype(BF16)
    query = (x_ref[0].astype(F32) + mm(b_ref[2], codes_q, TN)).astype(BF16).astype(F32)
    vals = (x_ref[2].astype(F32) + mm(b_ref[3], codes_v, TN)).astype(BF16).astype(F32)
    keys = x_ref[1].astype(F32)
    grad = x_ref[3].astype(F32)
    row = lax.broadcasted_iota(jnp.int32, (tokens, tokens), 0)
    col = lax.broadcasted_iota(jnp.int32, (tokens, tokens), 1)
    mask = lax.rem(row, sub) == lax.rem(col, sub)
    outs_h, d_query, d_vals = [], [], []
    for h in range(width // HEAD_DIM):
        dq, dv, out = head_backward(
            rows_of(query, h).astype(BF16),
            rows_of(keys, h).astype(BF16),
            rows_of(vals, h).astype(BF16),
            rows_of(grad, h).astype(BF16),
            mask,
            True,
        )
        outs_h.append(out)
        d_query.append(dq)
        d_vals.append(dv)
    d_query = jnp.concatenate(d_query, axis=0).astype(BF16)
    d_vals = jnp.concatenate(d_vals, axis=0).astype(BF16)
    d_codes = jnp.concatenate([mm(b_ref[2], d_query), mm(b_ref[3], d_vals)] * 4, axis=0)
    d_codes = d_codes.astype(BF16).astype(F32).T
    per = tokens // n_t
    for k in range(n_t):
        sends[k][...] = fold(d_codes[k * per : (k + 1) * per])
    out = jnp.concatenate(outs_h, axis=0).astype(BF16).T
    for k in range(n_t):
        outs[k][...] = out[k * per : (k + 1) * per]
    grad_b_ref[:RANK] = mm(codes_q, d_query, NT)
    grad_b_ref[RANK:] = mm(codes_v, d_vals, NT)


def place_codes_kernel(frames, sub, *refs):
    pieces, (out_ref, buf) = refs[:-2], refs[-2:]
    patch_dev = sub * len(pieces)
    for k, piece in enumerate(pieces):
        rows = unfold(piece[...])
        for f in range(frames):
            start = pl.multiple_of(f * patch_dev + peer("tm", k) * sub, sub)
            buf[pl.ds(start, sub)] = rows[f * sub : (f + 1) * sub]
    out_ref[...] = buf[...].T[: 2 * RANK].astype(BF16)


def space_backward_kernel(frames, n_s, qkv_ref, hidden_ref, grad_b_ref, at_ref, at_here_ref, b_here_ref, *refs):
    packed, dcodes, sends = refs[:n_s], refs[n_s : 2 * n_s], refs[2 * n_s : 3 * n_s]
    part_ref, cut_buf = refs[3 * n_s :]
    d_s = part_ref.shape[1]
    tokens = hidden_ref.shape[0]
    patch_dev = tokens // frames
    total = n_s * patch_dev
    step = min(total, 256)
    ups = jnp.concatenate([at_here_ref[2], at_here_ref[3]], axis=0).T
    grads = []
    for k in range(n_s):
        cot = packed[k][4 * d_s : 5 * d_s].astype(F32)
        grads.append((cot + mm(ups, dcodes[k][...])).astype(BF16))
    grad_b_q = grad_b_v = None
    codes = [x[5 * d_s :] for x in packed]
    for f in range(frames):
        query = qkv_ref[0, f].astype(F32)
        keys = qkv_ref[1, f].astype(F32)
        vals = qkv_ref[2, f].astype(F32)
        grad = frame_rows(grads, f, patch_dev).astype(F32)
        d_query, d_vals = [], []
        for h in range(d_s // HEAD_DIM):
            k_h = rows_of(keys, h).astype(BF16)
            v_h = rows_of(vals, h).astype(BF16)
            q_h = rows_of(query, h).astype(BF16)
            g_h = rows_of(grad, h).astype(BF16)
            dq_parts, dv_sum = [], None
            for s in range(0, total, step):
                dq, dv, _ = head_backward(q_h[:, s : s + step], k_h, v_h, g_h[:, s : s + step])
                dq_parts.append(dq)
                dv_sum = dv if dv_sum is None else dv_sum + dv
            d_query.append(
                dq_parts[0] if len(dq_parts) == 1 else jnp.concatenate(dq_parts, axis=1)
            )
            d_vals.append(dv_sum)
        d_query = jnp.concatenate(d_query, axis=0).astype(BF16)
        d_vals = jnp.concatenate(d_vals, axis=0).astype(BF16)
        partial = jnp.concatenate([mm(b_here_ref[0], d_query), mm(b_here_ref[1], d_vals)], axis=0)
        partial = partial.astype(BF16)
        blocks = [partial[:, m * patch_dev : (m + 1) * patch_dev] for m in range(n_s)]
        for k in range(n_s):
            turned = jnp.concatenate([blocks[m ^ k] for m in range(n_s)], axis=1)
            sends[k][:, f * total : (f + 1) * total] = turned
        frame_codes = frame_rows(codes, f, patch_dev)
        term_q = mm(frame_codes[:RANK], d_query, NT)
        term_v = mm(frame_codes[RANK:], d_vals, NT)
        grad_b_q = term_q if grad_b_q is None else grad_b_q + term_q
        grad_b_v = term_v if grad_b_v is None else grad_b_v + term_v
    part_ref[:RANK] = grad_b_q
    part_ref[RANK:] = grad_b_v
    grad_a = mm(dcodes[0][...], hidden_ref[...])
    pad = -(-d_s // 128) * 128
    for j in range(n_s):
        cut_buf[j, 0, :, :d_s] = grad_a[:, j * d_s : (j + 1) * d_s].astype(BF16)
        cut_buf[j, 1, :, :d_s] = grad_b_ref[:, j * d_s : (j + 1) * d_s].astype(BF16)
    for k in range(n_s):
        for index in range(2):
            start = frames * total + index * pad
            sends[k][:, start : start + pad] = cut_buf[peer("space", k), index]


def add_up(terms):
    result = None
    for term in terms:
        result = term if result is None else result + term
    return result


def merge_kernel(frames, n_s, n_d, part_ref, *refs):
    packed, recvs, refs = refs[:n_s], refs[n_s : 2 * n_s], refs[2 * n_s :]
    sends, buf = refs[:n_d], refs[n_d]
    d_s = part_ref.shape[1]
    tokens = packed[0].shape[1]
    patch_dev = tokens // frames
    total = n_s * patch_dev
    pad = -(-d_s // 128) * 128
    patches = [x[3 * d_s : 4 * d_s] for x in packed]
    terms = []
    for f in range(frames):
        codes = [recv[:, f * total : (f + 1) * total].astype(F32) for recv in recvs]
        terms.append(mm(add_up(codes).astype(BF16), frame_rows(patches, f, patch_dev), NT))
    start = frames * total
    time_a = add_up([recv[:, start : start + d_s].astype(F32) for recv in recvs])
    time_b = add_up([recv[:, start + pad : start + pad + d_s].astype(F32) for recv in recvs])
    rows = jnp.concatenate([add_up(terms), time_a, part_ref[...], time_b], axis=0)
    per = rows.shape[0] // n_d
    for d in range(n_d):
        buf[d] = rows[d * per : (d + 1) * per]
    for k in range(n_d):
        sends[k][...] = buf[peer("dp", k)]


def total_kernel(*refs):
    refs[-1][...] = add_up([ref[...].astype(F32) for ref in refs[:-1]]).astype(refs[-1].dtype)


def join_kernel(*refs):
    pieces, (out_ref, buf) = refs[:-2], refs[-2:]
    for k, piece in enumerate(pieces):
        buf[peer("space", k)] = piece[...]
    out_ref[...] = jnp.concatenate([buf[j] for j in range(len(pieces))], axis=1)


def final_kernel(factor, n_d, *refs):
    pieces, (a_ref, b_ref, buf) = refs[:n_d], refs[n_d:]
    for k, piece in enumerate(pieces):
        buf[peer("dp", k)] = piece[...]
    per = pieces[0].shape[0]
    half = n_d // 2
    for d in range(n_d):
        rows = buf[d].astype(F32) * factor
        target = a_ref if d < half else b_ref
        for r in range(0, per, min(per, RANK)):
            start = (d % half) * per + r
            size = min(per, RANK)
            target[start // RANK, start % RANK : start % RANK + size] = rows[r : r + size]


def mixed_kernel(frames, hidden_ref, *refs):
    pieces, (mixed_ref, buf) = refs[:-2], refs[-2:]
    n_t = len(pieces)
    tokens, width = hidden_ref.shape
    patch_dev = tokens // frames
    sub = patch_dev // n_t
    for k, piece in enumerate(pieces):
        for f in range(frames):
            start = pl.multiple_of(f * patch_dev + peer("tm", k) * sub, sub)
            buf[pl.ds(start, sub)] = piece[f * sub : (f + 1) * sub]
    total = hidden_ref[...].astype(F32) + buf[...].astype(F32)
    mixed_ref[0] = total.astype(BF16).reshape(frames, patch_dev, width)


def exchange(pieces, axis):
    size = lax.axis_size(axis)
    return [pieces[0]] + [
        lax.ppermute(pieces[k], axis, [(i, i ^ k) for i in range(size)]) for k in range(1, size)
    ]


def share(array, axis):
    return exchange([array] * lax.axis_size(axis), axis)


def per_device(
    patches, query_s, key_s, value_s, query_t, key_t, value_t, adapters_a, adapters_b, cotangent
):
    _, frames, patch_dev, width = patches.shape
    n_d, n_t, n_s = (lax.axis_size(name) for name in ("dp", "tm", "space"))
    tokens = frames * patch_dev
    sub = patch_dev // n_t
    d_s = width // n_s
    total = n_s * patch_dev
    factor = (tokens * n_d * n_t * n_s) ** (-0.5)
    here = lax.axis_index("space") * d_s
    downs = jnp.swapaxes(adapters_a, 1, 2)
    downs_here = lax.dynamic_slice_in_dim(downs, here, d_s, 2)
    ups_here = lax.dynamic_slice_in_dim(adapters_b, here, d_s, 2)
    dma = pltpu.SemaphoreType.DMA
    pad = -(-d_s // 128) * 128

    time_pieces = call(
        functools.partial(pack_time_kernel, n_t, sub),
        [shape((4, frames * sub, width), BF16)] * n_t,
        query_t, key_t, value_t, cotangent,
        scratch=[dma((4 * frames * n_t,))],
        hbm=True, limit=54,
    )
    time_pieces = exchange(time_pieces, "tm")
    packed = call(
        functools.partial(pack_space_kernel, n_s),
        [shape((5 * d_s + 2 * RANK, tokens), BF16)] * n_s,
        patches, downs, adapters_b, query_s, value_s, key_s, cotangent,
        scratch=[
            pltpu.VMEM(x.shape, BF16)
            for x in (patches, downs, adapters_b, query_s, value_s, key_s, cotangent)
        ]
        + [pltpu.VMEM((5, n_s, d_s, tokens), BF16), dma((7,))],
        hbm=True, limit=54,
    )
    packed = exchange(packed, "space")
    qkv, *out_s = call(
        functools.partial(space_forward_kernel, frames, n_s),
        [shape((3, frames, d_s, total), BF16)] + [shape((d_s, tokens), BF16)] * n_s,
        *packed,
    )
    out_s = exchange(out_s, "space")
    hidden, *codes = call(
        functools.partial(hidden_kernel, n_t, n_s),
        [shape((tokens, width), BF16)] + [shape((8, 128), F32)] * n_t,
        *out_s, patches, downs,
        scratch=[pltpu.VMEM((n_s, d_s, tokens), BF16), pltpu.VMEM((tokens, 128), F32)],
    )
    codes = exchange(codes, "tm")
    turned = call(turn_kernel, shape((4, width, n_t * frames * sub), BF16), *time_pieces)
    timed = call(
        functools.partial(time_kernel, n_t, sub),
        [shape((frames * sub, width), BF16)] * n_t
        + [shape((8, 128), F32)] * n_t
        + [shape((2 * RANK, width), F32)],
        turned, adapters_b, *codes,
    )
    out_t, dcodes, time_grad_b = timed[:n_t], timed[n_t : 2 * n_t], timed[2 * n_t]
    dcodes = exchange(dcodes, "tm")
    dcodes = call(
        functools.partial(place_codes_kernel, frames, sub),
        shape((2 * RANK, tokens), BF16),
        *dcodes,
        scratch=[pltpu.VMEM((tokens, 128), F32)],
    )
    dcodes = share(dcodes, "space")
    backward = call(
        functools.partial(space_backward_kernel, frames, n_s),
        [shape((2 * RANK, frames * total + 2 * pad), BF16)] * n_s + [shape((2 * RANK, d_s), F32)],
        qkv, hidden, time_grad_b, downs, downs_here, ups_here, *packed, *dcodes,
        scratch=[pltpu.VMEM((n_s, 2, 2 * RANK, pad), BF16)],
        carry=out_t,
    )
    partial, part, out_t = backward[:n_s], backward[n_s], backward[n_s + 1 :]
    partial = exchange(partial, "space")
    out_t = exchange(out_t, "tm")
    rows = 8 * RANK // n_d
    sums = call(
        functools.partial(merge_kernel, frames, n_s, n_d),
        [shape((rows, d_s), F32)] * n_d,
        part, *packed, *partial,
        scratch=[pltpu.VMEM((n_d, rows, d_s), F32)],
    )
    sums = call(total_kernel, shape((rows, d_s), BF16), *exchange(sums, "dp"), after=out_t[1:])
    step = 1
    while step < n_t:
        other = lax.ppermute(sums, "tm", [(i, i ^ step) for i in range(n_t)])
        sums = call(total_kernel, shape((rows, d_s), BF16), sums, other)
        step *= 2
    sums = call(
        join_kernel,
        shape((rows, width), BF16),
        *share(sums, "space"),
        scratch=[pltpu.VMEM((n_s, rows, d_s), BF16)],
    )
    grads_a, grads_b = call(
        functools.partial(final_kernel, factor, n_d),
        [shape((4, RANK, width), F32)] * 2,
        *share(sums, "dp"),
        scratch=[pltpu.VMEM((n_d, rows, width), BF16)],
    )
    mixed = call(
        functools.partial(mixed_kernel, frames),
        shape(patches.shape, BF16),
        hidden, *out_t,
        scratch=[pltpu.VMEM((tokens, width), BF16)],
    )
    return (mixed, jnp.swapaxes(grads_a, 1, 2), grads_b)


def solution(mesh):
    token = P("dp", "tm", "space", None)
    return jax.shard_map(
        per_device,
        mesh=mesh,
        in_specs=(token,) * 7 + (P(), P(), token),
        out_specs=(token, P(), P()),
        check_vma=False,
    )
```

```python
import functools

import jax
import jax.numpy as jnp
from jax import lax
from jax.experimental import pallas as pl
from jax.experimental.pallas import tpu as pltpu
from jax.sharding import PartitionSpec as P

HEAD_DIM = 72
RANK = 16
SCALE = HEAD_DIM ** (-0.5)
F32 = jnp.float32
BF16 = jnp.bfloat16
NN = (((1,), (0,)), ((), ()))
NT = (((1,), (1,)), ((), ()))
TN = (((0,), (0,)), ((), ()))


def mm(a, b, dims=NN):
    return lax.dot_general(a, b, dims, preferred_element_type=F32)


def call(kernel, out_shape, *args, scratch=(), hbm=False, limit=48, after=(), carry=()):
    vmem = pl.BlockSpec(memory_space=pltpu.VMEM)
    anywhere = pl.BlockSpec(memory_space=pl.ANY)
    main = pl.BlockSpec(memory_space=pltpu.HBM) if hbm else vmem
    single = not isinstance(out_shape, (tuple, list))
    outs = (out_shape,) if single else tuple(out_shape)
    used, extra = len(args), len(after) + len(carry)

    def body(*refs):
        inside = refs[:used] + refs[used + extra : used + extra + len(outs)]
        kernel(*inside, *refs[used + extra + len(outs) + len(carry) :])

    result = pl.pallas_call(
        body,
        out_shape=outs + tuple(shape(x.shape, x.dtype) for x in carry),
        in_specs=[main] * used + [anywhere] * extra,
        out_specs=(vmem,) * len(outs) + (anywhere,) * len(carry),
        scratch_shapes=list(scratch),
        input_output_aliases={used + len(after) + i: len(outs) + i for i in range(len(carry))},
        compiler_params=pltpu.CompilerParams(vmem_limit_bytes=limit * 1024 * 1024),
    )(*args, *after, *carry)
    return result[0] if single and not carry else list(result)


def shape(dims, dtype):
    return jax.ShapeDtypeStruct(tuple(dims), dtype)


def probs_of(keys, q_t, mask):
    scores = mm(keys, q_t) * SCALE
    if mask is not None:
        scores = jnp.where(mask, scores, -1e30)
    peak = jnp.max(scores, axis=0, keepdims=True)
    weights = jnp.exp(scores - peak)
    return weights / jnp.sum(weights, axis=0, keepdims=True)


def head_forward(q_t, k_t, v_t, mask=None):
    probs = probs_of(k_t.T, q_t, mask)
    return mm(v_t, probs.astype(BF16))


def head_backward(q_t, k_t, v_t, g_t, mask=None, forward=False):
    probs = probs_of(k_t.T, q_t, mask)
    low = probs.astype(BF16)
    dvals = mm(g_t, low, NT)
    dprob = mm(v_t.T, g_t)
    inner = jnp.sum(probs * dprob, axis=0, keepdims=True)
    dscore = (probs * (dprob - inner) * SCALE).astype(BF16)
    dquery = mm(k_t, dscore)
    out = mm(v_t, low) if forward else None
    return dquery, dvals, out


def rows_of(array, head):
    return array[head * HEAD_DIM : (head + 1) * HEAD_DIM]


def peer(axis, distance):
    return lax.axis_index(axis) ^ distance


def load_all(refs, buffers, sems):
    copies = [
        pltpu.make_async_copy(ref, buffer, sems.at[index])
        for index, (ref, buffer) in enumerate(zip(refs, buffers))
    ]
    for copy in copies:
        copy.start()
    return copies


def pack_time_kernel(n_t, sub, q_ref, k_ref, v_ref, g_ref, *rest):
    outs, sems = rest[:n_t], rest[n_t]
    frames = q_ref.shape[1]
    copies = []
    for k in range(n_t):
        start = pl.multiple_of(peer("tm", k) * sub, sub)
        for index, ref in enumerate((q_ref, k_ref, v_ref, g_ref)):
            for f in range(frames):
                copy = pltpu.make_async_copy(
                    ref.at[0, f, pl.ds(start, sub)],
                    outs[k].at[index, f * sub : (f + 1) * sub],
                    sems.at[len(copies)],
                )
                copy.start()
                copies.append(copy)
    for copy in copies:
        copy.wait()


def pack_space_kernel(n_s, *refs):
    ins, outs, refs = refs[:7], refs[7:9], refs[9:]
    buffers, sems = refs[:7], refs[7]
    send_ref, side_ref = outs
    p_buf, at_buf, b_buf, q_buf, v_buf, k_buf, g_buf = buffers
    copies = load_all(ins, buffers, sems)
    tokens = send_ref.shape[2]
    d_s = send_ref.shape[1] // 4

    def flat(ref):
        return ref[0].reshape(tokens, ref.shape[3])

    def send(array, target, index):
        turned = array.T
        for j in range(n_s):
            target[j, index * d_s : (index + 1) * d_s] = turned[j * d_s : (j + 1) * d_s]

    copies[0].wait()
    copies[1].wait()
    copies[2].wait()
    patches = flat(p_buf)
    codes_q = mm(patches, at_buf[0], NT).astype(BF16)
    codes_v = mm(patches, at_buf[1], NT).astype(BF16)
    send(patches, send_ref, 3)
    copies[3].wait()
    query = (flat(q_buf).astype(F32) + mm(codes_q, b_buf[0])).astype(BF16)
    send(query, send_ref, 0)
    copies[4].wait()
    value = (flat(v_buf).astype(F32) + mm(codes_v, b_buf[1])).astype(BF16)
    send(value, send_ref, 2)
    copies[5].wait()
    send(flat(k_buf), send_ref, 1)
    copies[6].wait()
    send(flat(g_buf), side_ref, 0)
    codes_t = jnp.concatenate([codes_q, codes_v], axis=1).T
    for j in range(n_s):
        side_ref[j, d_s:] = codes_t


def frame_rows(pieces, f, patch_dev):
    return jnp.concatenate([x[:, f * patch_dev : (f + 1) * patch_dev] for x in pieces], axis=1)


def space_forward_kernel(frames, packed_ref, qkv_ref, out_ref):
    n_s, d_s, tokens = out_ref.shape
    patch_dev = tokens // frames
    total = n_s * patch_dev
    step = min(total, 256)
    for index in range(3):
        pieces = [packed_ref[j, index * d_s : (index + 1) * d_s] for j in range(n_s)]
        for f in range(frames):
            qkv_ref[index, f] = frame_rows(pieces, f, patch_dev)
    for f in range(frames):
        query = qkv_ref[0, f].astype(F32)
        keys = qkv_ref[1, f].astype(F32)
        vals = qkv_ref[2, f].astype(F32)
        heads = []
        for h in range(d_s // HEAD_DIM):
            k_h = rows_of(keys, h).astype(BF16)
            v_h = rows_of(vals, h).astype(BF16)
            q_h = rows_of(query, h).astype(BF16)
            parts = [
                head_forward(q_h[:, s : s + step], k_h, v_h) for s in range(0, total, step)
            ]
            heads.append(parts[0] if len(parts) == 1 else jnp.concatenate(parts, axis=1))
        out = jnp.concatenate(heads, axis=0).astype(BF16)
        for j in range(n_s):
            out_ref[j, :, f * patch_dev : (f + 1) * patch_dev] = out[
                :, j * patch_dev : (j + 1) * patch_dev
            ]


def lane_block(rows):
    return lax.broadcasted_iota(jnp.int32, (rows, 128), 1) // (2 * RANK)


def fold(token_rows):
    block = lane_block(8)
    result = token_rows[0:8]
    for k in range(1, 4):
        result = jnp.where(block == k, token_rows[8 * k : 8 * k + 8], result)
    return result


def unfold(folded):
    pieces = [folded]
    for k in range(1, 4):
        pieces.append(pltpu.roll(folded, 128 - 2 * RANK * k, 1))
    return jnp.concatenate(pieces, axis=0)


def hidden_kernel(n_t, frames, out_ref, packed_ref, at_ref, hidden_ref, send_ref):
    n_s, d_s, tokens = out_ref.shape
    patch_dev = tokens // frames
    sub = patch_dev // n_t
    downs = jnp.concatenate([at_ref[2], at_ref[3]] * 4, axis=0)
    for j in range(n_s):
        hidden = (packed_ref[j, 3 * d_s :].astype(F32) + out_ref[j].astype(F32)).astype(BF16)
        hidden_ref[j] = hidden
        codes = mm(downs, hidden).T
        for i in range(n_t):
            rows = jnp.concatenate(
                [
                    codes[f * patch_dev + i * sub : f * patch_dev + (i + 1) * sub]
                    for f in range(frames)
                ],
                axis=0,
            )
            send_ref[i * n_s + j] = fold(rows)


def side_kernel(hidden_ref, side_ref, *outs):
    d_s = hidden_ref.shape[1]
    for k, out in enumerate(outs):
        out[:d_s] = hidden_ref[peer("space", k)]
        out[d_s:] = side_ref[peer("space", k)]


def turn_kernel(*refs):
    pieces, out_ref = refs[:-1], refs[-1]
    for index in range(4):
        rows = jnp.concatenate([piece[index] for piece in pieces], axis=0)
        out_ref[index] = rows.T


def add_up(terms):
    result = None
    for term in terms:
        result = term if result is None else result + term
    return result


def time_kernel(n_t, n_s, sub, x_ref, b_ref, codes_ref, send_ref, grad_b_ref, *outs):
    _, width, tokens = x_ref.shape
    pieces = []
    for k in range(n_t):
        start = peer("tm", k) * n_s
        pieces.append(unfold(add_up([codes_ref[start + j] for j in range(n_s)])))
    codes = jnp.concatenate(pieces, axis=0).T
    codes_q = codes[:RANK].astype(BF16)
    codes_v = codes[RANK : 2 * RANK].astype(BF16)
    query = (x_ref[0].astype(F32) + mm(b_ref[2], codes_q, TN)).astype(BF16).astype(F32)
    vals = (x_ref[2].astype(F32) + mm(b_ref[3], codes_v, TN)).astype(BF16).astype(F32)
    keys = x_ref[1].astype(F32)
    grad = x_ref[3].astype(F32)
    row = lax.broadcasted_iota(jnp.int32, (tokens, tokens), 0)
    col = lax.broadcasted_iota(jnp.int32, (tokens, tokens), 1)
    mask = lax.rem(row, sub) == lax.rem(col, sub)
    outs_h, d_query, d_vals = [], [], []
    for h in range(width // HEAD_DIM):
        dq, dv, out = head_backward(
            rows_of(query, h).astype(BF16),
            rows_of(keys, h).astype(BF16),
            rows_of(vals, h).astype(BF16),
            rows_of(grad, h).astype(BF16),
            mask,
            True,
        )
        outs_h.append(out)
        d_query.append(dq)
        d_vals.append(dv)
    d_query = jnp.concatenate(d_query, axis=0).astype(BF16)
    d_vals = jnp.concatenate(d_vals, axis=0).astype(BF16)
    d_codes = jnp.concatenate([mm(b_ref[2], d_query), mm(b_ref[3], d_vals)] * 4, axis=0)
    d_codes = d_codes.astype(BF16).astype(F32).T
    per = tokens // n_t
    for k in range(n_t):
        folded = fold(d_codes[k * per : (k + 1) * per])
        start = peer("tm", k) * n_s
        for j in range(n_s):
            send_ref[start + j] = folded
    out = jnp.concatenate(outs_h, axis=0).astype(BF16).T
    for k in range(n_t):
        outs[k][...] = out[k * per : (k + 1) * per]
    grad_b_ref[:RANK] = mm(codes_q, d_query, NT)
    grad_b_ref[RANK:] = mm(codes_v, d_vals, NT)


def space_backward_kernel(frames, n_s, qkv_ref, hidden_ref, grad_b_ref, codes_ref, at_ref, b_ref, *refs):
    sides, sends, (part_ref, cut_buf, side_buf) = refs[:n_s], refs[n_s : 2 * n_s], refs[2 * n_s :]
    n_s, d_s, tokens = hidden_ref.shape
    n_t = codes_ref.shape[0] // n_s
    patch_dev = tokens // frames
    sub = patch_dev // n_t
    total = n_s * patch_dev
    step = min(total, 256)
    for k in range(n_s):
        side_buf[peer("space", k)] = sides[k][d_s:]
    ups = jnp.concatenate([at_ref[2], at_ref[3]], axis=0).T
    grads, grad_a = [], None
    for j in range(n_s):
        chunks = [unfold(codes_ref[i * n_s + j]) for i in range(n_t)]
        rows = jnp.concatenate(
            [chunks[i][f * sub : (f + 1) * sub] for f in range(frames) for i in range(n_t)], axis=0
        )
        d_codes = rows.T[: 2 * RANK].astype(BF16)
        term = mm(d_codes, hidden_ref[j], NT)
        grad_a = term if grad_a is None else grad_a + term
        cot = side_buf[j, :d_s].astype(F32)
        grads.append((cot + mm(ups, d_codes)).astype(BF16))
    part_ref[: 2 * RANK] = grad_a
    grad_b_q = grad_b_v = None
    codes = [side_buf[j, d_s:] for j in range(n_s)]
    for f in range(frames):
        query = qkv_ref[0, f].astype(F32)
        keys = qkv_ref[1, f].astype(F32)
        vals = qkv_ref[2, f].astype(F32)
        grad = frame_rows(grads, f, patch_dev).astype(F32)
        d_query, d_vals = [], []
        for h in range(d_s // HEAD_DIM):
            k_h = rows_of(keys, h).astype(BF16)
            v_h = rows_of(vals, h).astype(BF16)
            q_h = rows_of(query, h).astype(BF16)
            g_h = rows_of(grad, h).astype(BF16)
            dq_parts, dv_sum = [], None
            for s in range(0, total, step):
                dq, dv, _ = head_backward(q_h[:, s : s + step], k_h, v_h, g_h[:, s : s + step])
                dq_parts.append(dq)
                dv_sum = dv if dv_sum is None else dv_sum + dv
            d_query.append(
                dq_parts[0] if len(dq_parts) == 1 else jnp.concatenate(dq_parts, axis=1)
            )
            d_vals.append(dv_sum)
        d_query = jnp.concatenate(d_query, axis=0).astype(BF16)
        d_vals = jnp.concatenate(d_vals, axis=0).astype(BF16)
        partial = jnp.concatenate([mm(b_ref[0], d_query), mm(b_ref[1], d_vals)], axis=0)
        for k in range(n_s):
            sends[k][:, f * total : (f + 1) * total] = partial.astype(BF16)
        frame_codes = frame_rows(codes, f, patch_dev)
        term_q = mm(frame_codes[:RANK], d_query, NT)
        term_v = mm(frame_codes[RANK:], d_vals, NT)
        grad_b_q = term_q if grad_b_q is None else grad_b_q + term_q
        grad_b_v = term_v if grad_b_v is None else grad_b_v + term_v
    part_ref[2 * RANK : 3 * RANK] = grad_b_q
    part_ref[3 * RANK :] = grad_b_v
    for j in range(n_s):
        cut_buf[j, :, :d_s] = grad_b_ref[:, j * d_s : (j + 1) * d_s].astype(BF16)
    for k in range(n_s):
        sends[k][:, frames * total :] = cut_buf[peer("space", k)]


def merge_kernel(frames, n_s, n_d, part_ref, packed_ref, *refs):
    recvs, sends, buf = refs[:n_s], refs[n_s : n_s + n_d], refs[n_s + n_d]
    d_s = part_ref.shape[1]
    tokens = packed_ref.shape[2]
    patch_dev = tokens // frames
    total = n_s * patch_dev
    patches = [packed_ref[j, 3 * d_s :] for j in range(n_s)]
    terms = []
    for f in range(frames):
        codes = [recv[:, f * total : (f + 1) * total].astype(F32) for recv in recvs]
        terms.append(mm(add_up(codes).astype(BF16), frame_rows(patches, f, patch_dev), NT))
    start = frames * total
    time_b = add_up([recv[:, start : start + d_s].astype(F32) for recv in recvs])
    rows = jnp.concatenate([add_up(terms), part_ref[...], time_b], axis=0)
    per = rows.shape[0] // n_d
    for d in range(n_d):
        buf[d] = rows[d * per : (d + 1) * per]
    for k in range(n_d):
        sends[k][...] = buf[peer("dp", k)]


def total_kernel(*refs):
    terms = [ref[...].astype(F32) for ref in refs[:-1]]
    while len(terms) > 1:
        terms = [terms[i] + terms[i + 1] for i in range(0, len(terms), 2)]
    refs[-1][...] = terms[0].astype(refs[-1].dtype)


def join_kernel(*refs):
    pieces, (out_ref, buf) = refs[:-2], refs[-2:]
    for k, piece in enumerate(pieces):
        buf[peer("space", k)] = piece[...]
    out_ref[...] = jnp.concatenate([buf[j] for j in range(len(pieces))], axis=1)


def final_kernel(factor, n_d, *refs):
    pieces, (a_ref, b_ref, buf) = refs[:n_d], refs[n_d:]
    for k, piece in enumerate(pieces):
        buf[peer("dp", k)] = piece[...]
    per = pieces[0].shape[0]
    half = n_d // 2
    for d in range(n_d):
        rows = buf[d].astype(F32) * factor
        target = a_ref if d < half else b_ref
        for r in range(0, per, min(per, RANK)):
            start = (d % half) * per + r
            size = min(per, RANK)
            target[start // RANK, start % RANK : start % RANK + size] = rows[r : r + size]


def mixed_kernel(frames, n_s, *refs):
    sides, pieces = refs[:n_s], refs[n_s:-3]
    mixed_ref, hidden_buf, buf = refs[-3:]
    n_t = len(pieces)
    _, d_s, tokens = hidden_buf.shape
    patch_dev = tokens // frames
    sub = patch_dev // n_t
    for k in range(n_s):
        hidden_buf[peer("space", k)] = sides[k][:d_s]
    for k, piece in enumerate(pieces):
        for f in range(frames):
            start = pl.multiple_of(f * patch_dev + peer("tm", k) * sub, sub)
            buf[pl.ds(start, sub)] = piece[f * sub : (f + 1) * sub]
    hidden = hidden_buf[...].reshape(n_s * d_s, tokens).T
    total = hidden.astype(F32) + buf[...].astype(F32)
    mixed_ref[0] = total.astype(BF16).reshape(frames, patch_dev, n_s * d_s)


def swap(array, axes):
    return lax.all_to_all(array, axes, split_axis=0, concat_axis=0, tiled=True)


def exchange(pieces, axis):
    size = lax.axis_size(axis)
    return [pieces[0]] + [
        lax.ppermute(pieces[k], axis, [(i, i ^ k) for i in range(size)]) for k in range(1, size)
    ]


def share(array, axis):
    return exchange([array] * lax.axis_size(axis), axis)


def per_device(
    patches, query_s, key_s, value_s, query_t, key_t, value_t, adapters_a, adapters_b, cotangent
):
    _, frames, patch_dev, width = patches.shape
    n_d, n_t, n_s = (lax.axis_size(name) for name in ("dp", "tm", "space"))
    tokens = frames * patch_dev
    sub = patch_dev // n_t
    d_s = width // n_s
    total = n_s * patch_dev
    factor = (tokens * n_d * n_t * n_s) ** (-0.5)
    here = lax.axis_index("space") * d_s
    downs = jnp.swapaxes(adapters_a, 1, 2)
    downs_here = lax.dynamic_slice_in_dim(downs, here, d_s, 2)
    ups_here = lax.dynamic_slice_in_dim(adapters_b, here, d_s, 2)
    dma = pltpu.SemaphoreType.DMA
    pad = -(-d_s // 128) * 128

    packed, side = call(
        functools.partial(pack_space_kernel, n_s),
        [shape((n_s, 4 * d_s, tokens), BF16), shape((n_s, d_s + 2 * RANK, tokens), BF16)],
        patches, downs, adapters_b, query_s, value_s, key_s, cotangent,
        scratch=[
            pltpu.VMEM(x.shape, BF16)
            for x in (patches, downs, adapters_b, query_s, value_s, key_s, cotangent)
        ]
        + [dma((7,))],
        hbm=True, limit=54,
    )
    time_pieces = call(
        functools.partial(pack_time_kernel, n_t, sub),
        [shape((4, frames * sub, width), BF16)] * n_t,
        query_t, key_t, value_t, cotangent,
        scratch=[dma((4 * frames * n_t,))],
        hbm=True, limit=54,
    )
    packed = swap(packed, "space")
    time_pieces = exchange(time_pieces, "tm")
    qkv, out_s = call(
        functools.partial(space_forward_kernel, frames),
        [shape((3, frames, d_s, total), BF16), shape((n_s, d_s, tokens), BF16)],
        packed,
    )
    hidden, codes = call(
        functools.partial(hidden_kernel, n_t, frames),
        [shape((n_s, d_s, tokens), BF16), shape((n_t * n_s, 8, 128), F32)],
        out_s, packed, downs_here,
    )
    codes = swap(codes, ("tm", "space"))
    sides = call(
        side_kernel, [shape((2 * d_s + 2 * RANK, tokens), BF16)] * n_s, hidden, side
    )
    sides = exchange(sides, "space")
    turned = call(turn_kernel, shape((4, width, n_t * frames * sub), BF16), *time_pieces)
    dcodes, time_grad_b, *out_t = call(
        functools.partial(time_kernel, n_t, n_s, sub),
        [shape((n_t * n_s, 8, 128), F32), shape((2 * RANK, width), F32)]
        + [shape((frames * sub, width), BF16)] * n_t,
        turned, adapters_b, codes,
        after=sides[1:],
    )
    dcodes = swap(dcodes, ("tm", "space"))
    out_t = exchange(out_t, "tm")
    *partial, part = call(
        functools.partial(space_backward_kernel, frames, n_s),
        [shape((2 * RANK, frames * total + pad), BF16)] * n_s + [shape((4 * RANK, d_s), F32)],
        qkv, hidden, time_grad_b, dcodes, downs_here, ups_here, *sides,
        scratch=[
            pltpu.VMEM((n_s, 2 * RANK, pad), BF16),
            pltpu.VMEM((n_s, d_s + 2 * RANK, tokens), BF16),
        ],
    )
    partial = exchange(partial, "space")
    rows = 8 * RANK // n_d
    sums = call(
        functools.partial(merge_kernel, frames, n_s, n_d),
        [shape((rows, d_s), F32)] * n_d,
        part, packed, *partial,
        scratch=[pltpu.VMEM((n_d, rows, d_s), F32)],
        after=out_t[1:],
    )
    sums = call(total_kernel, shape((rows, d_s), BF16), *exchange(sums, "dp"))
    sums = call(total_kernel, shape((rows, d_s), BF16), *share(sums, "tm"))
    sums = call(
        join_kernel,
        shape((rows, width), BF16),
        *share(sums, "space"),
        scratch=[pltpu.VMEM((n_s, rows, d_s), BF16)],
    )
    grads_a, grads_b = call(
        functools.partial(final_kernel, factor, n_d),
        [shape((4, RANK, width), F32)] * 2,
        *share(sums, "dp"),
        scratch=[pltpu.VMEM((n_d, rows, width), BF16)],
    )
    mixed = call(
        functools.partial(mixed_kernel, frames, n_s),
        shape(patches.shape, BF16),
        *sides, *out_t,
        scratch=[pltpu.VMEM((n_s, d_s, tokens), BF16), pltpu.VMEM((tokens, width), BF16)],
    )
    return (mixed, jnp.swapaxes(grads_a, 1, 2), grads_b)


def solution(mesh):
    token = P("dp", "tm", "space", None)
    return jax.shard_map(
        per_device,
        mesh=mesh,
        in_specs=(token,) * 7 + (P(), P(), token),
        out_specs=(token, P(), P()),
        check_vma=False,
    )
```

```python
import functools

import jax
import jax.numpy as jnp
from jax import lax
from jax.experimental import pallas as pl
from jax.experimental.pallas import tpu as pltpu
from jax.sharding import PartitionSpec as P

HEAD_DIM = 72
RANK = 16
SCALE = HEAD_DIM ** (-0.5)
F32 = jnp.float32
BF16 = jnp.bfloat16
NN = (((1,), (0,)), ((), ()))
NT = (((1,), (1,)), ((), ()))
TN = (((0,), (0,)), ((), ()))


def mm(a, b, dims=NN):
    return lax.dot_general(a, b, dims, preferred_element_type=F32)


def call(kernel, out_shape, *args, scratch=(), hbm=False, limit=24, after=(), carry=()):
    vmem = pl.BlockSpec(memory_space=pltpu.VMEM)
    anywhere = pl.BlockSpec(memory_space=pl.ANY)
    main = pl.BlockSpec(memory_space=pltpu.HBM) if hbm else vmem
    single = not isinstance(out_shape, (tuple, list))
    outs = (out_shape,) if single else tuple(out_shape)
    used, extra = len(args), len(after) + len(carry)

    def body(*refs):
        inside = refs[:used] + refs[used + extra : used + extra + len(outs)]
        kernel(*inside, *refs[used + extra + len(outs) + len(carry) :])

    result = pl.pallas_call(
        body,
        out_shape=outs + tuple(shape(x.shape, x.dtype) for x in carry),
        in_specs=[main] * used + [anywhere] * extra,
        out_specs=(anywhere if hbm else vmem,) * len(outs) + (anywhere,) * len(carry),
        scratch_shapes=list(scratch),
        input_output_aliases={used + len(after) + i: len(outs) + i for i in range(len(carry))},
        compiler_params=pltpu.CompilerParams(vmem_limit_bytes=limit * 1024 * 1024),
    )(*args, *after, *carry)
    return result[0] if single and not carry else list(result)


def shape(dims, dtype):
    return jax.ShapeDtypeStruct(tuple(dims), dtype)


def probs_of(keys, q_t, mask):
    scores = mm(keys, q_t) * SCALE
    if mask is not None:
        scores = jnp.where(mask, scores, -1e30)
    peak = jnp.max(scores, axis=0, keepdims=True)
    weights = jnp.exp(scores - peak)
    return weights * (1.0 / jnp.sum(weights, axis=0, keepdims=True))


def head_backward(probs, k_t, v_t, g_t, forward=False):
    low = probs.astype(BF16)
    dvals = mm(g_t, low, NT)
    dprob = mm(v_t.T, g_t)
    inner = jnp.sum(probs * dprob, axis=0, keepdims=True)
    dscore = (probs * (dprob - inner) * SCALE).astype(BF16)
    dquery = mm(k_t, dscore)
    out = mm(v_t, low) if forward else None
    return dquery, dvals, out


def rows_of(array, head):
    return array[head * HEAD_DIM : (head + 1) * HEAD_DIM]


def peer(axis, distance):
    return lax.axis_index(axis) ^ distance


def pack_kernel(n_t, n_s, sub, *refs):
    time_ins, ins, refs = refs[:4], refs[4:11], refs[11:]
    send_ref, sides, times = refs[0], refs[1 : 1 + n_s], refs[1 + n_s : 1 + n_s + n_t]
    refs = refs[1 + n_s + n_t :]
    buffers, (turned_ref, codes_ref, sems, out_sems) = refs[:7], refs[7:]
    k_buf, p_buf, at_buf, b_buf, q_buf, v_buf, g_buf = buffers
    copies = [
        pltpu.make_async_copy(ref, buffer, sems.at[index])
        for index, (ref, buffer) in enumerate(zip(ins, buffers))
    ]
    for copy in copies:
        copy.start()
    sent = []

    def start_copy(source, target):
        copy = pltpu.make_async_copy(source, target, out_sems.at[len(sent)])
        copy.start()
        sent.append(copy)

    frames = time_ins[0].shape[1]
    for k in range(n_t):
        start = pl.multiple_of(peer("tm", k) * sub, sub)
        for index, ref in enumerate(time_ins):
            for f in range(frames):
                start_copy(
                    ref.at[0, f, pl.ds(start, sub)],
                    times[k].at[index, f * sub : (f + 1) * sub],
                )
    d_s, tokens = turned_ref.shape[2:]

    def flat(ref):
        return ref[0].reshape(tokens, ref.shape[3])

    def turn(array, index):
        turned = array.T
        for j in range(n_s):
            turned_ref[index, j] = turned[j * d_s : (j + 1) * d_s]

    def send(array, index):
        turn(array, index)
        for j in range(n_s):
            start_copy(turned_ref.at[index, j], send_ref.at[j, index * d_s : (index + 1) * d_s])

    def side(array, index):
        turn(array, index)
        for k in range(n_s):
            place = (index - 3) * d_s
            start_copy(turned_ref.at[index, peer("space", k)], sides[k].at[place : place + d_s])

    copies[0].wait()
    send(flat(k_buf), 1)
    copies[1].wait()
    patches = flat(p_buf)
    copies[2].wait()
    copies[3].wait()
    codes_q = mm(patches, at_buf[0], NT).astype(BF16)
    codes_v = mm(patches, at_buf[1], NT).astype(BF16)
    copies[4].wait()
    query = (flat(q_buf).astype(F32) + mm(codes_q, b_buf[0])).astype(BF16)
    send(query, 0)
    copies[5].wait()
    value = (flat(v_buf).astype(F32) + mm(codes_v, b_buf[1])).astype(BF16)
    send(value, 2)
    side(patches, 3)
    codes_ref[...] = jnp.concatenate([codes_q, codes_v], axis=1).T
    for k in range(n_s):
        start_copy(codes_ref, sides[k].at[2 * d_s : 2 * d_s + 2 * RANK])
    copies[6].wait()
    side(flat(g_buf), 4)
    for copy in sent:
        copy.wait()


def frame_rows(pieces, f, patch_dev):
    return jnp.concatenate([x[:, f * patch_dev : (f + 1) * patch_dev] for x in pieces], axis=1)


def space_forward_kernel(frames, packed_ref, qkv_ref, probs_ref, *refs):
    *outs, out_buf = refs
    n_s, d_s, tokens = out_buf.shape
    patch_dev = tokens // frames
    total = n_s * patch_dev
    step = min(total, 256)
    for index in range(3):
        pieces = [packed_ref[j, index * d_s : (index + 1) * d_s] for j in range(n_s)]
        for f in range(frames):
            qkv_ref[index, f] = frame_rows(pieces, f, patch_dev)
    for f in range(frames):
        query = qkv_ref[0, f].astype(F32)
        keys = qkv_ref[1, f].astype(F32)
        vals = qkv_ref[2, f].astype(F32)
        heads = []
        for h in range(d_s // HEAD_DIM):
            k_h = rows_of(keys, h).astype(BF16)
            v_h = rows_of(vals, h).astype(BF16)
            q_h = rows_of(query, h).astype(BF16)
            parts = []
            for s in range(0, total, step):
                probs = probs_of(k_h.T, q_h[:, s : s + step], None)
                probs_ref[f, h, :, s : s + step] = probs
                parts.append(mm(v_h, probs.astype(BF16)))
            heads.append(parts[0] if len(parts) == 1 else jnp.concatenate(parts, axis=1))
        out = jnp.concatenate(heads, axis=0).astype(BF16)
        for j in range(n_s):
            out_buf[j, :, f * patch_dev : (f + 1) * patch_dev] = out[
                :, j * patch_dev : (j + 1) * patch_dev
            ]
    for k in range(n_s):
        outs[k][...] = out_buf[peer("space", k)]


def lane_block(rows):
    return lax.broadcasted_iota(jnp.int32, (rows, 128), 1) // (2 * RANK)


def fold(token_rows):
    block = lane_block(8)
    result = token_rows[0:8]
    for k in range(1, 4):
        result = jnp.where(block == k, token_rows[8 * k : 8 * k + 8], result)
    return result


def unfold(folded):
    pieces = [folded]
    for k in range(1, 4):
        pieces.append(pltpu.roll(folded, 128 - 2 * RANK * k, 1))
    return jnp.concatenate(pieces, axis=0)


def hidden_kernel(n_t, n_s, *refs):
    pieces, refs = refs[:n_s], refs[n_s:]
    p_ref, at_ref, hidden_ref = refs[:3]
    *sends, out_buf, codes_buf = refs[3:]
    _, frames, patch_dev, width = p_ref.shape
    tokens = frames * patch_dev
    sub = patch_dev // n_t
    for k in range(n_s):
        out_buf[peer("space", k)] = pieces[k][...]
    out = out_buf[...].reshape(width, tokens).T
    hidden = (p_ref[0].reshape(tokens, width).astype(F32) + out.astype(F32)).astype(BF16)
    hidden_ref[...] = hidden
    downs = jnp.concatenate([at_ref[2], at_ref[3]] * 4, axis=0)
    codes_buf[...] = mm(hidden, downs, NT).astype(BF16).astype(F32)
    for k in range(n_t):
        rows = [
            codes_buf[pl.ds(pl.multiple_of(f * patch_dev + peer("tm", k) * sub, sub), sub)]
            for f in range(frames)
        ]
        sends[k][...] = fold(jnp.concatenate(rows, axis=0))


def turn_kernel(*refs):
    pieces, out_ref = refs[:-1], refs[-1]
    for index in range(4):
        rows = jnp.concatenate([piece[index] for piece in pieces], axis=0)
        out_ref[index] = rows.T


def time_kernel(n_t, sub, x_ref, b_ref, *refs):
    codes_refs, refs = refs[:n_t], refs[n_t:]
    outs, sends, grad_b_ref = refs[:n_t], refs[n_t : n_t + 2], refs[n_t + 2]
    _, width, tokens = x_ref.shape
    codes = [unfold(ref[...]) for ref in codes_refs]
    codes = jnp.concatenate(codes, axis=0).T
    codes_q = codes[:RANK].astype(BF16)
    codes_v = codes[RANK : 2 * RANK].astype(BF16)
    query = (x_ref[0].astype(F32) + mm(b_ref[2], codes_q, TN)).astype(BF16).astype(F32)
    vals = (x_ref[2].astype(F32) + mm(b_ref[3], codes_v, TN)).astype(BF16).astype(F32)
    keys = x_ref[1].astype(F32)
    grad = x_ref[3].astype(F32)
    row = lax.broadcasted_iota(jnp.int32, (tokens, tokens), 0)
    col = lax.broadcasted_iota(jnp.int32, (tokens, tokens), 1)
    mask = lax.rem(row, sub) == lax.rem(col, sub)
    outs_h, d_query, d_vals = [], [], []
    for h in range(width // HEAD_DIM):
        k_h = rows_of(keys, h).astype(BF16)
        v_h = rows_of(vals, h).astype(BF16)
        probs = probs_of(k_h.T, rows_of(query, h).astype(BF16), mask)
        dq, dv, out = head_backward(probs, k_h, v_h, rows_of(grad, h).astype(BF16), True)
        outs_h.append(out)
        d_query.append(dq)
        d_vals.append(dv)
    d_query = jnp.concatenate(d_query, axis=0).astype(BF16)
    d_vals = jnp.concatenate(d_vals, axis=0).astype(BF16)
    d_codes = jnp.concatenate([mm(b_ref[2], d_query), mm(b_ref[3], d_vals)] * 4, axis=0)
    d_codes = d_codes.astype(BF16).astype(F32).T
    per = tokens // n_t
    for k in range(n_t):
        sends[k % 2][k // 2] = fold(d_codes[k * per : (k + 1) * per])
    out = jnp.concatenate(outs_h, axis=0).astype(BF16).T
    for k in range(n_t):
        outs[k][...] = out[k * per : (k + 1) * per]
    grad_b_ref[:RANK] = mm(codes_q, d_query, NT)
    grad_b_ref[RANK:] = mm(codes_v, d_vals, NT)


def place_codes_kernel(frames, sub, places, *refs):
    pieces, (out_ref, buf) = refs[:-2], refs[-2:]
    patch_dev = sub * len(pieces)
    for k, piece in enumerate(pieces):
        rows = unfold(piece[places[k]])
        for f in range(frames):
            start = pl.multiple_of(f * patch_dev + peer("tm", k) * sub, sub)
            buf[pl.ds(start, sub)] = rows[f * sub : (f + 1) * sub]
    out_ref[...] = buf[...].T[: 2 * RANK].astype(BF16)


def space_backward_kernel(
    frames, n_s, qkv_ref, probs_ref, hidden_ref, grad_b_ref, dcodes_ref, at_ref, at_here_ref, b_here_ref, *refs
):
    sides, sends, (part_ref, cut_buf, side_buf, dcodes_buf) = refs[:n_s], refs[n_s : 2 * n_s], refs[2 * n_s :]
    d_s = part_ref.shape[1]
    tokens = hidden_ref.shape[0]
    patch_dev = tokens // frames
    total = n_s * patch_dev
    step = min(total, 256)
    for k in range(n_s):
        side_buf[peer("space", k)] = sides[k][d_s:]
        dcodes_buf[peer("space", k)] = dcodes_ref[k]
    ups = jnp.concatenate([at_here_ref[2], at_here_ref[3]], axis=0).T
    grads = []
    for j in range(n_s):
        cot = side_buf[j, :d_s].astype(F32)
        grads.append((cot + mm(ups, dcodes_buf[j])).astype(BF16))
    codes = [side_buf[j, d_s:] for j in range(n_s)]
    grad_b_q = grad_b_v = None
    for f in range(frames):
        keys = qkv_ref[1, f].astype(F32)
        vals = qkv_ref[2, f].astype(F32)
        grad = frame_rows(grads, f, patch_dev).astype(F32)
        d_query, d_vals = [], []
        for h in range(d_s // HEAD_DIM):
            k_h = rows_of(keys, h).astype(BF16)
            v_h = rows_of(vals, h).astype(BF16)
            g_h = rows_of(grad, h).astype(BF16)
            dq_parts, dv_sum = [], None
            for s in range(0, total, step):
                probs = probs_ref[f, h, :, s : s + step]
                dq, dv, _ = head_backward(probs, k_h, v_h, g_h[:, s : s + step])
                dq_parts.append(dq)
                dv_sum = dv if dv_sum is None else dv_sum + dv
            d_query.append(
                dq_parts[0] if len(dq_parts) == 1 else jnp.concatenate(dq_parts, axis=1)
            )
            d_vals.append(dv_sum)
        d_query = jnp.concatenate(d_query, axis=0).astype(BF16)
        d_vals = jnp.concatenate(d_vals, axis=0).astype(BF16)
        partial = jnp.concatenate([mm(b_here_ref[0], d_query), mm(b_here_ref[1], d_vals)], axis=0)
        for k in range(n_s):
            sends[k][:, f * total : (f + 1) * total] = partial.astype(BF16)
        frame_codes = frame_rows(codes, f, patch_dev)
        term_q = mm(frame_codes[:RANK], d_query, NT)
        term_v = mm(frame_codes[RANK:], d_vals, NT)
        grad_b_q = term_q if grad_b_q is None else grad_b_q + term_q
        grad_b_v = term_v if grad_b_v is None else grad_b_v + term_v
    part_ref[:RANK] = grad_b_q
    part_ref[RANK:] = grad_b_v
    grad_a = mm(dcodes_ref[0], hidden_ref[...])
    pad = -(-d_s // 128) * 128
    for j in range(n_s):
        cut_buf[j, 0, :, :d_s] = grad_a[:, j * d_s : (j + 1) * d_s].astype(BF16)
        cut_buf[j, 1, :, :d_s] = grad_b_ref[:, j * d_s : (j + 1) * d_s].astype(BF16)
    for k in range(n_s):
        for index in range(2):
            start = frames * total + index * pad
            sends[k][:, start : start + pad] = cut_buf[peer("space", k), index]


def add_up(terms):
    result = None
    for term in terms:
        result = term if result is None else result + term
    return result


def merge_kernel(frames, n_s, n_d, part_ref, *refs):
    sides, recvs, refs = refs[:n_s], refs[n_s : 2 * n_s], refs[2 * n_s :]
    sends, (buf, patches_buf) = refs[:n_d], refs[n_d:]
    d_s = part_ref.shape[1]
    tokens = sides[0].shape[1]
    for k in range(n_s):
        patches_buf[peer("space", k)] = sides[k][:d_s]
    patch_dev = tokens // frames
    total = n_s * patch_dev
    pad = -(-d_s // 128) * 128
    patches = [patches_buf[j] for j in range(n_s)]
    terms = []
    for f in range(frames):
        codes = [recv[:, f * total : (f + 1) * total].astype(F32) for recv in recvs]
        terms.append(mm(add_up(codes).astype(BF16), frame_rows(patches, f, patch_dev), NT))
    start = frames * total
    time_a = add_up([recv[:, start : start + d_s].astype(F32) for recv in recvs])
    time_b = add_up([recv[:, start + pad : start + pad + d_s].astype(F32) for recv in recvs])
    rows = jnp.concatenate([add_up(terms), time_a, part_ref[...], time_b], axis=0)
    per = rows.shape[0] // n_d
    for d in range(n_d):
        buf[d] = rows[d * per : (d + 1) * per]
    for k in range(n_d):
        sends[k][...] = buf[peer("dp", k)]


def total_kernel(*refs):
    terms = [ref[...].astype(F32) for ref in refs[:-1]]
    while len(terms) > 1:
        terms = [terms[i] + terms[i + 1] for i in range(0, len(terms), 2)]
    refs[-1][...] = terms[0].astype(refs[-1].dtype)


def join_kernel(*refs):
    pieces, (out_ref, buf) = refs[:-2], refs[-2:]
    for k, piece in enumerate(pieces):
        buf[peer("space", k)] = piece[...]
    out_ref[...] = jnp.concatenate([buf[j] for j in range(len(pieces))], axis=1)


def final_kernel(factor, n_d, *refs):
    pieces, (a_ref, b_ref, buf) = refs[:n_d], refs[n_d:]
    for k, piece in enumerate(pieces):
        buf[peer("dp", k)] = piece[...]
    per = pieces[0].shape[0]
    half = n_d // 2
    for d in range(n_d):
        rows = buf[d].astype(F32) * factor
        target = a_ref if d < half else b_ref
        for r in range(0, per, min(per, RANK)):
            start = (d % half) * per + r
            size = min(per, RANK)
            target[start // RANK, start % RANK : start % RANK + size] = rows[r : r + size]


def mixed_kernel(frames, hidden_ref, *refs):
    pieces, (mixed_ref, buf) = refs[:-2], refs[-2:]
    n_t = len(pieces)
    tokens, width = hidden_ref.shape
    patch_dev = tokens // frames
    sub = patch_dev // n_t
    for k, piece in enumerate(pieces):
        for f in range(frames):
            start = pl.multiple_of(f * patch_dev + peer("tm", k) * sub, sub)
            buf[pl.ds(start, sub)] = piece[f * sub : (f + 1) * sub]
    total = hidden_ref[...].astype(F32) + buf[...].astype(F32)
    mixed_ref[0] = total.astype(BF16).reshape(frames, patch_dev, width)


def exchange(pieces, axis):
    size = lax.axis_size(axis)
    return [pieces[0]] + [
        lax.ppermute(pieces[k], axis, [(i, i ^ k) for i in range(size)]) for k in range(1, size)
    ]


def swap(array, axes):
    return lax.all_to_all(array, axes, split_axis=0, concat_axis=0, tiled=True)


def stack_kernel(places, *refs):
    for index, (ref, place) in enumerate(zip(refs[:-1], places)):
        refs[-1][index] = ref[place]


def exchange_steps(even, odd, axis):
    size = lax.axis_size(axis)
    held = [((even, odd)[k % 2], k // 2) for k in range(size)]
    step = 1
    while step < size:
        moving = [k for k in range(size) if k & step]
        sent = odd
        if step > 1:
            arrays, places = zip(*[held[k] for k in moving])
            sent = call(
                functools.partial(stack_kernel, places), shape(odd.shape, odd.dtype), *arrays
            )
        got = lax.ppermute(sent, axis, [(i, i ^ step) for i in range(size)])
        for index, k in enumerate(moving):
            held[k] = (got, index)
        step *= 2
    return [array for array, _ in held], [place for _, place in held]


def double_kernel(own_ref, got_ref, out_ref):
    size = own_ref.shape[0]
    out_ref[:size] = own_ref[...]
    out_ref[size:] = got_ref[...]


def share_steps(array, axis):
    size = lax.axis_size(axis)
    held = array[None]
    step = 1
    while step < size:
        got = lax.ppermute(held, axis, [(i, i ^ step) for i in range(size)])
        held = call(double_kernel, shape((2 * step,) + array.shape, array.dtype), held, got)
        step *= 2
    return held


def share(array, axis):
    return exchange([array] * lax.axis_size(axis), axis)


def per_device(
    patches, query_s, key_s, value_s, query_t, key_t, value_t, adapters_a, adapters_b, cotangent
):
    _, frames, patch_dev, width = patches.shape
    n_d, n_t, n_s = (lax.axis_size(name) for name in ("dp", "tm", "space"))
    tokens = frames * patch_dev
    sub = patch_dev // n_t
    d_s = width // n_s
    total = n_s * patch_dev
    factor = (tokens * n_d * n_t * n_s) ** (-0.5)
    here = lax.axis_index("space") * d_s
    downs = jnp.swapaxes(adapters_a, 1, 2)
    downs_here = lax.dynamic_slice_in_dim(downs, here, d_s, 2)
    ups_here = lax.dynamic_slice_in_dim(adapters_b, here, d_s, 2)
    dma = pltpu.SemaphoreType.DMA
    pad = -(-d_s // 128) * 128

    spatial = (key_s, patches, downs, adapters_b, query_s, value_s, cotangent)
    send, *pieces = call(
        functools.partial(pack_kernel, n_t, n_s, sub),
        [shape((n_s, 3 * d_s, tokens), BF16)]
        + [shape((2 * d_s + 2 * RANK, tokens), BF16)] * n_s
        + [shape((4, frames * sub, width), BF16)] * n_t,
        query_t, key_t, value_t, cotangent, *spatial,
        scratch=[pltpu.VMEM(x.shape, BF16) for x in spatial]
        + [
            pltpu.VMEM((5, n_s, d_s, tokens), BF16),
            pltpu.VMEM((2 * RANK, tokens), BF16),
            dma((7,)),
            dma((6 * n_s + 4 * frames * n_t,)),
        ],
        hbm=True, limit=54,
    )
    time_pieces = exchange(pieces[n_s:], "tm")
    packed = swap(send, "space")
    sides = exchange(pieces[:n_s], "space")
    qkv, probs, *out_s = call(
        functools.partial(space_forward_kernel, frames),
        [shape((3, frames, d_s, total), BF16), shape((frames, d_s // HEAD_DIM, total, total), F32)]
        + [shape((d_s, tokens), BF16)] * n_s,
        packed,
        scratch=[pltpu.VMEM((n_s, d_s, tokens), BF16)],
    )
    out_s = exchange(out_s, "space")
    hidden, *codes = call(
        functools.partial(hidden_kernel, n_t, n_s),
        [shape((tokens, width), BF16)] + [shape((8, 128), F32)] * n_t,
        *out_s, patches, downs,
        scratch=[pltpu.VMEM((n_s, d_s, tokens), BF16), pltpu.VMEM((tokens, 128), F32)],
    )
    codes = exchange(codes, "tm")
    turned = call(turn_kernel, shape((4, width, n_t * frames * sub), BF16), *time_pieces)
    timed = call(
        functools.partial(time_kernel, n_t, sub),
        [shape((frames * sub, width), BF16)] * n_t
        + [shape((n_t // 2, 8, 128), F32)] * 2
        + [shape((2 * RANK, width), F32)],
        turned, adapters_b, *codes,
        after=sides[1:],
    )
    out_t, (even, odd, time_grad_b) = timed[:n_t], timed[n_t:]
    dcodes, places = exchange_steps(even, odd, "tm")
    dcodes = call(
        functools.partial(place_codes_kernel, frames, sub, places),
        shape((2 * RANK, tokens), BF16),
        *dcodes,
        scratch=[pltpu.VMEM((tokens, 128), F32)],
    )
    dcodes = share_steps(dcodes, "space")

    def late(k):
        return lax.ppermute(out_t[k], "tm", [(i, i ^ k) for i in range(n_t)])

    out_t[1] = late(1)
    backward = call(
        functools.partial(space_backward_kernel, frames, n_s),
        [shape((2 * RANK, frames * total + 2 * pad), BF16)] * n_s + [shape((2 * RANK, d_s), F32)],
        qkv, probs, hidden, time_grad_b, dcodes, downs, downs_here, ups_here, *sides,
        scratch=[
            pltpu.VMEM((n_s, 2, 2 * RANK, pad), BF16),
            pltpu.VMEM((n_s, d_s + 2 * RANK, tokens), BF16),
            pltpu.VMEM((n_s, 2 * RANK, tokens), BF16),
        ],
        after=[out_t[1]],
        carry=[out_t[2]],
    )
    partial, part, out_t[2] = backward[:n_s], backward[n_s], backward[n_s + 1]
    partial = exchange(partial, "space")
    out_t[2] = late(2)
    rows = 8 * RANK // n_d
    *sums, out_t[3] = call(
        functools.partial(merge_kernel, frames, n_s, n_d),
        [shape((rows, d_s), F32)] * n_d,
        part, *sides, *partial,
        scratch=[pltpu.VMEM((n_d, rows, d_s), F32), pltpu.VMEM((n_s, d_s, tokens), BF16)],
        after=[out_t[2]],
        carry=[out_t[3]],
    )
    out_t[3] = late(3)
    sums = call(total_kernel, shape((rows, d_s), BF16), *exchange(sums, "dp"))
    sums = call(total_kernel, shape((rows, d_s), BF16), *share(sums, "tm"), after=[out_t[3]])
    sums = call(
        join_kernel,
        shape((rows, width), BF16),
        *share(sums, "space"),
        scratch=[pltpu.VMEM((n_s, rows, d_s), BF16)],
    )
    grads_a, grads_b = call(
        functools.partial(final_kernel, factor, n_d),
        [shape((4, RANK, width), F32)] * 2,
        *share(sums, "dp"),
        scratch=[pltpu.VMEM((n_d, rows, width), BF16)],
    )
    mixed = call(
        functools.partial(mixed_kernel, frames),
        shape(patches.shape, BF16),
        hidden, *out_t,
        scratch=[pltpu.VMEM((tokens, width), BF16)],
    )
    return (mixed, jnp.swapaxes(grads_a, 1, 2), grads_b)


def solution(mesh):
    token = P("dp", "tm", "space", None)
    return jax.shard_map(
        per_device,
        mesh=mesh,
        in_specs=(token,) * 7 + (P(), P(), token),
        out_specs=(token, P(), P()),
        check_vma=False,
    )
```

```python
import functools

import jax
import jax.numpy as jnp
from jax import lax
from jax.experimental import pallas as pl
from jax.experimental.pallas import tpu as pltpu
from jax.sharding import PartitionSpec as P

HEAD_DIM = 72
RANK = 16
SCALE = HEAD_DIM ** (-0.5)
F32 = jnp.float32
BF16 = jnp.bfloat16
NN = (((1,), (0,)), ((), ()))
NT = (((1,), (1,)), ((), ()))
TN = (((0,), (0,)), ((), ()))


def mm(a, b, dims=NN):
    return lax.dot_general(a, b, dims, preferred_element_type=F32)


def call(kernel, out_shape, *args, scratch=(), hbm=False, limit=24, after=(), carry=()):
    vmem = pl.BlockSpec(memory_space=pltpu.VMEM)
    anywhere = pl.BlockSpec(memory_space=pl.ANY)
    main = pl.BlockSpec(memory_space=pltpu.HBM) if hbm else vmem
    single = not isinstance(out_shape, (tuple, list))
    outs = (out_shape,) if single else tuple(out_shape)
    used, extra = len(args), len(after) + len(carry)

    def body(*refs):
        inside = refs[:used] + refs[used + extra : used + extra + len(outs)]
        kernel(*inside, *refs[used + extra + len(outs) + len(carry) :])

    result = pl.pallas_call(
        body,
        out_shape=outs + tuple(shape(x.shape, x.dtype) for x in carry),
        in_specs=[main] * used + [anywhere] * extra,
        out_specs=(anywhere if hbm else vmem,) * len(outs) + (anywhere,) * len(carry),
        scratch_shapes=list(scratch),
        input_output_aliases={used + len(after) + i: len(outs) + i for i in range(len(carry))},
        compiler_params=pltpu.CompilerParams(vmem_limit_bytes=limit * 1024 * 1024),
    )(*args, *after, *carry)
    return result[0] if single and not carry else list(result)


def shape(dims, dtype):
    return jax.ShapeDtypeStruct(tuple(dims), dtype)


def probs_of(keys, q_t, mask):
    scores = mm(keys, q_t) * SCALE
    if mask is not None:
        scores = jnp.where(mask, scores, -1e30)
    peak = jnp.max(scores, axis=0, keepdims=True)
    weights = jnp.exp(scores - peak)
    return weights * (1.0 / jnp.sum(weights, axis=0, keepdims=True))


def head_backward(probs, k_t, v_t, g_t, forward=False):
    low = probs.astype(BF16)
    dvals = mm(g_t, low, NT)
    dprob = mm(v_t.T, g_t)
    inner = jnp.sum(probs * dprob, axis=0, keepdims=True)
    dscore = (probs * (dprob - inner) * SCALE).astype(BF16)
    dquery = mm(k_t, dscore)
    out = mm(v_t, low) if forward else None
    return dquery, dvals, out


def rows_of(array, head):
    return array[head * HEAD_DIM : (head + 1) * HEAD_DIM]


def peer(axis, distance):
    return lax.axis_index(axis) ^ distance


def pack_kernel(n_t, n_s, sub, *refs):
    time_ins, ins, refs = refs[:4], refs[4:11], refs[11:]
    firsts, sides, times = refs[:n_s], refs[n_s : 2 * n_s], refs[2 * n_s : 2 * n_s + n_t]
    refs = refs[2 * n_s + n_t :]
    time_bufs, buffers, (turned_ref, codes_ref, sems, out_sems) = refs[:4], refs[4:11], refs[11:]
    k_buf, p_buf, at_buf, b_buf, q_buf, v_buf, g_buf = buffers
    copies = [
        pltpu.make_async_copy(ref, buffer, sems.at[index])
        for index, (ref, buffer) in enumerate(zip(ins + time_ins, buffers + time_bufs))
    ]
    for copy in copies:
        copy.start()
    sent = []

    def start_copy(source, target):
        copy = pltpu.make_async_copy(source, target, out_sems.at[len(sent)])
        copy.start()
        sent.append(copy)

    d_s, tokens = turned_ref.shape[2:]

    def flat(ref):
        return ref[0].reshape(tokens, ref.shape[3])

    def turn(array, index):
        turned = array.T
        for j in range(n_s):
            turned_ref[index, j] = turned[j * d_s : (j + 1) * d_s]

    def send(array, index):
        turn(array, index)
        for k in range(n_s):
            targets, place = (firsts, index) if index < 3 else (sides, index - 3)
            start_copy(
                turned_ref.at[index, peer("space", k)],
                targets[k].at[place * d_s : (place + 1) * d_s],
            )

    copies[0].wait()
    send(flat(k_buf), 1)
    copies[1].wait()
    patches = flat(p_buf)
    copies[2].wait()
    copies[3].wait()
    codes_q = mm(patches, at_buf[0], NT).astype(BF16)
    codes_v = mm(patches, at_buf[1], NT).astype(BF16)
    copies[4].wait()
    query = (flat(q_buf).astype(F32) + mm(codes_q, b_buf[0])).astype(BF16)
    send(query, 0)
    copies[5].wait()
    value = (flat(v_buf).astype(F32) + mm(codes_v, b_buf[1])).astype(BF16)
    send(value, 2)
    send(patches, 3)
    codes_ref[...] = jnp.concatenate([codes_q, codes_v], axis=1).T
    for k in range(n_s):
        start_copy(codes_ref, sides[k].at[2 * d_s : 2 * d_s + 2 * RANK])
    frames = time_ins[0].shape[1]
    for index, buffer in enumerate(time_bufs):
        copies[7 + index].wait()
        for k in range(n_t):
            start = pl.multiple_of(peer("tm", k) * sub, sub)
            for f in range(frames):
                start_copy(
                    buffer.at[0, f, pl.ds(start, sub)],
                    times[k].at[index, f * sub : (f + 1) * sub],
                )
    copies[6].wait()
    send(flat(g_buf), 4)
    for copy in sent:
        copy.wait()


def frame_rows(pieces, f, patch_dev):
    return jnp.concatenate([x[:, f * patch_dev : (f + 1) * patch_dev] for x in pieces], axis=1)


def space_forward_kernel(frames, n_s, *refs):
    packed, (qkv_ref, probs_ref, *outs) = refs[:n_s], refs[n_s:]
    d_s, tokens = outs[0].shape
    patch_dev = tokens // frames
    total = n_s * patch_dev
    step = min(total, 256)
    for index in range(3):
        pieces = [x[index * d_s : (index + 1) * d_s] for x in packed]
        for f in range(frames):
            qkv_ref[index, f] = frame_rows(pieces, f, patch_dev)
    for f in range(frames):
        query = qkv_ref[0, f].astype(F32)
        keys = qkv_ref[1, f].astype(F32)
        vals = qkv_ref[2, f].astype(F32)
        heads = []
        for h in range(d_s // HEAD_DIM):
            k_h = rows_of(keys, h).astype(BF16)
            v_h = rows_of(vals, h).astype(BF16)
            q_h = rows_of(query, h).astype(BF16)
            parts = []
            for s in range(0, total, step):
                probs = probs_of(k_h.T, q_h[:, s : s + step], None)
                probs_ref[f, h, :, s : s + step] = probs
                parts.append(mm(v_h, probs.astype(BF16)))
            heads.append(parts[0] if len(parts) == 1 else jnp.concatenate(parts, axis=1))
        out = jnp.concatenate(heads, axis=0).astype(BF16)
        for k in range(n_s):
            outs[k][:, f * patch_dev : (f + 1) * patch_dev] = out[
                :, k * patch_dev : (k + 1) * patch_dev
            ]


def lane_block(rows):
    return lax.broadcasted_iota(jnp.int32, (rows, 128), 1) // (2 * RANK)


def fold(token_rows):
    block = lane_block(8)
    result = token_rows[0:8]
    for k in range(1, 4):
        result = jnp.where(block == k, token_rows[8 * k : 8 * k + 8], result)
    return result


def unfold(folded):
    pieces = [folded]
    for k in range(1, 4):
        pieces.append(pltpu.roll(folded, 128 - 2 * RANK * k, 1))
    return jnp.concatenate(pieces, axis=0)


def hidden_kernel(n_t, n_s, *refs):
    pieces, refs = refs[:n_s], refs[n_s:]
    p_ref, at_ref, hidden_ref = refs[:3]
    *sends, out_buf, codes_buf = refs[3:]
    _, frames, patch_dev, width = p_ref.shape
    tokens = frames * patch_dev
    sub = patch_dev // n_t
    for k in range(n_s):
        out_buf[peer("space", k)] = pieces[k][...]
    out = out_buf[...].reshape(width, tokens).T
    hidden = (p_ref[0].reshape(tokens, width).astype(F32) + out.astype(F32)).astype(BF16)
    hidden_ref[...] = hidden
    downs = jnp.concatenate([at_ref[2], at_ref[3]] * 4, axis=0)
    codes_buf[...] = mm(hidden, downs, NT).astype(BF16).astype(F32)
    for k in range(n_t):
        rows = [
            codes_buf[pl.ds(pl.multiple_of(f * patch_dev + peer("tm", k) * sub, sub), sub)]
            for f in range(frames)
        ]
        sends[k][...] = fold(jnp.concatenate(rows, axis=0))


def turn_kernel(*refs):
    pieces, out_ref = refs[:-1], refs[-1]
    for index in range(4):
        rows = jnp.concatenate([piece[index] for piece in pieces], axis=0)
        out_ref[index] = rows.T


def time_kernel(n_t, sub, x_ref, b_ref, *refs):
    codes_refs, refs = refs[:n_t], refs[n_t:]
    outs, sends, grad_b_ref = refs[:n_t], refs[n_t : n_t + 2], refs[n_t + 2]
    _, width, tokens = x_ref.shape
    codes = [unfold(ref[...]) for ref in codes_refs]
    codes = jnp.concatenate(codes, axis=0).T
    codes_q = codes[:RANK].astype(BF16)
    codes_v = codes[RANK : 2 * RANK].astype(BF16)
    query = (x_ref[0].astype(F32) + mm(b_ref[2], codes_q, TN)).astype(BF16).astype(F32)
    vals = (x_ref[2].astype(F32) + mm(b_ref[3], codes_v, TN)).astype(BF16).astype(F32)
    keys = x_ref[1].astype(F32)
    grad = x_ref[3].astype(F32)
    row = lax.broadcasted_iota(jnp.int32, (tokens, tokens), 0)
    col = lax.broadcasted_iota(jnp.int32, (tokens, tokens), 1)
    mask = lax.rem(row, sub) == lax.rem(col, sub)
    outs_h, d_query, d_vals = [], [], []
    for h in range(width // HEAD_DIM):
        k_h = rows_of(keys, h).astype(BF16)
        v_h = rows_of(vals, h).astype(BF16)
        probs = probs_of(k_h.T, rows_of(query, h).astype(BF16), mask)
        dq, dv, out = head_backward(probs, k_h, v_h, rows_of(grad, h).astype(BF16), True)
        outs_h.append(out)
        d_query.append(dq)
        d_vals.append(dv)
    d_query = jnp.concatenate(d_query, axis=0).astype(BF16)
    d_vals = jnp.concatenate(d_vals, axis=0).astype(BF16)
    d_codes = jnp.concatenate([mm(b_ref[2], d_query), mm(b_ref[3], d_vals)] * 4, axis=0)
    d_codes = d_codes.astype(BF16).astype(F32).T
    per = tokens // n_t
    for k in range(n_t):
        sends[k % 2][k // 2] = fold(d_codes[k * per : (k + 1) * per])
    out = jnp.concatenate(outs_h, axis=0).astype(BF16).T
    for k in range(n_t):
        outs[k][...] = out[k * per : (k + 1) * per]
    grad_b_ref[:RANK] = mm(codes_q, d_query, NT)
    grad_b_ref[RANK:] = mm(codes_v, d_vals, NT)


def place_codes_kernel(frames, sub, places, *refs):
    pieces, (out_ref, buf) = refs[:-2], refs[-2:]
    patch_dev = sub * len(pieces)
    for k, piece in enumerate(pieces):
        rows = unfold(piece[places[k]])
        for f in range(frames):
            start = pl.multiple_of(f * patch_dev + peer("tm", k) * sub, sub)
            buf[pl.ds(start, sub)] = rows[f * sub : (f + 1) * sub]
    out_ref[...] = buf[...].T[: 2 * RANK].astype(BF16)


def space_backward_kernel(
    frames, n_s, qkv_ref, probs_ref, hidden_ref, grad_b_ref, dcodes_ref, at_ref, at_here_ref, b_here_ref, *refs
):
    sides, sends, (part_ref, cut_buf) = refs[:n_s], refs[n_s : 2 * n_s], refs[2 * n_s :]
    d_s = part_ref.shape[1]
    tokens = hidden_ref.shape[0]
    patch_dev = tokens // frames
    total = n_s * patch_dev
    step = min(total, 256)
    ups = jnp.concatenate([at_here_ref[2], at_here_ref[3]], axis=0).T
    grads = []
    for k in range(n_s):
        cot = sides[k][d_s : 2 * d_s].astype(F32)
        grads.append((cot + mm(ups, dcodes_ref[k])).astype(BF16))
    codes = [x[2 * d_s :] for x in sides]
    grad_b_q = grad_b_v = None
    for f in range(frames):
        keys = qkv_ref[1, f].astype(F32)
        vals = qkv_ref[2, f].astype(F32)
        grad = frame_rows(grads, f, patch_dev).astype(F32)
        d_query, d_vals = [], []
        for h in range(d_s // HEAD_DIM):
            k_h = rows_of(keys, h).astype(BF16)
            v_h = rows_of(vals, h).astype(BF16)
            g_h = rows_of(grad, h).astype(BF16)
            dq_parts, dv_sum = [], None
            for s in range(0, total, step):
                probs = probs_ref[f, h, :, s : s + step]
                dq, dv, _ = head_backward(probs, k_h, v_h, g_h[:, s : s + step])
                dq_parts.append(dq)
                dv_sum = dv if dv_sum is None else dv_sum + dv
            d_query.append(
                dq_parts[0] if len(dq_parts) == 1 else jnp.concatenate(dq_parts, axis=1)
            )
            d_vals.append(dv_sum)
        d_query = jnp.concatenate(d_query, axis=0).astype(BF16)
        d_vals = jnp.concatenate(d_vals, axis=0).astype(BF16)
        partial = jnp.concatenate([mm(b_here_ref[0], d_query), mm(b_here_ref[1], d_vals)], axis=0)
        partial = partial.astype(BF16)
        blocks = [partial[:, m * patch_dev : (m + 1) * patch_dev] for m in range(n_s)]
        for k in range(n_s):
            turned = jnp.concatenate([blocks[m ^ k] for m in range(n_s)], axis=1)
            sends[k][:, f * total : (f + 1) * total] = turned
        frame_codes = frame_rows(codes, f, patch_dev)
        term_q = mm(frame_codes[:RANK], d_query, NT)
        term_v = mm(frame_codes[RANK:], d_vals, NT)
        grad_b_q = term_q if grad_b_q is None else grad_b_q + term_q
        grad_b_v = term_v if grad_b_v is None else grad_b_v + term_v
    part_ref[:RANK] = grad_b_q
    part_ref[RANK:] = grad_b_v
    grad_a = mm(dcodes_ref[0], hidden_ref[...])
    pad = -(-d_s // 128) * 128
    for j in range(n_s):
        cut_buf[j, 0, :, :d_s] = grad_a[:, j * d_s : (j + 1) * d_s].astype(BF16)
        cut_buf[j, 1, :, :d_s] = grad_b_ref[:, j * d_s : (j + 1) * d_s].astype(BF16)
    for k in range(n_s):
        for index in range(2):
            start = frames * total + index * pad
            sends[k][:, start : start + pad] = cut_buf[peer("space", k), index]


def add_up(terms):
    result = None
    for term in terms:
        result = term if result is None else result + term
    return result


def merge_kernel(frames, n_s, n_d, part_ref, *refs):
    sides, recvs, refs = refs[:n_s], refs[n_s : 2 * n_s], refs[2 * n_s :]
    sends, buf = refs[:n_d], refs[n_d]
    d_s = part_ref.shape[1]
    tokens = sides[0].shape[1]
    patch_dev = tokens // frames
    total = n_s * patch_dev
    pad = -(-d_s // 128) * 128
    patches = [x[:d_s] for x in sides]
    terms = []
    for f in range(frames):
        codes = [recv[:, f * total : (f + 1) * total].astype(F32) for recv in recvs]
        terms.append(mm(add_up(codes).astype(BF16), frame_rows(patches, f, patch_dev), NT))
    start = frames * total
    time_a = add_up([recv[:, start : start + d_s].astype(F32) for recv in recvs])
    time_b = add_up([recv[:, start + pad : start + pad + d_s].astype(F32) for recv in recvs])
    rows = jnp.concatenate([add_up(terms), time_a, part_ref[...], time_b], axis=0)
    per = rows.shape[0] // n_d
    for d in range(n_d):
        buf[d] = rows[d * per : (d + 1) * per]
    for k in range(n_d):
        sends[k][...] = buf[peer("dp", k)]


def total_kernel(*refs):
    terms = [ref[...].astype(F32) for ref in refs[:-1]]
    while len(terms) > 1:
        terms = [terms[i] + terms[i + 1] for i in range(0, len(terms), 2)]
    refs[-1][...] = terms[0].astype(refs[-1].dtype)


def join_kernel(*refs):
    pieces, (out_ref, buf) = refs[:-2], refs[-2:]
    for k, piece in enumerate(pieces):
        buf[peer("space", k)] = piece[...]
    out_ref[...] = jnp.concatenate([buf[j] for j in range(len(pieces))], axis=1)


def final_kernel(factor, n_d, *refs):
    pieces, (a_ref, b_ref, buf) = refs[:n_d], refs[n_d:]
    for k, piece in enumerate(pieces):
        buf[peer("dp", k)] = piece[...]
    per = pieces[0].shape[0]
    half = n_d // 2
    for d in range(n_d):
        rows = buf[d].astype(F32) * factor
        target = a_ref if d < half else b_ref
        for r in range(0, per, min(per, RANK)):
            start = (d % half) * per + r
            size = min(per, RANK)
            target[start // RANK, start % RANK : start % RANK + size] = rows[r : r + size]


def mixed_kernel(frames, hidden_ref, *refs):
    pieces, (mixed_ref, buf) = refs[:-2], refs[-2:]
    n_t = len(pieces)
    tokens, width = hidden_ref.shape
    patch_dev = tokens // frames
    sub = patch_dev // n_t
    for k, piece in enumerate(pieces):
        for f in range(frames):
            start = pl.multiple_of(f * patch_dev + peer("tm", k) * sub, sub)
            buf[pl.ds(start, sub)] = piece[f * sub : (f + 1) * sub]
    total = hidden_ref[...].astype(F32) + buf[...].astype(F32)
    mixed_ref[0] = total.astype(BF16).reshape(frames, patch_dev, width)


def exchange(pieces, axis):
    return [pieces[0]] + hops(pieces[1:], axis, 1)


def stack_kernel(places, *refs):
    for index, (ref, place) in enumerate(zip(refs[:-1], places)):
        refs[-1][index] = ref[place]


def exchange_steps(even, odd, axis, carry=()):
    size = lax.axis_size(axis)
    held = [((even, odd)[k % 2], k // 2) for k in range(size)]
    step = 1
    while step < size:
        moving = [k for k in range(size) if k & step]
        sent = odd
        if step > 1:
            arrays, places = zip(*[held[k] for k in moving])
            sent, *carry = call(
                functools.partial(stack_kernel, places),
                [shape(odd.shape, odd.dtype)],
                *arrays,
                carry=carry,
            )
        got = lax.ppermute(sent, axis, [(i, i ^ step) for i in range(size)])
        for index, k in enumerate(moving):
            held[k] = (got, index)
        step *= 2
    return [array for array, _ in held], [place for _, place in held], carry


def double_kernel(own_ref, got_ref, out_ref):
    size = own_ref.shape[0]
    out_ref[:size] = own_ref[...]
    out_ref[size:] = got_ref[...]


def share_steps(array, axis):
    size = lax.axis_size(axis)
    held = array[None]
    step = 1
    while step < size:
        got = lax.ppermute(held, axis, [(i, i ^ step) for i in range(size)])
        held = call(double_kernel, shape((2 * step,) + array.shape, array.dtype), held, got)
        step *= 2
    return held


def hops(arrays, axis, first):
    size = lax.axis_size(axis)
    return [
        lax.ppermute(array, axis, [(i, i ^ k) for i in range(size)])
        for k, array in enumerate(arrays, first)
    ]


def share(array, axis):
    return exchange([array] * lax.axis_size(axis), axis)


def per_device(
    patches, query_s, key_s, value_s, query_t, key_t, value_t, adapters_a, adapters_b, cotangent
):
    _, frames, patch_dev, width = patches.shape
    n_d, n_t, n_s = (lax.axis_size(name) for name in ("dp", "tm", "space"))
    tokens = frames * patch_dev
    sub = patch_dev // n_t
    d_s = width // n_s
    total = n_s * patch_dev
    factor = (tokens * n_d * n_t * n_s) ** (-0.5)
    here = lax.axis_index("space") * d_s
    downs = jnp.swapaxes(adapters_a, 1, 2)
    downs_here = lax.dynamic_slice_in_dim(downs, here, d_s, 2)
    ups_here = lax.dynamic_slice_in_dim(adapters_b, here, d_s, 2)
    dma = pltpu.SemaphoreType.DMA
    pad = -(-d_s // 128) * 128

    spatial = (key_s, patches, downs, adapters_b, query_s, value_s, cotangent)
    pieces = call(
        functools.partial(pack_kernel, n_t, n_s, sub),
        [shape((3 * d_s, tokens), BF16)] * n_s
        + [shape((2 * d_s + 2 * RANK, tokens), BF16)] * n_s
        + [shape((4, frames * sub, width), BF16)] * n_t,
        query_t, key_t, value_t, cotangent, *spatial,
        scratch=[pltpu.VMEM(query_t.shape, BF16)] * 4
        + [pltpu.VMEM(x.shape, BF16) for x in spatial]
        + [
            pltpu.VMEM((5, n_s, d_s, tokens), BF16),
            pltpu.VMEM((2 * RANK, tokens), BF16),
            dma((11,)),
            dma((6 * n_s + 4 * frames * n_t,)),
        ],
        hbm=True, limit=54,
    )
    firsts = exchange(pieces[:n_s], "space")
    sides = pieces[n_s : 2 * n_s]
    time_pieces = exchange(pieces[2 * n_s :], "tm")
    qkv, probs, *out_s = call(
        functools.partial(space_forward_kernel, frames, n_s),
        [shape((3, frames, d_s, total), BF16), shape((frames, d_s // HEAD_DIM, total, total), F32)]
        + [shape((d_s, tokens), BF16)] * n_s,
        *firsts,
        after=[time_pieces[2]],
    )
    out_s = exchange(out_s, "space")
    third = -(-(n_s - 1) // 3)
    hidden, *codes = call(
        functools.partial(hidden_kernel, n_t, n_s),
        [shape((tokens, width), BF16)] + [shape((8, 128), F32)] * n_t,
        *out_s, patches, downs,
        carry=sides[1 : 1 + third],
        scratch=[pltpu.VMEM((n_s, d_s, tokens), BF16), pltpu.VMEM((tokens, 128), F32)],
    )
    codes, sides[1 : 1 + third] = exchange(codes[:n_t], "tm"), hops(codes[n_t:], "space", 1)
    turned = call(turn_kernel, shape((4, width, n_t * frames * sub), BF16), *time_pieces)
    timed = call(
        functools.partial(time_kernel, n_t, sub),
        [shape((frames * sub, width), BF16)] * n_t
        + [shape((n_t // 2, 8, 128), F32)] * 2
        + [shape((2 * RANK, width), F32)],
        turned, adapters_b, *codes,
        after=sides[1 : 1 + third],
        carry=sides[1 + third : 1 + 2 * third],
    )
    out_t, (even, odd, time_grad_b) = timed[:n_t], timed[n_t : n_t + 3]
    sides[1 + third : 1 + 2 * third] = hops(timed[n_t + 3 :], "space", 1 + third)
    dcodes, places, rest = exchange_steps(even, odd, "tm", sides[1 + 2 * third :])
    sides[1 + 2 * third :] = hops(rest, "space", 1 + 2 * third)
    dcodes = call(
        functools.partial(place_codes_kernel, frames, sub, places),
        shape((2 * RANK, tokens), BF16),
        *dcodes,
        scratch=[pltpu.VMEM((tokens, 128), F32)],
    )
    dcodes = share_steps(dcodes, "space")

    out_t[1:2] = hops(out_t[1:2], "tm", 1)
    backward = call(
        functools.partial(space_backward_kernel, frames, n_s),
        [shape((2 * RANK, frames * total + 2 * pad), BF16)] * n_s + [shape((2 * RANK, d_s), F32)],
        qkv, probs, hidden, time_grad_b, dcodes, downs, downs_here, ups_here, *sides,
        scratch=[
            pltpu.VMEM((n_s, 2, 2 * RANK, pad), BF16),
        ],
        after=[out_t[1]],
        carry=[out_t[2]],
    )
    partial, part, out_t[2] = backward[:n_s], backward[n_s], backward[n_s + 1]
    partial = exchange(partial, "space")
    out_t[2:3] = hops(out_t[2:3], "tm", 2)
    rows = 8 * RANK // n_d
    *sums, out_t[3] = call(
        functools.partial(merge_kernel, frames, n_s, n_d),
        [shape((rows, d_s), F32)] * n_d,
        part, *sides, *partial,
        scratch=[pltpu.VMEM((n_d, rows, d_s), F32)],
        after=[out_t[2]],
        carry=[out_t[3]],
    )
    out_t[3:] = hops(out_t[3:], "tm", 3)
    sums = call(total_kernel, shape((rows, d_s), BF16), *exchange(sums, "dp"))
    sums = call(total_kernel, shape((rows, d_s), BF16), *share(sums, "tm"), after=[out_t[3]])
    sums = call(
        join_kernel,
        shape((rows, width), BF16),
        *share(sums, "space"),
        scratch=[pltpu.VMEM((n_s, rows, d_s), BF16)],
    )
    grads_a, grads_b = call(
        functools.partial(final_kernel, factor, n_d),
        [shape((4, RANK, width), F32)] * 2,
        *share(sums, "dp"),
        scratch=[pltpu.VMEM((n_d, rows, width), BF16)],
    )
    mixed = call(
        functools.partial(mixed_kernel, frames),
        shape(patches.shape, BF16),
        hidden, *out_t,
        scratch=[pltpu.VMEM((tokens, width), BF16)],
    )
    return (mixed, jnp.swapaxes(grads_a, 1, 2), grads_b)


def solution(mesh):
    token = P("dp", "tm", "space", None)
    return jax.shard_map(
        per_device,
        mesh=mesh,
        in_specs=(token,) * 7 + (P(), P(), token),
        out_specs=(token, P(), P()),
        check_vma=False,
    )
```

```python
import functools

import jax
import jax.numpy as jnp
from jax import lax
from jax.experimental import pallas as pl
from jax.experimental.pallas import tpu as pltpu
from jax.sharding import PartitionSpec as P

HEAD_DIM = 72
RANK = 16
SCALE = HEAD_DIM ** (-0.5)
F32 = jnp.float32
BF16 = jnp.bfloat16
NN = (((1,), (0,)), ((), ()))
NT = (((1,), (1,)), ((), ()))
TN = (((0,), (0,)), ((), ()))


def mm(a, b, dims=NN):
    return lax.dot_general(a, b, dims, preferred_element_type=F32)


def call(kernel, out_shape, *args, scratch=(), hbm=False, limit=48, after=(), carry=()):
    vmem = pl.BlockSpec(memory_space=pltpu.VMEM)
    anywhere = pl.BlockSpec(memory_space=pl.ANY)
    main = pl.BlockSpec(memory_space=pltpu.HBM) if hbm else vmem
    single = not isinstance(out_shape, (tuple, list))
    outs = (out_shape,) if single else tuple(out_shape)
    used, extra = len(args), len(after) + len(carry)

    def body(*refs):
        inside = refs[:used] + refs[used + extra : used + extra + len(outs)]
        kernel(*inside, *refs[used + extra + len(outs) + len(carry) :])

    result = pl.pallas_call(
        body,
        out_shape=outs + tuple(shape(x.shape, x.dtype) for x in carry),
        in_specs=[main] * used + [anywhere] * extra,
        out_specs=(vmem,) * len(outs) + (anywhere,) * len(carry),
        scratch_shapes=list(scratch),
        input_output_aliases={used + len(after) + i: len(outs) + i for i in range(len(carry))},
        compiler_params=pltpu.CompilerParams(vmem_limit_bytes=limit * 1024 * 1024),
    )(*(pltpu.with_memory_space_constraint(x, pltpu.HBM) if hbm else x for x in args), *after, *carry)
    return result[0] if single and not carry else list(result)


def shape(dims, dtype):
    return jax.ShapeDtypeStruct(tuple(dims), dtype)


def probs_of(keys, q_t, mask):
    scores = mm(keys, q_t) * SCALE
    if mask is not None:
        scores = jnp.where(mask, scores, -1e30)
    peak = jnp.max(scores, axis=0, keepdims=True)
    weights = jnp.exp(scores - peak)
    return weights * (1.0 / jnp.sum(weights, axis=0, keepdims=True))


def head_backward(probs, k_t, v_t, g_t, forward=False):
    low = probs.astype(BF16)
    dvals = mm(g_t, low, NT)
    dprob = mm(v_t.T, g_t)
    inner = jnp.sum(probs * dprob, axis=0, keepdims=True)
    dscore = (probs * (dprob - inner) * SCALE).astype(BF16)
    dquery = mm(k_t, dscore)
    out = mm(v_t, low) if forward else None
    return dquery, dvals, out


def rows_of(array, head):
    return array[head * HEAD_DIM : (head + 1) * HEAD_DIM]


def peer(axis, distance):
    return lax.axis_index(axis) ^ distance


def load_all(refs, buffers, sems):
    copies = [
        pltpu.make_async_copy(ref, buffer, sems.at[index])
        for index, (ref, buffer) in enumerate(zip(refs, buffers))
    ]
    for copy in copies:
        copy.start()
    return copies


def pack_time_kernel(n_t, sub, q_ref, k_ref, v_ref, g_ref, *rest):
    outs, sems = rest[:n_t], rest[n_t]
    frames = q_ref.shape[1]
    copies = []
    for k in range(n_t):
        start = pl.multiple_of(peer("tm", k) * sub, sub)
        for index, ref in enumerate((q_ref, k_ref, v_ref, g_ref)):
            for f in range(frames):
                copy = pltpu.make_async_copy(
                    ref.at[0, f, pl.ds(start, sub)],
                    outs[k].at[index, f * sub : (f + 1) * sub],
                    sems.at[len(copies)],
                )
                copy.start()
                copies.append(copy)
    for copy in copies:
        copy.wait()


def pack_space_kernel(n_s, *refs):
    ins, refs = refs[:7], refs[7:]
    outs, buffers, (turned_ref, sems) = refs[:n_s], refs[n_s : n_s + 7], refs[n_s + 7 :]
    p_buf, at_buf, b_buf, q_buf, v_buf, k_buf, g_buf = buffers
    copies = load_all(ins, buffers, sems)
    d_s, tokens = turned_ref.shape[2:]

    def flat(ref):
        return ref[0].reshape(tokens, ref.shape[3])

    def send(array, index):
        turned = array.T
        for j in range(n_s):
            turned_ref[index, j] = turned[j * d_s : (j + 1) * d_s]
        for k in range(n_s):
            outs[k][index * d_s : (index + 1) * d_s] = turned_ref[index, peer("space", k)]

    copies[0].wait()
    copies[1].wait()
    copies[2].wait()
    patches = flat(p_buf)
    codes_q = mm(patches, at_buf[0], NT).astype(BF16)
    codes_v = mm(patches, at_buf[1], NT).astype(BF16)
    codes_t = jnp.concatenate([codes_q, codes_v], axis=1).T
    copies[3].wait()
    query = (flat(q_buf).astype(F32) + mm(codes_q, b_buf[0])).astype(BF16)
    send(query, 0)
    copies[4].wait()
    value = (flat(v_buf).astype(F32) + mm(codes_v, b_buf[1])).astype(BF16)
    send(value, 2)
    copies[5].wait()
    send(flat(k_buf), 1)
    send(patches, 3)
    copies[6].wait()
    send(flat(g_buf), 4)
    for k in range(n_s):
        outs[k][5 * d_s :] = codes_t


def frame_rows(pieces, f, patch_dev):
    return jnp.concatenate([x[:, f * patch_dev : (f + 1) * patch_dev] for x in pieces], axis=1)


def space_forward_kernel(frames, n_s, *refs):
    packed, (qkv_ref, probs_ref, *outs) = refs[:n_s], refs[n_s:]
    d_s, tokens = outs[0].shape
    patch_dev = tokens // frames
    total = n_s * patch_dev
    step = min(total, 256)
    for index in range(3):
        pieces = [x[index * d_s : (index + 1) * d_s] for x in packed]
        for f in range(frames):
            qkv_ref[index, f] = frame_rows(pieces, f, patch_dev)
    for f in range(frames):
        query = qkv_ref[0, f].astype(F32)
        keys = qkv_ref[1, f].astype(F32)
        vals = qkv_ref[2, f].astype(F32)
        heads = []
        for h in range(d_s // HEAD_DIM):
            k_h = rows_of(keys, h).astype(BF16)
            v_h = rows_of(vals, h).astype(BF16)
            q_h = rows_of(query, h).astype(BF16)
            parts = []
            for s in range(0, total, step):
                probs = probs_of(k_h.T, q_h[:, s : s + step], None)
                probs_ref[f, h, :, s : s + step] = probs
                parts.append(mm(v_h, probs.astype(BF16)))
            heads.append(parts[0] if len(parts) == 1 else jnp.concatenate(parts, axis=1))
        out = jnp.concatenate(heads, axis=0).astype(BF16)
        for k in range(n_s):
            outs[k][:, f * patch_dev : (f + 1) * patch_dev] = out[
                :, k * patch_dev : (k + 1) * patch_dev
            ]


def lane_block(rows):
    return lax.broadcasted_iota(jnp.int32, (rows, 128), 1) // (2 * RANK)


def fold(token_rows):
    block = lane_block(8)
    result = token_rows[0:8]
    for k in range(1, 4):
        result = jnp.where(block == k, token_rows[8 * k : 8 * k + 8], result)
    return result


def unfold(folded):
    pieces = [folded]
    for k in range(1, 4):
        pieces.append(pltpu.roll(folded, 128 - 2 * RANK * k, 1))
    return jnp.concatenate(pieces, axis=0)


def hidden_kernel(n_t, n_s, *refs):
    pieces, refs = refs[:n_s], refs[n_s:]
    p_ref, at_ref, hidden_ref = refs[:3]
    sends = refs[3 : 3 + n_t]
    out_buf, codes_buf = refs[3 + n_t :]
    _, frames, patch_dev, width = p_ref.shape
    tokens = frames * patch_dev
    sub = patch_dev // n_t
    for k in range(n_s):
        out_buf[peer("space", k)] = pieces[k][...]
    out = out_buf[...].reshape(width, tokens).T
    hidden = (p_ref[0].reshape(tokens, width).astype(F32) + out.astype(F32)).astype(BF16)
    hidden_ref[...] = hidden
    downs = jnp.concatenate([at_ref[2], at_ref[3]] * 4, axis=0)
    codes_buf[...] = mm(hidden, downs, NT).astype(BF16).astype(F32)
    for k in range(n_t):
        rows = [
            codes_buf[pl.ds(pl.multiple_of(f * patch_dev + peer("tm", k) * sub, sub), sub)]
            for f in range(frames)
        ]
        sends[k][...] = fold(jnp.concatenate(rows, axis=0))


def turn_kernel(*refs):
    pieces, out_ref = refs[:-1], refs[-1]
    for index in range(4):
        rows = jnp.concatenate([piece[index] for piece in pieces], axis=0)
        out_ref[index] = rows.T


def time_kernel(n_t, sub, x_ref, b_ref, *refs):
    codes_refs, refs = refs[:n_t], refs[n_t:]
    outs, sends, grad_b_ref = refs[:n_t], refs[n_t : 2 * n_t], refs[2 * n_t]
    _, width, tokens = x_ref.shape
    codes = jnp.concatenate([unfold(ref[...]) for ref in codes_refs], axis=0).T
    codes_q = codes[:RANK].astype(BF16)
    codes_v = codes[RANK : 2 * RANK].astype(BF16)
    query = (x_ref[0].astype(F32) + mm(b_ref[2], codes_q, TN)).astype(BF16).astype(F32)
    vals = (x_ref[2].astype(F32) + mm(b_ref[3], codes_v, TN)).astype(BF16).astype(F32)
    keys = x_ref[1].astype(F32)
    grad = x_ref[3].astype(F32)
    row = lax.broadcasted_iota(jnp.int32, (tokens, tokens), 0)
    col = lax.broadcasted_iota(jnp.int32, (tokens, tokens), 1)
    mask = lax.rem(row, sub) == lax.rem(col, sub)
    outs_h, d_query, d_vals = [], [], []
    for h in range(width // HEAD_DIM):
        k_h = rows_of(keys, h).astype(BF16)
        v_h = rows_of(vals, h).astype(BF16)
        probs = probs_of(k_h.T, rows_of(query, h).astype(BF16), mask)
        dq, dv, out = head_backward(probs, k_h, v_h, rows_of(grad, h).astype(BF16), True)
        outs_h.append(out)
        d_query.append(dq)
        d_vals.append(dv)
    d_query = jnp.concatenate(d_query, axis=0).astype(BF16)
    d_vals = jnp.concatenate(d_vals, axis=0).astype(BF16)
    d_codes = jnp.concatenate([mm(b_ref[2], d_query), mm(b_ref[3], d_vals)] * 4, axis=0)
    d_codes = d_codes.astype(BF16).astype(F32).T
    per = tokens // n_t
    for k in range(n_t):
        sends[k][...] = fold(d_codes[k * per : (k + 1) * per])
    out = jnp.concatenate(outs_h, axis=0).astype(BF16).T
    for k in range(n_t):
        outs[k][...] = out[k * per : (k + 1) * per]
    grad_b_ref[:RANK] = mm(codes_q, d_query, NT)
    grad_b_ref[RANK:] = mm(codes_v, d_vals, NT)


def place_codes_kernel(frames, sub, *refs):
    pieces, (out_ref, buf) = refs[:-2], refs[-2:]
    patch_dev = sub * len(pieces)
    for k, piece in enumerate(pieces):
        rows = unfold(piece[...])
        for f in range(frames):
            start = pl.multiple_of(f * patch_dev + peer("tm", k) * sub, sub)
            buf[pl.ds(start, sub)] = rows[f * sub : (f + 1) * sub]
    out_ref[...] = buf[...].T[: 2 * RANK].astype(BF16)


def space_backward_kernel(frames, n_s, qkv_ref, probs_ref, hidden_ref, grad_b_ref, at_ref, at_here_ref, b_here_ref, *refs):
    packed, dcodes, sends = refs[:n_s], refs[n_s : 2 * n_s], refs[2 * n_s : 3 * n_s]
    part_ref, cut_buf = refs[3 * n_s :]
    d_s = part_ref.shape[1]
    tokens = hidden_ref.shape[0]
    patch_dev = tokens // frames
    total = n_s * patch_dev
    step = min(total, 256)
    ups = jnp.concatenate([at_here_ref[2], at_here_ref[3]], axis=0).T
    grads = []
    for k in range(n_s):
        cot = packed[k][4 * d_s : 5 * d_s].astype(F32)
        grads.append((cot + mm(ups, dcodes[k][...])).astype(BF16))
    grad_b_q = grad_b_v = None
    codes = [x[5 * d_s :] for x in packed]
    for f in range(frames):
        keys = qkv_ref[1, f].astype(F32)
        vals = qkv_ref[2, f].astype(F32)
        grad = frame_rows(grads, f, patch_dev).astype(F32)
        d_query, d_vals = [], []
        for h in range(d_s // HEAD_DIM):
            k_h = rows_of(keys, h).astype(BF16)
            v_h = rows_of(vals, h).astype(BF16)
            g_h = rows_of(grad, h).astype(BF16)
            dq_parts, dv_sum = [], None
            for s in range(0, total, step):
                probs = probs_ref[f, h, :, s : s + step]
                dq, dv, _ = head_backward(probs, k_h, v_h, g_h[:, s : s + step])
                dq_parts.append(dq)
                dv_sum = dv if dv_sum is None else dv_sum + dv
            d_query.append(
                dq_parts[0] if len(dq_parts) == 1 else jnp.concatenate(dq_parts, axis=1)
            )
            d_vals.append(dv_sum)
        d_query = jnp.concatenate(d_query, axis=0).astype(BF16)
        d_vals = jnp.concatenate(d_vals, axis=0).astype(BF16)
        partial = jnp.concatenate([mm(b_here_ref[0], d_query), mm(b_here_ref[1], d_vals)], axis=0)
        partial = partial.astype(BF16)
        blocks = [partial[:, m * patch_dev : (m + 1) * patch_dev] for m in range(n_s)]
        for k in range(n_s):
            turned = jnp.concatenate([blocks[m ^ k] for m in range(n_s)], axis=1)
            sends[k][:, f * total : (f + 1) * total] = turned
        frame_codes = frame_rows(codes, f, patch_dev)
        term_q = mm(frame_codes[:RANK], d_query, NT)
        term_v = mm(frame_codes[RANK:], d_vals, NT)
        grad_b_q = term_q if grad_b_q is None else grad_b_q + term_q
        grad_b_v = term_v if grad_b_v is None else grad_b_v + term_v
    part_ref[:RANK] = grad_b_q
    part_ref[RANK:] = grad_b_v
    grad_a = mm(dcodes[0][...], hidden_ref[...])
    pad = -(-d_s // 128) * 128
    for j in range(n_s):
        cut_buf[j, 0, :, :d_s] = grad_a[:, j * d_s : (j + 1) * d_s].astype(BF16)
        cut_buf[j, 1, :, :d_s] = grad_b_ref[:, j * d_s : (j + 1) * d_s].astype(BF16)
    for k in range(n_s):
        for index in range(2):
            start = frames * total + index * pad
            sends[k][:, start : start + pad] = cut_buf[peer("space", k), index]


def add_up(terms):
    result = None
    for term in terms:
        result = term if result is None else result + term
    return result


def merge_kernel(frames, n_s, n_d, part_ref, *refs):
    packed, recvs, refs = refs[:n_s], refs[n_s : 2 * n_s], refs[2 * n_s :]
    sends, buf = refs[:n_d], refs[n_d]
    d_s = part_ref.shape[1]
    tokens = packed[0].shape[1]
    patch_dev = tokens // frames
    total = n_s * patch_dev
    pad = -(-d_s // 128) * 128
    patches = [x[3 * d_s : 4 * d_s] for x in packed]
    terms = []
    for f in range(frames):
        codes = [recv[:, f * total : (f + 1) * total].astype(F32) for recv in recvs]
        terms.append(mm(add_up(codes).astype(BF16), frame_rows(patches, f, patch_dev), NT))
    start = frames * total
    time_a = add_up([recv[:, start : start + d_s].astype(F32) for recv in recvs])
    time_b = add_up([recv[:, start + pad : start + pad + d_s].astype(F32) for recv in recvs])
    rows = jnp.concatenate([add_up(terms), time_a, part_ref[...], time_b], axis=0)
    per = rows.shape[0] // n_d
    for d in range(n_d):
        buf[d] = rows[d * per : (d + 1) * per]
    for k in range(n_d):
        sends[k][...] = buf[peer("dp", k)]


def total_kernel(*refs):
    terms = [ref[...].astype(F32) for ref in refs[:-1]]
    while len(terms) > 1:
        terms = [terms[i] + terms[i + 1] for i in range(0, len(terms), 2)]
    refs[-1][...] = terms[0].astype(refs[-1].dtype)


def join_kernel(*refs):
    pieces, (out_ref, buf) = refs[:-2], refs[-2:]
    for k, piece in enumerate(pieces):
        buf[peer("space", k)] = piece[...]
    out_ref[...] = jnp.concatenate([buf[j] for j in range(len(pieces))], axis=1)


def final_kernel(factor, n_d, *refs):
    pieces, (a_ref, b_ref, buf) = refs[:n_d], refs[n_d:]
    for k, piece in enumerate(pieces):
        buf[peer("dp", k)] = piece[...]
    per = pieces[0].shape[0]
    half = n_d // 2
    for d in range(n_d):
        rows = buf[d].astype(F32) * factor
        target = a_ref if d < half else b_ref
        for r in range(0, per, min(per, RANK)):
            start = (d % half) * per + r
            size = min(per, RANK)
            target[start // RANK, start % RANK : start % RANK + size] = rows[r : r + size]


def mixed_kernel(frames, hidden_ref, *refs):
    pieces, (mixed_ref, buf) = refs[:-2], refs[-2:]
    n_t = len(pieces)
    tokens, width = hidden_ref.shape
    patch_dev = tokens // frames
    sub = patch_dev // n_t
    for k, piece in enumerate(pieces):
        for f in range(frames):
            start = pl.multiple_of(f * patch_dev + peer("tm", k) * sub, sub)
            buf[pl.ds(start, sub)] = piece[f * sub : (f + 1) * sub]
    total = hidden_ref[...].astype(F32) + buf[...].astype(F32)
    mixed_ref[0] = total.astype(BF16).reshape(frames, patch_dev, width)


def hops(arrays, axis, first):
    size = lax.axis_size(axis)
    return [
        lax.ppermute(array, axis, [(i, i ^ k) for i in range(size)])
        for k, array in enumerate(arrays, first)
    ]


def exchange(pieces, axis):
    return [pieces[0]] + hops(pieces[1:], axis, 1)


def share(array, axis):
    return exchange([array] * lax.axis_size(axis), axis)


def per_device(
    patches, query_s, key_s, value_s, query_t, key_t, value_t, adapters_a, adapters_b, cotangent
):
    _, frames, patch_dev, width = patches.shape
    n_d, n_t, n_s = (lax.axis_size(name) for name in ("dp", "tm", "space"))
    tokens = frames * patch_dev
    sub = patch_dev // n_t
    d_s = width // n_s
    total = n_s * patch_dev
    factor = (tokens * n_d * n_t * n_s) ** (-0.5)
    here = lax.axis_index("space") * d_s
    downs = jnp.swapaxes(adapters_a, 1, 2)
    downs_here = lax.dynamic_slice_in_dim(downs, here, d_s, 2)
    ups_here = lax.dynamic_slice_in_dim(adapters_b, here, d_s, 2)
    dma = pltpu.SemaphoreType.DMA
    pad = -(-d_s // 128) * 128

    time_pieces = call(
        functools.partial(pack_time_kernel, n_t, sub),
        [shape((4, frames * sub, width), BF16)] * n_t,
        query_t, key_t, value_t, cotangent,
        scratch=[dma((4 * frames * n_t,))],
        hbm=True, limit=48,
    )
    time_pieces = exchange(time_pieces, "tm")
    packed = call(
        functools.partial(pack_space_kernel, n_s),
        [shape((5 * d_s + 2 * RANK, tokens), BF16)] * n_s,
        patches, downs, adapters_b, query_s, value_s, key_s, cotangent,
        scratch=[
            pltpu.VMEM(x.shape, BF16)
            for x in (patches, downs, adapters_b, query_s, value_s, key_s, cotangent)
        ]
        + [pltpu.VMEM((5, n_s, d_s, tokens), BF16), dma((7,))],
        hbm=True, limit=48,
    )
    packed = exchange(packed, "space")
    qkv, probs, *out_s = call(
        functools.partial(space_forward_kernel, frames, n_s),
        [shape((3, frames, d_s, total), BF16), shape((frames, d_s // HEAD_DIM, total, total), F32)]
        + [shape((d_s, tokens), BF16)] * n_s,
        *packed,
        after=[time_pieces[1]],
    )
    out_s = exchange(out_s, "space")
    hidden, *codes = call(
        functools.partial(hidden_kernel, n_t, n_s),
        [shape((tokens, width), BF16)] + [shape((8, 128), F32)] * n_t,
        *out_s, patches, downs,
        scratch=[pltpu.VMEM((n_s, d_s, tokens), BF16), pltpu.VMEM((tokens, 128), F32)],
    )
    codes = exchange(codes, "tm")
    turned = call(turn_kernel, shape((4, width, n_t * frames * sub), BF16), *time_pieces)
    timed = call(
        functools.partial(time_kernel, n_t, sub),
        [shape((frames * sub, width), BF16)] * n_t
        + [shape((8, 128), F32)] * n_t
        + [shape((2 * RANK, width), F32)],
        turned, adapters_b, *codes,
    )
    out_t, dcodes, time_grad_b = timed[:n_t], timed[n_t : 2 * n_t], timed[2 * n_t]
    dcodes = exchange(dcodes, "tm")
    out_t[1:2] = hops(out_t[1:2], "tm", 1)
    dcodes = call(
        functools.partial(place_codes_kernel, frames, sub),
        shape((2 * RANK, tokens), BF16),
        *dcodes,
        scratch=[pltpu.VMEM((tokens, 128), F32)],
    )
    dcodes = share(dcodes, "space")
    backward = call(
        functools.partial(space_backward_kernel, frames, n_s),
        [shape((2 * RANK, frames * total + 2 * pad), BF16)] * n_s + [shape((2 * RANK, d_s), F32)],
        qkv, probs, hidden, time_grad_b, downs, downs_here, ups_here, *packed, *dcodes,
        scratch=[pltpu.VMEM((n_s, 2, 2 * RANK, pad), BF16)],
        after=out_t[1:2],
        carry=out_t[2:],
    )
    partial, part = backward[:n_s], backward[n_s]
    partial = exchange(partial, "space")
    out_t[2:] = hops(backward[n_s + 1 :], "tm", 2)
    rows = 8 * RANK // n_d
    sums = call(
        functools.partial(merge_kernel, frames, n_s, n_d),
        [shape((rows, d_s), F32)] * n_d,
        part, *packed, *partial,
        scratch=[pltpu.VMEM((n_d, rows, d_s), F32)],
    )
    sums = call(total_kernel, shape((rows, d_s), BF16), *exchange(sums, "dp"), after=out_t[2:])
    sums = call(total_kernel, shape((rows, d_s), BF16), *share(sums, "tm"))
    sums = call(
        join_kernel,
        shape((rows, width), BF16),
        *share(sums, "space"),
        scratch=[pltpu.VMEM((n_s, rows, d_s), BF16)],
    )
    grads_a, grads_b = call(
        functools.partial(final_kernel, factor, n_d),
        [shape((4, RANK, width), F32)] * 2,
        *share(sums, "dp"),
        scratch=[pltpu.VMEM((n_d, rows, width), BF16)],
    )
    mixed = call(
        functools.partial(mixed_kernel, frames),
        shape(patches.shape, BF16),
        hidden, *out_t,
        scratch=[pltpu.VMEM((tokens, width), BF16)],
    )
    return (mixed, jnp.swapaxes(grads_a, 1, 2), grads_b)


def solution(mesh):
    token = P("dp", "tm", "space", None)
    return jax.shard_map(
        per_device,
        mesh=mesh,
        in_specs=(token,) * 7 + (P(), P(), token),
        out_specs=(token, P(), P()),
        check_vma=False,
    )
```

```python
import functools

import jax
import jax.numpy as jnp
from jax import lax
from jax.experimental import pallas as pl
from jax.experimental.pallas import tpu as pltpu
from jax.sharding import PartitionSpec as P

HEAD_DIM = 72
RANK = 16
SCALE = HEAD_DIM ** (-0.5)
F32 = jnp.float32
BF16 = jnp.bfloat16
NN = (((1,), (0,)), ((), ()))
NT = (((1,), (1,)), ((), ()))
TN = (((0,), (0,)), ((), ()))


def mm(a, b, dims=NN):
    return lax.dot_general(a, b, dims, preferred_element_type=F32)


def far(x):
    return pltpu.with_memory_space_constraint(x, pltpu.HBM)


def call(kernel, out_shape, *args, scratch=(), hbm=False, limit=48, after=(), carry=()):
    vmem = pl.BlockSpec(memory_space=pltpu.VMEM)
    anywhere = pl.BlockSpec(memory_space=pl.ANY)
    main = anywhere if hbm else vmem
    single = not isinstance(out_shape, (tuple, list))
    outs = (out_shape,) if single else tuple(out_shape)
    used, extra = len(args), len(after) + len(carry)

    def body(*refs):
        inside = refs[:used] + refs[used + extra : used + extra + len(outs)]
        kernel(*inside, *refs[used + extra + len(outs) + len(carry) :])

    result = pl.pallas_call(
        body,
        out_shape=outs + tuple(shape(x.shape, x.dtype) for x in carry),
        in_specs=[main] * used + [anywhere] * extra,
        out_specs=tuple(vmem if isinstance(o, jax.ShapeDtypeStruct) else anywhere for o in outs)
        + (anywhere,) * len(carry),
        scratch_shapes=list(scratch),
        input_output_aliases={used + len(after) + i: len(outs) + i for i in range(len(carry))},
        compiler_params=pltpu.CompilerParams(vmem_limit_bytes=limit * 1024 * 1024),
    )(*args, *after, *carry)
    return result[0] if single and not carry else list(result)


def shape(dims, dtype):
    return jax.ShapeDtypeStruct(tuple(dims), dtype)


def probs_of(keys, q_t, mask):
    scores = mm(keys, q_t) * SCALE
    if mask is not None:
        scores = jnp.where(mask, scores, -1e30)
    peak = jnp.max(scores, axis=0, keepdims=True)
    weights = jnp.exp(scores - peak)
    return weights * (1.0 / jnp.sum(weights, axis=0, keepdims=True))


def head_backward(probs, k_t, v_t, g_t, forward=False):
    low = probs.astype(BF16)
    dvals = mm(g_t, low, NT)
    dprob = mm(v_t.T, g_t)
    inner = jnp.sum(probs * dprob, axis=0, keepdims=True)
    dscore = (probs * (dprob - inner) * SCALE).astype(BF16)
    dquery = mm(k_t, dscore)
    out = mm(v_t, low) if forward else None
    return dquery, dvals, out


def rows_of(array, head):
    return array[head * HEAD_DIM : (head + 1) * HEAD_DIM]


def peer(axis, distance):
    return lax.axis_index(axis) ^ distance


def load_all(refs, buffers, sems):
    copies = [
        pltpu.make_async_copy(ref, buffer, sems.at[index])
        for index, (ref, buffer) in enumerate(zip(refs, buffers))
    ]
    for copy in copies:
        copy.start()
    return copies


def pack_kernel(n_s, n_t, sub, *refs):
    ins, time_ins, refs = refs[:7], refs[7:11], refs[11:]
    outs, time_outs, refs = refs[:n_s], refs[n_s : n_s + n_t - 1], refs[n_s + n_t - 1 :]
    buffers, (time_buf, turned_ref, sems, time_sems) = refs[:7], refs[7:]
    p_buf, at_buf, b_buf, q_buf, v_buf, k_buf, g_buf = buffers
    copies = load_all(ins, buffers, sems)
    time_copies = load_all(time_ins, [time_buf.at[index] for index in range(4)], time_sems)
    d_s, tokens = turned_ref.shape[2:]
    frames = time_buf.shape[2]

    def flat(ref):
        return ref[0].reshape(tokens, ref.shape[3])

    def send(array, index):
        turned = array.T
        for j in range(n_s):
            turned_ref[index, j] = turned[j * d_s : (j + 1) * d_s]
        for k in range(n_s):
            outs[k][index * d_s : (index + 1) * d_s] = turned_ref[index, peer("space", k)]

    copies[0].wait()
    copies[1].wait()
    copies[2].wait()
    patches = flat(p_buf)
    codes_q = mm(patches, at_buf[0], NT).astype(BF16)
    codes_v = mm(patches, at_buf[1], NT).astype(BF16)
    codes_t = jnp.concatenate([codes_q, codes_v], axis=1).T
    copies[3].wait()
    query = (flat(q_buf).astype(F32) + mm(codes_q, b_buf[0])).astype(BF16)
    send(query, 0)
    copies[4].wait()
    value = (flat(v_buf).astype(F32) + mm(codes_v, b_buf[1])).astype(BF16)
    send(value, 2)
    copies[5].wait()
    send(flat(k_buf), 1)
    send(patches, 3)
    copies[6].wait()
    send(flat(g_buf), 4)
    for k in range(n_s):
        outs[k][5 * d_s :] = codes_t
    for index, copy in enumerate(time_copies):
        copy.wait()
        for k in range(1, n_t):
            start = pl.multiple_of(peer("tm", k) * sub, sub)
            for f in range(frames):
                time_outs[k - 1][index, f * sub : (f + 1) * sub] = time_buf[
                    index, 0, f, pl.ds(start, sub)
                ]


def frame_rows(pieces, f, patch_dev):
    return jnp.concatenate([x[:, f * patch_dev : (f + 1) * patch_dev] for x in pieces], axis=1)


def space_forward_kernel(frames, n_s, *refs):
    packed, (qkv_ref, probs_ref, *outs) = refs[:n_s], refs[n_s : 2 * n_s + 2]
    probs_buf, sems = refs[2 * n_s + 2 :]
    copies = []
    d_s, tokens = outs[0].shape
    patch_dev = tokens // frames
    total = n_s * patch_dev
    step = min(total, 256)
    for index in range(3):
        pieces = [x[index * d_s : (index + 1) * d_s] for x in packed]
        for f in range(frames):
            qkv_ref[index, f] = frame_rows(pieces, f, patch_dev)
    for f in range(frames):
        query = qkv_ref[0, f].astype(F32)
        keys = qkv_ref[1, f].astype(F32)
        vals = qkv_ref[2, f].astype(F32)
        heads = []
        for h in range(d_s // HEAD_DIM):
            k_h = rows_of(keys, h).astype(BF16)
            v_h = rows_of(vals, h).astype(BF16)
            q_h = rows_of(query, h).astype(BF16)
            parts = []
            for s in range(0, total, step):
                probs = probs_of(k_h.T, q_h[:, s : s + step], None)
                probs_buf[f, h, :, s : s + step] = probs
                parts.append(mm(v_h, probs.astype(BF16)))
            heads.append(parts[0] if len(parts) == 1 else jnp.concatenate(parts, axis=1))
            copy = pltpu.make_async_copy(
                probs_buf.at[f, h], probs_ref.at[f, h], sems.at[len(copies)]
            )
            copy.start()
            copies.append(copy)
        out = jnp.concatenate(heads, axis=0).astype(BF16)
        for k in range(n_s):
            outs[k][:, f * patch_dev : (f + 1) * patch_dev] = out[
                :, k * patch_dev : (k + 1) * patch_dev
            ]
    for copy in copies:
        copy.wait()


def lane_block(rows):
    return lax.broadcasted_iota(jnp.int32, (rows, 128), 1) // (2 * RANK)


def fold(token_rows):
    block = lane_block(8)
    result = token_rows[0:8]
    for k in range(1, 4):
        result = jnp.where(block == k, token_rows[8 * k : 8 * k + 8], result)
    return result


def unfold(folded):
    pieces = [folded]
    for k in range(1, 4):
        pieces.append(pltpu.roll(folded, 128 - 2 * RANK * k, 1))
    return jnp.concatenate(pieces, axis=0)


def hidden_kernel(n_t, n_s, *refs):
    pieces, refs = refs[:n_s], refs[n_s:]
    p_ref, at_ref, hidden_ref = refs[:3]
    sends = refs[3 : 3 + n_t]
    out_buf, codes_buf = refs[3 + n_t :]
    _, frames, patch_dev, width = p_ref.shape
    tokens = frames * patch_dev
    sub = patch_dev // n_t
    for k in range(n_s):
        out_buf[peer("space", k)] = pieces[k][...]
    out = out_buf[...].reshape(width, tokens).T
    hidden = (p_ref[0].reshape(tokens, width).astype(F32) + out.astype(F32)).astype(BF16)
    hidden_ref[...] = hidden
    downs = jnp.concatenate([at_ref[2], at_ref[3]] * 4, axis=0)
    codes_buf[...] = mm(hidden, downs, NT).astype(BF16).astype(F32)
    for k in range(n_t):
        rows = [
            codes_buf[pl.ds(pl.multiple_of(f * patch_dev + peer("tm", k) * sub, sub), sub)]
            for f in range(frames)
        ]
        sends[k][...] = fold(jnp.concatenate(rows, axis=0))


def turn_kernel(frames, sub, q_ref, k_ref, v_ref, g_ref, *refs):
    *pieces, out_ref, own_buf, piece_buf, own_sems, sems = refs
    own = []
    start = pl.multiple_of(peer("tm", 0) * sub, sub)
    for index, ref in enumerate((q_ref, k_ref, v_ref, g_ref)):
        for f in range(frames):
            copy = pltpu.make_async_copy(
                ref.at[0, f, pl.ds(start, sub)],
                own_buf.at[index, f * sub : (f + 1) * sub],
                own_sems.at[index * frames + f],
            )
            copy.start()
            own.append(copy)
    copies = load_all(pieces, [piece_buf.at[k] for k in range(len(pieces))], sems)
    for copy in own + copies:
        copy.wait()
    for index in range(4):
        parts = [own_buf[index]] + [piece_buf[k, index] for k in range(len(pieces))]
        out_ref[index] = jnp.concatenate(parts, axis=0).T


def time_kernel(n_t, sub, x_ref, b_ref, *refs):
    codes_refs, refs = refs[:n_t], refs[n_t:]
    outs, sends, grad_b_ref = refs[:n_t], refs[n_t : 2 * n_t], refs[2 * n_t]
    _, width, tokens = x_ref.shape
    codes = jnp.concatenate([unfold(ref[...]) for ref in codes_refs], axis=0).T
    codes_q = codes[:RANK].astype(BF16)
    codes_v = codes[RANK : 2 * RANK].astype(BF16)
    query = (x_ref[0].astype(F32) + mm(b_ref[2], codes_q, TN)).astype(BF16).astype(F32)
    vals = (x_ref[2].astype(F32) + mm(b_ref[3], codes_v, TN)).astype(BF16).astype(F32)
    keys = x_ref[1].astype(F32)
    grad = x_ref[3].astype(F32)
    row = lax.broadcasted_iota(jnp.int32, (tokens, tokens), 0)
    col = lax.broadcasted_iota(jnp.int32, (tokens, tokens), 1)
    mask = lax.rem(row, sub) == lax.rem(col, sub)
    outs_h, d_query, d_vals = [], [], []
    for h in range(width // HEAD_DIM):
        k_h = rows_of(keys, h).astype(BF16)
        v_h = rows_of(vals, h).astype(BF16)
        probs = probs_of(k_h.T, rows_of(query, h).astype(BF16), mask)
        dq, dv, out = head_backward(probs, k_h, v_h, rows_of(grad, h).astype(BF16), True)
        outs_h.append(out)
        d_query.append(dq)
        d_vals.append(dv)
    d_query = jnp.concatenate(d_query, axis=0).astype(BF16)
    d_vals = jnp.concatenate(d_vals, axis=0).astype(BF16)
    d_codes = jnp.concatenate([mm(b_ref[2], d_query), mm(b_ref[3], d_vals)] * 4, axis=0)
    d_codes = d_codes.astype(BF16).astype(F32).T
    per = tokens // n_t
    for k in range(n_t):
        sends[k][...] = fold(d_codes[k * per : (k + 1) * per])
    out = jnp.concatenate(outs_h, axis=0).astype(BF16).T
    for k in range(n_t):
        outs[k][...] = out[k * per : (k + 1) * per]
    grad_b_ref[:RANK] = mm(codes_q, d_query, NT)
    grad_b_ref[RANK:] = mm(codes_v, d_vals, NT)


def place_codes_kernel(frames, sub, *refs):
    pieces, (out_ref, buf) = refs[:-2], refs[-2:]
    patch_dev = sub * len(pieces)
    for k, piece in enumerate(pieces):
        rows = unfold(piece[...])
        for f in range(frames):
            start = pl.multiple_of(f * patch_dev + peer("tm", k) * sub, sub)
            buf[pl.ds(start, sub)] = rows[f * sub : (f + 1) * sub]
    out_ref[...] = buf[...].T[: 2 * RANK].astype(BF16)


def space_backward_kernel(frames, n_s, qkv_ref, probs_ref, hidden_ref, grad_b_ref, at_ref, at_here_ref, b_here_ref, *refs):
    packed, dcodes, sends = refs[:n_s], refs[n_s : 2 * n_s], refs[2 * n_s : 3 * n_s]
    part_ref, cut_buf = refs[3 * n_s :]
    d_s = part_ref.shape[1]
    tokens = hidden_ref.shape[0]
    patch_dev = tokens // frames
    total = n_s * patch_dev
    step = min(total, 256)
    ups = jnp.concatenate([at_here_ref[2], at_here_ref[3]], axis=0).T
    grads = []
    for k in range(n_s):
        cot = packed[k][4 * d_s : 5 * d_s].astype(F32)
        grads.append((cot + mm(ups, dcodes[k][...])).astype(BF16))
    grad_b_q = grad_b_v = None
    codes = [x[5 * d_s :] for x in packed]
    for f in range(frames):
        keys = qkv_ref[1, f].astype(F32)
        vals = qkv_ref[2, f].astype(F32)
        grad = frame_rows(grads, f, patch_dev).astype(F32)
        d_query, d_vals = [], []
        for h in range(d_s // HEAD_DIM):
            k_h = rows_of(keys, h).astype(BF16)
            v_h = rows_of(vals, h).astype(BF16)
            g_h = rows_of(grad, h).astype(BF16)
            dq_parts, dv_sum = [], None
            for s in range(0, total, step):
                probs = probs_ref[f, h, :, s : s + step]
                dq, dv, _ = head_backward(probs, k_h, v_h, g_h[:, s : s + step])
                dq_parts.append(dq)
                dv_sum = dv if dv_sum is None else dv_sum + dv
            d_query.append(
                dq_parts[0] if len(dq_parts) == 1 else jnp.concatenate(dq_parts, axis=1)
            )
            d_vals.append(dv_sum)
        d_query = jnp.concatenate(d_query, axis=0).astype(BF16)
        d_vals = jnp.concatenate(d_vals, axis=0).astype(BF16)
        partial = jnp.concatenate([mm(b_here_ref[0], d_query), mm(b_here_ref[1], d_vals)], axis=0)
        partial = partial.astype(BF16)
        blocks = [partial[:, m * patch_dev : (m + 1) * patch_dev] for m in range(n_s)]
        for k in range(n_s):
            turned = jnp.concatenate([blocks[m ^ k] for m in range(n_s)], axis=1)
            sends[k][:, f * total : (f + 1) * total] = turned
        frame_codes = frame_rows(codes, f, patch_dev)
        term_q = mm(frame_codes[:RANK], d_query, NT)
        term_v = mm(frame_codes[RANK:], d_vals, NT)
        grad_b_q = term_q if grad_b_q is None else grad_b_q + term_q
        grad_b_v = term_v if grad_b_v is None else grad_b_v + term_v
    part_ref[:RANK] = grad_b_q
    part_ref[RANK:] = grad_b_v
    grad_a = mm(dcodes[0][...], hidden_ref[...])
    pad = -(-d_s // 128) * 128
    for j in range(n_s):
        cut_buf[j, 0, :, :d_s] = grad_a[:, j * d_s : (j + 1) * d_s].astype(BF16)
        cut_buf[j, 1, :, :d_s] = grad_b_ref[:, j * d_s : (j + 1) * d_s].astype(BF16)
    for k in range(n_s):
        for index in range(2):
            start = frames * total + index * pad
            sends[k][:, start : start + pad] = cut_buf[peer("space", k), index]


def add_up(terms):
    result = None
    for term in terms:
        result = term if result is None else result + term
    return result


def merge_kernel(frames, n_s, n_d, part_ref, *refs):
    packed, recvs, refs = refs[:n_s], refs[n_s : 2 * n_s], refs[2 * n_s :]
    sends, buf = refs[:n_d], refs[n_d]
    d_s = part_ref.shape[1]
    tokens = packed[0].shape[1]
    patch_dev = tokens // frames
    total = n_s * patch_dev
    pad = -(-d_s // 128) * 128
    patches = [x[3 * d_s : 4 * d_s] for x in packed]
    terms = []
    for f in range(frames):
        codes = [recv[:, f * total : (f + 1) * total].astype(F32) for recv in recvs]
        terms.append(mm(add_up(codes).astype(BF16), frame_rows(patches, f, patch_dev), NT))
    start = frames * total
    time_a = add_up([recv[:, start : start + d_s].astype(F32) for recv in recvs])
    time_b = add_up([recv[:, start + pad : start + pad + d_s].astype(F32) for recv in recvs])
    rows = jnp.concatenate([add_up(terms), time_a, part_ref[...], time_b], axis=0)
    per = rows.shape[0] // n_d
    for d in range(n_d):
        buf[d] = rows[d * per : (d + 1) * per]
    for k in range(n_d):
        sends[k][...] = buf[peer("dp", k)]


def total_kernel(*refs):
    terms = [ref[...].astype(F32) for ref in refs[:-1]]
    while len(terms) > 1:
        terms = [terms[i] + terms[i + 1] for i in range(0, len(terms), 2)]
    refs[-1][...] = terms[0].astype(refs[-1].dtype)


def join_kernel(*refs):
    pieces, (out_ref, buf) = refs[:-2], refs[-2:]
    for k, piece in enumerate(pieces):
        buf[peer("space", k)] = piece[...]
    out_ref[...] = jnp.concatenate([buf[j] for j in range(len(pieces))], axis=1)


def final_kernel(factor, n_d, *refs):
    pieces, (a_ref, b_ref, buf) = refs[:n_d], refs[n_d:]
    for k, piece in enumerate(pieces):
        buf[peer("dp", k)] = piece[...]
    per = pieces[0].shape[0]
    half = n_d // 2
    for d in range(n_d):
        rows = buf[d].astype(F32) * factor
        target = a_ref if d < half else b_ref
        for r in range(0, per, min(per, RANK)):
            start = (d % half) * per + r
            size = min(per, RANK)
            target[start // RANK, start % RANK : start % RANK + size] = rows[r : r + size]


def mixed_kernel(frames, hidden_ref, *refs):
    pieces, (mixed_ref, buf) = refs[:-2], refs[-2:]
    n_t = len(pieces)
    tokens, width = hidden_ref.shape
    patch_dev = tokens // frames
    sub = patch_dev // n_t
    for k, piece in enumerate(pieces):
        for f in range(frames):
            start = pl.multiple_of(f * patch_dev + peer("tm", k) * sub, sub)
            buf[pl.ds(start, sub)] = piece[f * sub : (f + 1) * sub]
    total = hidden_ref[...].astype(F32) + buf[...].astype(F32)
    mixed_ref[0] = total.astype(BF16).reshape(frames, patch_dev, width)


def hops(arrays, axis, first):
    size = lax.axis_size(axis)
    return [
        lax.ppermute(array, axis, [(i, i ^ k) for i in range(size)])
        for k, array in enumerate(arrays, first)
    ]


def exchange(pieces, axis):
    return [pieces[0]] + hops(pieces[1:], axis, 1)


def share(array, axis):
    return exchange([array] * lax.axis_size(axis), axis)


def per_device(
    patches, query_s, key_s, value_s, query_t, key_t, value_t, adapters_a, adapters_b, cotangent
):
    _, frames, patch_dev, width = patches.shape
    n_d, n_t, n_s = (lax.axis_size(name) for name in ("dp", "tm", "space"))
    tokens = frames * patch_dev
    sub = patch_dev // n_t
    d_s = width // n_s
    total = n_s * patch_dev
    factor = (tokens * n_d * n_t * n_s) ** (-0.5)
    here = lax.axis_index("space") * d_s
    downs = jnp.swapaxes(adapters_a, 1, 2)
    downs_here = lax.dynamic_slice_in_dim(downs, here, d_s, 2)
    ups_here = lax.dynamic_slice_in_dim(adapters_b, here, d_s, 2)
    dma = pltpu.SemaphoreType.DMA
    pad = -(-d_s // 128) * 128

    time_arrays = [far(x) for x in (query_t, key_t, value_t, cotangent)]
    space_arrays = [
        far(x) for x in (patches, downs, adapters_b, query_s, value_s, key_s, cotangent)
    ]
    packed = call(
        functools.partial(pack_kernel, n_s, n_t, sub),
        [shape((5 * d_s + 2 * RANK, tokens), BF16)] * n_s
        + [shape((4, frames * sub, width), BF16)] * (n_t - 1),
        *space_arrays, *time_arrays,
        scratch=[pltpu.VMEM(x.shape, BF16) for x in space_arrays]
        + [
            pltpu.VMEM((4,) + query_t.shape, BF16),
            pltpu.VMEM((5, n_s, d_s, tokens), BF16),
            dma((7,)),
            dma((4,)),
        ],
        hbm=True,
    )
    time_pieces = hops(packed[n_s:], "tm", 1)
    packed = exchange(packed[:n_s], "space")
    probs_dims = (frames, d_s // HEAD_DIM, total, total)
    qkv, probs, *out_s = call(
        functools.partial(space_forward_kernel, frames, n_s),
        [shape((3, frames, d_s, total), BF16), pltpu.HBM(probs_dims, F32)]
        + [shape((d_s, tokens), BF16)] * n_s,
        *packed,
        scratch=[pltpu.VMEM(probs_dims, F32), dma((probs_dims[0] * probs_dims[1],))],
        after=time_pieces[:1],
    )
    out_s = exchange(out_s, "space")
    hidden, *codes = call(
        functools.partial(hidden_kernel, n_t, n_s),
        [shape((tokens, width), BF16)] + [shape((8, 128), F32)] * n_t,
        *out_s, patches, downs,
        scratch=[pltpu.VMEM((n_s, d_s, tokens), BF16), pltpu.VMEM((tokens, 128), F32)],
    )
    codes = exchange(codes, "tm")
    turned = call(
        functools.partial(turn_kernel, frames, sub),
        shape((4, width, n_t * frames * sub), BF16),
        *time_arrays, *time_pieces,
        scratch=[
            pltpu.VMEM((4, frames * sub, width), BF16),
            pltpu.VMEM((n_t - 1, 4, frames * sub, width), BF16),
            dma((4 * frames,)),
            dma((n_t - 1,)),
        ],
        hbm=True,
    )
    timed = call(
        functools.partial(time_kernel, n_t, sub),
        [shape((frames * sub, width), BF16)] * n_t
        + [shape((8, 128), F32)] * n_t
        + [shape((2 * RANK, width), F32)],
        turned, adapters_b, *codes,
    )
    out_t, dcodes, time_grad_b = timed[:n_t], timed[n_t : 2 * n_t], timed[2 * n_t]
    dcodes = exchange(dcodes, "tm")
    out_t[1:2] = hops(out_t[1:2], "tm", 1)
    dcodes = call(
        functools.partial(place_codes_kernel, frames, sub),
        shape((2 * RANK, tokens), BF16),
        *dcodes,
        scratch=[pltpu.VMEM((tokens, 128), F32)],
    )
    dcodes = share(dcodes, "space")
    backward = call(
        functools.partial(space_backward_kernel, frames, n_s),
        [shape((2 * RANK, frames * total + 2 * pad), BF16)] * n_s + [shape((2 * RANK, d_s), F32)],
        qkv, probs, hidden, time_grad_b, downs, downs_here, ups_here, *packed, *dcodes,
        scratch=[pltpu.VMEM((n_s, 2, 2 * RANK, pad), BF16)],
        after=out_t[1:2],
        carry=out_t[2:],
    )
    partial, part = backward[:n_s], backward[n_s]
    partial = exchange(partial, "space")
    out_t[2:] = hops(backward[n_s + 1 :], "tm", 2)
    rows = 8 * RANK // n_d
    sums = call(
        functools.partial(merge_kernel, frames, n_s, n_d),
        [shape((rows, d_s), F32)] * n_d,
        part, *packed, *partial,
        scratch=[pltpu.VMEM((n_d, rows, d_s), F32)],
    )
    sums = call(total_kernel, shape((rows, d_s), BF16), *exchange(sums, "dp"), after=out_t[2:])
    sums = call(total_kernel, shape((rows, d_s), BF16), *share(sums, "tm"))
    sums = call(
        join_kernel,
        shape((rows, width), BF16),
        *share(sums, "space"),
        scratch=[pltpu.VMEM((n_s, rows, d_s), BF16)],
    )
    grads_a, grads_b = call(
        functools.partial(final_kernel, factor, n_d),
        [shape((4, RANK, width), F32)] * 2,
        *share(sums, "dp"),
        scratch=[pltpu.VMEM((n_d, rows, width), BF16)],
    )
    mixed = call(
        functools.partial(mixed_kernel, frames),
        shape(patches.shape, BF16),
        hidden, *out_t,
        scratch=[pltpu.VMEM((tokens, width), BF16)],
    )
    return (mixed, jnp.swapaxes(grads_a, 1, 2), grads_b)


def solution(mesh):
    token = P("dp", "tm", "space", None)
    return jax.shard_map(
        per_device,
        mesh=mesh,
        in_specs=(token,) * 7 + (P(), P(), token),
        out_specs=(token, P(), P()),
        check_vma=False,
    )
```

```python
import functools

import jax
import jax.numpy as jnp
from jax import lax
from jax.experimental import pallas as pl
from jax.experimental.pallas import tpu as pltpu
from jax.sharding import PartitionSpec as P

HEAD_DIM = 72
RANK = 16
SCALE = HEAD_DIM ** (-0.5)
F32 = jnp.float32
BF16 = jnp.bfloat16
NN = (((1,), (0,)), ((), ()))
NT = (((1,), (1,)), ((), ()))
TN = (((0,), (0,)), ((), ()))


def mm(a, b, dims=NN):
    return lax.dot_general(a, b, dims, preferred_element_type=F32)


def far(x):
    return pltpu.with_memory_space_constraint(x, pltpu.HBM)


def call(kernel, out_shape, *args, scratch=(), hbm=False, limit=48, after=(), carry=(), stay=False):
    vmem = pl.BlockSpec(memory_space=pltpu.VMEM)
    anywhere = pl.BlockSpec(memory_space=pl.ANY)
    main = anywhere if hbm else vmem
    single = not isinstance(out_shape, (tuple, list))
    outs = (out_shape,) if single else tuple(out_shape)
    used, extra = len(args), len(after) + len(carry)

    def body(*refs):
        inside = refs[:used] + refs[used + extra : used + extra + len(outs)]
        kernel(*inside, *refs[used + extra + len(outs) + len(carry) :])

    result = pl.pallas_call(
        body,
        out_shape=outs + tuple((pltpu.HBM if stay else shape)(x.shape, x.dtype) for x in carry),
        in_specs=[main] * used + [anywhere] * extra,
        out_specs=tuple(vmem if isinstance(o, jax.ShapeDtypeStruct) else anywhere for o in outs)
        + (anywhere,) * len(carry),
        scratch_shapes=list(scratch),
        input_output_aliases={used + len(after) + i: len(outs) + i for i in range(len(carry))},
        compiler_params=pltpu.CompilerParams(vmem_limit_bytes=limit * 1024 * 1024),
    )(*args, *after, *(far(x) if stay else x for x in carry))
    return result[0] if single and not carry else list(result)


def shape(dims, dtype):
    return jax.ShapeDtypeStruct(tuple(dims), dtype)


def probs_of(keys, q_t, mask):
    scores = mm(keys, q_t) * SCALE
    if mask is not None:
        scores = jnp.where(mask, scores, -1e30)
    peak = jnp.max(scores, axis=0, keepdims=True)
    weights = jnp.exp(scores - peak)
    return weights * (1.0 / jnp.sum(weights, axis=0, keepdims=True))


def head_backward(probs, k_t, v_t, g_t, forward=False):
    low = probs.astype(BF16)
    dvals = mm(g_t, low, NT)
    dprob = mm(v_t.T, g_t)
    inner = jnp.sum(probs * dprob, axis=0, keepdims=True)
    dscore = (probs * (dprob - inner) * SCALE).astype(BF16)
    dquery = mm(k_t, dscore)
    out = mm(v_t, low) if forward else None
    return dquery, dvals, out


def rows_of(array, head):
    return array[head * HEAD_DIM : (head + 1) * HEAD_DIM]


def peer(axis, distance):
    return lax.axis_index(axis) ^ distance


def load_all(refs, buffers, sems):
    copies = [
        pltpu.make_async_copy(ref, buffer, sems.at[index])
        for index, (ref, buffer) in enumerate(zip(refs, buffers))
    ]
    for copy in copies:
        copy.start()
    return copies


def pack_kernel(n_s, n_t, sub, *refs):
    ins, time_ins, refs = refs[:7], refs[7:11], refs[11:]
    outs, sides, refs = refs[:n_s], refs[n_s : 2 * n_s], refs[2 * n_s :]
    time_outs, buffers, refs = refs[: n_t - 1], refs[n_t - 1 : n_t + 6], refs[n_t + 6 :]
    time_buf, turned_ref, codes_ref, sems, time_sems, side_sems = refs
    p_buf, at_buf, b_buf, q_buf, v_buf, k_buf, g_buf = buffers
    copies = load_all(ins, buffers, sems)
    time_copies = load_all(time_ins, [time_buf.at[index] for index in range(4)], time_sems)
    d_s, tokens = turned_ref.shape[2:]
    frames = time_buf.shape[2]

    def flat(ref):
        return ref[0].reshape(tokens, ref.shape[3])

    def send(array, index):
        turned = array.T
        for j in range(n_s):
            turned_ref[index, j] = turned[j * d_s : (j + 1) * d_s]
        for k in range(n_s):
            source = turned_ref.at[index, peer("space", k)]
            if index < 3:
                outs[k][index * d_s : (index + 1) * d_s] = source[...]
            else:
                start_copy(source, sides[k].at[(index - 3) * d_s : (index - 2) * d_s])

    sent = []

    def start_copy(source, target):
        copy = pltpu.make_async_copy(source, target, side_sems.at[len(sent)])
        copy.start()
        sent.append(copy)

    copies[0].wait()
    copies[1].wait()
    copies[2].wait()
    patches = flat(p_buf)
    codes_q = mm(patches, at_buf[0], NT).astype(BF16)
    codes_v = mm(patches, at_buf[1], NT).astype(BF16)
    codes_ref[...] = jnp.concatenate([codes_q, codes_v], axis=1).T
    for k in range(n_s):
        start_copy(codes_ref, sides[k].at[2 * d_s : 2 * d_s + 2 * RANK])
    send(patches, 3)
    copies[3].wait()
    query = (flat(q_buf).astype(F32) + mm(codes_q, b_buf[0])).astype(BF16)
    send(query, 0)
    copies[4].wait()
    value = (flat(v_buf).astype(F32) + mm(codes_v, b_buf[1])).astype(BF16)
    send(value, 2)
    copies[5].wait()
    send(flat(k_buf), 1)
    copies[6].wait()
    send(flat(g_buf), 4)
    for index, copy in enumerate(time_copies):
        copy.wait()
        for k in range(1, n_t):
            start = pl.multiple_of(peer("tm", k) * sub, sub)
            for f in range(frames):
                time_outs[k - 1][index, f * sub : (f + 1) * sub] = time_buf[
                    index, 0, f, pl.ds(start, sub)
                ]
    for copy in sent:
        copy.wait()


def frame_rows(pieces, f, patch_dev):
    return jnp.concatenate([x[:, f * patch_dev : (f + 1) * patch_dev] for x in pieces], axis=1)


def space_forward_kernel(frames, n_s, *refs):
    packed, (qkv_ref, probs_ref, *outs) = refs[:n_s], refs[n_s : 2 * n_s + 2]
    probs_buf, sems = refs[2 * n_s + 2 :]
    copies = []
    d_s, tokens = outs[0].shape
    patch_dev = tokens // frames
    total = n_s * patch_dev
    step = min(total, 256)
    for index in range(3):
        pieces = [x[index * d_s : (index + 1) * d_s] for x in packed]
        for f in range(frames):
            qkv_ref[index, f] = frame_rows(pieces, f, patch_dev)
    for f in range(frames):
        query = qkv_ref[0, f].astype(F32)
        keys = qkv_ref[1, f].astype(F32)
        vals = qkv_ref[2, f].astype(F32)
        heads = []
        for h in range(d_s // HEAD_DIM):
            k_h = rows_of(keys, h).astype(BF16)
            v_h = rows_of(vals, h).astype(BF16)
            q_h = rows_of(query, h).astype(BF16)
            parts = []
            for s in range(0, total, step):
                probs = probs_of(k_h.T, q_h[:, s : s + step], None)
                probs_buf[f, h, :, s : s + step] = probs
                parts.append(mm(v_h, probs.astype(BF16)))
            heads.append(parts[0] if len(parts) == 1 else jnp.concatenate(parts, axis=1))
            copy = pltpu.make_async_copy(
                probs_buf.at[f, h], probs_ref.at[f, h], sems.at[len(copies)]
            )
            copy.start()
            copies.append(copy)
        out = jnp.concatenate(heads, axis=0).astype(BF16)
        for k in range(n_s):
            outs[k][:, f * patch_dev : (f + 1) * patch_dev] = out[
                :, k * patch_dev : (k + 1) * patch_dev
            ]
    for copy in copies:
        copy.wait()


def lane_block(rows):
    return lax.broadcasted_iota(jnp.int32, (rows, 128), 1) // (2 * RANK)


def fold(token_rows):
    block = lane_block(8)
    result = token_rows[0:8]
    for k in range(1, 4):
        result = jnp.where(block == k, token_rows[8 * k : 8 * k + 8], result)
    return result


def unfold(folded):
    pieces = [folded]
    for k in range(1, 4):
        pieces.append(pltpu.roll(folded, 128 - 2 * RANK * k, 1))
    return jnp.concatenate(pieces, axis=0)


def hidden_kernel(n_t, n_s, *refs):
    pieces, refs = refs[:n_s], refs[n_s:]
    p_ref, at_ref, hidden_ref = refs[:3]
    sends = refs[3 : 3 + n_t]
    out_buf, codes_buf = refs[3 + n_t :]
    _, frames, patch_dev, width = p_ref.shape
    tokens = frames * patch_dev
    sub = patch_dev // n_t
    for k in range(n_s):
        out_buf[peer("space", k)] = pieces[k][...]
    out = out_buf[...].reshape(width, tokens).T
    hidden = (p_ref[0].reshape(tokens, width).astype(F32) + out.astype(F32)).astype(BF16)
    hidden_ref[...] = hidden
    downs = jnp.concatenate([at_ref[2], at_ref[3]] * 4, axis=0)
    codes_buf[...] = mm(hidden, downs, NT).astype(BF16).astype(F32)
    for k in range(n_t):
        rows = [
            codes_buf[pl.ds(pl.multiple_of(f * patch_dev + peer("tm", k) * sub, sub), sub)]
            for f in range(frames)
        ]
        sends[k][...] = fold(jnp.concatenate(rows, axis=0))


def turn_kernel(frames, sub, q_ref, k_ref, v_ref, g_ref, *refs):
    *pieces, out_ref, own_buf, piece_buf, own_sems, sems = refs
    own = []
    start = pl.multiple_of(peer("tm", 0) * sub, sub)
    for index, ref in enumerate((q_ref, k_ref, v_ref, g_ref)):
        for f in range(frames):
            copy = pltpu.make_async_copy(
                ref.at[0, f, pl.ds(start, sub)],
                own_buf.at[index, f * sub : (f + 1) * sub],
                own_sems.at[index * frames + f],
            )
            copy.start()
            own.append(copy)
    copies = load_all(pieces, [piece_buf.at[k] for k in range(len(pieces))], sems)
    for copy in own + copies:
        copy.wait()
    for index in range(4):
        parts = [own_buf[index]] + [piece_buf[k, index] for k in range(len(pieces))]
        out_ref[index] = jnp.concatenate(parts, axis=0).T


def time_kernel(n_t, sub, x_ref, b_ref, *refs):
    codes_refs, refs = refs[:n_t], refs[n_t:]
    outs, sends, grad_b_ref = refs[:n_t], refs[n_t : 2 * n_t], refs[2 * n_t]
    _, width, tokens = x_ref.shape
    codes = jnp.concatenate([unfold(ref[...]) for ref in codes_refs], axis=0).T
    codes_q = codes[:RANK].astype(BF16)
    codes_v = codes[RANK : 2 * RANK].astype(BF16)
    query = (x_ref[0].astype(F32) + mm(b_ref[2], codes_q, TN)).astype(BF16).astype(F32)
    vals = (x_ref[2].astype(F32) + mm(b_ref[3], codes_v, TN)).astype(BF16).astype(F32)
    keys = x_ref[1].astype(F32)
    grad = x_ref[3].astype(F32)
    row = lax.broadcasted_iota(jnp.int32, (tokens, tokens), 0)
    col = lax.broadcasted_iota(jnp.int32, (tokens, tokens), 1)
    mask = lax.rem(row, sub) == lax.rem(col, sub)
    outs_h, d_query, d_vals = [], [], []
    for h in range(width // HEAD_DIM):
        k_h = rows_of(keys, h).astype(BF16)
        v_h = rows_of(vals, h).astype(BF16)
        probs = probs_of(k_h.T, rows_of(query, h).astype(BF16), mask)
        dq, dv, out = head_backward(probs, k_h, v_h, rows_of(grad, h).astype(BF16), True)
        outs_h.append(out)
        d_query.append(dq)
        d_vals.append(dv)
    d_query = jnp.concatenate(d_query, axis=0).astype(BF16)
    d_vals = jnp.concatenate(d_vals, axis=0).astype(BF16)
    d_codes = jnp.concatenate([mm(b_ref[2], d_query), mm(b_ref[3], d_vals)] * 4, axis=0)
    d_codes = d_codes.astype(BF16).astype(F32).T
    per = tokens // n_t
    for k in range(n_t):
        sends[k][...] = fold(d_codes[k * per : (k + 1) * per])
    out = jnp.concatenate(outs_h, axis=0).astype(BF16).T
    for k in range(n_t):
        outs[k][...] = out[k * per : (k + 1) * per]
    grad_b_ref[:RANK] = mm(codes_q, d_query, NT)
    grad_b_ref[RANK:] = mm(codes_v, d_vals, NT)


def place_codes_kernel(frames, sub, *refs):
    pieces, (out_ref, buf) = refs[:-2], refs[-2:]
    patch_dev = sub * len(pieces)
    for k, piece in enumerate(pieces):
        rows = unfold(piece[...])
        for f in range(frames):
            start = pl.multiple_of(f * patch_dev + peer("tm", k) * sub, sub)
            buf[pl.ds(start, sub)] = rows[f * sub : (f + 1) * sub]
    out_ref[...] = buf[...].T[: 2 * RANK].astype(BF16)


def space_backward_kernel(frames, n_s, qkv_ref, probs_ref, hidden_ref, grad_b_ref, at_ref, at_here_ref, b_here_ref, *refs):
    sides, dcodes, sends = refs[:n_s], refs[n_s : 2 * n_s], refs[2 * n_s : 3 * n_s]
    part_ref, cut_buf = refs[3 * n_s :]
    d_s = part_ref.shape[1]
    tokens = hidden_ref.shape[0]
    patch_dev = tokens // frames
    total = n_s * patch_dev
    step = min(total, 256)
    ups = jnp.concatenate([at_here_ref[2], at_here_ref[3]], axis=0).T
    grads = []
    for k in range(n_s):
        cot = sides[k][d_s : 2 * d_s].astype(F32)
        grads.append((cot + mm(ups, dcodes[k][...])).astype(BF16))
    grad_b_q = grad_b_v = None
    codes = [x[2 * d_s :] for x in sides]
    for f in range(frames):
        keys = qkv_ref[1, f].astype(F32)
        vals = qkv_ref[2, f].astype(F32)
        grad = frame_rows(grads, f, patch_dev).astype(F32)
        d_query, d_vals = [], []
        for h in range(d_s // HEAD_DIM):
            k_h = rows_of(keys, h).astype(BF16)
            v_h = rows_of(vals, h).astype(BF16)
            g_h = rows_of(grad, h).astype(BF16)
            dq_parts, dv_sum = [], None
            for s in range(0, total, step):
                probs = probs_ref[f, h, :, s : s + step]
                dq, dv, _ = head_backward(probs, k_h, v_h, g_h[:, s : s + step])
                dq_parts.append(dq)
                dv_sum = dv if dv_sum is None else dv_sum + dv
            d_query.append(
                dq_parts[0] if len(dq_parts) == 1 else jnp.concatenate(dq_parts, axis=1)
            )
            d_vals.append(dv_sum)
        d_query = jnp.concatenate(d_query, axis=0).astype(BF16)
        d_vals = jnp.concatenate(d_vals, axis=0).astype(BF16)
        partial = jnp.concatenate([mm(b_here_ref[0], d_query), mm(b_here_ref[1], d_vals)], axis=0)
        partial = partial.astype(BF16)
        blocks = [partial[:, m * patch_dev : (m + 1) * patch_dev] for m in range(n_s)]
        for k in range(n_s):
            turned = jnp.concatenate([blocks[m ^ k] for m in range(n_s)], axis=1)
            sends[k][:, f * total : (f + 1) * total] = turned
        frame_codes = frame_rows(codes, f, patch_dev)
        term_q = mm(frame_codes[:RANK], d_query, NT)
        term_v = mm(frame_codes[RANK:], d_vals, NT)
        grad_b_q = term_q if grad_b_q is None else grad_b_q + term_q
        grad_b_v = term_v if grad_b_v is None else grad_b_v + term_v
    part_ref[:RANK] = grad_b_q
    part_ref[RANK:] = grad_b_v
    grad_a = mm(dcodes[0][...], hidden_ref[...])
    pad = -(-d_s // 128) * 128
    for j in range(n_s):
        cut_buf[j, 0, :, :d_s] = grad_a[:, j * d_s : (j + 1) * d_s].astype(BF16)
        cut_buf[j, 1, :, :d_s] = grad_b_ref[:, j * d_s : (j + 1) * d_s].astype(BF16)
    for k in range(n_s):
        for index in range(2):
            start = frames * total + index * pad
            sends[k][:, start : start + pad] = cut_buf[peer("space", k), index]


def add_up(terms):
    result = None
    for term in terms:
        result = term if result is None else result + term
    return result


def merge_kernel(frames, n_s, n_d, part_ref, *refs):
    sides, recvs, refs = refs[:n_s], refs[n_s : 2 * n_s], refs[2 * n_s :]
    sends, buf = refs[:n_d], refs[n_d]
    d_s = part_ref.shape[1]
    tokens = sides[0].shape[1]
    patch_dev = tokens // frames
    total = n_s * patch_dev
    pad = -(-d_s // 128) * 128
    patches = [x[:d_s] for x in sides]
    terms = []
    for f in range(frames):
        codes = [recv[:, f * total : (f + 1) * total].astype(F32) for recv in recvs]
        terms.append(mm(add_up(codes).astype(BF16), frame_rows(patches, f, patch_dev), NT))
    start = frames * total
    time_a = add_up([recv[:, start : start + d_s].astype(F32) for recv in recvs])
    time_b = add_up([recv[:, start + pad : start + pad + d_s].astype(F32) for recv in recvs])
    rows = jnp.concatenate([add_up(terms), time_a, part_ref[...], time_b], axis=0)
    per = rows.shape[0] // n_d
    for d in range(n_d):
        buf[d] = rows[d * per : (d + 1) * per]
    for k in range(n_d):
        sends[k][...] = buf[peer("dp", k)]


def total_kernel(*refs):
    terms = [ref[...].astype(F32) for ref in refs[:-1]]
    while len(terms) > 1:
        terms = [terms[i] + terms[i + 1] for i in range(0, len(terms), 2)]
    refs[-1][...] = terms[0].astype(refs[-1].dtype)


def join_kernel(*refs):
    pieces, (out_ref, buf) = refs[:-2], refs[-2:]
    for k, piece in enumerate(pieces):
        buf[peer("space", k)] = piece[...]
    out_ref[...] = jnp.concatenate([buf[j] for j in range(len(pieces))], axis=1)


def final_kernel(factor, n_d, *refs):
    pieces, (a_ref, b_ref, buf) = refs[:n_d], refs[n_d:]
    for k, piece in enumerate(pieces):
        buf[peer("dp", k)] = piece[...]
    per = pieces[0].shape[0]
    half = n_d // 2
    for d in range(n_d):
        rows = buf[d].astype(F32) * factor
        target = a_ref if d < half else b_ref
        for r in range(0, per, min(per, RANK)):
            start = (d % half) * per + r
            size = min(per, RANK)
            target[start // RANK, start % RANK : start % RANK + size] = rows[r : r + size]


def mixed_kernel(frames, hidden_ref, *refs):
    pieces, (mixed_ref, buf) = refs[:-2], refs[-2:]
    n_t = len(pieces)
    tokens, width = hidden_ref.shape
    patch_dev = tokens // frames
    sub = patch_dev // n_t
    for k, piece in enumerate(pieces):
        for f in range(frames):
            start = pl.multiple_of(f * patch_dev + peer("tm", k) * sub, sub)
            buf[pl.ds(start, sub)] = piece[f * sub : (f + 1) * sub]
    total = hidden_ref[...].astype(F32) + buf[...].astype(F32)
    mixed_ref[0] = total.astype(BF16).reshape(frames, patch_dev, width)


def hops(arrays, axis, first):
    size = lax.axis_size(axis)
    return [
        lax.ppermute(array, axis, [(i, i ^ k) for i in range(size)])
        for k, array in enumerate(arrays, first)
    ]


def exchange(pieces, axis):
    return [pieces[0]] + hops(pieces[1:], axis, 1)


def share(array, axis):
    return exchange([array] * lax.axis_size(axis), axis)


def per_device(
    patches, query_s, key_s, value_s, query_t, key_t, value_t, adapters_a, adapters_b, cotangent
):
    _, frames, patch_dev, width = patches.shape
    n_d, n_t, n_s = (lax.axis_size(name) for name in ("dp", "tm", "space"))
    tokens = frames * patch_dev
    sub = patch_dev // n_t
    d_s = width // n_s
    total = n_s * patch_dev
    factor = (tokens * n_d * n_t * n_s) ** (-0.5)
    here = lax.axis_index("space") * d_s
    downs = jnp.swapaxes(adapters_a, 1, 2)
    downs_here = lax.dynamic_slice_in_dim(downs, here, d_s, 2)
    ups_here = lax.dynamic_slice_in_dim(adapters_b, here, d_s, 2)
    dma = pltpu.SemaphoreType.DMA
    pad = -(-d_s // 128) * 128

    time_arrays = [far(x) for x in (query_t, key_t, value_t, cotangent)]
    space_arrays = [
        far(x) for x in (patches, downs, adapters_b, query_s, value_s, key_s, cotangent)
    ]
    packed = call(
        functools.partial(pack_kernel, n_s, n_t, sub),
        [shape((3 * d_s, tokens), BF16)] * n_s
        + [pltpu.HBM((2 * d_s + 2 * RANK, tokens), BF16)] * n_s
        + [shape((4, frames * sub, width), BF16)] * (n_t - 1),
        *space_arrays, *time_arrays,
        scratch=[pltpu.VMEM(x.shape, BF16) for x in space_arrays]
        + [
            pltpu.VMEM((4,) + query_t.shape, BF16),
            pltpu.VMEM((5, n_s, d_s, tokens), BF16),
            pltpu.VMEM((2 * RANK, tokens), BF16),
            dma((7,)),
            dma((4,)),
            dma((3 * n_s,)),
        ],
        hbm=True,
    )
    sides, time_pieces = packed[n_s : 2 * n_s], hops(packed[2 * n_s :], "tm", 1)
    packed = exchange(packed[:n_s], "space")
    probs_dims = (frames, d_s // HEAD_DIM, total, total)
    qkv, probs, *out_s = call(
        functools.partial(space_forward_kernel, frames, n_s),
        [shape((3, frames, d_s, total), BF16), pltpu.HBM(probs_dims, F32)]
        + [shape((d_s, tokens), BF16)] * n_s,
        *packed,
        scratch=[pltpu.VMEM(probs_dims, F32), dma((probs_dims[0] * probs_dims[1],))],
        after=time_pieces[:1],
    )
    out_s = exchange(out_s, "space")
    hidden, *codes = call(
        functools.partial(hidden_kernel, n_t, n_s),
        [shape((tokens, width), BF16)] + [shape((8, 128), F32)] * n_t,
        *out_s, patches, downs,
        scratch=[pltpu.VMEM((n_s, d_s, tokens), BF16), pltpu.VMEM((tokens, 128), F32)],
    )
    codes = exchange(codes, "tm")
    turned = call(
        functools.partial(turn_kernel, frames, sub),
        shape((4, width, n_t * frames * sub), BF16),
        *time_arrays, *time_pieces,
        scratch=[
            pltpu.VMEM((4, frames * sub, width), BF16),
            pltpu.VMEM((n_t - 1, 4, frames * sub, width), BF16),
            dma((4 * frames,)),
            dma((n_t - 1,)),
        ],
        hbm=True,
    )
    timed = call(
        functools.partial(time_kernel, n_t, sub),
        [shape((frames * sub, width), BF16)] * n_t
        + [shape((8, 128), F32)] * n_t
        + [shape((2 * RANK, width), F32)],
        turned, adapters_b, *codes,
        carry=sides[1:],
        stay=True,
    )
    out_t, dcodes, time_grad_b = timed[:n_t], timed[n_t : 2 * n_t], timed[2 * n_t]
    sides[1:] = hops(timed[2 * n_t + 1 :], "space", 1)
    dcodes = exchange(dcodes, "tm")
    out_t[1:2] = hops(out_t[1:2], "tm", 1)
    dcodes = call(
        functools.partial(place_codes_kernel, frames, sub),
        shape((2 * RANK, tokens), BF16),
        *dcodes,
        scratch=[pltpu.VMEM((tokens, 128), F32)],
    )
    dcodes = share(dcodes, "space")
    backward = call(
        functools.partial(space_backward_kernel, frames, n_s),
        [shape((2 * RANK, frames * total + 2 * pad), BF16)] * n_s + [shape((2 * RANK, d_s), F32)],
        qkv, probs, hidden, time_grad_b, downs, downs_here, ups_here, *sides, *dcodes,
        scratch=[pltpu.VMEM((n_s, 2, 2 * RANK, pad), BF16)],
        after=out_t[1:2],
        carry=out_t[2:],
    )
    partial, part = backward[:n_s], backward[n_s]
    partial = exchange(partial, "space")
    out_t[2:] = hops(backward[n_s + 1 :], "tm", 2)
    rows = 8 * RANK // n_d
    sums = call(
        functools.partial(merge_kernel, frames, n_s, n_d),
        [shape((rows, d_s), F32)] * n_d,
        part, *sides, *partial,
        scratch=[pltpu.VMEM((n_d, rows, d_s), F32)],
    )
    sums = call(total_kernel, shape((rows, d_s), BF16), *exchange(sums, "dp"), after=out_t[2:])
    sums = call(total_kernel, shape((rows, d_s), BF16), *share(sums, "tm"))
    sums = call(
        join_kernel,
        shape((rows, width), BF16),
        *share(sums, "space"),
        scratch=[pltpu.VMEM((n_s, rows, d_s), BF16)],
    )
    grads_a, grads_b = call(
        functools.partial(final_kernel, factor, n_d),
        [shape((4, RANK, width), F32)] * 2,
        *share(sums, "dp"),
        scratch=[pltpu.VMEM((n_d, rows, width), BF16)],
    )
    mixed = call(
        functools.partial(mixed_kernel, frames),
        shape(patches.shape, BF16),
        hidden, *out_t,
        scratch=[pltpu.VMEM((tokens, width), BF16)],
    )
    return (mixed, jnp.swapaxes(grads_a, 1, 2), grads_b)


def solution(mesh):
    token = P("dp", "tm", "space", None)
    return jax.shard_map(
        per_device,
        mesh=mesh,
        in_specs=(token,) * 7 + (P(), P(), token),
        out_specs=(token, P(), P()),
        check_vma=False,
    )
```

```python
import functools

import jax
import jax.numpy as jnp
from jax import lax
from jax.experimental import pallas as pl
from jax.experimental.pallas import tpu as pltpu
from jax.sharding import PartitionSpec as P

HEAD_DIM = 72
RANK = 16
SCALE = HEAD_DIM ** (-0.5)
F32 = jnp.float32
BF16 = jnp.bfloat16
NN = (((1,), (0,)), ((), ()))
NT = (((1,), (1,)), ((), ()))
TN = (((0,), (0,)), ((), ()))


def mm(a, b, dims=NN):
    return lax.dot_general(a, b, dims, preferred_element_type=F32)


def far(x):
    return pltpu.with_memory_space_constraint(x, pltpu.HBM)


def call(kernel, out_shape, *args, scratch=(), hbm=False, limit=48, after=(), carry=()):
    vmem = pl.BlockSpec(memory_space=pltpu.VMEM)
    anywhere = pl.BlockSpec(memory_space=pl.ANY)
    main = anywhere if hbm else vmem
    single = not isinstance(out_shape, (tuple, list))
    outs = (out_shape,) if single else tuple(out_shape)
    used, extra = len(args), len(after) + len(carry)

    def body(*refs):
        inside = refs[:used] + refs[used + extra : used + extra + len(outs)]
        kernel(*inside, *refs[used + extra + len(outs) + len(carry) :])

    result = pl.pallas_call(
        body,
        out_shape=outs + tuple(shape(x.shape, x.dtype) for x in carry),
        in_specs=[main] * used + [anywhere] * extra,
        out_specs=tuple(vmem if isinstance(o, jax.ShapeDtypeStruct) else anywhere for o in outs)
        + (anywhere,) * len(carry),
        scratch_shapes=list(scratch),
        input_output_aliases={used + len(after) + i: len(outs) + i for i in range(len(carry))},
        compiler_params=pltpu.CompilerParams(vmem_limit_bytes=limit * 1024 * 1024),
    )(*args, *after, *carry)
    return result[0] if single and not carry else list(result)


def shape(dims, dtype):
    return jax.ShapeDtypeStruct(tuple(dims), dtype)


def probs_of(keys, q_t, mask):
    scores = mm(keys, q_t) * SCALE
    if mask is not None:
        scores = jnp.where(mask, scores, -1e30)
    peak = jnp.max(scores, axis=0, keepdims=True)
    weights = jnp.exp(scores - peak)
    return weights * (1.0 / jnp.sum(weights, axis=0, keepdims=True))


def head_backward(probs, k_t, v_t, g_t):
    low = probs.astype(BF16)
    dvals = mm(g_t, low, NT)
    dprob = mm(v_t.T, g_t)
    inner = jnp.sum(probs * dprob, axis=0, keepdims=True)
    dscore = (probs * (dprob - inner) * SCALE).astype(BF16)
    dquery = mm(k_t, dscore)
    return dquery, dvals


def rows_of(array, head):
    return array[head * HEAD_DIM : (head + 1) * HEAD_DIM]


def peer(axis, distance):
    return lax.axis_index(axis) ^ distance


def load_all(refs, buffers, sems):
    copies = [
        pltpu.make_async_copy(ref, buffer, sems.at[index])
        for index, (ref, buffer) in enumerate(zip(refs, buffers))
    ]
    for copy in copies:
        copy.start()
    return copies


def pack_kernel(n_s, n_t, sub, *refs):
    ins, time_ins, refs = refs[:7], refs[7:11], refs[11:]
    outs, time_outs, refs = refs[:n_s], refs[n_s : n_s + n_t - 1], refs[n_s + n_t - 1 :]
    buffers, (time_buf, turned_ref, sems, time_sems) = refs[:7], refs[7:]
    p_buf, at_buf, b_buf, q_buf, v_buf, k_buf, g_buf = buffers
    copies = load_all(ins, buffers, sems)
    time_copies = load_all(time_ins, [time_buf.at[index] for index in range(4)], time_sems)
    d_s, tokens = turned_ref.shape[2:]
    frames = time_buf.shape[2]

    def flat(ref):
        return ref[0].reshape(tokens, ref.shape[3])

    def send(array, index):
        turned = array.T
        for j in range(n_s):
            turned_ref[index, j] = turned[j * d_s : (j + 1) * d_s]
        for k in range(n_s):
            outs[k][index * d_s : (index + 1) * d_s] = turned_ref[index, peer("space", k)]

    copies[0].wait()
    copies[1].wait()
    copies[2].wait()
    patches = flat(p_buf)
    codes_q = mm(patches, at_buf[0], NT).astype(BF16)
    codes_v = mm(patches, at_buf[1], NT).astype(BF16)
    codes_t = jnp.concatenate([codes_q, codes_v], axis=1).T
    copies[3].wait()
    query = (flat(q_buf).astype(F32) + mm(codes_q, b_buf[0])).astype(BF16)
    send(query, 0)
    copies[4].wait()
    value = (flat(v_buf).astype(F32) + mm(codes_v, b_buf[1])).astype(BF16)
    send(value, 2)
    copies[5].wait()
    send(flat(k_buf), 1)
    send(patches, 3)
    copies[6].wait()
    send(flat(g_buf), 4)
    for k in range(n_s):
        outs[k][5 * d_s :] = codes_t
    for index, copy in enumerate(time_copies):
        copy.wait()
        for k in range(1, n_t):
            start = pl.multiple_of(peer("tm", k) * sub, sub)
            for f in range(frames):
                time_outs[k - 1][index, f * sub : (f + 1) * sub] = time_buf[
                    index, 0, f, pl.ds(start, sub)
                ]


def frame_rows(pieces, f, patch_dev):
    return jnp.concatenate([x[:, f * patch_dev : (f + 1) * patch_dev] for x in pieces], axis=1)


def space_forward_kernel(frames, n_s, *refs):
    packed, (qkv_ref, probs_ref, *outs) = refs[:n_s], refs[n_s : 2 * n_s + 2]
    probs_buf, sems = refs[2 * n_s + 2 :]
    copies = []
    d_s, tokens = outs[0].shape
    patch_dev = tokens // frames
    total = n_s * patch_dev
    step = min(total, 256)
    for index in range(3):
        pieces = [x[index * d_s : (index + 1) * d_s] for x in packed]
        for f in range(frames):
            qkv_ref[index, f] = frame_rows(pieces, f, patch_dev)
    for f in range(frames):
        query = qkv_ref[0, f].astype(F32)
        keys = qkv_ref[1, f].astype(F32)
        vals = qkv_ref[2, f].astype(F32)
        heads = []
        for h in range(d_s // HEAD_DIM):
            k_h = rows_of(keys, h).astype(BF16)
            v_h = rows_of(vals, h).astype(BF16)
            q_h = rows_of(query, h).astype(BF16)
            parts = []
            for s in range(0, total, step):
                probs = probs_of(k_h.T, q_h[:, s : s + step], None)
                probs_buf[f, h, :, s : s + step] = probs
                parts.append(mm(v_h, probs.astype(BF16)))
            heads.append(parts[0] if len(parts) == 1 else jnp.concatenate(parts, axis=1))
            copy = pltpu.make_async_copy(
                probs_buf.at[f, h], probs_ref.at[f, h], sems.at[len(copies)]
            )
            copy.start()
            copies.append(copy)
        out = jnp.concatenate(heads, axis=0).astype(BF16)
        for k in range(n_s):
            outs[k][:, f * patch_dev : (f + 1) * patch_dev] = out[
                :, k * patch_dev : (k + 1) * patch_dev
            ]
    for copy in copies:
        copy.wait()


def lane_block(rows):
    return lax.broadcasted_iota(jnp.int32, (rows, 128), 1) // (2 * RANK)


def fold(token_rows):
    block = lane_block(8)
    result = token_rows[0:8]
    for k in range(1, 4):
        result = jnp.where(block == k, token_rows[8 * k : 8 * k + 8], result)
    return result


def unfold(folded):
    pieces = [folded]
    for k in range(1, 4):
        pieces.append(pltpu.roll(folded, 128 - 2 * RANK * k, 1))
    return jnp.concatenate(pieces, axis=0)


def hidden_kernel(n_t, n_s, *refs):
    pieces, refs = refs[:n_s], refs[n_s:]
    p_ref, at_ref, hidden_ref = refs[:3]
    sends = refs[3 : 3 + n_t]
    out_buf, codes_buf = refs[3 + n_t :]
    _, frames, patch_dev, width = p_ref.shape
    tokens = frames * patch_dev
    sub = patch_dev // n_t
    for k in range(n_s):
        out_buf[peer("space", k)] = pieces[k][...]
    out = out_buf[...].reshape(width, tokens).T
    hidden = (p_ref[0].reshape(tokens, width).astype(F32) + out.astype(F32)).astype(BF16)
    hidden_ref[...] = hidden
    downs = jnp.concatenate([at_ref[2], at_ref[3]] * 4, axis=0)
    codes_buf[...] = mm(hidden, downs, NT).astype(BF16).astype(F32)
    for k in range(n_t):
        rows = [
            codes_buf[pl.ds(pl.multiple_of(f * patch_dev + peer("tm", k) * sub, sub), sub)]
            for f in range(frames)
        ]
        sends[k][...] = fold(jnp.concatenate(rows, axis=0))


def turn_kernel(frames, sub, q_ref, k_ref, v_ref, g_ref, *refs):
    *pieces, out_ref, own_buf, piece_buf, own_sems, sems = refs
    own = []
    start = pl.multiple_of(peer("tm", 0) * sub, sub)
    for index, ref in enumerate((q_ref, k_ref, v_ref, g_ref)):
        for f in range(frames):
            copy = pltpu.make_async_copy(
                ref.at[0, f, pl.ds(start, sub)],
                own_buf.at[index, f * sub : (f + 1) * sub],
                own_sems.at[index * frames + f],
            )
            copy.start()
            own.append(copy)
    copies = load_all(pieces, [piece_buf.at[k] for k in range(len(pieces))], sems)
    for copy in own + copies:
        copy.wait()
    for index in range(4):
        parts = [own_buf[index]] + [piece_buf[k, index] for k in range(len(pieces))]
        out_ref[index] = jnp.concatenate(parts, axis=0).T


def time_kernel(n_t, sub, x_ref, b_ref, *refs):
    codes_refs, refs = refs[:n_t], refs[n_t:]
    outs, sends, grad_b_ref = refs[:n_t], refs[n_t : 2 * n_t], refs[2 * n_t]
    _, width, tokens = x_ref.shape
    codes = jnp.concatenate([unfold(ref[...]) for ref in codes_refs], axis=0).T
    codes_q = codes[:RANK].astype(BF16)
    codes_v = codes[RANK : 2 * RANK].astype(BF16)
    query = (x_ref[0].astype(F32) + mm(b_ref[2], codes_q, TN)).astype(BF16).astype(F32)
    vals = (x_ref[2].astype(F32) + mm(b_ref[3], codes_v, TN)).astype(BF16).astype(F32)
    keys = x_ref[1].astype(F32)
    grad = x_ref[3].astype(F32)
    row = lax.broadcasted_iota(jnp.int32, (tokens, 2 * tokens), 0)
    col = lax.broadcasted_iota(jnp.int32, (tokens, 2 * tokens), 1)
    mask = lax.rem(row, sub) == lax.rem(col, sub)
    top = lax.broadcasted_iota(jnp.int32, (2 * HEAD_DIM, tokens), 0) < HEAD_DIM

    def spread(pair):
        return jnp.concatenate(
            [jnp.where(top, pair, 0.0), jnp.where(top, 0.0, pair)], axis=1
        ).astype(BF16)

    def pick(wide):
        return jnp.concatenate([wide[:HEAD_DIM, :tokens], wide[HEAD_DIM:, tokens:]], axis=0)

    outs_h, d_query, d_vals = [], [], []
    for h in range(0, width, 2 * HEAD_DIM):
        pair = slice(h, h + 2 * HEAD_DIM)
        k_h, v_h = keys[pair].astype(BF16), vals[pair].astype(BF16)
        g_h = spread(grad[pair])
        probs = probs_of(k_h.T, spread(query[pair]), mask)
        low = probs.astype(BF16)
        dprob = mm(v_h.T, g_h)
        inner = jnp.sum(probs * dprob, axis=0, keepdims=True)
        dscore = (probs * (dprob - inner) * SCALE).astype(BF16)
        outs_h.append(pick(mm(v_h, low)))
        d_vals.append(mm(g_h, low, NT))
        d_query.append(pick(mm(k_h, dscore)))
    d_query = jnp.concatenate(d_query, axis=0).astype(BF16)
    d_vals = jnp.concatenate(d_vals, axis=0).astype(BF16)
    d_codes = jnp.concatenate([mm(b_ref[2], d_query), mm(b_ref[3], d_vals)] * 4, axis=0)
    d_codes = d_codes.astype(BF16).astype(F32).T
    per = tokens // n_t
    for k in range(n_t):
        sends[k][...] = fold(d_codes[k * per : (k + 1) * per])
    out = jnp.concatenate(outs_h, axis=0).astype(BF16).T
    for k in range(n_t):
        outs[k][...] = out[k * per : (k + 1) * per]
    grad_b_ref[:RANK] = mm(codes_q, d_query, NT)
    grad_b_ref[RANK:] = mm(codes_v, d_vals, NT)


def place_codes_kernel(frames, sub, *refs):
    pieces, (out_ref, buf) = refs[:-2], refs[-2:]
    patch_dev = sub * len(pieces)
    for k, piece in enumerate(pieces):
        rows = unfold(piece[...])
        for f in range(frames):
            start = pl.multiple_of(f * patch_dev + peer("tm", k) * sub, sub)
            buf[pl.ds(start, sub)] = rows[f * sub : (f + 1) * sub]
    out_ref[...] = buf[...].T[: 2 * RANK].astype(BF16)


def space_backward_kernel(frames, n_s, qkv_ref, probs_ref, hidden_ref, grad_b_ref, at_ref, at_here_ref, b_here_ref, *refs):
    packed, dcodes, sends = refs[:n_s], refs[n_s : 2 * n_s], refs[2 * n_s : 3 * n_s]
    part_ref, cut_buf = refs[3 * n_s :]
    d_s = part_ref.shape[1]
    tokens = hidden_ref.shape[0]
    patch_dev = tokens // frames
    total = n_s * patch_dev
    step = min(total, 256)
    ups = jnp.concatenate([at_here_ref[2], at_here_ref[3]], axis=0).T
    grads = []
    for k in range(n_s):
        cot = packed[k][4 * d_s : 5 * d_s].astype(F32)
        grads.append((cot + mm(ups, dcodes[k][...])).astype(BF16))
    grad_b_q = grad_b_v = None
    codes = [x[5 * d_s :] for x in packed]
    for f in range(frames):
        keys = qkv_ref[1, f].astype(F32)
        vals = qkv_ref[2, f].astype(F32)
        grad = frame_rows(grads, f, patch_dev).astype(F32)
        d_query, d_vals = [], []
        for h in range(d_s // HEAD_DIM):
            k_h = rows_of(keys, h).astype(BF16)
            v_h = rows_of(vals, h).astype(BF16)
            g_h = rows_of(grad, h).astype(BF16)
            dq_parts, dv_sum = [], None
            for s in range(0, total, step):
                probs = probs_ref[f, h, :, s : s + step]
                dq, dv = head_backward(probs, k_h, v_h, g_h[:, s : s + step])
                dq_parts.append(dq)
                dv_sum = dv if dv_sum is None else dv_sum + dv
            d_query.append(
                dq_parts[0] if len(dq_parts) == 1 else jnp.concatenate(dq_parts, axis=1)
            )
            d_vals.append(dv_sum)
        d_query = jnp.concatenate(d_query, axis=0).astype(BF16)
        d_vals = jnp.concatenate(d_vals, axis=0).astype(BF16)
        partial = jnp.concatenate([mm(b_here_ref[0], d_query), mm(b_here_ref[1], d_vals)], axis=0)
        partial = partial.astype(BF16)
        blocks = [partial[:, m * patch_dev : (m + 1) * patch_dev] for m in range(n_s)]
        for k in range(n_s):
            turned = jnp.concatenate([blocks[m ^ k] for m in range(n_s)], axis=1)
            sends[k][:, f * total : (f + 1) * total] = turned
        frame_codes = frame_rows(codes, f, patch_dev)
        term_q = mm(frame_codes[:RANK], d_query, NT)
        term_v = mm(frame_codes[RANK:], d_vals, NT)
        grad_b_q = term_q if grad_b_q is None else grad_b_q + term_q
        grad_b_v = term_v if grad_b_v is None else grad_b_v + term_v
    part_ref[:RANK] = grad_b_q
    part_ref[RANK:] = grad_b_v
    grad_a = mm(dcodes[0][...], hidden_ref[...])
    for j in range(n_s):
        here = slice(j * d_s, (j + 1) * d_s)
        cut_buf[j, :, :d_s] = grad_a[:, here].astype(BF16)
        cut_buf[j, :, d_s:] = grad_b_ref[:, here].astype(BF16)
    for k in range(n_s):
        sends[k][:, frames * total :] = cut_buf[peer("space", k)]


def add_up(terms):
    result = None
    for term in terms:
        result = term if result is None else result + term
    return result


def merge_kernel(frames, n_s, n_d, part_ref, *refs):
    packed, recvs, refs = refs[:n_s], refs[n_s : 2 * n_s], refs[2 * n_s :]
    sends, buf = refs[:n_d], refs[n_d]
    d_s = part_ref.shape[1]
    tokens = packed[0].shape[1]
    patch_dev = tokens // frames
    total = n_s * patch_dev
    patches = [x[3 * d_s : 4 * d_s] for x in packed]
    terms = []
    for f in range(frames):
        codes = [recv[:, f * total : (f + 1) * total].astype(F32) for recv in recvs]
        terms.append(mm(add_up(codes).astype(BF16), frame_rows(patches, f, patch_dev), NT))
    start = frames * total
    time_a = add_up([recv[:, start : start + d_s].astype(F32) for recv in recvs])
    time_b = add_up([recv[:, start + d_s : start + 2 * d_s].astype(F32) for recv in recvs])
    rows = jnp.concatenate([add_up(terms), time_a, part_ref[...], time_b], axis=0)
    per = rows.shape[0] // n_d
    for d in range(n_d):
        mine = rows[d * per : (d + 1) * per]
        buf[d] = jnp.concatenate([mine[: per // 2], mine[per // 2 :]], axis=1)
    for k in range(n_d):
        sends[k][...] = buf[peer("dp", k)]


def total_kernel(*refs):
    terms = [ref[...].astype(F32) for ref in refs[:-1]]
    while len(terms) > 1:
        terms = [terms[i] + terms[i + 1] for i in range(0, len(terms), 2)]
    refs[-1][...] = terms[0].astype(refs[-1].dtype)


def join_kernel(*refs):
    pieces, (out_ref, buf) = refs[:-2], refs[-2:]
    for k, piece in enumerate(pieces):
        buf[peer("space", k)] = piece[...]
    half, d_s = buf.shape[1], buf.shape[2] // 2
    for h in range(2):
        cuts = [buf[j, :, h * d_s : (h + 1) * d_s] for j in range(len(pieces))]
        out_ref[h * half : (h + 1) * half] = jnp.concatenate(cuts, axis=1)


def final_kernel(factor, n_d, *refs):
    pieces, (a_ref, b_ref, buf) = refs[:n_d], refs[n_d:]
    for k, piece in enumerate(pieces):
        buf[peer("dp", k)] = piece[...]
    per = pieces[0].shape[0]
    half = n_d // 2
    for d in range(n_d):
        rows = buf[d].astype(F32) * factor
        target = a_ref if d < half else b_ref
        for r in range(0, per, min(per, RANK)):
            start = (d % half) * per + r
            size = min(per, RANK)
            target[start // RANK, start % RANK : start % RANK + size] = rows[r : r + size]


def mixed_kernel(frames, hidden_ref, *refs):
    pieces, (mixed_ref, buf) = refs[:-2], refs[-2:]
    n_t = len(pieces)
    tokens, width = hidden_ref.shape
    patch_dev = tokens // frames
    sub = patch_dev // n_t
    for k, piece in enumerate(pieces):
        for f in range(frames):
            start = pl.multiple_of(f * patch_dev + peer("tm", k) * sub, sub)
            buf[pl.ds(start, sub)] = piece[f * sub : (f + 1) * sub]
    total = hidden_ref[...].astype(F32) + buf[...].astype(F32)
    mixed_ref[0] = total.astype(BF16).reshape(frames, patch_dev, width)


def hops(arrays, axis, first):
    size = lax.axis_size(axis)
    return [
        lax.ppermute(array, axis, [(i, i ^ k) for i in range(size)])
        for k, array in enumerate(arrays, first)
    ]


def exchange(pieces, axis):
    return [pieces[0]] + hops(pieces[1:], axis, 1)


def share(array, axis):
    return exchange([array] * lax.axis_size(axis), axis)


def per_device(
    patches, query_s, key_s, value_s, query_t, key_t, value_t, adapters_a, adapters_b, cotangent
):
    _, frames, patch_dev, width = patches.shape
    n_d, n_t, n_s = (lax.axis_size(name) for name in ("dp", "tm", "space"))
    tokens = frames * patch_dev
    sub = patch_dev // n_t
    d_s = width // n_s
    total = n_s * patch_dev
    factor = (tokens * n_d * n_t * n_s) ** (-0.5)
    here = lax.axis_index("space") * d_s
    downs = jnp.swapaxes(adapters_a, 1, 2)
    downs_here = lax.dynamic_slice_in_dim(downs, here, d_s, 2)
    ups_here = lax.dynamic_slice_in_dim(adapters_b, here, d_s, 2)
    dma = pltpu.SemaphoreType.DMA

    time_arrays = [far(x) for x in (query_t, key_t, value_t, cotangent)]
    space_arrays = [
        far(x) for x in (patches, downs, adapters_b, query_s, value_s, key_s, cotangent)
    ]
    packed = call(
        functools.partial(pack_kernel, n_s, n_t, sub),
        [shape((5 * d_s + 2 * RANK, tokens), BF16)] * n_s
        + [shape((4, frames * sub, width), BF16)] * (n_t - 1),
        *space_arrays, *time_arrays,
        scratch=[pltpu.VMEM(x.shape, BF16) for x in space_arrays]
        + [
            pltpu.VMEM((4,) + query_t.shape, BF16),
            pltpu.VMEM((5, n_s, d_s, tokens), BF16),
            dma((7,)),
            dma((4,)),
        ],
        hbm=True,
    )
    time_pieces = hops(packed[n_s:], "tm", 1)
    packed = exchange(packed[:n_s], "space")
    probs_dims = (frames, d_s // HEAD_DIM, total, total)
    qkv, probs, *out_s = call(
        functools.partial(space_forward_kernel, frames, n_s),
        [shape((3, frames, d_s, total), BF16), pltpu.HBM(probs_dims, F32)]
        + [shape((d_s, tokens), BF16)] * n_s,
        *packed,
        scratch=[pltpu.VMEM(probs_dims, F32), dma((probs_dims[0] * probs_dims[1],))],
        after=time_pieces[:1],
    )
    out_s = exchange(out_s, "space")
    hidden, *codes = call(
        functools.partial(hidden_kernel, n_t, n_s),
        [shape((tokens, width), BF16)] + [shape((8, 128), F32)] * n_t,
        *out_s, patches, downs,
        scratch=[pltpu.VMEM((n_s, d_s, tokens), BF16), pltpu.VMEM((tokens, 128), F32)],
    )
    codes = exchange(codes, "tm")
    turned = call(
        functools.partial(turn_kernel, frames, sub),
        shape((4, width, n_t * frames * sub), BF16),
        *time_arrays, *time_pieces,
        scratch=[
            pltpu.VMEM((4, frames * sub, width), BF16),
            pltpu.VMEM((n_t - 1, 4, frames * sub, width), BF16),
            dma((4 * frames,)),
            dma((n_t - 1,)),
        ],
        hbm=True,
    )
    timed = call(
        functools.partial(time_kernel, n_t, sub),
        [shape((frames * sub, width), BF16)] * n_t
        + [shape((8, 128), F32)] * n_t
        + [shape((2 * RANK, width), F32)],
        turned, adapters_b, *codes,
    )
    out_t, dcodes, time_grad_b = timed[:n_t], timed[n_t : 2 * n_t], timed[2 * n_t]
    dcodes = exchange(dcodes, "tm")
    out_t[1:3] = hops(out_t[1:3], "tm", 1)
    dcodes = call(
        functools.partial(place_codes_kernel, frames, sub),
        shape((2 * RANK, tokens), BF16),
        *dcodes,
        scratch=[pltpu.VMEM((tokens, 128), F32)],
    )
    dcodes = share(dcodes, "space")
    backward = call(
        functools.partial(space_backward_kernel, frames, n_s),
        [shape((2 * RANK, frames * total + 2 * d_s), BF16)] * n_s + [shape((2 * RANK, d_s), F32)],
        qkv, probs, hidden, time_grad_b, downs, downs_here, ups_here, *packed, *dcodes,
        scratch=[pltpu.VMEM((n_s, 2 * RANK, 2 * d_s), BF16)],
        after=out_t[1:3],
        carry=out_t[3:],
    )
    partial, part = backward[:n_s], backward[n_s]
    partial = exchange(partial, "space")
    out_t[3:] = hops(backward[n_s + 1 :], "tm", 3)
    rows = 8 * RANK // n_d
    sums = call(
        functools.partial(merge_kernel, frames, n_s, n_d),
        [shape((rows // 2, 2 * d_s), F32)] * n_d,
        part, *packed, *partial,
        scratch=[pltpu.VMEM((n_d, rows // 2, 2 * d_s), F32)],
    )
    sums = call(total_kernel, shape((rows // 2, 2 * d_s), BF16), *exchange(sums, "dp"), after=out_t[3:])
    sums = call(total_kernel, shape((rows // 2, 2 * d_s), BF16), *share(sums, "tm"))
    sums = call(
        join_kernel,
        shape((rows, width), BF16),
        *share(sums, "space"),
        scratch=[pltpu.VMEM((n_s, rows // 2, 2 * d_s), BF16)],
    )
    grads_a, grads_b = call(
        functools.partial(final_kernel, factor, n_d),
        [shape((4, RANK, width), F32)] * 2,
        *share(sums, "dp"),
        scratch=[pltpu.VMEM((n_d, rows, width), BF16)],
    )
    mixed = call(
        functools.partial(mixed_kernel, frames),
        shape(patches.shape, BF16),
        hidden, *out_t,
        scratch=[pltpu.VMEM((tokens, width), BF16)],
    )
    return (mixed, jnp.swapaxes(grads_a, 1, 2), grads_b)


def solution(mesh):
    token = P("dp", "tm", "space", None)
    return jax.shard_map(
        per_device,
        mesh=mesh,
        in_specs=(token,) * 7 + (P(), P(), token),
        out_specs=(token, P(), P()),
        check_vma=False,
    )
```

```python
import functools

import jax
import jax.numpy as jnp
from jax import lax
from jax.experimental import pallas as pl
from jax.experimental.pallas import tpu as pltpu
from jax.sharding import PartitionSpec as P

HEAD_DIM = 72
RANK = 16
SCALE = HEAD_DIM ** (-0.5)
F32 = jnp.float32
BF16 = jnp.bfloat16
NN = (((1,), (0,)), ((), ()))
NT = (((1,), (1,)), ((), ()))
TN = (((0,), (0,)), ((), ()))


def mm(a, b, dims=NN):
    return lax.dot_general(a, b, dims, preferred_element_type=F32)


def far(x):
    return pltpu.with_memory_space_constraint(x, pltpu.HBM)


def call(kernel, out_shape, *args, scratch=(), hbm=False, limit=48, after=(), carry=()):
    vmem = pl.BlockSpec(memory_space=pltpu.VMEM)
    anywhere = pl.BlockSpec(memory_space=pl.ANY)
    main = anywhere if hbm else vmem
    single = not isinstance(out_shape, (tuple, list))
    outs = (out_shape,) if single else tuple(out_shape)
    used, extra = len(args), len(after) + len(carry)

    def body(*refs):
        inside = refs[:used] + refs[used + extra : used + extra + len(outs)]
        kernel(*inside, *refs[used + extra + len(outs) + len(carry) :])

    result = pl.pallas_call(
        body,
        out_shape=outs + tuple(shape(x.shape, x.dtype) for x in carry),
        in_specs=[main] * used + [anywhere] * extra,
        out_specs=tuple(vmem if isinstance(o, jax.ShapeDtypeStruct) else anywhere for o in outs)
        + (anywhere,) * len(carry),
        scratch_shapes=list(scratch),
        input_output_aliases={used + len(after) + i: len(outs) + i for i in range(len(carry))},
        compiler_params=pltpu.CompilerParams(vmem_limit_bytes=limit * 1024 * 1024),
    )(*args, *after, *carry)
    return result[0] if single and not carry else list(result)


def shape(dims, dtype):
    return jax.ShapeDtypeStruct(tuple(dims), dtype)


def probs_of(keys, q_t, mask):
    scores = mm(keys, q_t) * SCALE
    if mask is not None:
        scores = jnp.where(mask, scores, -1e30)
    peak = jnp.max(scores, axis=0, keepdims=True)
    weights = jnp.exp(scores - peak)
    return weights * (1.0 / jnp.sum(weights, axis=0, keepdims=True))


def head_backward(probs, k_t, v_t, g_t):
    low = probs.astype(BF16)
    dvals = mm(g_t, low, NT)
    dprob = mm(v_t.T, g_t)
    inner = jnp.sum(probs * dprob, axis=0, keepdims=True)
    dscore = (probs * (dprob - inner) * SCALE).astype(BF16)
    dquery = mm(k_t, dscore)
    return dquery, dvals


def rows_of(array, head):
    return array[head * HEAD_DIM : (head + 1) * HEAD_DIM]


def peer(axis, distance):
    return lax.axis_index(axis) ^ distance


def load_all(refs, buffers, sems):
    copies = [
        pltpu.make_async_copy(ref, buffer, sems.at[index])
        for index, (ref, buffer) in enumerate(zip(refs, buffers))
    ]
    for copy in copies:
        copy.start()
    return copies


def pack_kernel(n_s, n_t, sub, *refs):
    ins, time_ins, refs = refs[:7], refs[7:11], refs[11:]
    outs, time_outs, refs = refs[:n_s], refs[n_s : n_s + n_t - 1], refs[n_s + n_t - 1 :]
    buffers, (time_buf, turned_ref, sems, time_sems) = refs[:7], refs[7:]
    p_buf, at_buf, b_buf, q_buf, v_buf, k_buf, g_buf = buffers
    copies = load_all(ins, buffers, sems)
    time_copies = load_all(time_ins, [time_buf.at[index] for index in range(4)], time_sems)
    d_s, tokens = turned_ref.shape[2:]
    frames = time_buf.shape[2]

    def flat(ref):
        return ref[0].reshape(tokens, ref.shape[3])

    def send(array, index):
        turned = array.T
        for j in range(n_s):
            turned_ref[index, j] = turned[j * d_s : (j + 1) * d_s]
        for k in range(n_s):
            outs[k][index * d_s : (index + 1) * d_s] = turned_ref[index, peer("space", k)]

    copies[0].wait()
    copies[1].wait()
    copies[2].wait()
    patches = flat(p_buf)
    codes_q = mm(patches, at_buf[0], NT).astype(BF16)
    codes_v = mm(patches, at_buf[1], NT).astype(BF16)
    codes_t = jnp.concatenate([codes_q, codes_v], axis=1).T
    copies[3].wait()
    query = (flat(q_buf).astype(F32) + mm(codes_q, b_buf[0])).astype(BF16)
    send(query, 0)
    copies[4].wait()
    value = (flat(v_buf).astype(F32) + mm(codes_v, b_buf[1])).astype(BF16)
    send(value, 2)
    copies[5].wait()
    send(flat(k_buf), 1)
    send(patches, 3)
    copies[6].wait()
    send(flat(g_buf), 4)
    for k in range(n_s):
        outs[k][5 * d_s :] = codes_t
    for index, copy in enumerate(time_copies):
        copy.wait()
        for k in range(1, n_t):
            start = pl.multiple_of(peer("tm", k) * sub, sub)
            for f in range(frames):
                time_outs[k - 1][index, f * sub : (f + 1) * sub] = time_buf[
                    index, 0, f, pl.ds(start, sub)
                ]


def frame_rows(pieces, f, patch_dev):
    return jnp.concatenate([x[:, f * patch_dev : (f + 1) * patch_dev] for x in pieces], axis=1)


def space_forward_kernel(frames, n_s, *refs):
    packed, (qkv_ref, probs_ref, *outs) = refs[:n_s], refs[n_s : 2 * n_s + 2]
    probs_buf, sems = refs[2 * n_s + 2 :]
    copies = []
    d_s, tokens = outs[0].shape
    patch_dev = tokens // frames
    total = n_s * patch_dev
    step = min(total, 256)
    for index in range(3):
        pieces = [x[index * d_s : (index + 1) * d_s] for x in packed]
        for f in range(frames):
            qkv_ref[index, f] = frame_rows(pieces, f, patch_dev)
    for f in range(frames):
        query = qkv_ref[0, f].astype(F32)
        keys = qkv_ref[1, f].astype(F32)
        vals = qkv_ref[2, f].astype(F32)
        heads = []
        for h in range(d_s // HEAD_DIM):
            k_h = rows_of(keys, h).astype(BF16)
            v_h = rows_of(vals, h).astype(BF16)
            q_h = rows_of(query, h).astype(BF16)
            parts = []
            for s in range(0, total, step):
                probs = probs_of(k_h.T, q_h[:, s : s + step], None)
                probs_buf[f, h, :, s : s + step] = probs
                parts.append(mm(v_h, probs.astype(BF16)))
            heads.append(parts[0] if len(parts) == 1 else jnp.concatenate(parts, axis=1))
            copy = pltpu.make_async_copy(
                probs_buf.at[f, h], probs_ref.at[f, h], sems.at[len(copies)]
            )
            copy.start()
            copies.append(copy)
        out = jnp.concatenate(heads, axis=0).astype(BF16)
        for k in range(n_s):
            outs[k][:, f * patch_dev : (f + 1) * patch_dev] = out[
                :, k * patch_dev : (k + 1) * patch_dev
            ]
    for copy in copies:
        copy.wait()


def lane_block(rows):
    return lax.broadcasted_iota(jnp.int32, (rows, 128), 1) // (2 * RANK)


def fold(token_rows):
    block = lane_block(8)
    result = token_rows[0:8]
    for k in range(1, 4):
        result = jnp.where(block == k, token_rows[8 * k : 8 * k + 8], result)
    return result


def unfold(folded):
    pieces = [folded]
    for k in range(1, 4):
        pieces.append(pltpu.roll(folded, 128 - 2 * RANK * k, 1))
    return jnp.concatenate(pieces, axis=0)


def hidden_kernel(n_t, n_s, *refs):
    pieces, refs = refs[:n_s], refs[n_s:]
    p_ref, at_ref, hidden_ref = refs[:3]
    sends = refs[3 : 3 + n_t]
    out_buf, codes_buf = refs[3 + n_t :]
    _, frames, patch_dev, width = p_ref.shape
    tokens = frames * patch_dev
    sub = patch_dev // n_t
    for k in range(n_s):
        out_buf[peer("space", k)] = pieces[k][...]
    out = out_buf[...].reshape(width, tokens).T
    hidden = (p_ref[0].reshape(tokens, width).astype(F32) + out.astype(F32)).astype(BF16)
    hidden_ref[...] = hidden
    downs = jnp.concatenate([at_ref[2], at_ref[3]] * 4, axis=0)
    codes_buf[...] = mm(hidden, downs, NT).astype(BF16).astype(F32)
    for k in range(n_t):
        rows = [
            codes_buf[pl.ds(pl.multiple_of(f * patch_dev + peer("tm", k) * sub, sub), sub)]
            for f in range(frames)
        ]
        sends[k][...] = fold(jnp.concatenate(rows, axis=0))


def turn_kernel(frames, sub, q_ref, k_ref, v_ref, g_ref, *refs):
    *pieces, out_ref, own_buf, piece_buf, own_sems, sems = refs
    own = []
    start = pl.multiple_of(peer("tm", 0) * sub, sub)
    for index, ref in enumerate((q_ref, k_ref, v_ref, g_ref)):
        for f in range(frames):
            copy = pltpu.make_async_copy(
                ref.at[0, f, pl.ds(start, sub)],
                own_buf.at[index, f * sub : (f + 1) * sub],
                own_sems.at[index * frames + f],
            )
            copy.start()
            own.append(copy)
    copies = load_all(pieces, [piece_buf.at[k] for k in range(len(pieces))], sems)
    for copy in own + copies:
        copy.wait()
    for index in range(4):
        parts = [own_buf[index]] + [piece_buf[k, index] for k in range(len(pieces))]
        out_ref[index] = jnp.concatenate(parts, axis=0).T


def time_kernel(n_t, sub, x_ref, b_ref, *refs):
    codes_refs, refs = refs[:n_t], refs[n_t:]
    outs, sends, grad_b_ref = refs[:n_t], refs[n_t : 2 * n_t], refs[2 * n_t]
    _, width, tokens = x_ref.shape
    codes = jnp.concatenate([unfold(ref[...]) for ref in codes_refs], axis=0).T
    codes_q = codes[:RANK].astype(BF16)
    codes_v = codes[RANK : 2 * RANK].astype(BF16)
    query = (x_ref[0].astype(F32) + mm(b_ref[2], codes_q, TN)).astype(BF16).astype(F32)
    vals = (x_ref[2].astype(F32) + mm(b_ref[3], codes_v, TN)).astype(BF16).astype(F32)
    keys = x_ref[1].astype(F32)
    grad = x_ref[3].astype(F32)
    row = lax.broadcasted_iota(jnp.int32, (tokens, 2 * tokens), 0)
    col = lax.broadcasted_iota(jnp.int32, (tokens, 2 * tokens), 1)
    mask = lax.rem(row, sub) == lax.rem(col, sub)
    top = lax.broadcasted_iota(jnp.int32, (2 * HEAD_DIM, tokens), 0) < HEAD_DIM

    def spread(pair):
        return jnp.concatenate(
            [jnp.where(top, pair, 0.0), jnp.where(top, 0.0, pair)], axis=1
        ).astype(BF16)

    def pick(wide):
        return jnp.concatenate([wide[:HEAD_DIM, :tokens], wide[HEAD_DIM:, tokens:]], axis=0)

    outs_h, d_query, d_vals = [], [], []
    for h in range(0, width, 2 * HEAD_DIM):
        pair = slice(h, h + 2 * HEAD_DIM)
        k_h, v_h = keys[pair].astype(BF16), vals[pair].astype(BF16)
        g_h = spread(grad[pair])
        probs = probs_of(k_h.T, spread(query[pair]), mask)
        low = probs.astype(BF16)
        dprob = mm(v_h.T, g_h)
        inner = jnp.sum(probs * dprob, axis=0, keepdims=True)
        dscore = (probs * (dprob - inner) * SCALE).astype(BF16)
        outs_h.append(pick(mm(v_h, low)))
        d_vals.append(mm(g_h, low, NT))
        d_query.append(pick(mm(k_h, dscore)))
    d_query = jnp.concatenate(d_query, axis=0).astype(BF16)
    d_vals = jnp.concatenate(d_vals, axis=0).astype(BF16)
    d_codes = jnp.concatenate([mm(b_ref[2], d_query), mm(b_ref[3], d_vals)] * 4, axis=0)
    d_codes = d_codes.astype(BF16).astype(F32).T
    per = tokens // n_t
    for k in range(n_t):
        sends[k][...] = fold(d_codes[k * per : (k + 1) * per])
    out = jnp.concatenate(outs_h, axis=0).astype(BF16).T
    for k in range(n_t):
        outs[k][...] = out[k * per : (k + 1) * per]
    grad_b_ref[:RANK] = mm(codes_q, d_query, NT)
    grad_b_ref[RANK:] = mm(codes_v, d_vals, NT)


def place_codes_kernel(frames, sub, *refs):
    pieces, (out_ref, buf) = refs[:-2], refs[-2:]
    patch_dev = sub * len(pieces)
    for k, piece in enumerate(pieces):
        rows = unfold(piece[...])
        for f in range(frames):
            start = pl.multiple_of(f * patch_dev + peer("tm", k) * sub, sub)
            buf[pl.ds(start, sub)] = rows[f * sub : (f + 1) * sub]
    out_ref[...] = buf[...].T[: 2 * RANK].astype(BF16)


def space_backward_kernel(frames, n_s, qkv_ref, probs_ref, hidden_ref, grad_b_ref, at_ref, at_here_ref, b_here_ref, *refs):
    packed, dcodes, sends = refs[:n_s], refs[n_s : 2 * n_s], refs[2 * n_s : 3 * n_s]
    part_ref, cut_buf = refs[3 * n_s :]
    d_s = part_ref.shape[1]
    tokens = hidden_ref.shape[0]
    patch_dev = tokens // frames
    total = n_s * patch_dev
    step = min(total, 256)
    ups = jnp.concatenate([at_here_ref[2], at_here_ref[3]], axis=0).T
    grads = []
    for k in range(n_s):
        cot = packed[k][4 * d_s : 5 * d_s].astype(F32)
        grads.append((cot + mm(ups, dcodes[k][...])).astype(BF16))
    grad_b_q = grad_b_v = None
    codes = [x[5 * d_s :] for x in packed]
    for f in range(frames):
        keys = qkv_ref[1, f].astype(F32)
        vals = qkv_ref[2, f].astype(F32)
        grad = frame_rows(grads, f, patch_dev).astype(F32)
        d_query, d_vals = [], []
        for h in range(d_s // HEAD_DIM):
            k_h = rows_of(keys, h).astype(BF16)
            v_h = rows_of(vals, h).astype(BF16)
            g_h = rows_of(grad, h).astype(BF16)
            dq_parts, dv_sum = [], None
            for s in range(0, total, step):
                probs = probs_ref[f, h, :, s : s + step]
                dq, dv = head_backward(probs, k_h, v_h, g_h[:, s : s + step])
                dq_parts.append(dq)
                dv_sum = dv if dv_sum is None else dv_sum + dv
            d_query.append(
                dq_parts[0] if len(dq_parts) == 1 else jnp.concatenate(dq_parts, axis=1)
            )
            d_vals.append(dv_sum)
        d_query = jnp.concatenate(d_query, axis=0).astype(BF16)
        d_vals = jnp.concatenate(d_vals, axis=0).astype(BF16)
        partial = jnp.concatenate([mm(b_here_ref[0], d_query), mm(b_here_ref[1], d_vals)], axis=0)
        partial = partial.astype(BF16)
        blocks = [partial[:, m * patch_dev : (m + 1) * patch_dev] for m in range(n_s)]
        for k in range(n_s):
            turned = jnp.concatenate([blocks[m ^ k] for m in range(n_s)], axis=1)
            sends[k][:, f * total : (f + 1) * total] = turned
        frame_codes = frame_rows(codes, f, patch_dev)
        term_q = mm(frame_codes[:RANK], d_query, NT)
        term_v = mm(frame_codes[RANK:], d_vals, NT)
        grad_b_q = term_q if grad_b_q is None else grad_b_q + term_q
        grad_b_v = term_v if grad_b_v is None else grad_b_v + term_v
    part_ref[:RANK] = grad_b_q
    part_ref[RANK:] = grad_b_v
    grad_a = mm(dcodes[0][...], hidden_ref[...])
    for j in range(n_s):
        here = slice(j * d_s, (j + 1) * d_s)
        cut_buf[j, :, :d_s] = grad_a[:, here].astype(BF16)
        cut_buf[j, :, d_s:] = grad_b_ref[:, here].astype(BF16)
    for k in range(n_s):
        sends[k][:, frames * total :] = cut_buf[peer("space", k)]


def add_up(terms):
    result = None
    for term in terms:
        result = term if result is None else result + term
    return result


def merge_kernel(frames, n_s, n_d, part_ref, *refs):
    packed, recvs, refs = refs[:n_s], refs[n_s : 2 * n_s], refs[2 * n_s :]
    sends, buf = refs[:n_d], refs[n_d]
    d_s = part_ref.shape[1]
    tokens = packed[0].shape[1]
    patch_dev = tokens // frames
    total = n_s * patch_dev
    patches = [x[3 * d_s : 4 * d_s] for x in packed]
    terms = []
    for f in range(frames):
        codes = [recv[:, f * total : (f + 1) * total].astype(F32) for recv in recvs]
        terms.append(mm(add_up(codes).astype(BF16), frame_rows(patches, f, patch_dev), NT))
    start = frames * total
    time_a = add_up([recv[:, start : start + d_s].astype(F32) for recv in recvs])
    time_b = add_up([recv[:, start + d_s : start + 2 * d_s].astype(F32) for recv in recvs])
    rows = jnp.concatenate([add_up(terms), time_a, part_ref[...], time_b], axis=0)
    per = rows.shape[0] // n_d
    for d in range(n_d):
        mine = rows[d * per : (d + 1) * per]
        buf[d] = jnp.concatenate([mine[: per // 2], mine[per // 2 :]], axis=1)
    for k in range(n_d):
        sends[k][...] = buf[peer("dp", k)]


def total_kernel(*refs):
    terms = [ref[...].astype(F32) for ref in refs[:-1]]
    while len(terms) > 1:
        terms = [terms[i] + terms[i + 1] for i in range(0, len(terms), 2)]
    refs[-1][...] = terms[0].astype(refs[-1].dtype)


def join_kernel(*refs):
    pieces, (out_ref, buf) = refs[:-2], refs[-2:]
    for k, piece in enumerate(pieces):
        buf[peer("space", k)] = piece[...]
    half, d_s = buf.shape[1], buf.shape[2] // 2
    for h in range(2):
        cuts = [buf[j, :, h * d_s : (h + 1) * d_s] for j in range(len(pieces))]
        out_ref[h * half : (h + 1) * half] = jnp.concatenate(cuts, axis=1)


def final_kernel(factor, n_d, *refs):
    pieces, (a_ref, b_ref, buf) = refs[:n_d], refs[n_d:]
    for k, piece in enumerate(pieces):
        buf[peer("dp", k)] = piece[...]
    per = pieces[0].shape[0]
    half = n_d // 2
    for d in range(n_d):
        rows = buf[d].astype(F32) * factor
        target = a_ref if d < half else b_ref
        for r in range(0, per, min(per, RANK)):
            start = (d % half) * per + r
            size = min(per, RANK)
            target[start // RANK, start % RANK : start % RANK + size] = rows[r : r + size]


def mixed_kernel(frames, hidden_ref, *refs):
    pieces, (mixed_ref, buf) = refs[:-2], refs[-2:]
    n_t = len(pieces)
    tokens, width = hidden_ref.shape
    patch_dev = tokens // frames
    sub = patch_dev // n_t
    for k, piece in enumerate(pieces):
        for f in range(frames):
            start = pl.multiple_of(f * patch_dev + peer("tm", k) * sub, sub)
            buf[pl.ds(start, sub)] = piece[f * sub : (f + 1) * sub]
    total = hidden_ref[...].astype(F32) + buf[...].astype(F32)
    mixed_ref[0] = total.astype(BF16).reshape(frames, patch_dev, width)


def hops(arrays, axis, first):
    size = lax.axis_size(axis)
    return [
        lax.ppermute(array, axis, [(i, i ^ k) for i in range(size)])
        for k, array in enumerate(arrays, first)
    ]


def exchange(pieces, axis):
    return [pieces[0]] + hops(pieces[1:], axis, 1)


def share(array, axis):
    return exchange([array] * lax.axis_size(axis), axis)


def per_device(
    patches, query_s, key_s, value_s, query_t, key_t, value_t, adapters_a, adapters_b, cotangent
):
    _, frames, patch_dev, width = patches.shape
    n_d, n_t, n_s = (lax.axis_size(name) for name in ("dp", "tm", "space"))
    tokens = frames * patch_dev
    sub = patch_dev // n_t
    d_s = width // n_s
    total = n_s * patch_dev
    factor = (tokens * n_d * n_t * n_s) ** (-0.5)
    here = lax.axis_index("space") * d_s
    downs = jnp.swapaxes(adapters_a, 1, 2)
    downs_here = lax.dynamic_slice_in_dim(downs, here, d_s, 2)
    ups_here = lax.dynamic_slice_in_dim(adapters_b, here, d_s, 2)
    dma = pltpu.SemaphoreType.DMA

    time_arrays = [far(x) for x in (query_t, key_t, value_t, cotangent)]
    space_arrays = [
        far(x) for x in (patches, downs, adapters_b, query_s, value_s, key_s, cotangent)
    ]
    packed = call(
        functools.partial(pack_kernel, n_s, n_t, sub),
        [shape((5 * d_s + 2 * RANK, tokens), BF16)] * n_s
        + [shape((4, frames * sub, width), BF16)] * (n_t - 1),
        *space_arrays, *time_arrays,
        scratch=[pltpu.VMEM(x.shape, BF16) for x in space_arrays]
        + [
            pltpu.VMEM((4,) + query_t.shape, BF16),
            pltpu.VMEM((5, n_s, d_s, tokens), BF16),
            dma((7,)),
            dma((4,)),
        ],
        hbm=True,
    )
    time_pieces = hops(packed[n_s:], "tm", 1)
    packed = exchange(packed[:n_s], "space")
    probs_dims = (frames, d_s // HEAD_DIM, total, total)
    qkv, probs, *out_s = call(
        functools.partial(space_forward_kernel, frames, n_s),
        [shape((3, frames, d_s, total), BF16), pltpu.HBM(probs_dims, F32)]
        + [shape((d_s, tokens), BF16)] * n_s,
        *packed,
        scratch=[pltpu.VMEM(probs_dims, F32), dma((probs_dims[0] * probs_dims[1],))],
        after=time_pieces[:1],
    )
    out_s = exchange(out_s, "space")
    hidden, *codes = call(
        functools.partial(hidden_kernel, n_t, n_s),
        [shape((tokens, width), BF16)] + [shape((8, 128), F32)] * n_t,
        *out_s, patches, downs,
        scratch=[pltpu.VMEM((n_s, d_s, tokens), BF16), pltpu.VMEM((tokens, 128), F32)],
    )
    codes = exchange(codes, "tm")
    turned = call(
        functools.partial(turn_kernel, frames, sub),
        shape((4, width, n_t * frames * sub), BF16),
        *time_arrays, *time_pieces,
        scratch=[
            pltpu.VMEM((4, frames * sub, width), BF16),
            pltpu.VMEM((n_t - 1, 4, frames * sub, width), BF16),
            dma((4 * frames,)),
            dma((n_t - 1,)),
        ],
        hbm=True,
    )
    timed = call(
        functools.partial(time_kernel, n_t, sub),
        [shape((frames * sub, width), BF16)] * n_t
        + [shape((8, 128), F32)] * n_t
        + [shape((2 * RANK, width), F32)],
        turned, adapters_b, *codes,
    )
    out_t, dcodes, time_grad_b = timed[:n_t], timed[n_t : 2 * n_t], timed[2 * n_t]
    dcodes = exchange(dcodes, "tm")
    out_t[1:3] = hops(out_t[1:3], "tm", 1)
    dcodes, *rest = call(
        functools.partial(place_codes_kernel, frames, sub),
        shape((2 * RANK, tokens), BF16),
        *dcodes,
        scratch=[pltpu.VMEM((tokens, 128), F32)],
        after=out_t[1:2],
        carry=out_t[3:],
    )
    dcodes = share(dcodes, "space")
    out_t[3:] = hops(rest, "tm", 3)
    backward = call(
        functools.partial(space_backward_kernel, frames, n_s),
        [shape((2 * RANK, frames * total + 2 * d_s), BF16)] * n_s + [shape((2 * RANK, d_s), F32)],
        qkv, probs, hidden, time_grad_b, downs, downs_here, ups_here, *packed, *dcodes,
        scratch=[pltpu.VMEM((n_s, 2 * RANK, 2 * d_s), BF16)],
        after=out_t[2:],
    )
    partial, part = exchange(backward[:n_s], "space"), backward[n_s]
    rows = 8 * RANK // n_d
    sums = call(
        functools.partial(merge_kernel, frames, n_s, n_d),
        [shape((rows // 2, 2 * d_s), F32)] * n_d,
        part, *packed, *partial,
        scratch=[pltpu.VMEM((n_d, rows // 2, 2 * d_s), F32)],
    )
    sums = call(total_kernel, shape((rows // 2, 2 * d_s), BF16), *exchange(sums, "dp"))
    sums = call(total_kernel, shape((rows // 2, 2 * d_s), BF16), *share(sums, "tm"))
    sums = call(
        join_kernel,
        shape((rows, width), BF16),
        *share(sums, "space"),
        scratch=[pltpu.VMEM((n_s, rows // 2, 2 * d_s), BF16)],
    )
    grads_a, grads_b = call(
        functools.partial(final_kernel, factor, n_d),
        [shape((4, RANK, width), F32)] * 2,
        *share(sums, "dp"),
        scratch=[pltpu.VMEM((n_d, rows, width), BF16)],
    )
    mixed = call(
        functools.partial(mixed_kernel, frames),
        shape(patches.shape, BF16),
        hidden, *out_t,
        scratch=[pltpu.VMEM((tokens, width), BF16)],
    )
    return (mixed, jnp.swapaxes(grads_a, 1, 2), grads_b)


def solution(mesh):
    token = P("dp", "tm", "space", None)
    return jax.shard_map(
        per_device,
        mesh=mesh,
        in_specs=(token,) * 7 + (P(), P(), token),
        out_specs=(token, P(), P()),
        check_vma=False,
    )
```

```python
import functools
import math

import jax
import jax.numpy as jnp
from jax import lax
from jax.experimental import pallas as pl
from jax.experimental.pallas import tpu as pltpu
from jax.sharding import PartitionSpec as P

HEAD_DIM = 72
RANK = 16
SCALE = HEAD_DIM ** (-0.5)
F32 = jnp.float32
BF16 = jnp.bfloat16
NN = (((1,), (0,)), ((), ()))
NT = (((1,), (1,)), ((), ()))
TN = (((0,), (0,)), ((), ()))


def mm(a, b, dims=NN):
    return lax.dot_general(a, b, dims, preferred_element_type=F32)


def far(x):
    return pltpu.with_memory_space_constraint(x, pltpu.HBM)


def call(kernel, out_shape, *args, scratch=(), hbm=False, limit=48, after=(), carry=()):
    vmem = pl.BlockSpec(memory_space=pltpu.VMEM)
    anywhere = pl.BlockSpec(memory_space=pl.ANY)
    main = anywhere if hbm else vmem
    single = not isinstance(out_shape, (tuple, list))
    outs = (out_shape,) if single else tuple(out_shape)
    used, extra = len(args), len(after) + len(carry)

    def body(*refs):
        inside = refs[:used] + refs[used + extra : used + extra + len(outs)]
        kernel(*inside, *refs[used + extra + len(outs) + len(carry) :])

    result = pl.pallas_call(
        body,
        out_shape=outs + tuple(shape(x.shape, x.dtype) for x in carry),
        in_specs=[main] * used + [anywhere] * extra,
        out_specs=tuple(vmem if isinstance(o, jax.ShapeDtypeStruct) else anywhere for o in outs)
        + (anywhere,) * len(carry),
        scratch_shapes=list(scratch),
        input_output_aliases={used + len(after) + i: len(outs) + i for i in range(len(carry))},
        compiler_params=pltpu.CompilerParams(vmem_limit_bytes=limit * 1024 * 1024),
    )(*args, *after, *carry)
    return result[0] if single and not carry else list(result)


def shape(dims, dtype):
    return jax.ShapeDtypeStruct(tuple(dims), dtype)


def probs_of(keys, q_t, mask):
    scores = mm(keys, q_t) * SCALE
    if mask is not None:
        scores = jnp.where(mask, scores, -1e30)
    peak = jnp.max(scores, axis=0, keepdims=True)
    weights = jnp.exp(scores - peak)
    return weights * (1.0 / jnp.sum(weights, axis=0, keepdims=True))


def head_backward(probs, k_t, v_t, g_t):
    low = probs.astype(BF16)
    dvals = mm(g_t, low, NT)
    dprob = mm(v_t.T, g_t)
    inner = jnp.sum(probs * dprob, axis=0, keepdims=True)
    dscore = (probs * (dprob - inner) * SCALE).astype(BF16)
    dquery = mm(k_t, dscore)
    return dquery, dvals


def rows_of(array, head):
    return array[head * HEAD_DIM : (head + 1) * HEAD_DIM]


def peer(axis, distance):
    return lax.axis_index(axis) ^ distance


def load_all(refs, buffers, sems):
    copies = [
        pltpu.make_async_copy(ref, buffer, sems.at[index])
        for index, (ref, buffer) in enumerate(zip(refs, buffers))
    ]
    for copy in copies:
        copy.start()
    return copies


def pack_kernel(n_s, n_t, sub, *refs):
    ins, time_ins, refs = refs[:7], refs[7:11], refs[11:]
    outs, time_outs, refs = refs[:n_s], refs[n_s : n_s + n_t - 1], refs[n_s + n_t - 1 :]
    buffers, (time_buf, turned_ref, sems, time_sems) = refs[:7], refs[7:]
    p_buf, at_buf, b_buf, q_buf, v_buf, k_buf, g_buf = buffers
    copies = load_all(ins, buffers, sems)
    time_copies = load_all(time_ins, [time_buf.at[index] for index in range(4)], time_sems)
    d_s, tokens = turned_ref.shape[2:]
    frames = time_buf.shape[2]

    def flat(ref):
        return ref[0].reshape(tokens, ref.shape[3])

    def send(array, index):
        turned = array.T
        for j in range(n_s):
            turned_ref[index, j] = turned[j * d_s : (j + 1) * d_s]
        for k in range(n_s):
            outs[k][index * d_s : (index + 1) * d_s] = turned_ref[index, peer("space", k)]

    copies[0].wait()
    copies[1].wait()
    copies[2].wait()
    patches = flat(p_buf)
    codes_q = mm(patches, at_buf[0], NT).astype(BF16)
    codes_v = mm(patches, at_buf[1], NT).astype(BF16)
    codes_t = jnp.concatenate([codes_q, codes_v], axis=1).T
    copies[3].wait()
    query = (flat(q_buf).astype(F32) + mm(codes_q, b_buf[0])).astype(BF16)
    send(query, 0)
    copies[4].wait()
    value = (flat(v_buf).astype(F32) + mm(codes_v, b_buf[1])).astype(BF16)
    send(value, 2)
    copies[5].wait()
    send(flat(k_buf), 1)
    copies[6].wait()
    send(flat(g_buf), 3)
    for k in range(n_s):
        outs[k][4 * d_s :] = codes_t
    for index, copy in enumerate(time_copies):
        copy.wait()
        for k in range(1, n_t):
            start = pl.multiple_of(peer("tm", k) * sub, sub)
            for f in range(frames):
                time_outs[k - 1][index, f * sub : (f + 1) * sub] = time_buf[
                    index, 0, f, pl.ds(start, sub)
                ]


def frame_rows(pieces, f, patch_dev):
    return jnp.concatenate([x[:, f * patch_dev : (f + 1) * patch_dev] for x in pieces], axis=1)


def space_forward_kernel(frames, n_s, *refs):
    packed, (qkv_ref, probs_ref, *outs) = refs[:n_s], refs[n_s : 2 * n_s + 2]
    probs_buf, sems = refs[2 * n_s + 2 :]
    copies = []
    d_s, tokens = outs[0].shape
    patch_dev = tokens // frames
    total = n_s * patch_dev
    step = min(total, 256)
    for index in range(3):
        pieces = [x[index * d_s : (index + 1) * d_s] for x in packed]
        for f in range(frames):
            qkv_ref[index, f] = frame_rows(pieces, f, patch_dev)
    for f in range(frames):
        query = qkv_ref[0, f].astype(F32)
        keys = qkv_ref[1, f].astype(F32)
        vals = qkv_ref[2, f].astype(F32)
        heads = []
        for h in range(d_s // HEAD_DIM):
            k_h = rows_of(keys, h).astype(BF16)
            v_h = rows_of(vals, h).astype(BF16)
            q_h = rows_of(query, h).astype(BF16)
            parts = []
            for s in range(0, total, step):
                probs = probs_of(k_h.T, q_h[:, s : s + step], None)
                probs_buf[f, h, :, s : s + step] = probs
                parts.append(mm(v_h, probs.astype(BF16)))
            heads.append(parts[0] if len(parts) == 1 else jnp.concatenate(parts, axis=1))
            copy = pltpu.make_async_copy(
                probs_buf.at[f, h], probs_ref.at[f, h], sems.at[len(copies)]
            )
            copy.start()
            copies.append(copy)
        out = jnp.concatenate(heads, axis=0).astype(BF16)
        for k in range(n_s):
            outs[k][:, f * patch_dev : (f + 1) * patch_dev] = out[
                :, k * patch_dev : (k + 1) * patch_dev
            ]
    for copy in copies:
        copy.wait()


def lane_block(rows):
    return lax.broadcasted_iota(jnp.int32, (rows, 128), 1) // (2 * RANK)


def fold(token_rows):
    block = lane_block(8)
    result = token_rows[0:8]
    for k in range(1, 4):
        result = jnp.where(block == k, token_rows[8 * k : 8 * k + 8], result)
    return result


def unfold(folded):
    pieces = [folded]
    for k in range(1, 4):
        pieces.append(pltpu.roll(folded, 128 - 2 * RANK * k, 1))
    return jnp.concatenate(pieces, axis=0)


def hidden_kernel(n_t, n_s, *refs):
    pieces, refs = refs[:n_s], refs[n_s:]
    p_ref, at_ref, hidden_ref = refs[:3]
    sends = refs[3 : 3 + n_t]
    out_buf, codes_buf = refs[3 + n_t :]
    _, frames, patch_dev, width = p_ref.shape
    tokens = frames * patch_dev
    sub = patch_dev // n_t
    for k in range(n_s):
        out_buf[peer("space", k)] = pieces[k][...]
    out = out_buf[...].reshape(width, tokens).T
    hidden = (p_ref[0].reshape(tokens, width).astype(F32) + out.astype(F32)).astype(BF16)
    hidden_ref[...] = hidden
    downs = jnp.concatenate([at_ref[2], at_ref[3]] * 4, axis=0)
    codes_buf[...] = mm(hidden, downs, NT).astype(BF16).astype(F32)
    for k in range(n_t):
        rows = [
            codes_buf[pl.ds(pl.multiple_of(f * patch_dev + peer("tm", k) * sub, sub), sub)]
            for f in range(frames)
        ]
        sends[k][...] = fold(jnp.concatenate(rows, axis=0))


def turn_kernel(frames, sub, q_ref, k_ref, v_ref, g_ref, *refs):
    *pieces, out_ref, own_buf, piece_buf, own_sems, sems = refs
    own = []
    start = pl.multiple_of(peer("tm", 0) * sub, sub)
    for index, ref in enumerate((q_ref, k_ref, v_ref, g_ref)):
        for f in range(frames):
            copy = pltpu.make_async_copy(
                ref.at[0, f, pl.ds(start, sub)],
                own_buf.at[index, f * sub : (f + 1) * sub],
                own_sems.at[index * frames + f],
            )
            copy.start()
            own.append(copy)
    copies = load_all(pieces, [piece_buf.at[k] for k in range(len(pieces))], sems)
    for copy in own + copies:
        copy.wait()
    for index in range(4):
        parts = [own_buf[index]] + [piece_buf[k, index] for k in range(len(pieces))]
        out_ref[index] = jnp.concatenate(parts, axis=0).T


def time_kernel(n_t, sub, x_ref, b_ref, *refs):
    codes_refs, refs = refs[:n_t], refs[n_t:]
    outs, sends, grad_b_ref = refs[:n_t], refs[n_t : 2 * n_t], refs[2 * n_t]
    _, width, tokens = x_ref.shape
    codes = jnp.concatenate([unfold(ref[...]) for ref in codes_refs], axis=0).T
    codes_q = codes[:RANK].astype(BF16)
    codes_v = codes[RANK : 2 * RANK].astype(BF16)
    query = (x_ref[0].astype(F32) + mm(b_ref[2], codes_q, TN)).astype(BF16).astype(F32)
    vals = (x_ref[2].astype(F32) + mm(b_ref[3], codes_v, TN)).astype(BF16).astype(F32)
    keys = x_ref[1].astype(F32)
    grad = x_ref[3].astype(F32)
    row = lax.broadcasted_iota(jnp.int32, (tokens, 2 * tokens), 0)
    col = lax.broadcasted_iota(jnp.int32, (tokens, 2 * tokens), 1)
    mask = lax.rem(row, sub) == lax.rem(col, sub)
    top = lax.broadcasted_iota(jnp.int32, (2 * HEAD_DIM, tokens), 0) < HEAD_DIM

    def spread(pair):
        return jnp.concatenate(
            [jnp.where(top, pair, 0.0), jnp.where(top, 0.0, pair)], axis=1
        ).astype(BF16)

    def pick(wide):
        return jnp.concatenate([wide[:HEAD_DIM, :tokens], wide[HEAD_DIM:, tokens:]], axis=0)

    outs_h, d_query, d_vals = [], [], []
    for h in range(0, width, 2 * HEAD_DIM):
        pair = slice(h, h + 2 * HEAD_DIM)
        k_h, v_h = keys[pair].astype(BF16), vals[pair].astype(BF16)
        g_h = spread(grad[pair])
        probs = probs_of(k_h.T, spread(query[pair]), mask)
        low = probs.astype(BF16)
        dprob = mm(v_h.T, g_h)
        inner = jnp.sum(probs * dprob, axis=0, keepdims=True)
        dscore = (probs * (dprob - inner) * SCALE).astype(BF16)
        outs_h.append(pick(mm(v_h, low)))
        d_vals.append(mm(g_h, low, NT))
        d_query.append(pick(mm(k_h, dscore)))
    d_query = jnp.concatenate(d_query, axis=0).astype(BF16)
    d_vals = jnp.concatenate(d_vals, axis=0).astype(BF16)
    d_codes = jnp.concatenate([mm(b_ref[2], d_query), mm(b_ref[3], d_vals)] * 4, axis=0)
    d_codes = d_codes.astype(BF16).astype(F32).T
    per = tokens // n_t
    for k in range(n_t):
        sends[k][...] = fold(d_codes[k * per : (k + 1) * per])
    out = jnp.concatenate(outs_h, axis=0).astype(BF16).T
    for k in range(n_t):
        outs[k][...] = out[k * per : (k + 1) * per]
    grad_b_ref[:RANK] = mm(codes_q, d_query, NT)
    grad_b_ref[RANK:] = mm(codes_v, d_vals, NT)


def place_codes_kernel(frames, sub, *refs):
    pieces, (out_ref, buf) = refs[:-2], refs[-2:]
    patch_dev = sub * len(pieces)
    for k, piece in enumerate(pieces):
        rows = unfold(piece[...])
        for f in range(frames):
            start = pl.multiple_of(f * patch_dev + peer("tm", k) * sub, sub)
            buf[pl.ds(start, sub)] = rows[f * sub : (f + 1) * sub]
    out_ref[...] = buf[...].T[: 2 * RANK].astype(BF16)


def space_backward_kernel(frames, n_s, qkv_ref, probs_ref, hidden_ref, grad_b_ref, at_ref, at_here_ref, b_here_ref, *refs):
    packed, dcodes, sends = refs[:n_s], refs[n_s : 2 * n_s], refs[2 * n_s : 3 * n_s]
    part_ref, cut_buf = refs[3 * n_s :]
    d_s = part_ref.shape[1]
    tokens = hidden_ref.shape[0]
    patch_dev = tokens // frames
    total = n_s * patch_dev
    step = min(total, 256)
    ups = jnp.concatenate([at_here_ref[2], at_here_ref[3]], axis=0).T
    grads = []
    for k in range(n_s):
        cot = packed[k][3 * d_s : 4 * d_s].astype(F32)
        grads.append((cot + mm(ups, dcodes[k][...])).astype(BF16))
    grad_b_q = grad_b_v = None
    codes = [x[4 * d_s :] for x in packed]
    for f in range(frames):
        keys = qkv_ref[1, f].astype(F32)
        vals = qkv_ref[2, f].astype(F32)
        grad = frame_rows(grads, f, patch_dev).astype(F32)
        d_query, d_vals = [], []
        for h in range(d_s // HEAD_DIM):
            k_h = rows_of(keys, h).astype(BF16)
            v_h = rows_of(vals, h).astype(BF16)
            g_h = rows_of(grad, h).astype(BF16)
            dq_parts, dv_sum = [], None
            for s in range(0, total, step):
                probs = probs_ref[f, h, :, s : s + step]
                dq, dv = head_backward(probs, k_h, v_h, g_h[:, s : s + step])
                dq_parts.append(dq)
                dv_sum = dv if dv_sum is None else dv_sum + dv
            d_query.append(
                dq_parts[0] if len(dq_parts) == 1 else jnp.concatenate(dq_parts, axis=1)
            )
            d_vals.append(dv_sum)
        d_query = jnp.concatenate(d_query, axis=0).astype(BF16)
        d_vals = jnp.concatenate(d_vals, axis=0).astype(BF16)
        partial = jnp.concatenate([mm(b_here_ref[0], d_query), mm(b_here_ref[1], d_vals)], axis=0)
        for k in range(n_s):
            place = slice(f * patch_dev, (f + 1) * patch_dev)
            sends[k][:, place] = partial[:, k * patch_dev : (k + 1) * patch_dev].astype(BF16)
        frame_codes = frame_rows(codes, f, patch_dev)
        term_q = mm(frame_codes[:RANK], d_query, NT)
        term_v = mm(frame_codes[RANK:], d_vals, NT)
        grad_b_q = term_q if grad_b_q is None else grad_b_q + term_q
        grad_b_v = term_v if grad_b_v is None else grad_b_v + term_v
    part_ref[:RANK] = grad_b_q
    part_ref[RANK:] = grad_b_v
    grad_a = mm(dcodes[0][...], hidden_ref[...])
    for j in range(n_s):
        here = slice(j * d_s, (j + 1) * d_s)
        cut_buf[j, :, :d_s] = grad_a[:, here].astype(BF16)
        cut_buf[j, :, d_s:] = grad_b_ref[:, here].astype(BF16)
    for k in range(n_s):
        sends[k][:, tokens:] = cut_buf[peer("space", k)]


def add_up(terms):
    result = None
    for term in terms:
        result = term if result is None else result + term
    return result


def merge_kernel(n_s, n_d, part_ref, patches_ref, *refs):
    recvs, sends, buf = refs[:n_s], refs[n_s : n_s + n_d], refs[n_s + n_d]
    d_s = part_ref.shape[1]
    tokens = recvs[0].shape[1] - 2 * d_s
    codes = add_up([recv[:, :tokens].astype(F32) for recv in recvs]).astype(BF16)
    full = mm(codes, patches_ref[0].reshape(tokens, n_s * d_s))
    time_a = add_up([recv[:, tokens : tokens + d_s].astype(F32) for recv in recvs])
    time_b = add_up([recv[:, tokens + d_s :].astype(F32) for recv in recvs])
    split = jnp.concatenate([time_a, part_ref[...], time_b], axis=0)
    per, per_full = split.shape[0] // n_d, full.shape[0] // n_d
    for d in range(n_d):
        mine = [split[d * per : (d + 1) * per]]
        rows = full[d * per_full : (d + 1) * per_full]
        mine += [rows[:, j * d_s : (j + 1) * d_s] for j in range(n_s)]
        mine = jnp.concatenate(mine, axis=0)
        half = mine.shape[0] // 2
        buf[d] = jnp.concatenate([mine[:half], mine[half:]], axis=1)
    for k in range(n_d):
        sends[k][...] = buf[peer("dp", k)]


def total_kernel(*refs):
    terms = [ref[...].astype(F32) for ref in refs[:-1]]
    while len(terms) > 1:
        terms = [terms[i] + terms[i + 1] for i in range(0, len(terms), 2)]
    refs[-1][...] = terms[0].astype(refs[-1].dtype)


def join_kernel(n_full, *refs):
    pieces, (out_ref, buf) = refs[:-2], refs[-2:]
    n_s, d_s = len(pieces), buf.shape[2] // 2
    for k, piece in enumerate(pieces):
        buf[peer("space", k)] = piece[...]
    rows = [
        jnp.concatenate([buf[j, :, :d_s], buf[j, :, d_s:]], axis=0).astype(F32) for j in range(n_s)
    ]
    n_split = rows[0].shape[0] - n_s * n_full
    out_ref[n_full:] = jnp.concatenate([x[:n_split] for x in rows], axis=1).astype(BF16)
    full = add_up([x[n_split:] for x in rows])
    cuts = [full[j * n_full : (j + 1) * n_full] for j in range(n_s)]
    out_ref[:n_full] = jnp.concatenate(cuts, axis=1).astype(BF16)


def final_kernel(factor, n_d, n_full, *refs):
    pieces, (a_ref, b_ref, buf) = refs[:n_d], refs[n_d:]
    for k, piece in enumerate(pieces):
        buf[peer("dp", k)] = piece[...]
    n_split = pieces[0].shape[0] - n_full
    size = math.gcd(n_full, n_split, RANK)
    for d in range(n_d):
        rows = buf[d].astype(F32) * factor
        for r in range(0, n_full + n_split, size):
            row = d * n_full + r if r < n_full else 2 * RANK + d * n_split + r - n_full
            target = a_ref if row < 4 * RANK else b_ref
            row %= 4 * RANK
            target[row // RANK, row % RANK : row % RANK + size] = rows[r : r + size]


def mixed_kernel(frames, hidden_ref, *refs):
    pieces, (mixed_ref, buf) = refs[:-2], refs[-2:]
    n_t = len(pieces)
    tokens, width = hidden_ref.shape
    patch_dev = tokens // frames
    sub = patch_dev // n_t
    for k, piece in enumerate(pieces):
        for f in range(frames):
            start = pl.multiple_of(f * patch_dev + peer("tm", k) * sub, sub)
            buf[pl.ds(start, sub)] = piece[f * sub : (f + 1) * sub]
    total = hidden_ref[...].astype(F32) + buf[...].astype(F32)
    mixed_ref[0] = total.astype(BF16).reshape(frames, patch_dev, width)


def hops(arrays, axis, first):
    size = lax.axis_size(axis)
    return [
        lax.ppermute(array, axis, [(i, i ^ k) for i in range(size)])
        for k, array in enumerate(arrays, first)
    ]


def exchange(pieces, axis):
    return [pieces[0]] + hops(pieces[1:], axis, 1)


def share(array, axis):
    return exchange([array] * lax.axis_size(axis), axis)


def per_device(
    patches, query_s, key_s, value_s, query_t, key_t, value_t, adapters_a, adapters_b, cotangent
):
    _, frames, patch_dev, width = patches.shape
    n_d, n_t, n_s = (lax.axis_size(name) for name in ("dp", "tm", "space"))
    tokens = frames * patch_dev
    sub = patch_dev // n_t
    d_s = width // n_s
    total = n_s * patch_dev
    factor = (tokens * n_d * n_t * n_s) ** (-0.5)
    here = lax.axis_index("space") * d_s
    downs = jnp.swapaxes(adapters_a, 1, 2)
    downs_here = lax.dynamic_slice_in_dim(downs, here, d_s, 2)
    ups_here = lax.dynamic_slice_in_dim(adapters_b, here, d_s, 2)
    dma = pltpu.SemaphoreType.DMA

    time_arrays = [far(x) for x in (query_t, key_t, value_t, cotangent)]
    space_arrays = [
        far(x) for x in (patches, downs, adapters_b, query_s, value_s, key_s, cotangent)
    ]
    packed = call(
        functools.partial(pack_kernel, n_s, n_t, sub),
        [shape((4 * d_s + 2 * RANK, tokens), BF16)] * n_s
        + [shape((4, frames * sub, width), BF16)] * (n_t - 1),
        *space_arrays, *time_arrays,
        scratch=[pltpu.VMEM(x.shape, BF16) for x in space_arrays]
        + [
            pltpu.VMEM((4,) + query_t.shape, BF16),
            pltpu.VMEM((4, n_s, d_s, tokens), BF16),
            dma((7,)),
            dma((4,)),
        ],
        hbm=True,
    )
    time_pieces = hops(packed[n_s:], "tm", 1)
    packed = exchange(packed[:n_s], "space")
    probs_dims = (frames, d_s // HEAD_DIM, total, total)
    qkv, probs, *out_s = call(
        functools.partial(space_forward_kernel, frames, n_s),
        [shape((3, frames, d_s, total), BF16), pltpu.HBM(probs_dims, F32)]
        + [shape((d_s, tokens), BF16)] * n_s,
        *packed,
        scratch=[pltpu.VMEM(probs_dims, F32), dma((probs_dims[0] * probs_dims[1],))],
        after=time_pieces[:1],
    )
    out_s = exchange(out_s, "space")
    hidden, *codes = call(
        functools.partial(hidden_kernel, n_t, n_s),
        [shape((tokens, width), BF16)] + [shape((8, 128), F32)] * n_t,
        *out_s, patches, downs,
        scratch=[pltpu.VMEM((n_s, d_s, tokens), BF16), pltpu.VMEM((tokens, 128), F32)],
    )
    codes = exchange(codes, "tm")
    turned = call(
        functools.partial(turn_kernel, frames, sub),
        shape((4, width, n_t * frames * sub), BF16),
        *time_arrays, *time_pieces,
        scratch=[
            pltpu.VMEM((4, frames * sub, width), BF16),
            pltpu.VMEM((n_t - 1, 4, frames * sub, width), BF16),
            dma((4 * frames,)),
            dma((n_t - 1,)),
        ],
        hbm=True,
    )
    timed = call(
        functools.partial(time_kernel, n_t, sub),
        [shape((frames * sub, width), BF16)] * n_t
        + [shape((8, 128), F32)] * n_t
        + [shape((2 * RANK, width), F32)],
        turned, adapters_b, *codes,
    )
    out_t, dcodes, time_grad_b = timed[:n_t], timed[n_t : 2 * n_t], timed[2 * n_t]
    dcodes = exchange(dcodes, "tm")
    out_t[1:3] = hops(out_t[1:3], "tm", 1)
    dcodes = call(
        functools.partial(place_codes_kernel, frames, sub),
        shape((2 * RANK, tokens), BF16),
        *dcodes,
        scratch=[pltpu.VMEM((tokens, 128), F32)],
    )
    dcodes = share(dcodes, "space")
    backward = call(
        functools.partial(space_backward_kernel, frames, n_s),
        [shape((2 * RANK, tokens + 2 * d_s), BF16)] * n_s + [shape((2 * RANK, d_s), F32)],
        qkv, probs, hidden, time_grad_b, downs, downs_here, ups_here, *packed, *dcodes,
        scratch=[pltpu.VMEM((n_s, 2 * RANK, 2 * d_s), BF16)],
        after=out_t[1:3],
        carry=out_t[3:],
    )
    partial, part = backward[:n_s], backward[n_s]
    partial = exchange(partial, "space")
    out_t[3:] = hops(backward[n_s + 1 :], "tm", 3)
    n_full, n_split = 2 * RANK // n_d, 6 * RANK // n_d
    dims = ((n_s * n_full + n_split) // 2, 2 * d_s)
    sums = call(
        functools.partial(merge_kernel, n_s, n_d),
        [shape(dims, F32)] * n_d,
        part, patches, *partial,
        scratch=[pltpu.VMEM((n_d,) + dims, F32)],
        after=out_t[3:],
    )
    sums = call(total_kernel, shape(dims, BF16), *exchange(sums, "dp"))
    sums = call(total_kernel, shape(dims, BF16), *share(sums, "tm"))
    sums = call(
        functools.partial(join_kernel, n_full),
        shape((n_full + n_split, width), BF16),
        *share(sums, "space"),
        scratch=[pltpu.VMEM((n_s,) + dims, BF16)],
    )
    grads_a, grads_b = call(
        functools.partial(final_kernel, factor, n_d, n_full),
        [shape((4, RANK, width), F32)] * 2,
        *share(sums, "dp"),
        scratch=[pltpu.VMEM((n_d, n_full + n_split, width), BF16)],
    )
    mixed = call(
        functools.partial(mixed_kernel, frames),
        shape(patches.shape, BF16),
        hidden, *out_t,
        scratch=[pltpu.VMEM((tokens, width), BF16)],
    )
    return (mixed, jnp.swapaxes(grads_a, 1, 2), grads_b)


def solution(mesh):
    token = P("dp", "tm", "space", None)
    return jax.shard_map(
        per_device,
        mesh=mesh,
        in_specs=(token,) * 7 + (P(), P(), token),
        out_specs=(token, P(), P()),
        check_vma=False,
    )
```

```python
import functools
import math

import jax
import jax.numpy as jnp
from jax import lax
from jax.experimental import pallas as pl
from jax.experimental.pallas import tpu as pltpu
from jax.sharding import PartitionSpec as P

HEAD_DIM = 72
RANK = 16
SCALE = HEAD_DIM ** (-0.5)
F32 = jnp.float32
BF16 = jnp.bfloat16
NN = (((1,), (0,)), ((), ()))
NT = (((1,), (1,)), ((), ()))
TN = (((0,), (0,)), ((), ()))


def mm(a, b, dims=NN):
    return lax.dot_general(a, b, dims, preferred_element_type=F32)


def far(x):
    return pltpu.with_memory_space_constraint(x, pltpu.HBM)


def call(kernel, out_shape, *args, scratch=(), hbm=False, limit=48, after=(), carry=()):
    vmem = pl.BlockSpec(memory_space=pltpu.VMEM)
    anywhere = pl.BlockSpec(memory_space=pl.ANY)
    main = anywhere if hbm else vmem
    single = not isinstance(out_shape, (tuple, list))
    outs = (out_shape,) if single else tuple(out_shape)
    used, extra = len(args), len(after) + len(carry)

    def body(*refs):
        inside = refs[:used] + refs[used + extra : used + extra + len(outs)]
        kernel(*inside, *refs[used + extra + len(outs) + len(carry) :])

    result = pl.pallas_call(
        body,
        out_shape=outs + tuple(shape(x.shape, x.dtype) for x in carry),
        in_specs=[main] * used + [anywhere] * extra,
        out_specs=tuple(vmem if isinstance(o, jax.ShapeDtypeStruct) else anywhere for o in outs)
        + (anywhere,) * len(carry),
        scratch_shapes=list(scratch),
        input_output_aliases={used + len(after) + i: len(outs) + i for i in range(len(carry))},
        compiler_params=pltpu.CompilerParams(vmem_limit_bytes=limit * 1024 * 1024),
    )(*args, *after, *carry)
    return result[0] if single and not carry else list(result)


def shape(dims, dtype):
    return jax.ShapeDtypeStruct(tuple(dims), dtype)


def probs_of(keys, q_t, mask):
    scores = mm(keys, q_t) * SCALE
    if mask is not None:
        scores = jnp.where(mask, scores, -1e30)
    peak = jnp.max(scores, axis=0, keepdims=True)
    weights = jnp.exp(scores - peak)
    return weights * (1.0 / jnp.sum(weights, axis=0, keepdims=True))


def head_backward(probs, k_t, v_t, g_t):
    low = probs.astype(BF16)
    dvals = mm(g_t, low, NT)
    dprob = mm(v_t.T, g_t)
    inner = jnp.sum(probs * dprob, axis=0, keepdims=True)
    dscore = (probs * (dprob - inner) * SCALE).astype(BF16)
    dquery = mm(k_t, dscore)
    return dquery, dvals


def rows_of(array, head):
    return array[head * HEAD_DIM : (head + 1) * HEAD_DIM]


def peer(axis, distance):
    return lax.axis_index(axis) ^ distance


def load_all(refs, buffers, sems):
    copies = [
        pltpu.make_async_copy(ref, buffer, sems.at[index])
        for index, (ref, buffer) in enumerate(zip(refs, buffers))
    ]
    for copy in copies:
        copy.start()
    return copies


def pack_kernel(n_s, n_t, sub, *refs):
    ins, time_ins, refs = refs[:7], refs[7:11], refs[11:]
    outs, time_outs, refs = refs[:n_s], refs[n_s : n_s + n_t - 1], refs[n_s + n_t - 1 :]
    buffers, (time_buf, turned_ref, sems, time_sems) = refs[:7], refs[7:]
    p_buf, at_buf, b_buf, q_buf, v_buf, k_buf, g_buf = buffers
    copies = load_all(ins, buffers, sems)
    time_copies = load_all(time_ins, [time_buf.at[index] for index in range(4)], time_sems)
    d_s, tokens = turned_ref.shape[2:]
    frames = time_buf.shape[2]

    def flat(ref):
        return ref[0].reshape(tokens, ref.shape[3])

    def send(array, index):
        turned = array.T
        for j in range(n_s):
            turned_ref[index, j] = turned[j * d_s : (j + 1) * d_s]
        for k in range(n_s):
            outs[k][index * d_s : (index + 1) * d_s] = turned_ref[index, peer("space", k)]

    copies[0].wait()
    copies[1].wait()
    copies[2].wait()
    patches = flat(p_buf)
    codes_q = mm(patches, at_buf[0], NT).astype(BF16)
    codes_v = mm(patches, at_buf[1], NT).astype(BF16)
    codes_t = jnp.concatenate([codes_q, codes_v], axis=1).T
    copies[3].wait()
    query = (flat(q_buf).astype(F32) + mm(codes_q, b_buf[0])).astype(BF16)
    send(query, 0)
    copies[4].wait()
    value = (flat(v_buf).astype(F32) + mm(codes_v, b_buf[1])).astype(BF16)
    send(value, 2)
    copies[5].wait()
    send(flat(k_buf), 1)
    copies[6].wait()
    send(flat(g_buf), 3)
    for k in range(n_s):
        outs[k][4 * d_s :] = codes_t
    for index, copy in enumerate(time_copies):
        copy.wait()
        for k in range(1, n_t):
            start = pl.multiple_of(peer("tm", k) * sub, sub)
            for f in range(frames):
                time_outs[k - 1][index, f * sub : (f + 1) * sub] = time_buf[
                    index, 0, f, pl.ds(start, sub)
                ]


def frame_rows(pieces, f, patch_dev):
    return jnp.concatenate([x[:, f * patch_dev : (f + 1) * patch_dev] for x in pieces], axis=1)


def space_forward_kernel(frames, n_s, *refs):
    packed, (qkv_ref, probs_ref, *outs) = refs[:n_s], refs[n_s : 2 * n_s + 2]
    probs_buf, sems = refs[2 * n_s + 2 :]
    copies = []
    d_s, tokens = outs[0].shape
    patch_dev = tokens // frames
    total = n_s * patch_dev
    step = min(total, 256)
    for index in range(3):
        pieces = [x[index * d_s : (index + 1) * d_s] for x in packed]
        for f in range(frames):
            qkv_ref[index, f] = frame_rows(pieces, f, patch_dev)
    for f in range(frames):
        query = qkv_ref[0, f].astype(F32)
        keys = qkv_ref[1, f].astype(F32)
        vals = qkv_ref[2, f].astype(F32)
        heads = []
        for h in range(d_s // HEAD_DIM):
            k_h = rows_of(keys, h).astype(BF16)
            v_h = rows_of(vals, h).astype(BF16)
            q_h = rows_of(query, h).astype(BF16)
            parts = []
            for s in range(0, total, step):
                probs = probs_of(k_h.T, q_h[:, s : s + step], None)
                probs_buf[f, h, :, s : s + step] = probs
                parts.append(mm(v_h, probs.astype(BF16)))
            heads.append(parts[0] if len(parts) == 1 else jnp.concatenate(parts, axis=1))
            copy = pltpu.make_async_copy(
                probs_buf.at[f, h], probs_ref.at[f, h], sems.at[len(copies)]
            )
            copy.start()
            copies.append(copy)
        out = jnp.concatenate(heads, axis=0).astype(BF16)
        for k in range(n_s):
            outs[k][:, f * patch_dev : (f + 1) * patch_dev] = out[
                :, k * patch_dev : (k + 1) * patch_dev
            ]
    for copy in copies:
        copy.wait()


def lane_block(rows):
    return lax.broadcasted_iota(jnp.int32, (rows, 128), 1) // (2 * RANK)


def fold(token_rows):
    block = lane_block(8)
    result = token_rows[0:8]
    for k in range(1, 4):
        result = jnp.where(block == k, token_rows[8 * k : 8 * k + 8], result)
    return result


def unfold(folded):
    pieces = [folded]
    for k in range(1, 4):
        pieces.append(pltpu.roll(folded, 128 - 2 * RANK * k, 1))
    return jnp.concatenate(pieces, axis=0)


def hidden_kernel(n_t, n_s, *refs):
    pieces, refs = refs[:n_s], refs[n_s:]
    p_ref, at_ref, hidden_ref = refs[:3]
    sends = refs[3 : 3 + n_t]
    out_buf, codes_buf = refs[3 + n_t :]
    _, frames, patch_dev, width = p_ref.shape
    tokens = frames * patch_dev
    sub = patch_dev // n_t
    for k in range(n_s):
        out_buf[peer("space", k)] = pieces[k][...]
    out = out_buf[...].reshape(width, tokens).T
    hidden = (p_ref[0].reshape(tokens, width).astype(F32) + out.astype(F32)).astype(BF16)
    hidden_ref[...] = hidden
    downs = jnp.concatenate([at_ref[2], at_ref[3]] * 4, axis=0)
    codes_buf[...] = mm(hidden, downs, NT).astype(BF16).astype(F32)
    for k in range(n_t):
        rows = [
            codes_buf[pl.ds(pl.multiple_of(f * patch_dev + peer("tm", k) * sub, sub), sub)]
            for f in range(frames)
        ]
        sends[k][...] = fold(jnp.concatenate(rows, axis=0))


def turn_kernel(frames, sub, q_ref, k_ref, v_ref, g_ref, *refs):
    *pieces, out_ref, own_buf, piece_buf, own_sems, sems = refs
    own = []
    start = pl.multiple_of(peer("tm", 0) * sub, sub)
    for index, ref in enumerate((q_ref, k_ref, v_ref, g_ref)):
        for f in range(frames):
            copy = pltpu.make_async_copy(
                ref.at[0, f, pl.ds(start, sub)],
                own_buf.at[index, f * sub : (f + 1) * sub],
                own_sems.at[index * frames + f],
            )
            copy.start()
            own.append(copy)
    copies = load_all(pieces, [piece_buf.at[k] for k in range(len(pieces))], sems)
    for copy in own + copies:
        copy.wait()
    for index in range(4):
        parts = [own_buf[index]] + [piece_buf[k, index] for k in range(len(pieces))]
        out_ref[index] = jnp.concatenate(parts, axis=0).T


def time_kernel(n_t, sub, x_ref, b_ref, *refs):
    codes_refs, refs = refs[:n_t], refs[n_t:]
    outs, sends, grad_b_ref = refs[:n_t], refs[n_t : 2 * n_t], refs[2 * n_t]
    _, width, tokens = x_ref.shape
    codes = jnp.concatenate([unfold(ref[...]) for ref in codes_refs], axis=0).T
    codes_q = codes[:RANK].astype(BF16)
    codes_v = codes[RANK : 2 * RANK].astype(BF16)
    query = (x_ref[0].astype(F32) + mm(b_ref[2], codes_q, TN)).astype(BF16).astype(F32)
    vals = (x_ref[2].astype(F32) + mm(b_ref[3], codes_v, TN)).astype(BF16).astype(F32)
    keys = x_ref[1].astype(F32)
    grad = x_ref[3].astype(F32)
    row = lax.broadcasted_iota(jnp.int32, (tokens, 2 * tokens), 0)
    col = lax.broadcasted_iota(jnp.int32, (tokens, 2 * tokens), 1)
    mask = lax.rem(row, sub) == lax.rem(col, sub)
    top = lax.broadcasted_iota(jnp.int32, (2 * HEAD_DIM, tokens), 0) < HEAD_DIM

    def spread(pair):
        return jnp.concatenate(
            [jnp.where(top, pair, 0.0), jnp.where(top, 0.0, pair)], axis=1
        ).astype(BF16)

    def pick(wide):
        return jnp.concatenate([wide[:HEAD_DIM, :tokens], wide[HEAD_DIM:, tokens:]], axis=0)

    outs_h, d_query, d_vals = [], [], []
    for h in range(0, width, 2 * HEAD_DIM):
        pair = slice(h, h + 2 * HEAD_DIM)
        k_h, v_h = keys[pair].astype(BF16), vals[pair].astype(BF16)
        g_h = spread(grad[pair])
        probs = probs_of(k_h.T, spread(query[pair]), mask)
        low = probs.astype(BF16)
        dprob = mm(v_h.T, g_h)
        inner = jnp.sum(probs * dprob, axis=0, keepdims=True)
        dscore = (probs * (dprob - inner) * SCALE).astype(BF16)
        outs_h.append(pick(mm(v_h, low)))
        d_vals.append(mm(g_h, low, NT))
        d_query.append(pick(mm(k_h, dscore)))
    d_query = jnp.concatenate(d_query, axis=0).astype(BF16)
    d_vals = jnp.concatenate(d_vals, axis=0).astype(BF16)
    d_codes = jnp.concatenate([mm(b_ref[2], d_query), mm(b_ref[3], d_vals)] * 4, axis=0)
    d_codes = d_codes.astype(BF16).astype(F32).T
    per = tokens // n_t
    for k in range(n_t):
        sends[k][...] = fold(d_codes[k * per : (k + 1) * per])
    out = jnp.concatenate(outs_h, axis=0).astype(BF16).T
    for k in range(n_t):
        outs[k][...] = out[k * per : (k + 1) * per]
    grad_b_ref[:RANK] = mm(codes_q, d_query, NT)
    grad_b_ref[RANK:] = mm(codes_v, d_vals, NT)


def place_codes_kernel(frames, sub, *refs):
    pieces, (out_ref, buf) = refs[:-2], refs[-2:]
    patch_dev = sub * len(pieces)
    for k, piece in enumerate(pieces):
        rows = unfold(piece[...])
        for f in range(frames):
            start = pl.multiple_of(f * patch_dev + peer("tm", k) * sub, sub)
            buf[pl.ds(start, sub)] = rows[f * sub : (f + 1) * sub]
    out_ref[...] = buf[...].T[: 2 * RANK].astype(BF16)


def space_backward_kernel(frames, n_s, qkv_ref, probs_ref, hidden_ref, grad_b_ref, at_ref, at_here_ref, b_here_ref, *refs):
    packed, dcodes, sends = refs[:n_s], refs[n_s : 2 * n_s], refs[2 * n_s : 3 * n_s]
    part_ref, cut_buf = refs[3 * n_s :]
    d_s = part_ref.shape[1]
    tokens = hidden_ref.shape[0]
    patch_dev = tokens // frames
    total = n_s * patch_dev
    step = min(total, 256)
    ups = jnp.concatenate([at_here_ref[2], at_here_ref[3]], axis=0).T
    grads = []
    for k in range(n_s):
        cot = packed[k][3 * d_s : 4 * d_s].astype(F32)
        grads.append((cot + mm(ups, dcodes[k][...])).astype(BF16))
    grad_b_q = grad_b_v = None
    codes = [x[4 * d_s :] for x in packed]
    for f in range(frames):
        keys = qkv_ref[1, f].astype(F32)
        vals = qkv_ref[2, f].astype(F32)
        grad = frame_rows(grads, f, patch_dev).astype(F32)
        d_query, d_vals = [], []
        for h in range(d_s // HEAD_DIM):
            k_h = rows_of(keys, h).astype(BF16)
            v_h = rows_of(vals, h).astype(BF16)
            g_h = rows_of(grad, h).astype(BF16)
            dq_parts, dv_sum = [], None
            for s in range(0, total, step):
                probs = probs_ref[f, h, :, s : s + step]
                dq, dv = head_backward(probs, k_h, v_h, g_h[:, s : s + step])
                dq_parts.append(dq)
                dv_sum = dv if dv_sum is None else dv_sum + dv
            d_query.append(
                dq_parts[0] if len(dq_parts) == 1 else jnp.concatenate(dq_parts, axis=1)
            )
            d_vals.append(dv_sum)
        d_query = jnp.concatenate(d_query, axis=0).astype(BF16)
        d_vals = jnp.concatenate(d_vals, axis=0).astype(BF16)
        partial = jnp.concatenate([mm(b_here_ref[0], d_query), mm(b_here_ref[1], d_vals)], axis=0)
        for k in range(n_s):
            place = slice(f * patch_dev, (f + 1) * patch_dev)
            sends[k][:, place] = partial[:, k * patch_dev : (k + 1) * patch_dev].astype(BF16)
        frame_codes = frame_rows(codes, f, patch_dev)
        term_q = mm(frame_codes[:RANK], d_query, NT)
        term_v = mm(frame_codes[RANK:], d_vals, NT)
        grad_b_q = term_q if grad_b_q is None else grad_b_q + term_q
        grad_b_v = term_v if grad_b_v is None else grad_b_v + term_v
    part_ref[:RANK] = grad_b_q
    part_ref[RANK:] = grad_b_v
    grad_a = mm(dcodes[0][...], hidden_ref[...])
    for j in range(n_s):
        here = slice(j * d_s, (j + 1) * d_s)
        cut_buf[j, :, :d_s] = grad_a[:, here].astype(BF16)
        cut_buf[j, :, d_s:] = grad_b_ref[:, here].astype(BF16)
    for k in range(n_s):
        sends[k][:, tokens:] = cut_buf[peer("space", k)]


def add_up(terms):
    result = None
    for term in terms:
        result = term if result is None else result + term
    return result


def merge_kernel(n_s, n_d, part_ref, patches_ref, *refs):
    recvs, sends, buf = refs[:n_s], refs[n_s : n_s + n_d], refs[n_s + n_d]
    d_s = part_ref.shape[1]
    tokens = recvs[0].shape[1] - 2 * d_s
    codes = add_up([recv[:, :tokens].astype(F32) for recv in recvs]).astype(BF16)
    full = mm(codes, patches_ref[0].reshape(tokens, n_s * d_s))
    time_a = add_up([recv[:, tokens : tokens + d_s].astype(F32) for recv in recvs])
    time_b = add_up([recv[:, tokens + d_s :].astype(F32) for recv in recvs])
    split = jnp.concatenate([time_a, part_ref[...], time_b], axis=0)
    per, per_full = split.shape[0] // n_d, full.shape[0] // n_d
    for d in range(n_d):
        mine = [split[d * per : (d + 1) * per]]
        rows = full[d * per_full : (d + 1) * per_full]
        mine += [rows[:, j * d_s : (j + 1) * d_s] for j in range(n_s)]
        mine = jnp.concatenate(mine, axis=0)
        half = mine.shape[0] // 2
        buf[d] = jnp.concatenate([mine[:half], mine[half:]], axis=1).astype(BF16)
    for k in range(n_d):
        sends[k][...] = buf[peer("dp", k)]


def total_kernel(*refs):
    terms = [ref[...].astype(F32) for ref in refs[:-1]]
    while len(terms) > 1:
        terms = [terms[i] + terms[i + 1] for i in range(0, len(terms), 2)]
    refs[-1][...] = terms[0].astype(refs[-1].dtype)


def join_kernel(n_full, *refs):
    pieces, (out_ref, buf) = refs[:-2], refs[-2:]
    n_s, d_s = len(pieces), buf.shape[2] // 2
    for k, piece in enumerate(pieces):
        buf[peer("space", k)] = piece[...]
    rows = [
        jnp.concatenate([buf[j, :, :d_s], buf[j, :, d_s:]], axis=0).astype(F32) for j in range(n_s)
    ]
    n_split = rows[0].shape[0] - n_s * n_full
    out_ref[n_full:] = jnp.concatenate([x[:n_split] for x in rows], axis=1).astype(BF16)
    full = add_up([x[n_split:] for x in rows])
    cuts = [full[j * n_full : (j + 1) * n_full] for j in range(n_s)]
    out_ref[:n_full] = jnp.concatenate(cuts, axis=1).astype(BF16)


def final_kernel(factor, n_d, n_full, *refs):
    pieces, (a_ref, b_ref, buf) = refs[:n_d], refs[n_d:]
    for k, piece in enumerate(pieces):
        buf[peer("dp", k)] = piece[...]
    n_split = pieces[0].shape[0] - n_full
    size = math.gcd(n_full, n_split, RANK)
    for d in range(n_d):
        rows = buf[d].astype(F32) * factor
        for r in range(0, n_full + n_split, size):
            row = d * n_full + r if r < n_full else 2 * RANK + d * n_split + r - n_full
            target = a_ref if row < 4 * RANK else b_ref
            row %= 4 * RANK
            target[row // RANK, row % RANK : row % RANK + size] = rows[r : r + size]


def mixed_kernel(frames, hidden_ref, *refs):
    pieces, (mixed_ref, buf) = refs[:-2], refs[-2:]
    n_t = len(pieces)
    tokens, width = hidden_ref.shape
    patch_dev = tokens // frames
    sub = patch_dev // n_t
    for k, piece in enumerate(pieces):
        for f in range(frames):
            start = pl.multiple_of(f * patch_dev + peer("tm", k) * sub, sub)
            buf[pl.ds(start, sub)] = piece[f * sub : (f + 1) * sub]
    total = hidden_ref[...].astype(F32) + buf[...].astype(F32)
    mixed_ref[0] = total.astype(BF16).reshape(frames, patch_dev, width)


def hops(arrays, axis, first):
    size = lax.axis_size(axis)
    return [
        lax.ppermute(array, axis, [(i, i ^ k) for i in range(size)])
        for k, array in enumerate(arrays, first)
    ]


def exchange(pieces, axis):
    return [pieces[0]] + hops(pieces[1:], axis, 1)


def share(array, axis):
    return exchange([array] * lax.axis_size(axis), axis)


def per_device(
    patches, query_s, key_s, value_s, query_t, key_t, value_t, adapters_a, adapters_b, cotangent
):
    _, frames, patch_dev, width = patches.shape
    n_d, n_t, n_s = (lax.axis_size(name) for name in ("dp", "tm", "space"))
    tokens = frames * patch_dev
    sub = patch_dev // n_t
    d_s = width // n_s
    total = n_s * patch_dev
    factor = (tokens * n_d * n_t * n_s) ** (-0.5)
    here = lax.axis_index("space") * d_s
    downs = jnp.swapaxes(adapters_a, 1, 2)
    downs_here = lax.dynamic_slice_in_dim(downs, here, d_s, 2)
    ups_here = lax.dynamic_slice_in_dim(adapters_b, here, d_s, 2)
    dma = pltpu.SemaphoreType.DMA

    time_arrays = [far(x) for x in (query_t, key_t, value_t, cotangent)]
    space_arrays = [
        far(x) for x in (patches, downs, adapters_b, query_s, value_s, key_s, cotangent)
    ]
    packed = call(
        functools.partial(pack_kernel, n_s, n_t, sub),
        [shape((4 * d_s + 2 * RANK, tokens), BF16)] * n_s
        + [shape((4, frames * sub, width), BF16)] * (n_t - 1),
        *space_arrays, *time_arrays,
        scratch=[pltpu.VMEM(x.shape, BF16) for x in space_arrays]
        + [
            pltpu.VMEM((4,) + query_t.shape, BF16),
            pltpu.VMEM((4, n_s, d_s, tokens), BF16),
            dma((7,)),
            dma((4,)),
        ],
        hbm=True,
    )
    time_pieces = hops(packed[n_s:], "tm", 1)
    packed = exchange(packed[:n_s], "space")
    probs_dims = (frames, d_s // HEAD_DIM, total, total)
    qkv, probs, *out_s = call(
        functools.partial(space_forward_kernel, frames, n_s),
        [shape((3, frames, d_s, total), BF16), pltpu.HBM(probs_dims, F32)]
        + [shape((d_s, tokens), BF16)] * n_s,
        *packed,
        scratch=[pltpu.VMEM(probs_dims, F32), dma((probs_dims[0] * probs_dims[1],))],
        after=time_pieces[:1],
    )
    out_s = exchange(out_s, "space")
    hidden, *codes = call(
        functools.partial(hidden_kernel, n_t, n_s),
        [shape((tokens, width), BF16)] + [shape((8, 128), F32)] * n_t,
        *out_s, patches, downs,
        scratch=[pltpu.VMEM((n_s, d_s, tokens), BF16), pltpu.VMEM((tokens, 128), F32)],
    )
    codes = exchange(codes, "tm")
    turned = call(
        functools.partial(turn_kernel, frames, sub),
        shape((4, width, n_t * frames * sub), BF16),
        *time_arrays, *time_pieces,
        scratch=[
            pltpu.VMEM((4, frames * sub, width), BF16),
            pltpu.VMEM((n_t - 1, 4, frames * sub, width), BF16),
            dma((4 * frames,)),
            dma((n_t - 1,)),
        ],
        hbm=True,
    )
    timed = call(
        functools.partial(time_kernel, n_t, sub),
        [shape((frames * sub, width), BF16)] * n_t
        + [shape((8, 128), F32)] * n_t
        + [shape((2 * RANK, width), F32)],
        turned, adapters_b, *codes,
    )
    out_t, dcodes, time_grad_b = timed[:n_t], timed[n_t : 2 * n_t], timed[2 * n_t]
    dcodes = exchange(dcodes, "tm")
    out_t[1:3] = hops(out_t[1:3], "tm", 1)
    dcodes = call(
        functools.partial(place_codes_kernel, frames, sub),
        shape((2 * RANK, tokens), BF16),
        *dcodes,
        scratch=[pltpu.VMEM((tokens, 128), F32)],
    )
    dcodes = share(dcodes, "space")
    backward = call(
        functools.partial(space_backward_kernel, frames, n_s),
        [shape((2 * RANK, tokens + 2 * d_s), BF16)] * n_s + [shape((2 * RANK, d_s), F32)],
        qkv, probs, hidden, time_grad_b, downs, downs_here, ups_here, *packed, *dcodes,
        scratch=[pltpu.VMEM((n_s, 2 * RANK, 2 * d_s), BF16)],
        after=out_t[1:3],
        carry=out_t[3:],
    )
    partial, part = backward[:n_s], backward[n_s]
    partial = exchange(partial, "space")
    out_t[3:] = hops(backward[n_s + 1 :], "tm", 3)
    n_full, n_split = 2 * RANK // n_d, 6 * RANK // n_d
    dims = ((n_s * n_full + n_split) // 2, 2 * d_s)
    sums = call(
        functools.partial(merge_kernel, n_s, n_d),
        [shape(dims, BF16)] * n_d,
        part, patches, *partial,
        scratch=[pltpu.VMEM((n_d,) + dims, BF16)],
    )
    sums = call(total_kernel, shape(dims, BF16), *exchange(sums, "dp"), after=out_t[3:])
    sums = call(total_kernel, shape(dims, BF16), *share(sums, "tm"))
    sums = call(
        functools.partial(join_kernel, n_full),
        shape((n_full + n_split, width), BF16),
        *share(sums, "space"),
        scratch=[pltpu.VMEM((n_s,) + dims, BF16)],
    )
    grads_a, grads_b = call(
        functools.partial(final_kernel, factor, n_d, n_full),
        [shape((4, RANK, width), F32)] * 2,
        *share(sums, "dp"),
        scratch=[pltpu.VMEM((n_d, n_full + n_split, width), BF16)],
    )
    mixed = call(
        functools.partial(mixed_kernel, frames),
        shape(patches.shape, BF16),
        hidden, *out_t,
        scratch=[pltpu.VMEM((tokens, width), BF16)],
    )
    return (mixed, jnp.swapaxes(grads_a, 1, 2), grads_b)


def solution(mesh):
    token = P("dp", "tm", "space", None)
    return jax.shard_map(
        per_device,
        mesh=mesh,
        in_specs=(token,) * 7 + (P(), P(), token),
        out_specs=(token, P(), P()),
        check_vma=False,
    )
```

```python
import functools
import math

import jax
import jax.numpy as jnp
from jax import lax
from jax.experimental import pallas as pl
from jax.experimental.pallas import tpu as pltpu
from jax.sharding import PartitionSpec as P

HEAD_DIM = 72
RANK = 16
SCALE = HEAD_DIM ** (-0.5)
F32 = jnp.float32
BF16 = jnp.bfloat16
NN = (((1,), (0,)), ((), ()))
NT = (((1,), (1,)), ((), ()))
TN = (((0,), (0,)), ((), ()))


def mm(a, b, dims=NN):
    return lax.dot_general(a, b, dims, preferred_element_type=F32)


def far(x):
    return pltpu.with_memory_space_constraint(x, pltpu.HBM)


def call(kernel, out_shape, *args, scratch=(), hbm=False, limit=48, after=(), carry=()):
    vmem = pl.BlockSpec(memory_space=pltpu.VMEM)
    anywhere = pl.BlockSpec(memory_space=pl.ANY)
    main = anywhere if hbm else vmem
    single = not isinstance(out_shape, (tuple, list))
    outs = (out_shape,) if single else tuple(out_shape)
    used, extra = len(args), len(after) + len(carry)

    def body(*refs):
        inside = refs[:used] + refs[used + extra : used + extra + len(outs)]
        kernel(*inside, *refs[used + extra + len(outs) + len(carry) :])

    result = pl.pallas_call(
        body,
        out_shape=outs + tuple(shape(x.shape, x.dtype) for x in carry),
        in_specs=[main] * used + [anywhere] * extra,
        out_specs=tuple(vmem if isinstance(o, jax.ShapeDtypeStruct) else anywhere for o in outs)
        + (anywhere,) * len(carry),
        scratch_shapes=list(scratch),
        input_output_aliases={used + len(after) + i: len(outs) + i for i in range(len(carry))},
        compiler_params=pltpu.CompilerParams(vmem_limit_bytes=limit * 1024 * 1024),
    )(*args, *after, *carry)
    return result[0] if single and not carry else list(result)


def shape(dims, dtype):
    return jax.ShapeDtypeStruct(tuple(dims), dtype)


def probs_of(keys, q_t, mask):
    scores = mm(keys, q_t) * SCALE
    if mask is not None:
        scores = jnp.where(mask, scores, -1e30)
    peak = jnp.max(scores, axis=0, keepdims=True)
    weights = jnp.exp(scores - peak)
    return weights * (1.0 / jnp.sum(weights, axis=0, keepdims=True))


def head_backward(probs, k_t, v_t, g_t):
    low = probs.astype(BF16)
    dvals = mm(g_t, low, NT)
    dprob = mm(v_t.T, g_t)
    inner = jnp.sum(probs * dprob, axis=0, keepdims=True)
    dscore = (probs * (dprob - inner) * SCALE).astype(BF16)
    dquery = mm(k_t, dscore)
    return dquery, dvals


def rows_of(array, head):
    return array[head * HEAD_DIM : (head + 1) * HEAD_DIM]


def peer(axis, distance):
    return lax.axis_index(axis) ^ distance


def load_all(refs, buffers, sems):
    copies = [
        pltpu.make_async_copy(ref, buffer, sems.at[index])
        for index, (ref, buffer) in enumerate(zip(refs, buffers))
    ]
    for copy in copies:
        copy.start()
    return copies


def pack_kernel(n_s, n_t, sub, *refs):
    ins, time_ins, refs = refs[:6], refs[6:10], refs[10:]
    outs, time_outs, refs = refs[:n_s], refs[n_s : n_s + n_t - 1], refs[n_s + n_t - 1 :]
    buffers, (time_buf, turned_ref, sems, time_sems) = refs[:6], refs[6:]
    p_buf, at_buf, b_buf, q_buf, v_buf, k_buf = buffers
    copies = load_all(ins, buffers, sems)
    time_copies = load_all(time_ins, [time_buf.at[index] for index in range(4)], time_sems)
    d_s, tokens = turned_ref.shape[2:]
    frames = time_buf.shape[2]

    def flat(ref):
        return ref[0].reshape(tokens, ref.shape[3])

    def send(array, index):
        turned = array.T
        for j in range(n_s):
            turned_ref[index, j] = turned[j * d_s : (j + 1) * d_s]
        for k in range(n_s):
            outs[k][index * d_s : (index + 1) * d_s] = turned_ref[index, peer("space", k)]

    copies[0].wait()
    copies[1].wait()
    copies[2].wait()
    patches = flat(p_buf)
    codes_q = mm(patches, at_buf[0], NT).astype(BF16)
    codes_v = mm(patches, at_buf[1], NT).astype(BF16)
    codes_t = jnp.concatenate([codes_q, codes_v], axis=1).T
    copies[3].wait()
    query = (flat(q_buf).astype(F32) + mm(codes_q, b_buf[0])).astype(BF16)
    send(query, 0)
    copies[4].wait()
    value = (flat(v_buf).astype(F32) + mm(codes_v, b_buf[1])).astype(BF16)
    send(value, 2)
    copies[5].wait()
    send(flat(k_buf), 1)
    for k in range(n_s):
        outs[k][3 * d_s :] = codes_t
    for index, copy in enumerate(time_copies):
        copy.wait()
        for k in range(1, n_t):
            start = pl.multiple_of(peer("tm", k) * sub, sub)
            for f in range(frames):
                time_outs[k - 1][index, f * sub : (f + 1) * sub] = time_buf[
                    index, 0, f, pl.ds(start, sub)
                ]


def frame_rows(pieces, f, patch_dev):
    return jnp.concatenate([x[:, f * patch_dev : (f + 1) * patch_dev] for x in pieces], axis=1)


def space_forward_kernel(frames, n_s, *refs):
    packed, (qkv_ref, probs_ref, *outs) = refs[:n_s], refs[n_s : 2 * n_s + 2]
    probs_buf, sems = refs[2 * n_s + 2 :]
    copies = []
    d_s, tokens = outs[0].shape
    patch_dev = tokens // frames
    total = n_s * patch_dev
    step = min(total, 256)
    for index in range(3):
        pieces = [x[index * d_s : (index + 1) * d_s] for x in packed]
        for f in range(frames):
            qkv_ref[index, f] = frame_rows(pieces, f, patch_dev)
    for f in range(frames):
        query = qkv_ref[0, f].astype(F32)
        keys = qkv_ref[1, f].astype(F32)
        vals = qkv_ref[2, f].astype(F32)
        heads = []
        for h in range(d_s // HEAD_DIM):
            k_h = rows_of(keys, h).astype(BF16)
            v_h = rows_of(vals, h).astype(BF16)
            q_h = rows_of(query, h).astype(BF16)
            parts = []
            for s in range(0, total, step):
                probs = probs_of(k_h.T, q_h[:, s : s + step], None)
                probs_buf[f, h, :, s : s + step] = probs
                parts.append(mm(v_h, probs.astype(BF16)))
            heads.append(parts[0] if len(parts) == 1 else jnp.concatenate(parts, axis=1))
            copy = pltpu.make_async_copy(
                probs_buf.at[f, h], probs_ref.at[f, h], sems.at[len(copies)]
            )
            copy.start()
            copies.append(copy)
        out = jnp.concatenate(heads, axis=0).astype(BF16)
        for k in range(n_s):
            outs[k][:, f * patch_dev : (f + 1) * patch_dev] = out[
                :, k * patch_dev : (k + 1) * patch_dev
            ]
    for copy in copies:
        copy.wait()


def lane_block(rows):
    return lax.broadcasted_iota(jnp.int32, (rows, 128), 1) // (2 * RANK)


def fold(token_rows):
    block = lane_block(8)
    result = token_rows[0:8]
    for k in range(1, 4):
        result = jnp.where(block == k, token_rows[8 * k : 8 * k + 8], result)
    return result


def unfold(folded):
    pieces = [folded]
    for k in range(1, 4):
        pieces.append(pltpu.roll(folded, 128 - 2 * RANK * k, 1))
    return jnp.concatenate(pieces, axis=0)


def hidden_kernel(n_t, n_s, *refs):
    pieces, refs = refs[:n_s], refs[n_s:]
    p_ref, at_ref, hidden_ref = refs[:3]
    sends = refs[3 : 3 + n_t]
    out_buf, codes_buf = refs[3 + n_t :]
    _, frames, patch_dev, width = p_ref.shape
    tokens = frames * patch_dev
    sub = patch_dev // n_t
    for k in range(n_s):
        out_buf[peer("space", k)] = pieces[k][...]
    out = out_buf[...].reshape(width, tokens).T
    hidden = (p_ref[0].reshape(tokens, width).astype(F32) + out.astype(F32)).astype(BF16)
    hidden_ref[...] = hidden
    downs = jnp.concatenate([at_ref[2], at_ref[3]] * 4, axis=0)
    codes_buf[...] = mm(hidden, downs, NT).astype(BF16).astype(F32)
    for k in range(n_t):
        rows = [
            codes_buf[pl.ds(pl.multiple_of(f * patch_dev + peer("tm", k) * sub, sub), sub)]
            for f in range(frames)
        ]
        sends[k][...] = fold(jnp.concatenate(rows, axis=0))


def turn_kernel(frames, sub, q_ref, k_ref, v_ref, g_ref, *refs):
    *pieces, out_ref, own_buf, piece_buf, own_sems, sems = refs
    own = []
    start = pl.multiple_of(peer("tm", 0) * sub, sub)
    for index, ref in enumerate((q_ref, k_ref, v_ref, g_ref)):
        for f in range(frames):
            copy = pltpu.make_async_copy(
                ref.at[0, f, pl.ds(start, sub)],
                own_buf.at[index, f * sub : (f + 1) * sub],
                own_sems.at[index * frames + f],
            )
            copy.start()
            own.append(copy)
    copies = load_all(pieces, [piece_buf.at[k] for k in range(len(pieces))], sems)
    for copy in own + copies:
        copy.wait()
    for index in range(4):
        parts = [own_buf[index]] + [piece_buf[k, index] for k in range(len(pieces))]
        out_ref[index] = jnp.concatenate(parts, axis=0).T


def time_kernel(n_t, sub, x_ref, b_ref, *refs):
    codes_refs, refs = refs[:n_t], refs[n_t:]
    outs, sends, grad_b_ref = refs[:n_t], refs[n_t : 2 * n_t], refs[2 * n_t]
    _, width, tokens = x_ref.shape
    codes = jnp.concatenate([unfold(ref[...]) for ref in codes_refs], axis=0).T
    codes_q = codes[:RANK].astype(BF16)
    codes_v = codes[RANK : 2 * RANK].astype(BF16)
    query = (x_ref[0].astype(F32) + mm(b_ref[2], codes_q, TN)).astype(BF16).astype(F32)
    vals = (x_ref[2].astype(F32) + mm(b_ref[3], codes_v, TN)).astype(BF16).astype(F32)
    keys = x_ref[1].astype(F32)
    grad = x_ref[3].astype(F32)
    row = lax.broadcasted_iota(jnp.int32, (tokens, 2 * tokens), 0)
    col = lax.broadcasted_iota(jnp.int32, (tokens, 2 * tokens), 1)
    mask = lax.rem(row, sub) == lax.rem(col, sub)
    top = lax.broadcasted_iota(jnp.int32, (2 * HEAD_DIM, tokens), 0) < HEAD_DIM

    def spread(pair):
        return jnp.concatenate(
            [jnp.where(top, pair, 0.0), jnp.where(top, 0.0, pair)], axis=1
        ).astype(BF16)

    def pick(wide):
        return jnp.concatenate([wide[:HEAD_DIM, :tokens], wide[HEAD_DIM:, tokens:]], axis=0)

    outs_h, d_query, d_vals = [], [], []
    for h in range(0, width, 2 * HEAD_DIM):
        pair = slice(h, h + 2 * HEAD_DIM)
        k_h, v_h = keys[pair].astype(BF16), vals[pair].astype(BF16)
        g_h = spread(grad[pair])
        probs = probs_of(k_h.T, spread(query[pair]), mask)
        low = probs.astype(BF16)
        dprob = mm(v_h.T, g_h)
        inner = jnp.sum(probs * dprob, axis=0, keepdims=True)
        dscore = (probs * (dprob - inner) * SCALE).astype(BF16)
        outs_h.append(pick(mm(v_h, low)))
        d_vals.append(mm(g_h, low, NT))
        d_query.append(pick(mm(k_h, dscore)))
    d_query = jnp.concatenate(d_query, axis=0).astype(BF16)
    d_vals = jnp.concatenate(d_vals, axis=0).astype(BF16)
    d_codes = jnp.concatenate([mm(b_ref[2], d_query), mm(b_ref[3], d_vals)] * 4, axis=0)
    d_codes = d_codes.astype(BF16).astype(F32).T
    per = tokens // n_t
    for k in range(n_t):
        sends[k][...] = fold(d_codes[k * per : (k + 1) * per])
    out = jnp.concatenate(outs_h, axis=0).astype(BF16).T
    for k in range(n_t):
        outs[k][...] = out[k * per : (k + 1) * per]
    grad_b_ref[:RANK] = mm(codes_q, d_query, NT)
    grad_b_ref[RANK:] = mm(codes_v, d_vals, NT)


def hidden_grad_kernel(frames, n_s, sub, g_ref, at_ref, *refs):
    *pieces, codes_ref = refs[: -n_s - 2]
    outs, (buf, turned_ref) = refs[-n_s - 2 : -2], refs[-2:]
    patch_dev = sub * len(pieces)
    _, d_s, tokens = turned_ref.shape
    for k, piece in enumerate(pieces):
        rows = unfold(piece[...])
        for f in range(frames):
            start = pl.multiple_of(f * patch_dev + peer("tm", k) * sub, sub)
            buf[pl.ds(start, sub)] = rows[f * sub : (f + 1) * sub]
    codes = buf[:, : 2 * RANK].astype(BF16)
    codes_ref[...] = buf[...].T[: 2 * RANK].astype(BF16)
    downs = jnp.concatenate([at_ref[2], at_ref[3]], axis=0)
    grad = g_ref[0].reshape(tokens, n_s * d_s).astype(F32) + mm(codes, downs)
    turned = grad.astype(BF16).T
    for j in range(n_s):
        turned_ref[j] = turned[j * d_s : (j + 1) * d_s]
    for k in range(n_s):
        outs[k][...] = turned_ref[peer("space", k)]


def space_backward_kernel(frames, n_s, qkv_ref, probs_ref, hidden_ref, grad_b_ref, dcodes_ref, b_here_ref, *refs):
    packed, grads, sends = refs[:n_s], refs[n_s : 2 * n_s], refs[2 * n_s : 3 * n_s]
    part_ref, cut_buf = refs[3 * n_s :]
    d_s = part_ref.shape[1]
    tokens = hidden_ref.shape[0]
    patch_dev = tokens // frames
    total = n_s * patch_dev
    step = min(total, 256)
    grads = [x[...] for x in grads]
    grad_b_q = grad_b_v = None
    codes = [x[3 * d_s :] for x in packed]
    for f in range(frames):
        keys = qkv_ref[1, f].astype(F32)
        vals = qkv_ref[2, f].astype(F32)
        grad = frame_rows(grads, f, patch_dev).astype(F32)
        d_query, d_vals = [], []
        for h in range(d_s // HEAD_DIM):
            k_h = rows_of(keys, h).astype(BF16)
            v_h = rows_of(vals, h).astype(BF16)
            g_h = rows_of(grad, h).astype(BF16)
            dq_parts, dv_sum = [], None
            for s in range(0, total, step):
                probs = probs_ref[f, h, :, s : s + step]
                dq, dv = head_backward(probs, k_h, v_h, g_h[:, s : s + step])
                dq_parts.append(dq)
                dv_sum = dv if dv_sum is None else dv_sum + dv
            d_query.append(
                dq_parts[0] if len(dq_parts) == 1 else jnp.concatenate(dq_parts, axis=1)
            )
            d_vals.append(dv_sum)
        d_query = jnp.concatenate(d_query, axis=0).astype(BF16)
        d_vals = jnp.concatenate(d_vals, axis=0).astype(BF16)
        partial = jnp.concatenate([mm(b_here_ref[0], d_query), mm(b_here_ref[1], d_vals)], axis=0)
        for k in range(n_s):
            place = slice(f * patch_dev, (f + 1) * patch_dev)
            sends[k][:, place] = partial[:, k * patch_dev : (k + 1) * patch_dev].astype(BF16)
        frame_codes = frame_rows(codes, f, patch_dev)
        term_q = mm(frame_codes[:RANK], d_query, NT)
        term_v = mm(frame_codes[RANK:], d_vals, NT)
        grad_b_q = term_q if grad_b_q is None else grad_b_q + term_q
        grad_b_v = term_v if grad_b_v is None else grad_b_v + term_v
    part_ref[:RANK] = grad_b_q
    part_ref[RANK:] = grad_b_v
    grad_a = mm(dcodes_ref[...], hidden_ref[...])
    for j in range(n_s):
        here = slice(j * d_s, (j + 1) * d_s)
        cut_buf[j, :, :d_s] = grad_a[:, here].astype(BF16)
        cut_buf[j, :, d_s:] = grad_b_ref[:, here].astype(BF16)
    for k in range(n_s):
        sends[k][:, tokens:] = cut_buf[peer("space", k)]


def add_up(terms):
    result = None
    for term in terms:
        result = term if result is None else result + term
    return result


def merge_kernel(n_s, n_d, part_ref, patches_ref, *refs):
    recvs, sends, buf = refs[:n_s], refs[n_s : n_s + n_d], refs[n_s + n_d]
    d_s = part_ref.shape[1]
    tokens = recvs[0].shape[1] - 2 * d_s
    codes = add_up([recv[:, :tokens].astype(F32) for recv in recvs]).astype(BF16)
    full = mm(codes, patches_ref[0].reshape(tokens, n_s * d_s))
    time_a = add_up([recv[:, tokens : tokens + d_s].astype(F32) for recv in recvs])
    time_b = add_up([recv[:, tokens + d_s :].astype(F32) for recv in recvs])
    split = jnp.concatenate([time_a, part_ref[...], time_b], axis=0)
    per, per_full = split.shape[0] // n_d, full.shape[0] // n_d
    for d in range(n_d):
        mine = [split[d * per : (d + 1) * per]]
        rows = full[d * per_full : (d + 1) * per_full]
        mine += [rows[:, j * d_s : (j + 1) * d_s] for j in range(n_s)]
        mine = jnp.concatenate(mine, axis=0)
        half = mine.shape[0] // 2
        buf[d] = jnp.concatenate([mine[:half], mine[half:]], axis=1).astype(BF16)
    for k in range(n_d):
        sends[k][...] = buf[peer("dp", k)]


def total_kernel(*refs):
    terms = [ref[...].astype(F32) for ref in refs[:-1]]
    while len(terms) > 1:
        terms = [terms[i] + terms[i + 1] for i in range(0, len(terms), 2)]
    refs[-1][...] = terms[0].astype(refs[-1].dtype)


def join_kernel(n_full, *refs):
    pieces, (out_ref, buf) = refs[:-2], refs[-2:]
    n_s, d_s = len(pieces), buf.shape[2] // 2
    for k, piece in enumerate(pieces):
        buf[peer("space", k)] = piece[...]
    rows = [
        jnp.concatenate([buf[j, :, :d_s], buf[j, :, d_s:]], axis=0).astype(F32) for j in range(n_s)
    ]
    n_split = rows[0].shape[0] - n_s * n_full
    out_ref[n_full:] = jnp.concatenate([x[:n_split] for x in rows], axis=1).astype(BF16)
    full = add_up([x[n_split:] for x in rows])
    cuts = [full[j * n_full : (j + 1) * n_full] for j in range(n_s)]
    out_ref[:n_full] = jnp.concatenate(cuts, axis=1).astype(BF16)


def final_kernel(factor, n_d, n_full, *refs):
    pieces, (a_ref, b_ref, buf) = refs[:n_d], refs[n_d:]
    for k, piece in enumerate(pieces):
        buf[peer("dp", k)] = piece[...]
    n_split = pieces[0].shape[0] - n_full
    size = math.gcd(n_full, n_split, RANK)
    for d in range(n_d):
        rows = buf[d].astype(F32) * factor
        for r in range(0, n_full + n_split, size):
            row = d * n_full + r if r < n_full else 2 * RANK + d * n_split + r - n_full
            target = a_ref if row < 4 * RANK else b_ref
            row %= 4 * RANK
            target[row // RANK, row % RANK : row % RANK + size] = rows[r : r + size]


def mixed_kernel(frames, hidden_ref, *refs):
    pieces, (mixed_ref, buf) = refs[:-2], refs[-2:]
    n_t = len(pieces)
    tokens, width = hidden_ref.shape
    patch_dev = tokens // frames
    sub = patch_dev // n_t
    for k, piece in enumerate(pieces):
        for f in range(frames):
            start = pl.multiple_of(f * patch_dev + peer("tm", k) * sub, sub)
            buf[pl.ds(start, sub)] = piece[f * sub : (f + 1) * sub]
    total = hidden_ref[...].astype(F32) + buf[...].astype(F32)
    mixed_ref[0] = total.astype(BF16).reshape(frames, patch_dev, width)


def hops(arrays, axis, first):
    size = lax.axis_size(axis)
    return [
        lax.ppermute(array, axis, [(i, i ^ k) for i in range(size)])
        for k, array in enumerate(arrays, first)
    ]


def exchange(pieces, axis):
    return [pieces[0]] + hops(pieces[1:], axis, 1)


def share(array, axis):
    return exchange([array] * lax.axis_size(axis), axis)


def per_device(
    patches, query_s, key_s, value_s, query_t, key_t, value_t, adapters_a, adapters_b, cotangent
):
    _, frames, patch_dev, width = patches.shape
    n_d, n_t, n_s = (lax.axis_size(name) for name in ("dp", "tm", "space"))
    tokens = frames * patch_dev
    sub = patch_dev // n_t
    d_s = width // n_s
    total = n_s * patch_dev
    factor = (tokens * n_d * n_t * n_s) ** (-0.5)
    here = lax.axis_index("space") * d_s
    downs = jnp.swapaxes(adapters_a, 1, 2)
    ups_here = lax.dynamic_slice_in_dim(adapters_b, here, d_s, 2)
    dma = pltpu.SemaphoreType.DMA

    time_arrays = [far(x) for x in (query_t, key_t, value_t, cotangent)]
    space_arrays = [
        far(x) for x in (patches, downs, adapters_b, query_s, value_s, key_s)
    ]
    packed = call(
        functools.partial(pack_kernel, n_s, n_t, sub),
        [shape((3 * d_s + 2 * RANK, tokens), BF16)] * n_s
        + [shape((4, frames * sub, width), BF16)] * (n_t - 1),
        *space_arrays, *time_arrays,
        scratch=[pltpu.VMEM(x.shape, BF16) for x in space_arrays]
        + [
            pltpu.VMEM((4,) + query_t.shape, BF16),
            pltpu.VMEM((3, n_s, d_s, tokens), BF16),
            dma((6,)),
            dma((4,)),
        ],
        hbm=True,
    )
    time_pieces = hops(packed[n_s:], "tm", 1)
    packed = exchange(packed[:n_s], "space")
    probs_dims = (frames, d_s // HEAD_DIM, total, total)
    qkv, probs, *out_s = call(
        functools.partial(space_forward_kernel, frames, n_s),
        [shape((3, frames, d_s, total), BF16), pltpu.HBM(probs_dims, F32)]
        + [shape((d_s, tokens), BF16)] * n_s,
        *packed,
        scratch=[pltpu.VMEM(probs_dims, F32), dma((probs_dims[0] * probs_dims[1],))],
        after=time_pieces[:1],
    )
    out_s = exchange(out_s, "space")
    hidden, *codes = call(
        functools.partial(hidden_kernel, n_t, n_s),
        [shape((tokens, width), BF16)] + [shape((8, 128), F32)] * n_t,
        *out_s, patches, downs,
        scratch=[pltpu.VMEM((n_s, d_s, tokens), BF16), pltpu.VMEM((tokens, 128), F32)],
    )
    codes = exchange(codes, "tm")
    turned = call(
        functools.partial(turn_kernel, frames, sub),
        shape((4, width, n_t * frames * sub), BF16),
        *time_arrays, *time_pieces,
        scratch=[
            pltpu.VMEM((4, frames * sub, width), BF16),
            pltpu.VMEM((n_t - 1, 4, frames * sub, width), BF16),
            dma((4 * frames,)),
            dma((n_t - 1,)),
        ],
        hbm=True,
    )
    timed = call(
        functools.partial(time_kernel, n_t, sub),
        [shape((frames * sub, width), BF16)] * n_t
        + [shape((8, 128), F32)] * n_t
        + [shape((2 * RANK, width), F32)],
        turned, adapters_b, *codes,
    )
    out_t, dcodes, time_grad_b = timed[:n_t], timed[n_t : 2 * n_t], timed[2 * n_t]
    dcodes = exchange(dcodes, "tm")
    out_t[1:3] = hops(out_t[1:3], "tm", 1)
    dcodes, *grads = call(
        functools.partial(hidden_grad_kernel, frames, n_s, sub),
        [shape((2 * RANK, tokens), BF16)] + [shape((d_s, tokens), BF16)] * n_s,
        cotangent, downs, *dcodes,
        scratch=[pltpu.VMEM((tokens, 128), F32), pltpu.VMEM((n_s, d_s, tokens), BF16)],
    )
    grads = exchange(grads, "space")
    backward = call(
        functools.partial(space_backward_kernel, frames, n_s),
        [shape((2 * RANK, tokens + 2 * d_s), BF16)] * n_s + [shape((2 * RANK, d_s), F32)],
        qkv, probs, hidden, time_grad_b, dcodes, ups_here, *packed, *grads,
        scratch=[pltpu.VMEM((n_s, 2 * RANK, 2 * d_s), BF16)],
        carry=out_t[3:],
    )
    partial, part = backward[:n_s], backward[n_s]
    partial = exchange(partial, "space")
    out_t[3:] = hops(backward[n_s + 1 :], "tm", 3)
    n_full, n_split = 2 * RANK // n_d, 6 * RANK // n_d
    dims = ((n_s * n_full + n_split) // 2, 2 * d_s)
    sums = call(
        functools.partial(merge_kernel, n_s, n_d),
        [shape(dims, BF16)] * n_d,
        part, patches, *partial,
        scratch=[pltpu.VMEM((n_d,) + dims, BF16)],
        after=out_t[1:3],
    )
    sums = call(total_kernel, shape(dims, BF16), *exchange(sums, "dp"), after=out_t[3:])
    sums = call(total_kernel, shape(dims, BF16), *share(sums, "tm"))
    sums = call(
        functools.partial(join_kernel, n_full),
        shape((n_full + n_split, width), BF16),
        *share(sums, "space"),
        scratch=[pltpu.VMEM((n_s,) + dims, BF16)],
    )
    grads_a, grads_b = call(
        functools.partial(final_kernel, factor, n_d, n_full),
        [shape((4, RANK, width), F32)] * 2,
        *share(sums, "dp"),
        scratch=[pltpu.VMEM((n_d, n_full + n_split, width), BF16)],
    )
    mixed = call(
        functools.partial(mixed_kernel, frames),
        shape(patches.shape, BF16),
        hidden, *out_t,
        scratch=[pltpu.VMEM((tokens, width), BF16)],
    )
    return (mixed, jnp.swapaxes(grads_a, 1, 2), grads_b)


def solution(mesh):
    token = P("dp", "tm", "space", None)
    return jax.shard_map(
        per_device,
        mesh=mesh,
        in_specs=(token,) * 7 + (P(), P(), token),
        out_specs=(token, P(), P()),
        check_vma=False,
    )
```

```python
import functools
import math

import jax
import jax.numpy as jnp
from jax import lax
from jax.experimental import pallas as pl
from jax.experimental.pallas import tpu as pltpu
from jax.sharding import PartitionSpec as P

HEAD_DIM = 72
RANK = 16
SCALE = HEAD_DIM ** (-0.5)
F32 = jnp.float32
BF16 = jnp.bfloat16
NN = (((1,), (0,)), ((), ()))
NT = (((1,), (1,)), ((), ()))
TN = (((0,), (0,)), ((), ()))


def mm(a, b, dims=NN):
    return lax.dot_general(a, b, dims, preferred_element_type=F32)


def far(x):
    return pltpu.with_memory_space_constraint(x, pltpu.HBM)


def call(kernel, out_shape, *args, scratch=(), hbm=False, limit=48, after=(), carry=()):
    vmem = pl.BlockSpec(memory_space=pltpu.VMEM)
    anywhere = pl.BlockSpec(memory_space=pl.ANY)
    main = anywhere if hbm else vmem
    single = not isinstance(out_shape, (tuple, list))
    outs = (out_shape,) if single else tuple(out_shape)
    used, extra = len(args), len(after) + len(carry)

    def body(*refs):
        inside = refs[:used] + refs[used + extra : used + extra + len(outs)]
        kernel(*inside, *refs[used + extra + len(outs) + len(carry) :])

    result = pl.pallas_call(
        body,
        out_shape=outs + tuple(shape(x.shape, x.dtype) for x in carry),
        in_specs=[main] * used + [anywhere] * extra,
        out_specs=tuple(vmem if isinstance(o, jax.ShapeDtypeStruct) else anywhere for o in outs)
        + (anywhere,) * len(carry),
        scratch_shapes=list(scratch),
        input_output_aliases={used + len(after) + i: len(outs) + i for i in range(len(carry))},
        compiler_params=pltpu.CompilerParams(vmem_limit_bytes=limit * 1024 * 1024),
    )(*args, *after, *carry)
    return result[0] if single and not carry else list(result)


def shape(dims, dtype):
    return jax.ShapeDtypeStruct(tuple(dims), dtype)


def probs_of(keys, q_t, mask):
    scores = mm(keys, q_t) * SCALE
    if mask is not None:
        scores = jnp.where(mask, scores, -1e30)
    peak = jnp.max(scores, axis=0, keepdims=True)
    weights = jnp.exp(scores - peak)
    return weights * (1.0 / jnp.sum(weights, axis=0, keepdims=True))


def head_backward(probs, k_t, v_t, g_t):
    low = probs.astype(BF16)
    dvals = mm(g_t, low, NT)
    dprob = mm(v_t.T, g_t)
    inner = jnp.sum(probs * dprob, axis=0, keepdims=True)
    dscore = (probs * (dprob - inner) * SCALE).astype(BF16)
    dquery = mm(k_t, dscore)
    return dquery, dvals


def rows_of(array, head):
    return array[head * HEAD_DIM : (head + 1) * HEAD_DIM]


def peer(axis, distance):
    return lax.axis_index(axis) ^ distance


def load_all(refs, buffers, sems):
    copies = [
        pltpu.make_async_copy(ref, buffer, sems.at[index])
        for index, (ref, buffer) in enumerate(zip(refs, buffers))
    ]
    for copy in copies:
        copy.start()
    return copies


def pack_kernel(n_s, n_t, sub, *refs):
    ins, time_ins, refs = refs[:6], refs[6:10], refs[10:]
    outs, here_ref, refs = refs[:n_s], refs[n_s], refs[n_s + 1 :]
    time_outs, refs = refs[: n_t - 1], refs[n_t - 1 :]
    buffers, (time_buf, turned_ref, maps_ref, sems, time_sems) = refs[:6], refs[6:]
    p_buf, at_buf, b_buf, q_buf, v_buf, k_buf = buffers
    copies = load_all(ins, buffers, sems)
    time_copies = load_all(time_ins, [time_buf.at[index] for index in range(4)], time_sems)
    d_s, tokens = turned_ref.shape[2:]
    frames = time_buf.shape[2]

    def flat(ref):
        return ref[0].reshape(tokens, ref.shape[3])

    def send(array, index):
        turned = array.T
        for j in range(n_s):
            turned_ref[index, j] = turned[j * d_s : (j + 1) * d_s]
        for k in range(n_s):
            outs[k][index * d_s : (index + 1) * d_s] = turned_ref[index, peer("space", k)]

    copies[0].wait()
    copies[1].wait()
    copies[2].wait()
    patches = flat(p_buf)
    codes_q = mm(patches, at_buf[0], NT).astype(BF16)
    codes_v = mm(patches, at_buf[1], NT).astype(BF16)
    codes_t = jnp.concatenate([codes_q, codes_v], axis=1).T
    maps = jnp.concatenate([b_buf[0], b_buf[1]], axis=0).T
    for j in range(n_s):
        maps_ref[j] = maps[j * d_s : (j + 1) * d_s]
    here_ref[...] = maps_ref[peer("space", 0)]
    copies[3].wait()
    query = (flat(q_buf).astype(F32) + mm(codes_q, b_buf[0])).astype(BF16)
    send(query, 0)
    copies[4].wait()
    value = (flat(v_buf).astype(F32) + mm(codes_v, b_buf[1])).astype(BF16)
    send(value, 2)
    copies[5].wait()
    send(flat(k_buf), 1)
    for k in range(n_s):
        outs[k][3 * d_s :] = codes_t
    for index, copy in enumerate(time_copies):
        copy.wait()
        for k in range(1, n_t):
            start = pl.multiple_of(peer("tm", k) * sub, sub)
            for f in range(frames):
                time_outs[k - 1][index, f * sub : (f + 1) * sub] = time_buf[
                    index, 0, f, pl.ds(start, sub)
                ]


def frame_rows(pieces, f, patch_dev):
    return jnp.concatenate([x[:, f * patch_dev : (f + 1) * patch_dev] for x in pieces], axis=1)


def space_forward_kernel(frames, n_s, *refs):
    packed, (qkv_ref, probs_ref, *outs) = refs[:n_s], refs[n_s : 2 * n_s + 2]
    probs_buf, sems = refs[2 * n_s + 2 :]
    copies = []
    d_s, tokens = outs[0].shape
    patch_dev = tokens // frames
    total = n_s * patch_dev
    step = min(total, 256)
    for index in range(3):
        pieces = [x[index * d_s : (index + 1) * d_s] for x in packed]
        for f in range(frames):
            qkv_ref[index, f] = frame_rows(pieces, f, patch_dev)
    for f in range(frames):
        query = qkv_ref[0, f].astype(F32)
        keys = qkv_ref[1, f].astype(F32)
        vals = qkv_ref[2, f].astype(F32)
        heads = []
        for h in range(d_s // HEAD_DIM):
            k_h = rows_of(keys, h).astype(BF16)
            v_h = rows_of(vals, h).astype(BF16)
            q_h = rows_of(query, h).astype(BF16)
            parts = []
            for s in range(0, total, step):
                probs = probs_of(k_h.T, q_h[:, s : s + step], None)
                probs_buf[f, h, :, s : s + step] = probs
                parts.append(mm(v_h, probs.astype(BF16)))
            heads.append(parts[0] if len(parts) == 1 else jnp.concatenate(parts, axis=1))
            copy = pltpu.make_async_copy(
                probs_buf.at[f, h], probs_ref.at[f, h], sems.at[len(copies)]
            )
            copy.start()
            copies.append(copy)
        out = jnp.concatenate(heads, axis=0).astype(BF16)
        for k in range(n_s):
            outs[k][:, f * patch_dev : (f + 1) * patch_dev] = out[
                :, k * patch_dev : (k + 1) * patch_dev
            ]
    for copy in copies:
        copy.wait()


def lane_block(rows):
    return lax.broadcasted_iota(jnp.int32, (rows, 128), 1) // (2 * RANK)


def fold(token_rows):
    block = lane_block(8)
    result = token_rows[0:8]
    for k in range(1, 4):
        result = jnp.where(block == k, token_rows[8 * k : 8 * k + 8], result)
    return result


def unfold(folded):
    pieces = [folded]
    for k in range(1, 4):
        pieces.append(pltpu.roll(folded, 128 - 2 * RANK * k, 1))
    return jnp.concatenate(pieces, axis=0)


def hidden_kernel(n_t, n_s, *refs):
    pieces, refs = refs[:n_s], refs[n_s:]
    p_ref, at_ref, hidden_ref = refs[:3]
    sends = refs[3 : 3 + n_t]
    out_buf, codes_buf = refs[3 + n_t :]
    _, frames, patch_dev, width = p_ref.shape
    tokens = frames * patch_dev
    sub = patch_dev // n_t
    for k in range(n_s):
        out_buf[peer("space", k)] = pieces[k][...]
    out = out_buf[...].reshape(width, tokens).T
    hidden = (p_ref[0].reshape(tokens, width).astype(F32) + out.astype(F32)).astype(BF16)
    hidden_ref[...] = hidden
    downs = jnp.concatenate([at_ref[2], at_ref[3]] * 4, axis=0)
    codes_buf[...] = mm(hidden, downs, NT).astype(BF16).astype(F32)
    for k in range(n_t):
        rows = [
            codes_buf[pl.ds(pl.multiple_of(f * patch_dev + peer("tm", k) * sub, sub), sub)]
            for f in range(frames)
        ]
        sends[k][...] = fold(jnp.concatenate(rows, axis=0))


def turn_kernel(frames, sub, q_ref, k_ref, v_ref, g_ref, *refs):
    *pieces, out_ref, own_buf, piece_buf, own_sems, sems = refs
    own = []
    start = pl.multiple_of(peer("tm", 0) * sub, sub)
    for index, ref in enumerate((q_ref, k_ref, v_ref, g_ref)):
        for f in range(frames):
            copy = pltpu.make_async_copy(
                ref.at[0, f, pl.ds(start, sub)],
                own_buf.at[index, f * sub : (f + 1) * sub],
                own_sems.at[index * frames + f],
            )
            copy.start()
            own.append(copy)
    copies = load_all(pieces, [piece_buf.at[k] for k in range(len(pieces))], sems)
    for copy in own + copies:
        copy.wait()
    for index in range(4):
        parts = [own_buf[index]] + [piece_buf[k, index] for k in range(len(pieces))]
        out_ref[index] = jnp.concatenate(parts, axis=0).T


def time_kernel(n_t, sub, x_ref, b_ref, *refs):
    codes_refs, refs = refs[:n_t], refs[n_t:]
    outs, sends, grad_b_ref = refs[:n_t], refs[n_t : 2 * n_t], refs[2 * n_t]
    _, width, tokens = x_ref.shape
    codes = jnp.concatenate([unfold(ref[...]) for ref in codes_refs], axis=0).T
    codes_q = codes[:RANK].astype(BF16)
    codes_v = codes[RANK : 2 * RANK].astype(BF16)
    query = (x_ref[0].astype(F32) + mm(b_ref[2], codes_q, TN)).astype(BF16).astype(F32)
    vals = (x_ref[2].astype(F32) + mm(b_ref[3], codes_v, TN)).astype(BF16).astype(F32)
    keys = x_ref[1].astype(F32)
    grad = x_ref[3].astype(F32)
    row = lax.broadcasted_iota(jnp.int32, (tokens, 2 * tokens), 0)
    col = lax.broadcasted_iota(jnp.int32, (tokens, 2 * tokens), 1)
    mask = lax.rem(row, sub) == lax.rem(col, sub)
    top = lax.broadcasted_iota(jnp.int32, (2 * HEAD_DIM, tokens), 0) < HEAD_DIM

    def spread(pair):
        return jnp.concatenate(
            [jnp.where(top, pair, 0.0), jnp.where(top, 0.0, pair)], axis=1
        ).astype(BF16)

    def pick(wide):
        return jnp.concatenate([wide[:HEAD_DIM, :tokens], wide[HEAD_DIM:, tokens:]], axis=0)

    outs_h, d_query, d_vals = [], [], []
    for h in range(0, width, 2 * HEAD_DIM):
        pair = slice(h, h + 2 * HEAD_DIM)
        k_h, v_h = keys[pair].astype(BF16), vals[pair].astype(BF16)
        g_h = spread(grad[pair])
        probs = probs_of(k_h.T, spread(query[pair]), mask)
        low = probs.astype(BF16)
        dprob = mm(v_h.T, g_h)
        inner = jnp.sum(probs * dprob, axis=0, keepdims=True)
        dscore = (probs * (dprob - inner) * SCALE).astype(BF16)
        outs_h.append(pick(mm(v_h, low)))
        d_vals.append(mm(g_h, low, NT))
        d_query.append(pick(mm(k_h, dscore)))
    d_query = jnp.concatenate(d_query, axis=0).astype(BF16)
    d_vals = jnp.concatenate(d_vals, axis=0).astype(BF16)
    d_codes = jnp.concatenate([mm(b_ref[2], d_query), mm(b_ref[3], d_vals)] * 4, axis=0)
    d_codes = d_codes.astype(BF16).astype(F32).T
    per = tokens // n_t
    for k in range(n_t):
        sends[k][...] = fold(d_codes[k * per : (k + 1) * per])
    out = jnp.concatenate(outs_h, axis=0).astype(BF16).T
    for k in range(n_t):
        outs[k][...] = out[k * per : (k + 1) * per]
    grad_b_ref[:RANK] = mm(codes_q, d_query, NT)
    grad_b_ref[RANK:] = mm(codes_v, d_vals, NT)


def hidden_grad_kernel(frames, n_s, sub, g_ref, at_ref, *refs):
    *pieces, codes_ref = refs[: -n_s - 2]
    outs, (buf, turned_ref) = refs[-n_s - 2 : -2], refs[-2:]
    patch_dev = sub * len(pieces)
    _, d_s, tokens = turned_ref.shape
    for k, piece in enumerate(pieces):
        rows = unfold(piece[...])
        for f in range(frames):
            start = pl.multiple_of(f * patch_dev + peer("tm", k) * sub, sub)
            buf[pl.ds(start, sub)] = rows[f * sub : (f + 1) * sub]
    codes = buf[:, : 2 * RANK].astype(BF16)
    codes_ref[...] = buf[...].T[: 2 * RANK].astype(BF16)
    downs = jnp.concatenate([at_ref[2], at_ref[3]], axis=0)
    grad = g_ref[0].reshape(tokens, n_s * d_s).astype(F32) + mm(codes, downs)
    turned = grad.astype(BF16).T
    for j in range(n_s):
        turned_ref[j] = turned[j * d_s : (j + 1) * d_s]
    for k in range(n_s):
        outs[k][...] = turned_ref[peer("space", k)]


def space_backward_kernel(frames, n_s, qkv_ref, probs_ref, hidden_ref, grad_b_ref, dcodes_ref, here_ref, *refs):
    packed, grads, sends = refs[:n_s], refs[n_s : 2 * n_s], refs[2 * n_s : 3 * n_s]
    part_ref, cut_buf = refs[3 * n_s :]
    d_s = part_ref.shape[1]
    tokens = hidden_ref.shape[0]
    patch_dev = tokens // frames
    total = n_s * patch_dev
    step = min(total, 256)
    b_here = here_ref[...].T
    grads = [x[...] for x in grads]
    grad_b_q = grad_b_v = None
    codes = [x[3 * d_s :] for x in packed]
    for f in range(frames):
        keys = qkv_ref[1, f].astype(F32)
        vals = qkv_ref[2, f].astype(F32)
        grad = frame_rows(grads, f, patch_dev).astype(F32)
        d_query, d_vals = [], []
        for h in range(d_s // HEAD_DIM):
            k_h = rows_of(keys, h).astype(BF16)
            v_h = rows_of(vals, h).astype(BF16)
            g_h = rows_of(grad, h).astype(BF16)
            dq_parts, dv_sum = [], None
            for s in range(0, total, step):
                probs = probs_ref[f, h, :, s : s + step]
                dq, dv = head_backward(probs, k_h, v_h, g_h[:, s : s + step])
                dq_parts.append(dq)
                dv_sum = dv if dv_sum is None else dv_sum + dv
            d_query.append(
                dq_parts[0] if len(dq_parts) == 1 else jnp.concatenate(dq_parts, axis=1)
            )
            d_vals.append(dv_sum)
        d_query = jnp.concatenate(d_query, axis=0).astype(BF16)
        d_vals = jnp.concatenate(d_vals, axis=0).astype(BF16)
        partial = jnp.concatenate([mm(b_here[:RANK], d_query), mm(b_here[RANK:], d_vals)], axis=0)
        for k in range(n_s):
            place = slice(f * patch_dev, (f + 1) * patch_dev)
            sends[k][:, place] = partial[:, k * patch_dev : (k + 1) * patch_dev].astype(BF16)
        frame_codes = frame_rows(codes, f, patch_dev)
        term_q = mm(frame_codes[:RANK], d_query, NT)
        term_v = mm(frame_codes[RANK:], d_vals, NT)
        grad_b_q = term_q if grad_b_q is None else grad_b_q + term_q
        grad_b_v = term_v if grad_b_v is None else grad_b_v + term_v
    part_ref[:RANK] = grad_b_q
    part_ref[RANK:] = grad_b_v
    grad_a = mm(dcodes_ref[...], hidden_ref[...])
    for j in range(n_s):
        here = slice(j * d_s, (j + 1) * d_s)
        cut_buf[j, :, :d_s] = grad_a[:, here].astype(BF16)
        cut_buf[j, :, d_s:] = grad_b_ref[:, here].astype(BF16)
    for k in range(n_s):
        sends[k][:, tokens:] = cut_buf[peer("space", k)]


def add_up(terms):
    result = None
    for term in terms:
        result = term if result is None else result + term
    return result


def merge_kernel(n_s, n_d, part_ref, patches_ref, *refs):
    recvs, sends, buf = refs[:n_s], refs[n_s : n_s + n_d], refs[n_s + n_d]
    d_s = part_ref.shape[1]
    tokens = recvs[0].shape[1] - 2 * d_s
    codes = add_up([recv[:, :tokens].astype(F32) for recv in recvs]).astype(BF16)
    full = mm(codes, patches_ref[0].reshape(tokens, n_s * d_s))
    time_a = add_up([recv[:, tokens : tokens + d_s].astype(F32) for recv in recvs])
    time_b = add_up([recv[:, tokens + d_s :].astype(F32) for recv in recvs])
    split = jnp.concatenate([time_a, part_ref[...], time_b], axis=0)
    per, per_full = split.shape[0] // n_d, full.shape[0] // n_d
    for d in range(n_d):
        mine = [split[d * per : (d + 1) * per]]
        rows = full[d * per_full : (d + 1) * per_full]
        mine += [rows[:, j * d_s : (j + 1) * d_s] for j in range(n_s)]
        mine = jnp.concatenate(mine, axis=0)
        half = mine.shape[0] // 2
        buf[d] = jnp.concatenate([mine[:half], mine[half:]], axis=1).astype(BF16)
    for k in range(n_d):
        sends[k][...] = buf[peer("dp", k)]


def total_kernel(*refs):
    terms = [ref[...].astype(F32) for ref in refs[:-1]]
    while len(terms) > 1:
        terms = [terms[i] + terms[i + 1] for i in range(0, len(terms), 2)]
    refs[-1][...] = terms[0].astype(refs[-1].dtype)


def join_kernel(n_full, *refs):
    pieces, (out_ref, buf) = refs[:-2], refs[-2:]
    n_s, d_s = len(pieces), buf.shape[2] // 2
    for k, piece in enumerate(pieces):
        buf[peer("space", k)] = piece[...]
    rows = [
        jnp.concatenate([buf[j, :, :d_s], buf[j, :, d_s:]], axis=0).astype(F32) for j in range(n_s)
    ]
    n_split = rows[0].shape[0] - n_s * n_full
    out_ref[n_full:] = jnp.concatenate([x[:n_split] for x in rows], axis=1).astype(BF16)
    full = add_up([x[n_split:] for x in rows])
    cuts = [full[j * n_full : (j + 1) * n_full] for j in range(n_s)]
    out_ref[:n_full] = jnp.concatenate(cuts, axis=1).astype(BF16)


def final_kernel(factor, n_d, n_full, *refs):
    pieces, (a_ref, b_ref, buf) = refs[:n_d], refs[n_d:]
    for k, piece in enumerate(pieces):
        buf[peer("dp", k)] = piece[...]
    n_split = pieces[0].shape[0] - n_full
    size = math.gcd(n_full, n_split, RANK)
    for d in range(n_d):
        rows = buf[d].astype(F32) * factor
        for r in range(0, n_full + n_split, size):
            row = d * n_full + r if r < n_full else 2 * RANK + d * n_split + r - n_full
            target = a_ref if row < 4 * RANK else b_ref
            row %= 4 * RANK
            target[row // RANK, row % RANK : row % RANK + size] = rows[r : r + size]


def mixed_kernel(frames, hidden_ref, *refs):
    pieces, (mixed_ref, buf) = refs[:-2], refs[-2:]
    n_t = len(pieces)
    tokens, width = hidden_ref.shape
    patch_dev = tokens // frames
    sub = patch_dev // n_t
    for k, piece in enumerate(pieces):
        for f in range(frames):
            start = pl.multiple_of(f * patch_dev + peer("tm", k) * sub, sub)
            buf[pl.ds(start, sub)] = piece[f * sub : (f + 1) * sub]
    total = hidden_ref[...].astype(F32) + buf[...].astype(F32)
    mixed_ref[0] = total.astype(BF16).reshape(frames, patch_dev, width)


def hops(arrays, axis, first):
    size = lax.axis_size(axis)
    return [
        lax.ppermute(array, axis, [(i, i ^ k) for i in range(size)])
        for k, array in enumerate(arrays, first)
    ]


def exchange(pieces, axis):
    return [pieces[0]] + hops(pieces[1:], axis, 1)


def share(array, axis):
    return exchange([array] * lax.axis_size(axis), axis)


def per_device(
    patches, query_s, key_s, value_s, query_t, key_t, value_t, adapters_a, adapters_b, cotangent
):
    _, frames, patch_dev, width = patches.shape
    n_d, n_t, n_s = (lax.axis_size(name) for name in ("dp", "tm", "space"))
    tokens = frames * patch_dev
    sub = patch_dev // n_t
    d_s = width // n_s
    total = n_s * patch_dev
    factor = (tokens * n_d * n_t * n_s) ** (-0.5)
    downs = jnp.swapaxes(adapters_a, 1, 2)
    dma = pltpu.SemaphoreType.DMA

    time_arrays = [far(x) for x in (query_t, key_t, value_t, cotangent)]
    space_arrays = [
        far(x) for x in (patches, downs, adapters_b, query_s, value_s, key_s)
    ]
    packed = call(
        functools.partial(pack_kernel, n_s, n_t, sub),
        [shape((3 * d_s + 2 * RANK, tokens), BF16)] * n_s
        + [shape((d_s, 2 * RANK), BF16)]
        + [shape((4, frames * sub, width), BF16)] * (n_t - 1),
        *space_arrays, *time_arrays,
        scratch=[pltpu.VMEM(x.shape, BF16) for x in space_arrays]
        + [
            pltpu.VMEM((4,) + query_t.shape, BF16),
            pltpu.VMEM((3, n_s, d_s, tokens), BF16),
            pltpu.VMEM((n_s, d_s, 2 * RANK), BF16),
            dma((6,)),
            dma((4,)),
        ],
        hbm=True,
    )
    here, time_pieces = packed[n_s], hops(packed[n_s + 1 :], "tm", 1)
    packed = exchange(packed[:n_s], "space")
    probs_dims = (frames, d_s // HEAD_DIM, total, total)
    qkv, probs, *out_s = call(
        functools.partial(space_forward_kernel, frames, n_s),
        [shape((3, frames, d_s, total), BF16), pltpu.HBM(probs_dims, F32)]
        + [shape((d_s, tokens), BF16)] * n_s,
        *packed,
        scratch=[pltpu.VMEM(probs_dims, F32), dma((probs_dims[0] * probs_dims[1],))],
        after=time_pieces[:1],
    )
    out_s = exchange(out_s, "space")
    hidden, *codes = call(
        functools.partial(hidden_kernel, n_t, n_s),
        [shape((tokens, width), BF16)] + [shape((8, 128), F32)] * n_t,
        *out_s, patches, downs,
        scratch=[pltpu.VMEM((n_s, d_s, tokens), BF16), pltpu.VMEM((tokens, 128), F32)],
    )
    codes = exchange(codes, "tm")
    turned = call(
        functools.partial(turn_kernel, frames, sub),
        shape((4, width, n_t * frames * sub), BF16),
        *time_arrays, *time_pieces,
        scratch=[
            pltpu.VMEM((4, frames * sub, width), BF16),
            pltpu.VMEM((n_t - 1, 4, frames * sub, width), BF16),
            dma((4 * frames,)),
            dma((n_t - 1,)),
        ],
        hbm=True,
    )
    timed = call(
        functools.partial(time_kernel, n_t, sub),
        [shape((frames * sub, width), BF16)] * n_t
        + [shape((8, 128), F32)] * n_t
        + [shape((2 * RANK, width), F32)],
        turned, adapters_b, *codes,
    )
    out_t, dcodes, time_grad_b = timed[:n_t], timed[n_t : 2 * n_t], timed[2 * n_t]
    dcodes = exchange(dcodes, "tm")
    out_t[1:3] = hops(out_t[1:3], "tm", 1)
    dcodes, *grads = call(
        functools.partial(hidden_grad_kernel, frames, n_s, sub),
        [shape((2 * RANK, tokens), BF16)] + [shape((d_s, tokens), BF16)] * n_s,
        cotangent, downs, *dcodes,
        scratch=[pltpu.VMEM((tokens, 128), F32), pltpu.VMEM((n_s, d_s, tokens), BF16)],
    )
    grads = exchange(grads, "space")
    backward = call(
        functools.partial(space_backward_kernel, frames, n_s),
        [shape((2 * RANK, tokens + 2 * d_s), BF16)] * n_s + [shape((2 * RANK, d_s), F32)],
        qkv, probs, hidden, time_grad_b, dcodes, here, *packed, *grads,
        scratch=[pltpu.VMEM((n_s, 2 * RANK, 2 * d_s), BF16)],
        carry=out_t[3:],
    )
    partial, part = backward[:n_s], backward[n_s]
    partial = exchange(partial, "space")
    out_t[3:] = hops(backward[n_s + 1 :], "tm", 3)
    n_full, n_split = 2 * RANK // n_d, 6 * RANK // n_d
    dims = ((n_s * n_full + n_split) // 2, 2 * d_s)
    sums = call(
        functools.partial(merge_kernel, n_s, n_d),
        [shape(dims, BF16)] * n_d,
        part, patches, *partial,
        scratch=[pltpu.VMEM((n_d,) + dims, BF16)],
        after=out_t[1:3],
    )
    sums = call(total_kernel, shape(dims, BF16), *exchange(sums, "dp"), after=out_t[3:])
    sums = call(total_kernel, shape(dims, BF16), *share(sums, "tm"))
    sums = call(
        functools.partial(join_kernel, n_full),
        shape((n_full + n_split, width), BF16),
        *share(sums, "space"),
        scratch=[pltpu.VMEM((n_s,) + dims, BF16)],
    )
    grads_a, grads_b = call(
        functools.partial(final_kernel, factor, n_d, n_full),
        [shape((4, RANK, width), F32)] * 2,
        *share(sums, "dp"),
        scratch=[pltpu.VMEM((n_d, n_full + n_split, width), BF16)],
    )
    mixed = call(
        functools.partial(mixed_kernel, frames),
        shape(patches.shape, BF16),
        hidden, *out_t,
        scratch=[pltpu.VMEM((tokens, width), BF16)],
    )
    return (mixed, jnp.swapaxes(grads_a, 1, 2), grads_b)


def solution(mesh):
    token = P("dp", "tm", "space", None)
    return jax.shard_map(
        per_device,
        mesh=mesh,
        in_specs=(token,) * 7 + (P(), P(), token),
        out_specs=(token, P(), P()),
        check_vma=False,
    )
```

```python
import functools
import math

import jax
import jax.numpy as jnp
from jax import lax
from jax.experimental import pallas as pl
from jax.experimental.pallas import tpu as pltpu
from jax.sharding import PartitionSpec as P

HEAD_DIM = 72
RANK = 16
SCALE = HEAD_DIM ** (-0.5)
F32 = jnp.float32
BF16 = jnp.bfloat16
NN = (((1,), (0,)), ((), ()))
NT = (((1,), (1,)), ((), ()))
TN = (((0,), (0,)), ((), ()))


def mm(a, b, dims=NN):
    return lax.dot_general(a, b, dims, preferred_element_type=F32)


def far(x):
    return pltpu.with_memory_space_constraint(x, pltpu.HBM)


def call(kernel, out_shape, *args, scratch=(), hbm=False, limit=48, after=(), carry=()):
    vmem = pl.BlockSpec(memory_space=pltpu.VMEM)
    anywhere = pl.BlockSpec(memory_space=pl.ANY)
    main = anywhere if hbm else vmem
    single = not isinstance(out_shape, (tuple, list))
    outs = (out_shape,) if single else tuple(out_shape)
    used, extra = len(args), len(after) + len(carry)

    def body(*refs):
        inside = refs[:used] + refs[used + extra : used + extra + len(outs)]
        kernel(*inside, *refs[used + extra + len(outs) + len(carry) :])

    result = pl.pallas_call(
        body,
        out_shape=outs + tuple(shape(x.shape, x.dtype) for x in carry),
        in_specs=[main] * used + [anywhere] * extra,
        out_specs=tuple(vmem if isinstance(o, jax.ShapeDtypeStruct) else anywhere for o in outs)
        + (anywhere,) * len(carry),
        scratch_shapes=list(scratch),
        input_output_aliases={used + len(after) + i: len(outs) + i for i in range(len(carry))},
        compiler_params=pltpu.CompilerParams(vmem_limit_bytes=limit * 1024 * 1024),
    )(*args, *after, *carry)
    return result[0] if single and not carry else list(result)


def shape(dims, dtype):
    return jax.ShapeDtypeStruct(tuple(dims), dtype)


def probs_of(keys, q_t, mask):
    scores = mm(keys, q_t) * SCALE
    if mask is not None:
        scores = jnp.where(mask, scores, -1e30)
    peak = jnp.max(scores, axis=0, keepdims=True)
    weights = jnp.exp(scores - peak)
    return weights * (1.0 / jnp.sum(weights, axis=0, keepdims=True))


def head_backward(probs, k_t, v_t, g_t):
    low = probs.astype(BF16)
    dvals = mm(g_t, low, NT)
    dprob = mm(v_t.T, g_t)
    inner = jnp.sum(probs * dprob, axis=0, keepdims=True)
    dscore = (probs * (dprob - inner) * SCALE).astype(BF16)
    dquery = mm(k_t, dscore)
    return dquery, dvals


def rows_of(array, head):
    return array[head * HEAD_DIM : (head + 1) * HEAD_DIM]


def peer(axis, distance):
    return lax.axis_index(axis) ^ distance


def load_all(refs, buffers, sems):
    copies = [
        pltpu.make_async_copy(ref, buffer, sems.at[index])
        for index, (ref, buffer) in enumerate(zip(refs, buffers))
    ]
    for copy in copies:
        copy.start()
    return copies


def pack_kernel(n_s, n_t, sub, *refs):
    ins, time_ins, refs = refs[:6], refs[6:10], refs[10:]
    outs, here_ref, refs = refs[:n_s], refs[n_s], refs[n_s + 1 :]
    time_outs, refs = refs[: n_t - 1], refs[n_t - 1 :]
    buffers, (time_buf, turned_ref, maps_ref, sems, time_sems) = refs[:6], refs[6:]
    p_buf, at_buf, b_buf, q_buf, v_buf, k_buf = buffers
    copies = load_all(ins, buffers, sems)
    time_copies = load_all(time_ins, [time_buf.at[index] for index in range(4)], time_sems)
    d_s, tokens = turned_ref.shape[2:]
    frames = time_buf.shape[2]

    def flat(ref):
        return ref[0].reshape(tokens, ref.shape[3])

    def send(array, index):
        turned = array.T
        for j in range(n_s):
            turned_ref[index, j] = turned[j * d_s : (j + 1) * d_s]
        for k in range(n_s):
            outs[k][index * d_s : (index + 1) * d_s] = turned_ref[index, peer("space", k)]

    copies[0].wait()
    copies[1].wait()
    copies[2].wait()
    patches = flat(p_buf)
    codes_q = mm(patches, at_buf[0], NT).astype(BF16)
    codes_v = mm(patches, at_buf[1], NT).astype(BF16)
    codes_t = jnp.concatenate([codes_q, codes_v], axis=1).T
    maps = jnp.concatenate([b_buf[0], b_buf[1]], axis=0).T
    for j in range(n_s):
        maps_ref[j] = maps[j * d_s : (j + 1) * d_s]
    here_ref[...] = maps_ref[peer("space", 0)]
    copies[3].wait()
    query = (flat(q_buf).astype(F32) + mm(codes_q, b_buf[0])).astype(BF16)
    send(query, 0)
    copies[4].wait()
    value = (flat(v_buf).astype(F32) + mm(codes_v, b_buf[1])).astype(BF16)
    send(value, 2)
    copies[5].wait()
    send(flat(k_buf), 1)
    for k in range(n_s):
        outs[k][3 * d_s :] = codes_t
    for index, copy in enumerate(time_copies):
        copy.wait()
        for k in range(1, n_t):
            start = pl.multiple_of(peer("tm", k) * sub, sub)
            for f in range(frames):
                time_outs[k - 1][index, f * sub : (f + 1) * sub] = time_buf[
                    index, 0, f, pl.ds(start, sub)
                ]


def frame_rows(pieces, f, patch_dev):
    return jnp.concatenate([x[:, f * patch_dev : (f + 1) * patch_dev] for x in pieces], axis=1)


def space_forward_kernel(frames, n_s, *refs):
    packed, (qkv_ref, probs_ref, *outs) = refs[:n_s], refs[n_s : 2 * n_s + 2]
    probs_buf, sems = refs[2 * n_s + 2 :]
    copies = []
    d_s, tokens = outs[0].shape
    patch_dev = tokens // frames
    total = n_s * patch_dev
    step = min(total, 256)
    for index in range(3):
        pieces = [x[index * d_s : (index + 1) * d_s] for x in packed]
        for f in range(frames):
            qkv_ref[index, f] = frame_rows(pieces, f, patch_dev)
    for f in range(frames):
        query = qkv_ref[0, f].astype(F32)
        keys = qkv_ref[1, f].astype(F32)
        vals = qkv_ref[2, f].astype(F32)
        heads = []
        for h in range(d_s // HEAD_DIM):
            k_h = rows_of(keys, h).astype(BF16)
            v_h = rows_of(vals, h).astype(BF16)
            q_h = rows_of(query, h).astype(BF16)
            parts = []
            for s in range(0, total, step):
                probs = probs_of(k_h.T, q_h[:, s : s + step], None)
                probs_buf[f, h, :, s : s + step] = probs
                parts.append(mm(v_h, probs.astype(BF16)))
            heads.append(parts[0] if len(parts) == 1 else jnp.concatenate(parts, axis=1))
            copy = pltpu.make_async_copy(
                probs_buf.at[f, h], probs_ref.at[f, h], sems.at[len(copies)]
            )
            copy.start()
            copies.append(copy)
        out = jnp.concatenate(heads, axis=0).astype(BF16)
        for k in range(n_s):
            outs[k][:, f * patch_dev : (f + 1) * patch_dev] = out[
                :, k * patch_dev : (k + 1) * patch_dev
            ]
    for copy in copies:
        copy.wait()


def lane_block(rows):
    return lax.broadcasted_iota(jnp.int32, (rows, 128), 1) // (2 * RANK)


def fold(token_rows):
    block = lane_block(8)
    result = token_rows[0:8]
    for k in range(1, 4):
        result = jnp.where(block == k, token_rows[8 * k : 8 * k + 8], result)
    return result


def unfold(folded):
    pieces = [folded]
    for k in range(1, 4):
        pieces.append(pltpu.roll(folded, 128 - 2 * RANK * k, 1))
    return jnp.concatenate(pieces, axis=0)


def hidden_kernel(n_t, n_s, *refs):
    pieces, refs = refs[:n_s][::-1], refs[n_s:]
    p_ref, at_ref, hidden_ref = refs[:3]
    sends = refs[3 : 3 + n_t]
    out_buf, codes_buf = refs[3 + n_t :]
    _, frames, patch_dev, width = p_ref.shape
    tokens = frames * patch_dev
    sub = patch_dev // n_t
    for k in range(n_s):
        out_buf[peer("space", k)] = pieces[k][...]
    out = out_buf[...].reshape(width, tokens).T
    hidden = (p_ref[0].reshape(tokens, width).astype(F32) + out.astype(F32)).astype(BF16)
    hidden_ref[...] = hidden
    downs = jnp.concatenate([at_ref[2], at_ref[3]] * 4, axis=0)
    codes_buf[...] = mm(hidden, downs, NT).astype(BF16).astype(F32)
    for k in range(n_t):
        rows = [
            codes_buf[pl.ds(pl.multiple_of(f * patch_dev + peer("tm", k) * sub, sub), sub)]
            for f in range(frames)
        ]
        sends[k][...] = fold(jnp.concatenate(rows, axis=0))


def turn_kernel(frames, sub, q_ref, k_ref, v_ref, g_ref, *refs):
    *pieces, out_ref, own_buf, piece_buf, own_sems, sems = refs
    own = []
    start = pl.multiple_of(peer("tm", 0) * sub, sub)
    for index, ref in enumerate((q_ref, k_ref, v_ref, g_ref)):
        for f in range(frames):
            copy = pltpu.make_async_copy(
                ref.at[0, f, pl.ds(start, sub)],
                own_buf.at[index, f * sub : (f + 1) * sub],
                own_sems.at[index * frames + f],
            )
            copy.start()
            own.append(copy)
    copies = load_all(pieces, [piece_buf.at[k] for k in range(len(pieces))], sems)
    for copy in own + copies:
        copy.wait()
    for index in range(4):
        parts = [own_buf[index]] + [piece_buf[k, index] for k in range(len(pieces))]
        out_ref[index] = jnp.concatenate(parts, axis=0).T


def time_kernel(n_t, sub, x_ref, b_ref, *refs):
    codes_refs, refs = refs[:n_t][::-1], refs[n_t:]
    outs, sends, grad_b_ref = refs[:n_t], refs[n_t : 2 * n_t], refs[2 * n_t]
    _, width, tokens = x_ref.shape
    codes = jnp.concatenate([unfold(ref[...]) for ref in codes_refs], axis=0).T
    codes_q = codes[:RANK].astype(BF16)
    codes_v = codes[RANK : 2 * RANK].astype(BF16)
    query = (x_ref[0].astype(F32) + mm(b_ref[2], codes_q, TN)).astype(BF16).astype(F32)
    vals = (x_ref[2].astype(F32) + mm(b_ref[3], codes_v, TN)).astype(BF16).astype(F32)
    keys = x_ref[1].astype(F32)
    grad = x_ref[3].astype(F32)
    row = lax.broadcasted_iota(jnp.int32, (tokens, 2 * tokens), 0)
    col = lax.broadcasted_iota(jnp.int32, (tokens, 2 * tokens), 1)
    mask = lax.rem(row, sub) == lax.rem(col, sub)
    top = lax.broadcasted_iota(jnp.int32, (2 * HEAD_DIM, tokens), 0) < HEAD_DIM

    def spread(pair):
        return jnp.concatenate(
            [jnp.where(top, pair, 0.0), jnp.where(top, 0.0, pair)], axis=1
        ).astype(BF16)

    def pick(wide):
        return jnp.concatenate([wide[:HEAD_DIM, :tokens], wide[HEAD_DIM:, tokens:]], axis=0)

    outs_h, d_query, d_vals = [], [], []
    for h in range(0, width, 2 * HEAD_DIM):
        pair = slice(h, h + 2 * HEAD_DIM)
        k_h, v_h = keys[pair].astype(BF16), vals[pair].astype(BF16)
        g_h = spread(grad[pair])
        probs = probs_of(k_h.T, spread(query[pair]), mask)
        low = probs.astype(BF16)
        dprob = mm(v_h.T, g_h)
        inner = jnp.sum(probs * dprob, axis=0, keepdims=True)
        dscore = (probs * (dprob - inner) * SCALE).astype(BF16)
        outs_h.append(pick(mm(v_h, low)))
        d_vals.append(mm(g_h, low, NT))
        d_query.append(pick(mm(k_h, dscore)))
    d_query = jnp.concatenate(d_query, axis=0).astype(BF16)
    d_vals = jnp.concatenate(d_vals, axis=0).astype(BF16)
    d_codes = jnp.concatenate([mm(b_ref[2], d_query), mm(b_ref[3], d_vals)] * 4, axis=0)
    d_codes = d_codes.astype(BF16).astype(F32).T
    per = tokens // n_t
    for k in range(n_t):
        sends[k][...] = fold(d_codes[k * per : (k + 1) * per])
    out = jnp.concatenate(outs_h, axis=0).astype(BF16).T
    for k in range(n_t):
        outs[k][...] = out[k * per : (k + 1) * per]
    grad_b_ref[:RANK] = mm(codes_q, d_query, NT)
    grad_b_ref[RANK:] = mm(codes_v, d_vals, NT)


def hidden_grad_kernel(frames, n_s, sub, g_ref, at_ref, *refs):
    *pieces, codes_ref = refs[: -n_s - 2]
    pieces = pieces[::-1]
    outs, (buf, turned_ref) = refs[-n_s - 2 : -2], refs[-2:]
    patch_dev = sub * len(pieces)
    _, d_s, tokens = turned_ref.shape
    for k, piece in enumerate(pieces):
        rows = unfold(piece[...])
        for f in range(frames):
            start = pl.multiple_of(f * patch_dev + peer("tm", k) * sub, sub)
            buf[pl.ds(start, sub)] = rows[f * sub : (f + 1) * sub]
    codes = buf[:, : 2 * RANK].astype(BF16)
    codes_ref[...] = buf[...].T[: 2 * RANK].astype(BF16)
    downs = jnp.concatenate([at_ref[2], at_ref[3]], axis=0)
    grad = g_ref[0].reshape(tokens, n_s * d_s).astype(F32) + mm(codes, downs)
    turned = grad.astype(BF16).T
    for j in range(n_s):
        turned_ref[j] = turned[j * d_s : (j + 1) * d_s]
    for k in range(n_s):
        outs[k][...] = turned_ref[peer("space", k)]


def space_backward_kernel(frames, n_s, qkv_ref, probs_ref, hidden_ref, grad_b_ref, dcodes_ref, here_ref, *refs):
    packed, grads, sends = refs[:n_s], refs[n_s : 2 * n_s][::-1], refs[2 * n_s : 3 * n_s]
    part_ref, cut_buf = refs[3 * n_s :]
    d_s = part_ref.shape[1]
    tokens = hidden_ref.shape[0]
    patch_dev = tokens // frames
    total = n_s * patch_dev
    step = min(total, 256)
    b_here = here_ref[...].T
    grads = [x[...] for x in grads]
    grad_b_q = grad_b_v = None
    codes = [x[3 * d_s :] for x in packed]
    for f in range(frames):
        keys = qkv_ref[1, f].astype(F32)
        vals = qkv_ref[2, f].astype(F32)
        grad = frame_rows(grads, f, patch_dev).astype(F32)
        d_query, d_vals = [], []
        for h in range(d_s // HEAD_DIM):
            k_h = rows_of(keys, h).astype(BF16)
            v_h = rows_of(vals, h).astype(BF16)
            g_h = rows_of(grad, h).astype(BF16)
            dq_parts, dv_sum = [], None
            for s in range(0, total, step):
                probs = probs_ref[f, h, :, s : s + step]
                dq, dv = head_backward(probs, k_h, v_h, g_h[:, s : s + step])
                dq_parts.append(dq)
                dv_sum = dv if dv_sum is None else dv_sum + dv
            d_query.append(
                dq_parts[0] if len(dq_parts) == 1 else jnp.concatenate(dq_parts, axis=1)
            )
            d_vals.append(dv_sum)
        d_query = jnp.concatenate(d_query, axis=0).astype(BF16)
        d_vals = jnp.concatenate(d_vals, axis=0).astype(BF16)
        partial = jnp.concatenate([mm(b_here[:RANK], d_query), mm(b_here[RANK:], d_vals)], axis=0)
        for k in range(n_s):
            place = slice(f * patch_dev, (f + 1) * patch_dev)
            sends[k][:, place] = partial[:, k * patch_dev : (k + 1) * patch_dev].astype(BF16)
        frame_codes = frame_rows(codes, f, patch_dev)
        term_q = mm(frame_codes[:RANK], d_query, NT)
        term_v = mm(frame_codes[RANK:], d_vals, NT)
        grad_b_q = term_q if grad_b_q is None else grad_b_q + term_q
        grad_b_v = term_v if grad_b_v is None else grad_b_v + term_v
    part_ref[:RANK] = grad_b_q
    part_ref[RANK:] = grad_b_v
    grad_a = mm(dcodes_ref[...], hidden_ref[...])
    for j in range(n_s):
        here = slice(j * d_s, (j + 1) * d_s)
        cut_buf[j, :, :d_s] = grad_a[:, here].astype(BF16)
        cut_buf[j, :, d_s:] = grad_b_ref[:, here].astype(BF16)
    for k in range(n_s):
        sends[k][:, tokens:] = cut_buf[peer("space", k)]


def add_up(terms):
    result = None
    for term in terms:
        result = term if result is None else result + term
    return result


def merge_kernel(n_s, n_d, part_ref, patches_ref, *refs):
    recvs, sends, buf = refs[:n_s][::-1], refs[n_s : n_s + n_d], refs[n_s + n_d]
    d_s = part_ref.shape[1]
    tokens = recvs[0].shape[1] - 2 * d_s
    codes = add_up([recv[:, :tokens].astype(F32) for recv in recvs]).astype(BF16)
    full = mm(codes, patches_ref[0].reshape(tokens, n_s * d_s))
    time_a = add_up([recv[:, tokens : tokens + d_s].astype(F32) for recv in recvs])
    time_b = add_up([recv[:, tokens + d_s :].astype(F32) for recv in recvs])
    split = jnp.concatenate([time_a, part_ref[...], time_b], axis=0)
    per, per_full = split.shape[0] // n_d, full.shape[0] // n_d
    for d in range(n_d):
        mine = [split[d * per : (d + 1) * per]]
        rows = full[d * per_full : (d + 1) * per_full]
        mine += [rows[:, j * d_s : (j + 1) * d_s] for j in range(n_s)]
        mine = jnp.concatenate(mine, axis=0)
        half = mine.shape[0] // 2
        buf[d] = jnp.concatenate([mine[:half], mine[half:]], axis=1).astype(BF16)
    for k in range(n_d):
        sends[k][...] = buf[peer("dp", k)]


def total_kernel(*refs):
    terms = [ref[...].astype(F32) for ref in refs[:-1]]
    while len(terms) > 1:
        terms = [terms[i] + terms[i + 1] for i in range(0, len(terms), 2)]
    refs[-1][...] = terms[0].astype(refs[-1].dtype)


def join_kernel(n_full, *refs):
    pieces, (out_ref, buf) = refs[:-2], refs[-2:]
    n_s, d_s = len(pieces), buf.shape[2] // 2
    for k, piece in enumerate(pieces):
        buf[peer("space", k)] = piece[...]
    rows = [
        jnp.concatenate([buf[j, :, :d_s], buf[j, :, d_s:]], axis=0).astype(F32) for j in range(n_s)
    ]
    n_split = rows[0].shape[0] - n_s * n_full
    out_ref[n_full:] = jnp.concatenate([x[:n_split] for x in rows], axis=1).astype(BF16)
    full = add_up([x[n_split:] for x in rows])
    cuts = [full[j * n_full : (j + 1) * n_full] for j in range(n_s)]
    out_ref[:n_full] = jnp.concatenate(cuts, axis=1).astype(BF16)


def final_kernel(factor, n_d, n_full, *refs):
    pieces, (a_ref, b_ref, buf) = refs[:n_d], refs[n_d:]
    for k, piece in enumerate(pieces):
        buf[peer("dp", k)] = piece[...]
    n_split = pieces[0].shape[0] - n_full
    size = math.gcd(n_full, n_split, RANK)
    for d in range(n_d):
        rows = buf[d].astype(F32) * factor
        for r in range(0, n_full + n_split, size):
            row = d * n_full + r if r < n_full else 2 * RANK + d * n_split + r - n_full
            target = a_ref if row < 4 * RANK else b_ref
            row %= 4 * RANK
            target[row // RANK, row % RANK : row % RANK + size] = rows[r : r + size]


def mixed_kernel(frames, hidden_ref, *refs):
    pieces, (mixed_ref, buf) = refs[:-2], refs[-2:]
    n_t = len(pieces)
    tokens, width = hidden_ref.shape
    patch_dev = tokens // frames
    sub = patch_dev // n_t
    for k, piece in enumerate(pieces):
        for f in range(frames):
            start = pl.multiple_of(f * patch_dev + peer("tm", k) * sub, sub)
            buf[pl.ds(start, sub)] = piece[f * sub : (f + 1) * sub]
    total = hidden_ref[...].astype(F32) + buf[...].astype(F32)
    mixed_ref[0] = total.astype(BF16).reshape(frames, patch_dev, width)


def hops(arrays, axis, first):
    size = lax.axis_size(axis)
    return [
        lax.ppermute(array, axis, [(i, i ^ k) for i in range(size)])
        for k, array in enumerate(arrays, first)
    ]


def exchange(pieces, axis):
    return [pieces[0]] + hops(pieces[1:], axis, 1)


def share(array, axis):
    return exchange([array] * lax.axis_size(axis), axis)


def per_device(
    patches, query_s, key_s, value_s, query_t, key_t, value_t, adapters_a, adapters_b, cotangent
):
    _, frames, patch_dev, width = patches.shape
    n_d, n_t, n_s = (lax.axis_size(name) for name in ("dp", "tm", "space"))
    tokens = frames * patch_dev
    sub = patch_dev // n_t
    d_s = width // n_s
    total = n_s * patch_dev
    factor = (tokens * n_d * n_t * n_s) ** (-0.5)
    downs = jnp.swapaxes(adapters_a, 1, 2)
    dma = pltpu.SemaphoreType.DMA

    time_arrays = [far(x) for x in (query_t, key_t, value_t, cotangent)]
    space_arrays = [
        far(x) for x in (patches, downs, adapters_b, query_s, value_s, key_s)
    ]
    packed = call(
        functools.partial(pack_kernel, n_s, n_t, sub),
        [shape((3 * d_s + 2 * RANK, tokens), BF16)] * n_s
        + [shape((d_s, 2 * RANK), BF16)]
        + [shape((4, frames * sub, width), BF16)] * (n_t - 1),
        *space_arrays, *time_arrays,
        scratch=[pltpu.VMEM(x.shape, BF16) for x in space_arrays]
        + [
            pltpu.VMEM((4,) + query_t.shape, BF16),
            pltpu.VMEM((3, n_s, d_s, tokens), BF16),
            pltpu.VMEM((n_s, d_s, 2 * RANK), BF16),
            dma((6,)),
            dma((4,)),
        ],
        hbm=True,
    )
    here, time_pieces = packed[n_s], hops(packed[n_s + 1 :], "tm", 1)
    packed = exchange(packed[:n_s], "space")
    probs_dims = (frames, d_s // HEAD_DIM, total, total)
    qkv, probs, *out_s = call(
        functools.partial(space_forward_kernel, frames, n_s),
        [shape((3, frames, d_s, total), BF16), pltpu.HBM(probs_dims, F32)]
        + [shape((d_s, tokens), BF16)] * n_s,
        *packed,
        scratch=[pltpu.VMEM(probs_dims, F32), dma((probs_dims[0] * probs_dims[1],))],
        after=time_pieces[:1],
    )
    out_s = exchange(out_s, "space")
    hidden, *codes = call(
        functools.partial(hidden_kernel, n_t, n_s),
        [shape((tokens, width), BF16)] + [shape((8, 128), F32)] * n_t,
        *out_s[::-1], patches, downs,
        scratch=[pltpu.VMEM((n_s, d_s, tokens), BF16), pltpu.VMEM((tokens, 128), F32)],
    )
    codes = exchange(codes, "tm")
    turned = call(
        functools.partial(turn_kernel, frames, sub),
        shape((4, width, n_t * frames * sub), BF16),
        *time_arrays, *time_pieces,
        scratch=[
            pltpu.VMEM((4, frames * sub, width), BF16),
            pltpu.VMEM((n_t - 1, 4, frames * sub, width), BF16),
            dma((4 * frames,)),
            dma((n_t - 1,)),
        ],
        hbm=True,
    )
    timed = call(
        functools.partial(time_kernel, n_t, sub),
        [shape((frames * sub, width), BF16)] * n_t
        + [shape((8, 128), F32)] * n_t
        + [shape((2 * RANK, width), F32)],
        turned, adapters_b, *codes[::-1],
    )
    out_t, dcodes, time_grad_b = timed[:n_t], timed[n_t : 2 * n_t], timed[2 * n_t]
    dcodes = exchange(dcodes, "tm")
    out_t[2:] = hops(out_t[2:], "tm", 2)
    dcodes, *grads = call(
        functools.partial(hidden_grad_kernel, frames, n_s, sub),
        [shape((2 * RANK, tokens), BF16)] + [shape((d_s, tokens), BF16)] * n_s,
        cotangent, downs, *dcodes[::-1],
        scratch=[pltpu.VMEM((tokens, 128), F32), pltpu.VMEM((n_s, d_s, tokens), BF16)],
    )
    grads = exchange(grads, "space")
    backward = call(
        functools.partial(space_backward_kernel, frames, n_s),
        [shape((2 * RANK, tokens + 2 * d_s), BF16)] * n_s + [shape((2 * RANK, d_s), F32)],
        qkv, probs, hidden, time_grad_b, dcodes, here, *packed, *grads[::-1],
        scratch=[pltpu.VMEM((n_s, 2 * RANK, 2 * d_s), BF16)],
        carry=out_t[1:2],
    )
    partial, part = backward[:n_s], backward[n_s]
    partial = exchange(partial, "space")
    out_t[1:2] = hops(backward[n_s + 1 :], "tm", 1)
    n_full, n_split = 2 * RANK // n_d, 6 * RANK // n_d
    dims = ((n_s * n_full + n_split) // 2, 2 * d_s)
    sums = call(
        functools.partial(merge_kernel, n_s, n_d),
        [shape(dims, BF16)] * n_d,
        part, patches, *partial[::-1],
        scratch=[pltpu.VMEM((n_d,) + dims, BF16)],
        after=out_t[2:],
    )
    sums = call(total_kernel, shape(dims, BF16), *exchange(sums, "dp"), after=out_t[1:2])
    sums = call(total_kernel, shape(dims, BF16), *share(sums, "tm"))
    sums = call(
        functools.partial(join_kernel, n_full),
        shape((n_full + n_split, width), BF16),
        *share(sums, "space"),
        scratch=[pltpu.VMEM((n_s,) + dims, BF16)],
    )
    grads_a, grads_b = call(
        functools.partial(final_kernel, factor, n_d, n_full),
        [shape((4, RANK, width), F32)] * 2,
        *share(sums, "dp"),
        scratch=[pltpu.VMEM((n_d, n_full + n_split, width), BF16)],
    )
    mixed = call(
        functools.partial(mixed_kernel, frames),
        shape(patches.shape, BF16),
        hidden, *out_t,
        scratch=[pltpu.VMEM((tokens, width), BF16)],
    )
    return (mixed, jnp.swapaxes(grads_a, 1, 2), grads_b)


def solution(mesh):
    token = P("dp", "tm", "space", None)
    return jax.shard_map(
        per_device,
        mesh=mesh,
        in_specs=(token,) * 7 + (P(), P(), token),
        out_specs=(token, P(), P()),
        check_vma=False,
    )
```

```python
import functools
import math

import jax
import jax.numpy as jnp
from jax import lax
from jax.experimental import pallas as pl
from jax.experimental.pallas import tpu as pltpu
from jax.sharding import PartitionSpec as P

HEAD_DIM = 72
RANK = 16
SCALE = HEAD_DIM ** (-0.5)
F32 = jnp.float32
BF16 = jnp.bfloat16
NN = (((1,), (0,)), ((), ()))
NT = (((1,), (1,)), ((), ()))
TN = (((0,), (0,)), ((), ()))


def mm(a, b, dims=NN):
    return lax.dot_general(a, b, dims, preferred_element_type=F32)


def far(x):
    return pltpu.with_memory_space_constraint(x, pltpu.HBM)


def call(kernel, out_shape, *args, scratch=(), hbm=False, limit=48, after=(), carry=()):
    vmem = pl.BlockSpec(memory_space=pltpu.VMEM)
    anywhere = pl.BlockSpec(memory_space=pl.ANY)
    main = anywhere if hbm else vmem
    single = not isinstance(out_shape, (tuple, list))
    outs = (out_shape,) if single else tuple(out_shape)
    used, extra = len(args), len(after) + len(carry)

    def body(*refs):
        inside = refs[:used] + refs[used + extra : used + extra + len(outs)]
        kernel(*inside, *refs[used + extra + len(outs) + len(carry) :])

    result = pl.pallas_call(
        body,
        out_shape=outs + tuple(shape(x.shape, x.dtype) for x in carry),
        in_specs=[main] * used + [anywhere] * extra,
        out_specs=tuple(vmem if isinstance(o, jax.ShapeDtypeStruct) else anywhere for o in outs)
        + (anywhere,) * len(carry),
        scratch_shapes=list(scratch),
        input_output_aliases={used + len(after) + i: len(outs) + i for i in range(len(carry))},
        compiler_params=pltpu.CompilerParams(vmem_limit_bytes=limit * 1024 * 1024),
    )(*args, *after, *carry)
    return result[0] if single and not carry else list(result)


def shape(dims, dtype):
    return jax.ShapeDtypeStruct(tuple(dims), dtype)


def probs_of(keys, q_t, mask):
    scores = mm(keys, q_t) * SCALE
    if mask is not None:
        scores = jnp.where(mask, scores, -1e30)
    peak = jnp.max(scores, axis=0, keepdims=True)
    weights = jnp.exp(scores - peak)
    return weights * (1.0 / jnp.sum(weights, axis=0, keepdims=True))


def head_backward(probs, k_t, v_t, g_t):
    low = probs.astype(BF16)
    dvals = mm(g_t, low, NT)
    dprob = mm(v_t.T, g_t)
    inner = jnp.sum(probs * dprob, axis=0, keepdims=True)
    dscore = (probs * (dprob - inner) * SCALE).astype(BF16)
    dquery = mm(k_t, dscore)
    return dquery, dvals


def rows_of(array, head):
    return array[head * HEAD_DIM : (head + 1) * HEAD_DIM]


def peer(axis, distance):
    return lax.axis_index(axis) ^ distance


def load_all(refs, buffers, sems):
    copies = [
        pltpu.make_async_copy(ref, buffer, sems.at[index])
        for index, (ref, buffer) in enumerate(zip(refs, buffers))
    ]
    for copy in copies:
        copy.start()
    return copies


def pack_kernel(n_s, n_t, sub, *refs):
    ins, time_ins, refs = refs[:6], refs[6:10], refs[10:]
    outs, here_ref, refs = refs[:n_s], refs[n_s], refs[n_s + 1 :]
    time_outs, refs = refs[: n_t - 1], refs[n_t - 1 :]
    buffers, (time_buf, turned_ref, maps_ref, sems, time_sems) = refs[:6], refs[6:]
    k_buf, p_buf, at_buf, b_buf, q_buf, v_buf = buffers
    copies = load_all(ins, buffers, sems)
    time_copies = load_all(time_ins, [time_buf.at[index] for index in range(4)], time_sems)
    d_s, tokens = turned_ref.shape[2:]
    frames = time_buf.shape[2]

    def flat(ref):
        return ref[0].reshape(tokens, ref.shape[3])

    def send(array, index):
        turned = array.T
        for j in range(n_s):
            turned_ref[index, j] = turned[j * d_s : (j + 1) * d_s]
        for k in range(n_s):
            outs[k][index * d_s : (index + 1) * d_s] = turned_ref[index, peer("space", k)]

    copies[0].wait()
    send(flat(k_buf), 1)
    for copy in copies[1:4]:
        copy.wait()
    patches = flat(p_buf)
    codes_q = mm(patches, at_buf[0], NT).astype(BF16)
    codes_v = mm(patches, at_buf[1], NT).astype(BF16)
    codes_t = jnp.concatenate([codes_q, codes_v], axis=1).T
    copies[4].wait()
    query = (flat(q_buf).astype(F32) + mm(codes_q, b_buf[0])).astype(BF16)
    send(query, 0)
    copies[5].wait()
    value = (flat(v_buf).astype(F32) + mm(codes_v, b_buf[1])).astype(BF16)
    send(value, 2)
    maps = jnp.concatenate([b_buf[0], b_buf[1]], axis=0).T
    for j in range(n_s):
        maps_ref[j] = maps[j * d_s : (j + 1) * d_s]
    here_ref[...] = maps_ref[peer("space", 0)]
    for k in range(n_s):
        outs[k][3 * d_s :] = codes_t
    for index, copy in enumerate(time_copies):
        copy.wait()
        for k in range(1, n_t):
            start = pl.multiple_of(peer("tm", k) * sub, sub)
            for f in range(frames):
                time_outs[k - 1][index, f * sub : (f + 1) * sub] = time_buf[
                    index, 0, f, pl.ds(start, sub)
                ]


def frame_rows(pieces, f, patch_dev):
    return jnp.concatenate([x[:, f * patch_dev : (f + 1) * patch_dev] for x in pieces], axis=1)


def space_forward_kernel(frames, n_s, *refs):
    packed, (qkv_ref, probs_ref, *outs) = refs[:n_s][::-1], refs[n_s : 2 * n_s + 2]
    probs_buf, sems = refs[2 * n_s + 2 :]
    copies = []
    d_s, tokens = outs[0].shape
    patch_dev = tokens // frames
    total = n_s * patch_dev
    step = min(total, 256)
    for index in range(3):
        pieces = [x[index * d_s : (index + 1) * d_s] for x in packed]
        for f in range(frames):
            qkv_ref[index, f] = frame_rows(pieces, f, patch_dev)
    for f in range(frames):
        query = qkv_ref[0, f].astype(F32)
        keys = qkv_ref[1, f].astype(F32)
        vals = qkv_ref[2, f].astype(F32)
        heads = []
        for h in range(d_s // HEAD_DIM):
            k_h = rows_of(keys, h).astype(BF16)
            v_h = rows_of(vals, h).astype(BF16)
            q_h = rows_of(query, h).astype(BF16)
            parts = []
            for s in range(0, total, step):
                probs = probs_of(k_h.T, q_h[:, s : s + step], None)
                probs_buf[f, h, :, s : s + step] = probs
                parts.append(mm(v_h, probs.astype(BF16)))
            heads.append(parts[0] if len(parts) == 1 else jnp.concatenate(parts, axis=1))
            copy = pltpu.make_async_copy(
                probs_buf.at[f, h], probs_ref.at[f, h], sems.at[len(copies)]
            )
            copy.start()
            copies.append(copy)
        out = jnp.concatenate(heads, axis=0).astype(BF16)
        for k in range(n_s):
            outs[k][:, f * patch_dev : (f + 1) * patch_dev] = out[
                :, k * patch_dev : (k + 1) * patch_dev
            ]
    for copy in copies:
        copy.wait()


def lane_block(rows):
    return lax.broadcasted_iota(jnp.int32, (rows, 128), 1) // (2 * RANK)


def fold(token_rows):
    block = lane_block(8)
    result = token_rows[0:8]
    for k in range(1, 4):
        result = jnp.where(block == k, token_rows[8 * k : 8 * k + 8], result)
    return result


def unfold(folded):
    pieces = [folded]
    for k in range(1, 4):
        pieces.append(pltpu.roll(folded, 128 - 2 * RANK * k, 1))
    return jnp.concatenate(pieces, axis=0)


def hidden_kernel(n_t, n_s, *refs):
    pieces, refs = refs[:n_s][::-1], refs[n_s:]
    p_ref, at_ref, hidden_ref = refs[:3]
    sends = refs[3 : 3 + n_t]
    out_buf, codes_buf = refs[3 + n_t :]
    _, frames, patch_dev, width = p_ref.shape
    tokens = frames * patch_dev
    sub = patch_dev // n_t
    for k in range(n_s):
        out_buf[peer("space", k)] = pieces[k][...]
    out = out_buf[...].reshape(width, tokens).T
    hidden = (p_ref[0].reshape(tokens, width).astype(F32) + out.astype(F32)).astype(BF16)
    hidden_ref[...] = hidden
    downs = jnp.concatenate([at_ref[2], at_ref[3]] * 4, axis=0)
    codes_buf[...] = mm(hidden, downs, NT).astype(BF16).astype(F32)
    for k in range(n_t):
        rows = [
            codes_buf[pl.ds(pl.multiple_of(f * patch_dev + peer("tm", k) * sub, sub), sub)]
            for f in range(frames)
        ]
        sends[k][...] = fold(jnp.concatenate(rows, axis=0))


def turn_kernel(frames, sub, q_ref, k_ref, v_ref, g_ref, *refs):
    *pieces, out_ref, own_buf, piece_buf, own_sems, sems = refs
    own = []
    start = pl.multiple_of(peer("tm", 0) * sub, sub)
    for index, ref in enumerate((q_ref, k_ref, v_ref, g_ref)):
        for f in range(frames):
            copy = pltpu.make_async_copy(
                ref.at[0, f, pl.ds(start, sub)],
                own_buf.at[index, f * sub : (f + 1) * sub],
                own_sems.at[index * frames + f],
            )
            copy.start()
            own.append(copy)
    copies = load_all(pieces, [piece_buf.at[k] for k in range(len(pieces))], sems)
    for copy in own + copies:
        copy.wait()
    for index in range(4):
        parts = [own_buf[index]] + [piece_buf[k, index] for k in range(len(pieces))]
        out_ref[index] = jnp.concatenate(parts, axis=0).T


def time_kernel(n_t, sub, x_ref, b_ref, *refs):
    codes_refs, refs = refs[:n_t][::-1], refs[n_t:]
    outs, sends, grad_b_ref = refs[:n_t], refs[n_t : 2 * n_t], refs[2 * n_t]
    _, width, tokens = x_ref.shape
    codes = jnp.concatenate([unfold(ref[...]) for ref in codes_refs], axis=0).T
    codes_q = codes[:RANK].astype(BF16)
    codes_v = codes[RANK : 2 * RANK].astype(BF16)
    query = (x_ref[0].astype(F32) + mm(b_ref[2], codes_q, TN)).astype(BF16).astype(F32)
    vals = (x_ref[2].astype(F32) + mm(b_ref[3], codes_v, TN)).astype(BF16).astype(F32)
    keys = x_ref[1].astype(F32)
    grad = x_ref[3].astype(F32)
    row = lax.broadcasted_iota(jnp.int32, (tokens, 2 * tokens), 0)
    col = lax.broadcasted_iota(jnp.int32, (tokens, 2 * tokens), 1)
    mask = lax.rem(row, sub) == lax.rem(col, sub)
    top = lax.broadcasted_iota(jnp.int32, (2 * HEAD_DIM, tokens), 0) < HEAD_DIM

    def spread(pair):
        return jnp.concatenate(
            [jnp.where(top, pair, 0.0), jnp.where(top, 0.0, pair)], axis=1
        ).astype(BF16)

    def pick(wide):
        return jnp.concatenate([wide[:HEAD_DIM, :tokens], wide[HEAD_DIM:, tokens:]], axis=0)

    outs_h, d_query, d_vals = [], [], []
    for h in range(0, width, 2 * HEAD_DIM):
        pair = slice(h, h + 2 * HEAD_DIM)
        k_h, v_h = keys[pair].astype(BF16), vals[pair].astype(BF16)
        g_h = spread(grad[pair])
        probs = probs_of(k_h.T, spread(query[pair]), mask)
        low = probs.astype(BF16)
        dprob = mm(v_h.T, g_h)
        inner = jnp.sum(probs * dprob, axis=0, keepdims=True)
        dscore = (probs * (dprob - inner) * SCALE).astype(BF16)
        outs_h.append(pick(mm(v_h, low)))
        d_vals.append(mm(g_h, low, NT))
        d_query.append(pick(mm(k_h, dscore)))
    d_query = jnp.concatenate(d_query, axis=0).astype(BF16)
    d_vals = jnp.concatenate(d_vals, axis=0).astype(BF16)
    d_codes = jnp.concatenate([mm(b_ref[2], d_query), mm(b_ref[3], d_vals)] * 4, axis=0)
    d_codes = d_codes.astype(BF16).astype(F32).T
    per = tokens // n_t
    for k in range(n_t):
        sends[k][...] = fold(d_codes[k * per : (k + 1) * per])
    out = jnp.concatenate(outs_h, axis=0).astype(BF16).T
    for k in range(n_t):
        outs[k][...] = out[k * per : (k + 1) * per]
    grad_b_ref[:RANK] = mm(codes_q, d_query, NT)
    grad_b_ref[RANK:] = mm(codes_v, d_vals, NT)


def hidden_grad_kernel(frames, n_s, sub, g_ref, at_ref, *refs):
    *pieces, codes_ref = refs[: -n_s - 2]
    pieces = pieces[::-1]
    outs, (buf, turned_ref) = refs[-n_s - 2 : -2], refs[-2:]
    patch_dev = sub * len(pieces)
    _, d_s, tokens = turned_ref.shape
    for k, piece in enumerate(pieces):
        rows = unfold(piece[...])
        for f in range(frames):
            start = pl.multiple_of(f * patch_dev + peer("tm", k) * sub, sub)
            buf[pl.ds(start, sub)] = rows[f * sub : (f + 1) * sub]
    codes = buf[:, : 2 * RANK].astype(BF16)
    codes_ref[...] = buf[...].T[: 2 * RANK].astype(BF16)
    downs = jnp.concatenate([at_ref[2], at_ref[3]], axis=0)
    grad = g_ref[0].reshape(tokens, n_s * d_s).astype(F32) + mm(codes, downs)
    turned = grad.astype(BF16).T
    for j in range(n_s):
        turned_ref[j] = turned[j * d_s : (j + 1) * d_s]
    for k in range(n_s):
        outs[k][...] = turned_ref[peer("space", k)]


def space_backward_kernel(frames, n_s, qkv_ref, probs_ref, hidden_ref, grad_b_ref, dcodes_ref, here_ref, *refs):
    packed, grads, sends = refs[:n_s][::-1], refs[n_s : 2 * n_s][::-1], refs[2 * n_s : 3 * n_s]
    part_ref, cut_buf = refs[3 * n_s :]
    d_s = part_ref.shape[1]
    tokens = hidden_ref.shape[0]
    patch_dev = tokens // frames
    total = n_s * patch_dev
    step = min(total, 256)
    b_here = here_ref[...].T
    grads = [x[...] for x in grads]
    grad_b_q = grad_b_v = None
    codes = [x[3 * d_s :] for x in packed]
    for f in range(frames):
        keys = qkv_ref[1, f].astype(F32)
        vals = qkv_ref[2, f].astype(F32)
        grad = frame_rows(grads, f, patch_dev).astype(F32)
        d_query, d_vals = [], []
        for h in range(d_s // HEAD_DIM):
            k_h = rows_of(keys, h).astype(BF16)
            v_h = rows_of(vals, h).astype(BF16)
            g_h = rows_of(grad, h).astype(BF16)
            dq_parts, dv_sum = [], None
            for s in range(0, total, step):
                probs = probs_ref[f, h, :, s : s + step]
                dq, dv = head_backward(probs, k_h, v_h, g_h[:, s : s + step])
                dq_parts.append(dq)
                dv_sum = dv if dv_sum is None else dv_sum + dv
            d_query.append(
                dq_parts[0] if len(dq_parts) == 1 else jnp.concatenate(dq_parts, axis=1)
            )
            d_vals.append(dv_sum)
        d_query = jnp.concatenate(d_query, axis=0).astype(BF16)
        d_vals = jnp.concatenate(d_vals, axis=0).astype(BF16)
        partial = jnp.concatenate([mm(b_here[:RANK], d_query), mm(b_here[RANK:], d_vals)], axis=0)
        for k in range(n_s):
            place = slice(f * patch_dev, (f + 1) * patch_dev)
            sends[k][:, place] = partial[:, k * patch_dev : (k + 1) * patch_dev].astype(BF16)
        frame_codes = frame_rows(codes, f, patch_dev)
        term_q = mm(frame_codes[:RANK], d_query, NT)
        term_v = mm(frame_codes[RANK:], d_vals, NT)
        grad_b_q = term_q if grad_b_q is None else grad_b_q + term_q
        grad_b_v = term_v if grad_b_v is None else grad_b_v + term_v
    part_ref[:RANK] = grad_b_q
    part_ref[RANK:] = grad_b_v
    grad_a = mm(dcodes_ref[...], hidden_ref[...])
    for j in range(n_s):
        here = slice(j * d_s, (j + 1) * d_s)
        cut_buf[j, :, :d_s] = grad_a[:, here].astype(BF16)
        cut_buf[j, :, d_s:] = grad_b_ref[:, here].astype(BF16)
    for k in range(n_s):
        sends[k][:, tokens:] = cut_buf[peer("space", k)]


def add_up(terms):
    result = None
    for term in terms:
        result = term if result is None else result + term
    return result


def merge_kernel(n_s, n_d, part_ref, patches_ref, *refs):
    recvs, sends, buf = refs[:n_s][::-1], refs[n_s : n_s + n_d], refs[n_s + n_d]
    d_s = part_ref.shape[1]
    tokens = recvs[0].shape[1] - 2 * d_s
    codes = add_up([recv[:, :tokens].astype(F32) for recv in recvs]).astype(BF16)
    full = mm(codes, patches_ref[0].reshape(tokens, n_s * d_s))
    time_a = add_up([recv[:, tokens : tokens + d_s].astype(F32) for recv in recvs])
    time_b = add_up([recv[:, tokens + d_s :].astype(F32) for recv in recvs])
    split = jnp.concatenate([time_a, part_ref[...], time_b], axis=0)
    per, per_full = split.shape[0] // n_d, full.shape[0] // n_d
    for d in range(n_d):
        mine = [split[d * per : (d + 1) * per]]
        rows = full[d * per_full : (d + 1) * per_full]
        mine += [rows[:, j * d_s : (j + 1) * d_s] for j in range(n_s)]
        mine = jnp.concatenate(mine, axis=0)
        half = mine.shape[0] // 2
        buf[d] = jnp.concatenate([mine[:half], mine[half:]], axis=1).astype(BF16)
    for k in range(n_d):
        sends[k][...] = buf[peer("dp", k)]


def total_kernel(*refs):
    terms = [ref[...].astype(F32) for ref in refs[:-1]]
    while len(terms) > 1:
        terms = [terms[i] + terms[i + 1] for i in range(0, len(terms), 2)]
    refs[-1][...] = terms[0].astype(refs[-1].dtype)


def join_kernel(n_full, *refs):
    pieces, (out_ref, buf) = refs[:-2], refs[-2:]
    n_s, d_s = len(pieces), buf.shape[2] // 2
    for k, piece in enumerate(pieces):
        buf[peer("space", k)] = piece[...]
    rows = [
        jnp.concatenate([buf[j, :, :d_s], buf[j, :, d_s:]], axis=0).astype(F32) for j in range(n_s)
    ]
    n_split = rows[0].shape[0] - n_s * n_full
    out_ref[n_full:] = jnp.concatenate([x[:n_split] for x in rows], axis=1).astype(BF16)
    full = add_up([x[n_split:] for x in rows])
    cuts = [full[j * n_full : (j + 1) * n_full] for j in range(n_s)]
    out_ref[:n_full] = jnp.concatenate(cuts, axis=1).astype(BF16)


def final_kernel(factor, n_d, n_full, *refs):
    pieces, (a_ref, b_ref, buf, out_buf, sems) = refs[:n_d], refs[n_d:]
    for k, piece in enumerate(pieces):
        buf[peer("dp", k)] = piece[...]
    n_split = pieces[0].shape[0] - n_full
    size = math.gcd(n_full, n_split, RANK)
    filled, copies = [0] * 8, []
    for d in range(n_d):
        rows = buf[d].astype(F32) * factor
        for r in range(0, n_full + n_split, size):
            row = d * n_full + r if r < n_full else 2 * RANK + d * n_split + r - n_full
            index = row // RANK
            out_buf[index, row % RANK : row % RANK + size] = rows[r : r + size]
            filled[index] += size
            if filled[index] == RANK:
                target = (a_ref if index < 4 else b_ref).at[index % 4]
                copies.append(pltpu.make_async_copy(out_buf.at[index], target, sems.at[index]))
                copies[-1].start()
    for copy in copies:
        copy.wait()


def mixed_kernel(frames, hidden_ref, *refs):
    pieces, (mixed_ref, buf) = refs[:-2], refs[-2:]
    n_t = len(pieces)
    tokens, width = hidden_ref.shape
    patch_dev = tokens // frames
    sub = patch_dev // n_t
    for k, piece in enumerate(pieces):
        for f in range(frames):
            start = pl.multiple_of(f * patch_dev + peer("tm", k) * sub, sub)
            buf[pl.ds(start, sub)] = piece[f * sub : (f + 1) * sub]
    total = hidden_ref[...].astype(F32) + buf[...].astype(F32)
    mixed_ref[0] = total.astype(BF16).reshape(frames, patch_dev, width)


def hops(arrays, axis, first):
    size = lax.axis_size(axis)
    return [
        lax.ppermute(array, axis, [(i, i ^ k) for i in range(size)])
        for k, array in enumerate(arrays, first)
    ]


def exchange(pieces, axis):
    return [pieces[0]] + hops(pieces[1:], axis, 1)


def share(array, axis):
    return exchange([array] * lax.axis_size(axis), axis)


def per_device(
    patches, query_s, key_s, value_s, query_t, key_t, value_t, adapters_a, adapters_b, cotangent
):
    _, frames, patch_dev, width = patches.shape
    n_d, n_t, n_s = (lax.axis_size(name) for name in ("dp", "tm", "space"))
    tokens = frames * patch_dev
    sub = patch_dev // n_t
    d_s = width // n_s
    total = n_s * patch_dev
    factor = (tokens * n_d * n_t * n_s) ** (-0.5)
    downs = jnp.swapaxes(adapters_a, 1, 2)
    dma = pltpu.SemaphoreType.DMA

    time_arrays = [far(x) for x in (query_t, key_t, value_t, cotangent)]
    space_arrays = [
        far(x) for x in (key_s, patches, downs, adapters_b, query_s, value_s)
    ]
    packed = call(
        functools.partial(pack_kernel, n_s, n_t, sub),
        [shape((3 * d_s + 2 * RANK, tokens), BF16)] * n_s
        + [shape((d_s, 2 * RANK), BF16)]
        + [shape((4, frames * sub, width), BF16)] * (n_t - 1),
        *space_arrays, *time_arrays,
        scratch=[pltpu.VMEM(x.shape, BF16) for x in space_arrays]
        + [
            pltpu.VMEM((4,) + query_t.shape, BF16),
            pltpu.VMEM((3, n_s, d_s, tokens), BF16),
            pltpu.VMEM((n_s, d_s, 2 * RANK), BF16),
            dma((6,)),
            dma((4,)),
        ],
        hbm=True,
    )
    here, time_pieces = packed[n_s], hops(packed[n_s + 1 :], "tm", 1)
    packed = exchange(packed[:n_s], "space")
    probs_dims = (frames, d_s // HEAD_DIM, total, total)
    qkv, probs, *out_s = call(
        functools.partial(space_forward_kernel, frames, n_s),
        [shape((3, frames, d_s, total), BF16), pltpu.HBM(probs_dims, F32)]
        + [shape((d_s, tokens), BF16)] * n_s,
        *packed[::-1],
        scratch=[pltpu.VMEM(probs_dims, F32), dma((probs_dims[0] * probs_dims[1],))],
        after=time_pieces[:1],
    )
    out_s = exchange(out_s, "space")
    hidden, *codes = call(
        functools.partial(hidden_kernel, n_t, n_s),
        [shape((tokens, width), BF16)] + [shape((8, 128), F32)] * n_t,
        *out_s[::-1], patches, downs,
        scratch=[pltpu.VMEM((n_s, d_s, tokens), BF16), pltpu.VMEM((tokens, 128), F32)],
    )
    codes = exchange(codes, "tm")
    turned = call(
        functools.partial(turn_kernel, frames, sub),
        shape((4, width, n_t * frames * sub), BF16),
        *time_arrays, *time_pieces,
        scratch=[
            pltpu.VMEM((4, frames * sub, width), BF16),
            pltpu.VMEM((n_t - 1, 4, frames * sub, width), BF16),
            dma((4 * frames,)),
            dma((n_t - 1,)),
        ],
        hbm=True,
    )
    timed = call(
        functools.partial(time_kernel, n_t, sub),
        [shape((frames * sub, width), BF16)] * n_t
        + [shape((8, 128), F32)] * n_t
        + [shape((2 * RANK, width), F32)],
        turned, adapters_b, *codes[::-1],
    )
    out_t, dcodes, time_grad_b = timed[:n_t], timed[n_t : 2 * n_t], timed[2 * n_t]
    dcodes = exchange(dcodes, "tm")
    out_t[2:] = hops(out_t[2:], "tm", 2)
    dcodes, *grads = call(
        functools.partial(hidden_grad_kernel, frames, n_s, sub),
        [shape((2 * RANK, tokens), BF16)] + [shape((d_s, tokens), BF16)] * n_s,
        cotangent, downs, *dcodes[::-1],
        scratch=[pltpu.VMEM((tokens, 128), F32), pltpu.VMEM((n_s, d_s, tokens), BF16)],
    )
    grads = exchange(grads, "space")
    backward = call(
        functools.partial(space_backward_kernel, frames, n_s),
        [shape((2 * RANK, tokens + 2 * d_s), BF16)] * n_s + [shape((2 * RANK, d_s), F32)],
        qkv, probs, hidden, time_grad_b, dcodes, here, *packed[::-1], *grads[::-1],
        scratch=[pltpu.VMEM((n_s, 2 * RANK, 2 * d_s), BF16)],
        carry=out_t[1:2],
    )
    partial, part = backward[:n_s], backward[n_s]
    partial = exchange(partial, "space")
    out_t[1:2] = hops(backward[n_s + 1 :], "tm", 1)
    n_full, n_split = 2 * RANK // n_d, 6 * RANK // n_d
    dims = ((n_s * n_full + n_split) // 2, 2 * d_s)
    sums = call(
        functools.partial(merge_kernel, n_s, n_d),
        [shape(dims, BF16)] * n_d,
        part, patches, *partial[::-1],
        scratch=[pltpu.VMEM((n_d,) + dims, BF16)],
        after=out_t[2:],
    )
    sums = call(total_kernel, shape(dims, BF16), *exchange(sums, "dp"), after=out_t[1:2])
    sums = call(total_kernel, shape(dims, BF16), *share(sums, "tm"))
    sums = call(
        functools.partial(join_kernel, n_full),
        shape((n_full + n_split, width), BF16),
        *share(sums, "space"),
        scratch=[pltpu.VMEM((n_s,) + dims, BF16)],
    )
    grads_a, grads_b = call(
        functools.partial(final_kernel, factor, n_d, n_full),
        [pltpu.HBM((4, RANK, width), F32)] * 2,
        *share(sums, "dp"),
        scratch=[
            pltpu.VMEM((n_d, n_full + n_split, width), BF16),
            pltpu.VMEM((8, RANK, width), F32),
            dma((8,)),
        ],
    )
    mixed = call(
        functools.partial(mixed_kernel, frames),
        shape(patches.shape, BF16),
        hidden, *out_t,
        scratch=[pltpu.VMEM((tokens, width), BF16)],
    )
    return (mixed, jnp.swapaxes(grads_a, 1, 2), grads_b)


def solution(mesh):
    token = P("dp", "tm", "space", None)
    return jax.shard_map(
        per_device,
        mesh=mesh,
        in_specs=(token,) * 7 + (P(), P(), token),
        out_specs=(token, P(), P()),
        check_vma=False,
    )
```

```python
import functools
import math

import jax
import jax.numpy as jnp
from jax import lax
from jax.experimental import pallas as pl
from jax.experimental.pallas import tpu as pltpu
from jax.sharding import PartitionSpec as P

HEAD_DIM = 72
RANK = 16
SCALE = HEAD_DIM ** (-0.5)
F32 = jnp.float32
BF16 = jnp.bfloat16
NN = (((1,), (0,)), ((), ()))
NT = (((1,), (1,)), ((), ()))
TN = (((0,), (0,)), ((), ()))


def mm(a, b, dims=NN):
    return lax.dot_general(a, b, dims, preferred_element_type=F32)


def far(x):
    return pltpu.with_memory_space_constraint(x, pltpu.HBM)


def call(kernel, out_shape, *args, scratch=(), hbm=False, limit=48, after=(), carry=()):
    vmem = pl.BlockSpec(memory_space=pltpu.VMEM)
    anywhere = pl.BlockSpec(memory_space=pl.ANY)
    main = anywhere if hbm else vmem
    single = not isinstance(out_shape, (tuple, list))
    outs = (out_shape,) if single else tuple(out_shape)
    used, extra = len(args), len(after) + len(carry)

    def body(*refs):
        inside = refs[:used] + refs[used + extra : used + extra + len(outs)]
        kernel(*inside, *refs[used + extra + len(outs) + len(carry) :])

    result = pl.pallas_call(
        body,
        out_shape=outs + tuple(shape(x.shape, x.dtype) for x in carry),
        in_specs=[main] * used + [anywhere] * extra,
        out_specs=tuple(vmem if isinstance(o, jax.ShapeDtypeStruct) else anywhere for o in outs)
        + (anywhere,) * len(carry),
        scratch_shapes=list(scratch),
        input_output_aliases={used + len(after) + i: len(outs) + i for i in range(len(carry))},
        compiler_params=pltpu.CompilerParams(vmem_limit_bytes=limit * 1024 * 1024),
    )(*args, *after, *carry)
    return result[0] if single and not carry else list(result)


def shape(dims, dtype):
    return jax.ShapeDtypeStruct(tuple(dims), dtype)


def probs_of(keys, q_t, mask):
    scores = mm(keys, q_t) * SCALE
    if mask is not None:
        scores = jnp.where(mask, scores, -1e30)
    peak = jnp.max(scores, axis=0, keepdims=True)
    weights = jnp.exp(scores - peak)
    return weights * (1.0 / jnp.sum(weights, axis=0, keepdims=True))


def head_backward(probs, k_t, v_t, g_t):
    low = probs.astype(BF16)
    dvals = mm(g_t, low, NT)
    dprob = mm(v_t.T, g_t)
    inner = jnp.sum(probs * dprob, axis=0, keepdims=True)
    dscore = (probs * (dprob - inner) * SCALE).astype(BF16)
    dquery = mm(k_t, dscore)
    return dquery, dvals


def rows_of(array, head):
    return array[head * HEAD_DIM : (head + 1) * HEAD_DIM]


def peer(axis, distance):
    return lax.axis_index(axis) ^ distance


def load_all(refs, buffers, sems):
    copies = [
        pltpu.make_async_copy(ref, buffer, sems.at[index])
        for index, (ref, buffer) in enumerate(zip(refs, buffers))
    ]
    for copy in copies:
        copy.start()
    return copies


def pack_kernel(n_s, n_t, sub, *refs):
    ins, time_ins, refs = refs[:6], refs[6:10], refs[10:]
    outs, here_ref, refs = refs[:n_s], refs[n_s], refs[n_s + 1 :]
    time_outs, refs = refs[: n_t - 1], refs[n_t - 1 :]
    buffers, (time_buf, turned_ref, maps_ref, sems, time_sems) = refs[:6], refs[6:]
    p_buf, at_buf, b_buf, q_buf, v_buf, k_buf = buffers
    copies = load_all(ins, buffers, sems)
    time_copies = load_all(time_ins, [time_buf.at[index] for index in range(4)], time_sems)
    d_s, tokens = turned_ref.shape[2:]
    frames = time_buf.shape[2]

    def flat(ref):
        return ref[0].reshape(tokens, ref.shape[3])

    def send(array, index):
        turned = array.T
        for j in range(n_s):
            turned_ref[index, j] = turned[j * d_s : (j + 1) * d_s]
        for k in range(n_s):
            outs[k][index * d_s : (index + 1) * d_s] = turned_ref[index, peer("space", k)]

    copies[0].wait()
    copies[1].wait()
    copies[2].wait()
    patches = flat(p_buf)
    codes_q = mm(patches, at_buf[0], NT).astype(BF16)
    codes_v = mm(patches, at_buf[1], NT).astype(BF16)
    codes_t = jnp.concatenate([codes_q, codes_v], axis=1).T
    maps = jnp.concatenate([b_buf[0], b_buf[1]], axis=0).T
    for j in range(n_s):
        maps_ref[j] = maps[j * d_s : (j + 1) * d_s]
    here_ref[...] = maps_ref[peer("space", 0)]
    copies[3].wait()
    query = (flat(q_buf).astype(F32) + mm(codes_q, b_buf[0])).astype(BF16)
    send(query, 0)
    copies[4].wait()
    value = (flat(v_buf).astype(F32) + mm(codes_v, b_buf[1])).astype(BF16)
    send(value, 2)
    copies[5].wait()
    send(flat(k_buf), 1)
    for k in range(n_s):
        outs[k][3 * d_s :] = codes_t
    for index, copy in enumerate(time_copies):
        copy.wait()
        for k in range(1, n_t):
            start = pl.multiple_of(peer("tm", k) * sub, sub)
            for f in range(frames):
                time_outs[k - 1][index, f * sub : (f + 1) * sub] = time_buf[
                    index, 0, f, pl.ds(start, sub)
                ]


def frame_rows(pieces, f, patch_dev):
    return jnp.concatenate([x[:, f * patch_dev : (f + 1) * patch_dev] for x in pieces], axis=1)


def space_forward_kernel(frames, n_s, *refs):
    packed, (qkv_ref, probs_ref, *outs) = refs[:n_s], refs[n_s:]
    d_s, tokens = outs[0].shape
    patch_dev = tokens // frames
    total = n_s * patch_dev
    step = min(total, 256)
    for index in range(3):
        pieces = [x[index * d_s : (index + 1) * d_s] for x in packed]
        for f in range(frames):
            qkv_ref[index, f] = frame_rows(pieces, f, patch_dev)
    for f in range(frames):
        query = qkv_ref[0, f].astype(F32)
        keys = qkv_ref[1, f].astype(F32)
        vals = qkv_ref[2, f].astype(F32)
        heads = []
        for h in range(d_s // HEAD_DIM):
            k_h = rows_of(keys, h).astype(BF16)
            v_h = rows_of(vals, h).astype(BF16)
            q_h = rows_of(query, h).astype(BF16)
            parts = []
            for s in range(0, total, step):
                probs = probs_of(k_h.T, q_h[:, s : s + step], None)
                probs_ref[f, h, :, s : s + step] = probs
                parts.append(mm(v_h, probs.astype(BF16)))
            heads.append(parts[0] if len(parts) == 1 else jnp.concatenate(parts, axis=1))
        out = jnp.concatenate(heads, axis=0).astype(BF16)
        for k in range(n_s):
            outs[k][:, f * patch_dev : (f + 1) * patch_dev] = out[
                :, k * patch_dev : (k + 1) * patch_dev
            ]


def lane_block(rows):
    return lax.broadcasted_iota(jnp.int32, (rows, 128), 1) // (2 * RANK)


def fold(token_rows):
    block = lane_block(8)
    result = token_rows[0:8]
    for k in range(1, 4):
        result = jnp.where(block == k, token_rows[8 * k : 8 * k + 8], result)
    return result


def unfold(folded):
    pieces = [folded]
    for k in range(1, 4):
        pieces.append(pltpu.roll(folded, 128 - 2 * RANK * k, 1))
    return jnp.concatenate(pieces, axis=0)


def hidden_kernel(n_t, n_s, *refs):
    pieces, refs = refs[:n_s][::-1], refs[n_s:]
    p_ref, at_ref, hidden_ref = refs[:3]
    sends = refs[3 : 3 + n_t]
    out_buf, codes_buf = refs[3 + n_t :]
    _, frames, patch_dev, width = p_ref.shape
    tokens = frames * patch_dev
    sub = patch_dev // n_t
    for k in range(n_s):
        out_buf[peer("space", k)] = pieces[k][...]
    out = out_buf[...].reshape(width, tokens).T
    hidden = (p_ref[0].reshape(tokens, width).astype(F32) + out.astype(F32)).astype(BF16)
    hidden_ref[...] = hidden
    downs = jnp.concatenate([at_ref[2], at_ref[3]] * 4, axis=0)
    codes_buf[...] = mm(hidden, downs, NT).astype(BF16).astype(F32)
    for k in range(n_t):
        rows = [
            codes_buf[pl.ds(pl.multiple_of(f * patch_dev + peer("tm", k) * sub, sub), sub)]
            for f in range(frames)
        ]
        sends[k][...] = fold(jnp.concatenate(rows, axis=0))


def turn_kernel(frames, sub, q_ref, k_ref, v_ref, g_ref, *refs):
    *pieces, out_ref, own_buf, piece_buf, own_sems, sems = refs
    own = []
    start = pl.multiple_of(peer("tm", 0) * sub, sub)
    for index, ref in enumerate((q_ref, k_ref, v_ref, g_ref)):
        for f in range(frames):
            copy = pltpu.make_async_copy(
                ref.at[0, f, pl.ds(start, sub)],
                own_buf.at[index, f * sub : (f + 1) * sub],
                own_sems.at[index * frames + f],
            )
            copy.start()
            own.append(copy)
    copies = load_all(pieces, [piece_buf.at[k] for k in range(len(pieces))], sems)
    for copy in own + copies:
        copy.wait()
    for index in range(4):
        parts = [own_buf[index]] + [piece_buf[k, index] for k in range(len(pieces))]
        out_ref[index] = jnp.concatenate(parts, axis=0).T


def time_kernel(n_t, sub, x_ref, b_ref, *refs):
    codes_refs, refs = refs[:n_t][::-1], refs[n_t:]
    outs, sends, grad_b_ref = refs[:n_t], refs[n_t : 2 * n_t], refs[2 * n_t]
    _, width, tokens = x_ref.shape
    codes = jnp.concatenate([unfold(ref[...]) for ref in codes_refs], axis=0).T
    codes_q = codes[:RANK].astype(BF16)
    codes_v = codes[RANK : 2 * RANK].astype(BF16)
    query = (x_ref[0].astype(F32) + mm(b_ref[2], codes_q, TN)).astype(BF16).astype(F32)
    vals = (x_ref[2].astype(F32) + mm(b_ref[3], codes_v, TN)).astype(BF16).astype(F32)
    keys = x_ref[1].astype(F32)
    grad = x_ref[3].astype(F32)
    row = lax.broadcasted_iota(jnp.int32, (tokens, 2 * tokens), 0)
    col = lax.broadcasted_iota(jnp.int32, (tokens, 2 * tokens), 1)
    mask = lax.rem(row, sub) == lax.rem(col, sub)
    top = lax.broadcasted_iota(jnp.int32, (2 * HEAD_DIM, tokens), 0) < HEAD_DIM

    def spread(pair):
        return jnp.concatenate(
            [jnp.where(top, pair, 0.0), jnp.where(top, 0.0, pair)], axis=1
        ).astype(BF16)

    def pick(wide):
        return jnp.concatenate([wide[:HEAD_DIM, :tokens], wide[HEAD_DIM:, tokens:]], axis=0)

    outs_h, d_query, d_vals = [], [], []
    for h in range(0, width, 2 * HEAD_DIM):
        pair = slice(h, h + 2 * HEAD_DIM)
        k_h, v_h = keys[pair].astype(BF16), vals[pair].astype(BF16)
        g_h = spread(grad[pair])
        probs = probs_of(k_h.T, spread(query[pair]), mask)
        low = probs.astype(BF16)
        dprob = mm(v_h.T, g_h)
        inner = jnp.sum(probs * dprob, axis=0, keepdims=True)
        dscore = (probs * (dprob - inner) * SCALE).astype(BF16)
        outs_h.append(pick(mm(v_h, low)))
        d_vals.append(mm(g_h, low, NT))
        d_query.append(pick(mm(k_h, dscore)))
    d_query = jnp.concatenate(d_query, axis=0).astype(BF16)
    d_vals = jnp.concatenate(d_vals, axis=0).astype(BF16)
    d_codes = jnp.concatenate([mm(b_ref[2], d_query), mm(b_ref[3], d_vals)] * 4, axis=0)
    d_codes = d_codes.astype(BF16).astype(F32).T
    per = tokens // n_t
    for k in range(n_t):
        sends[k][...] = fold(d_codes[k * per : (k + 1) * per])
    out = jnp.concatenate(outs_h, axis=0).astype(BF16).T
    for k in range(n_t):
        outs[k][...] = out[k * per : (k + 1) * per]
    grad_b_ref[:RANK] = mm(codes_q, d_query, NT)
    grad_b_ref[RANK:] = mm(codes_v, d_vals, NT)


def hidden_grad_kernel(frames, n_s, sub, g_ref, at_ref, *refs):
    *pieces, codes_ref = refs[: -n_s - 2]
    pieces = pieces[::-1]
    outs, (buf, turned_ref) = refs[-n_s - 2 : -2], refs[-2:]
    patch_dev = sub * len(pieces)
    _, d_s, tokens = turned_ref.shape
    for k, piece in enumerate(pieces):
        rows = unfold(piece[...])
        for f in range(frames):
            start = pl.multiple_of(f * patch_dev + peer("tm", k) * sub, sub)
            buf[pl.ds(start, sub)] = rows[f * sub : (f + 1) * sub]
    codes = buf[:, : 2 * RANK].astype(BF16)
    codes_ref[...] = buf[...].T[: 2 * RANK].astype(BF16)
    downs = jnp.concatenate([at_ref[2], at_ref[3]], axis=0)
    grad = g_ref[0].reshape(tokens, n_s * d_s).astype(F32) + mm(codes, downs)
    turned = grad.astype(BF16).T
    for j in range(n_s):
        turned_ref[j] = turned[j * d_s : (j + 1) * d_s]
    for k in range(n_s):
        outs[k][...] = turned_ref[peer("space", k)]


def space_backward_kernel(frames, n_s, qkv_ref, probs_ref, hidden_ref, grad_b_ref, dcodes_ref, here_ref, *refs):
    packed, grads, sends = refs[:n_s], refs[n_s : 2 * n_s][::-1], refs[2 * n_s : 3 * n_s]
    part_ref, cut_buf = refs[3 * n_s :]
    d_s = part_ref.shape[1]
    tokens = hidden_ref.shape[0]
    patch_dev = tokens // frames
    total = n_s * patch_dev
    step = min(total, 256)
    b_here = here_ref[...].T
    grads = [x[...] for x in grads]
    grad_b_q = grad_b_v = None
    codes = [x[3 * d_s :] for x in packed]
    for f in range(frames):
        keys = qkv_ref[1, f].astype(F32)
        vals = qkv_ref[2, f].astype(F32)
        grad = frame_rows(grads, f, patch_dev).astype(F32)
        d_query, d_vals = [], []
        for h in range(d_s // HEAD_DIM):
            k_h = rows_of(keys, h).astype(BF16)
            v_h = rows_of(vals, h).astype(BF16)
            g_h = rows_of(grad, h).astype(BF16)
            dq_parts, dv_sum = [], None
            for s in range(0, total, step):
                probs = probs_ref[f, h, :, s : s + step]
                dq, dv = head_backward(probs, k_h, v_h, g_h[:, s : s + step])
                dq_parts.append(dq)
                dv_sum = dv if dv_sum is None else dv_sum + dv
            d_query.append(
                dq_parts[0] if len(dq_parts) == 1 else jnp.concatenate(dq_parts, axis=1)
            )
            d_vals.append(dv_sum)
        d_query = jnp.concatenate(d_query, axis=0).astype(BF16)
        d_vals = jnp.concatenate(d_vals, axis=0).astype(BF16)
        partial = jnp.concatenate([mm(b_here[:RANK], d_query), mm(b_here[RANK:], d_vals)], axis=0)
        for k in range(n_s):
            place = slice(f * patch_dev, (f + 1) * patch_dev)
            sends[k][:, place] = partial[:, k * patch_dev : (k + 1) * patch_dev].astype(BF16)
        frame_codes = frame_rows(codes, f, patch_dev)
        term_q = mm(frame_codes[:RANK], d_query, NT)
        term_v = mm(frame_codes[RANK:], d_vals, NT)
        grad_b_q = term_q if grad_b_q is None else grad_b_q + term_q
        grad_b_v = term_v if grad_b_v is None else grad_b_v + term_v
    part_ref[:RANK] = grad_b_q
    part_ref[RANK:] = grad_b_v
    grad_a = mm(dcodes_ref[...], hidden_ref[...])
    for j in range(n_s):
        here = slice(j * d_s, (j + 1) * d_s)
        cut_buf[j, :, :d_s] = grad_a[:, here].astype(BF16)
        cut_buf[j, :, d_s:] = grad_b_ref[:, here].astype(BF16)
    for k in range(n_s):
        sends[k][:, tokens:] = cut_buf[peer("space", k)]


def add_up(terms):
    result = None
    for term in terms:
        result = term if result is None else result + term
    return result


def merge_kernel(n_s, n_d, part_ref, patches_ref, *refs):
    recvs, sends, buf = refs[:n_s][::-1], refs[n_s : n_s + n_d], refs[n_s + n_d]
    d_s = part_ref.shape[1]
    tokens = recvs[0].shape[1] - 2 * d_s
    codes = add_up([recv[:, :tokens].astype(F32) for recv in recvs]).astype(BF16)
    full = mm(codes, patches_ref[0].reshape(tokens, n_s * d_s))
    time_a = add_up([recv[:, tokens : tokens + d_s].astype(F32) for recv in recvs])
    time_b = add_up([recv[:, tokens + d_s :].astype(F32) for recv in recvs])
    split = jnp.concatenate([time_a, part_ref[...], time_b], axis=0)
    per, per_full = split.shape[0] // n_d, full.shape[0] // n_d
    for d in range(n_d):
        mine = [split[d * per : (d + 1) * per]]
        rows = full[d * per_full : (d + 1) * per_full]
        mine += [rows[:, j * d_s : (j + 1) * d_s] for j in range(n_s)]
        mine = jnp.concatenate(mine, axis=0)
        half = mine.shape[0] // 2
        buf[d] = jnp.concatenate([mine[:half], mine[half:]], axis=1).astype(BF16)
    for k in range(n_d):
        sends[k][...] = buf[peer("dp", k)]


def total_kernel(*refs):
    terms = [ref[...].astype(F32) for ref in refs[:-1]]
    while len(terms) > 1:
        terms = [terms[i] + terms[i + 1] for i in range(0, len(terms), 2)]
    refs[-1][...] = terms[0].astype(refs[-1].dtype)


def join_kernel(n_full, *refs):
    pieces, (out_ref, buf) = refs[:-2], refs[-2:]
    n_s, d_s = len(pieces), buf.shape[2] // 2
    for k, piece in enumerate(pieces):
        buf[peer("space", k)] = piece[...]
    rows = [
        jnp.concatenate([buf[j, :, :d_s], buf[j, :, d_s:]], axis=0).astype(F32) for j in range(n_s)
    ]
    n_split = rows[0].shape[0] - n_s * n_full
    out_ref[n_full:] = jnp.concatenate([x[:n_split] for x in rows], axis=1).astype(BF16)
    full = add_up([x[n_split:] for x in rows])
    cuts = [full[j * n_full : (j + 1) * n_full] for j in range(n_s)]
    out_ref[:n_full] = jnp.concatenate(cuts, axis=1).astype(BF16)


def final_kernel(factor, n_d, n_full, *refs):
    pieces, (a_ref, b_ref, buf) = refs[:n_d], refs[n_d:]
    for k, piece in enumerate(pieces):
        buf[peer("dp", k)] = piece[...]
    n_split = pieces[0].shape[0] - n_full
    size = math.gcd(n_full, n_split, RANK)
    for d in range(n_d):
        rows = buf[d].astype(F32) * factor
        for r in range(0, n_full + n_split, size):
            row = d * n_full + r if r < n_full else 2 * RANK + d * n_split + r - n_full
            target = a_ref if row < 4 * RANK else b_ref
            row %= 4 * RANK
            target[row // RANK, row % RANK : row % RANK + size] = rows[r : r + size]


def mixed_kernel(frames, hidden_ref, *refs):
    pieces, (mixed_ref, buf) = refs[:-2], refs[-2:]
    n_t = len(pieces)
    tokens, width = hidden_ref.shape
    patch_dev = tokens // frames
    sub = patch_dev // n_t
    for k, piece in enumerate(pieces):
        for f in range(frames):
            start = pl.multiple_of(f * patch_dev + peer("tm", k) * sub, sub)
            buf[pl.ds(start, sub)] = piece[f * sub : (f + 1) * sub]
    total = hidden_ref[...].astype(F32) + buf[...].astype(F32)
    mixed_ref[0] = total.astype(BF16).reshape(frames, patch_dev, width)


def hops(arrays, axis, first):
    size = lax.axis_size(axis)
    return [
        lax.ppermute(array, axis, [(i, i ^ k) for i in range(size)])
        for k, array in enumerate(arrays, first)
    ]


def exchange(pieces, axis):
    return [pieces[0]] + hops(pieces[1:], axis, 1)


def share(array, axis):
    return exchange([array] * lax.axis_size(axis), axis)


def per_device(
    patches, query_s, key_s, value_s, query_t, key_t, value_t, adapters_a, adapters_b, cotangent
):
    _, frames, patch_dev, width = patches.shape
    n_d, n_t, n_s = (lax.axis_size(name) for name in ("dp", "tm", "space"))
    tokens = frames * patch_dev
    sub = patch_dev // n_t
    d_s = width // n_s
    total = n_s * patch_dev
    factor = (tokens * n_d * n_t * n_s) ** (-0.5)
    downs = jnp.swapaxes(adapters_a, 1, 2)
    dma = pltpu.SemaphoreType.DMA

    time_arrays = [far(x) for x in (query_t, key_t, value_t, cotangent)]
    space_arrays = [
        far(x) for x in (patches, downs, adapters_b, query_s, value_s, key_s)
    ]
    packed = call(
        functools.partial(pack_kernel, n_s, n_t, sub),
        [shape((3 * d_s + 2 * RANK, tokens), BF16)] * n_s
        + [shape((d_s, 2 * RANK), BF16)]
        + [shape((4, frames * sub, width), BF16)] * (n_t - 1),
        *space_arrays, *time_arrays,
        scratch=[pltpu.VMEM(x.shape, BF16) for x in space_arrays]
        + [
            pltpu.VMEM((4,) + query_t.shape, BF16),
            pltpu.VMEM((3, n_s, d_s, tokens), BF16),
            pltpu.VMEM((n_s, d_s, 2 * RANK), BF16),
            dma((6,)),
            dma((4,)),
        ],
        hbm=True,
    )
    here, time_pieces = packed[n_s], hops(packed[n_s + 1 :], "tm", 1)
    packed = exchange(packed[:n_s], "space")
    probs_dims = (frames, d_s // HEAD_DIM, total, total)
    qkv, probs, *out_s = call(
        functools.partial(space_forward_kernel, frames, n_s),
        [shape((3, frames, d_s, total), BF16), shape(probs_dims, F32)]
        + [shape((d_s, tokens), BF16)] * n_s,
        *packed,
        after=time_pieces[:1],
    )
    out_s = exchange(out_s, "space")
    hidden, *codes = call(
        functools.partial(hidden_kernel, n_t, n_s),
        [shape((tokens, width), BF16)] + [shape((8, 128), F32)] * n_t,
        *out_s[::-1], patches, downs,
        scratch=[pltpu.VMEM((n_s, d_s, tokens), BF16), pltpu.VMEM((tokens, 128), F32)],
    )
    codes = exchange(codes, "tm")
    turned = call(
        functools.partial(turn_kernel, frames, sub),
        shape((4, width, n_t * frames * sub), BF16),
        *time_arrays, *time_pieces,
        scratch=[
            pltpu.VMEM((4, frames * sub, width), BF16),
            pltpu.VMEM((n_t - 1, 4, frames * sub, width), BF16),
            dma((4 * frames,)),
            dma((n_t - 1,)),
        ],
        hbm=True,
    )
    timed = call(
        functools.partial(time_kernel, n_t, sub),
        [shape((frames * sub, width), BF16)] * n_t
        + [shape((8, 128), F32)] * n_t
        + [shape((2 * RANK, width), F32)],
        turned, adapters_b, *codes[::-1],
    )
    out_t, dcodes, time_grad_b = timed[:n_t], timed[n_t : 2 * n_t], timed[2 * n_t]
    dcodes = exchange(dcodes, "tm")
    out_t[2:] = hops(out_t[2:], "tm", 2)
    dcodes, *grads = call(
        functools.partial(hidden_grad_kernel, frames, n_s, sub),
        [shape((2 * RANK, tokens), BF16)] + [shape((d_s, tokens), BF16)] * n_s,
        cotangent, downs, *dcodes[::-1],
        scratch=[pltpu.VMEM((tokens, 128), F32), pltpu.VMEM((n_s, d_s, tokens), BF16)],
    )
    grads = exchange(grads, "space")
    backward = call(
        functools.partial(space_backward_kernel, frames, n_s),
        [shape((2 * RANK, tokens + 2 * d_s), BF16)] * n_s + [shape((2 * RANK, d_s), F32)],
        qkv, probs, hidden, time_grad_b, dcodes, here, *packed, *grads[::-1],
        scratch=[pltpu.VMEM((n_s, 2 * RANK, 2 * d_s), BF16)],
        carry=out_t[1:2],
    )
    partial, part = backward[:n_s], backward[n_s]
    partial = exchange(partial, "space")
    out_t[1:2] = hops(backward[n_s + 1 :], "tm", 1)
    n_full, n_split = 2 * RANK // n_d, 6 * RANK // n_d
    dims = ((n_s * n_full + n_split) // 2, 2 * d_s)
    sums = call(
        functools.partial(merge_kernel, n_s, n_d),
        [shape(dims, BF16)] * n_d,
        part, patches, *partial[::-1],
        scratch=[pltpu.VMEM((n_d,) + dims, BF16)],
        after=out_t[2:],
    )
    sums = call(total_kernel, shape(dims, BF16), *exchange(sums, "dp"), after=out_t[1:2])
    sums = call(total_kernel, shape(dims, BF16), *share(sums, "tm"))
    sums = call(
        functools.partial(join_kernel, n_full),
        shape((n_full + n_split, width), BF16),
        *share(sums, "space"),
        scratch=[pltpu.VMEM((n_s,) + dims, BF16)],
    )
    grads_a, grads_b = call(
        functools.partial(final_kernel, factor, n_d, n_full),
        [shape((4, RANK, width), F32)] * 2,
        *share(sums, "dp"),
        scratch=[pltpu.VMEM((n_d, n_full + n_split, width), BF16)],
    )
    mixed = call(
        functools.partial(mixed_kernel, frames),
        shape(patches.shape, BF16),
        hidden, *out_t,
        scratch=[pltpu.VMEM((tokens, width), BF16)],
    )
    return (mixed, jnp.swapaxes(grads_a, 1, 2), grads_b)


def solution(mesh):
    token = P("dp", "tm", "space", None)
    return jax.shard_map(
        per_device,
        mesh=mesh,
        in_specs=(token,) * 7 + (P(), P(), token),
        out_specs=(token, P(), P()),
        check_vma=False,
    )
```

```python
import functools
import math

import jax
import jax.numpy as jnp
from jax import lax
from jax.experimental import pallas as pl
from jax.experimental.pallas import tpu as pltpu
from jax.sharding import PartitionSpec as P

HEAD_DIM = 72
RANK = 16
SCALE = HEAD_DIM ** (-0.5)
F32 = jnp.float32
BF16 = jnp.bfloat16
NN = (((1,), (0,)), ((), ()))
NT = (((1,), (1,)), ((), ()))
TN = (((0,), (0,)), ((), ()))


def mm(a, b, dims=NN):
    return lax.dot_general(a, b, dims, preferred_element_type=F32)


def far(x):
    return pltpu.with_memory_space_constraint(x, pltpu.HBM)


def call(kernel, out_shape, *args, scratch=(), hbm=False, limit=48, after=(), carry=()):
    vmem = pl.BlockSpec(memory_space=pltpu.VMEM)
    anywhere = pl.BlockSpec(memory_space=pl.ANY)
    main = anywhere if hbm else vmem
    single = not isinstance(out_shape, (tuple, list))
    outs = (out_shape,) if single else tuple(out_shape)
    used, extra = len(args), len(after) + len(carry)

    def body(*refs):
        inside = refs[:used] + refs[used + extra : used + extra + len(outs)]
        kernel(*inside, *refs[used + extra + len(outs) + len(carry) :])

    result = pl.pallas_call(
        body,
        out_shape=outs + tuple(shape(x.shape, x.dtype) for x in carry),
        in_specs=[main] * used + [anywhere] * extra,
        out_specs=tuple(vmem if isinstance(o, jax.ShapeDtypeStruct) else anywhere for o in outs)
        + (anywhere,) * len(carry),
        scratch_shapes=list(scratch),
        input_output_aliases={used + len(after) + i: len(outs) + i for i in range(len(carry))},
        compiler_params=pltpu.CompilerParams(vmem_limit_bytes=limit * 1024 * 1024),
    )(*args, *after, *carry)
    return result[0] if single and not carry else list(result)


def shape(dims, dtype):
    return jax.ShapeDtypeStruct(tuple(dims), dtype)


def probs_of(keys, q_t, mask):
    scores = mm(keys, q_t) * SCALE
    if mask is not None:
        scores = jnp.where(mask, scores, -1e30)
    peak = jnp.max(scores, axis=0, keepdims=True)
    weights = jnp.exp(scores - peak)
    return weights * (1.0 / jnp.sum(weights, axis=0, keepdims=True))


def head_backward(probs, k_t, v_t, g_t):
    low = probs.astype(BF16)
    dvals = mm(g_t, low, NT)
    dprob = mm(v_t.T, g_t)
    inner = jnp.sum(probs * dprob, axis=0, keepdims=True)
    dscore = (probs * (dprob - inner) * SCALE).astype(BF16)
    dquery = mm(k_t, dscore)
    return dquery, dvals


def rows_of(array, head):
    return array[head * HEAD_DIM : (head + 1) * HEAD_DIM]


def peer(axis, distance):
    return lax.axis_index(axis) ^ distance


def load_all(refs, buffers, sems):
    copies = [
        pltpu.make_async_copy(ref, buffer, sems.at[index])
        for index, (ref, buffer) in enumerate(zip(refs, buffers))
    ]
    for copy in copies:
        copy.start()
    return copies


def pack_kernel(n_s, n_t, sub, *refs):
    ins, time_ins, refs = refs[:6], refs[6:10], refs[10:]
    outs, here_ref, refs = refs[:n_s], refs[n_s], refs[n_s + 1 :]
    time_outs, refs = refs[: n_t - 1], refs[n_t - 1 :]
    buffers, (time_buf, turned_ref, maps_ref, sems, time_sems) = refs[:6], refs[6:]
    p_buf, at_buf, b_buf, q_buf, v_buf, k_buf = buffers
    copies = load_all(ins, buffers, sems)
    time_copies = load_all(time_ins, [time_buf.at[index] for index in range(4)], time_sems)
    d_s, tokens = turned_ref.shape[2:]
    frames = time_buf.shape[2]

    def flat(ref):
        return ref[0].reshape(tokens, ref.shape[3])

    def send(array, index):
        turned = array.T
        for j in range(n_s):
            turned_ref[index, j] = turned[j * d_s : (j + 1) * d_s]
        for k in range(n_s):
            outs[k][index * d_s : (index + 1) * d_s] = turned_ref[index, peer("space", k)]

    copies[0].wait()
    copies[1].wait()
    copies[2].wait()
    patches = flat(p_buf)
    codes_q = mm(patches, at_buf[0], NT).astype(BF16)
    codes_v = mm(patches, at_buf[1], NT).astype(BF16)
    codes_t = jnp.concatenate([codes_q, codes_v], axis=1).T
    maps = jnp.concatenate([b_buf[0], b_buf[1]], axis=0).T
    for j in range(n_s):
        maps_ref[j] = maps[j * d_s : (j + 1) * d_s]
    here_ref[...] = maps_ref[peer("space", 0)]
    copies[3].wait()
    query = (flat(q_buf).astype(F32) + mm(codes_q, b_buf[0])).astype(BF16)
    send(query, 0)
    copies[4].wait()
    value = (flat(v_buf).astype(F32) + mm(codes_v, b_buf[1])).astype(BF16)
    send(value, 2)
    copies[5].wait()
    send(flat(k_buf), 1)
    for k in range(n_s):
        outs[k][3 * d_s :] = codes_t
    for index, copy in enumerate(time_copies):
        copy.wait()
        for k in range(1, n_t):
            start = pl.multiple_of(peer("tm", k) * sub, sub)
            for f in range(frames):
                time_outs[k - 1][index, f * sub : (f + 1) * sub] = time_buf[
                    index, 0, f, pl.ds(start, sub)
                ]


def frame_rows(pieces, f, patch_dev):
    return jnp.concatenate([x[:, f * patch_dev : (f + 1) * patch_dev] for x in pieces], axis=1)


def space_forward_kernel(frames, n_s, *refs):
    packed, (qkv_ref, probs_ref, *outs) = refs[:n_s], refs[n_s:]
    d_s, tokens = outs[0].shape
    patch_dev = tokens // frames
    total = n_s * patch_dev
    step = min(total, 256)
    for index in range(3):
        pieces = [x[index * d_s : (index + 1) * d_s] for x in packed]
        for f in range(frames):
            qkv_ref[index, f] = frame_rows(pieces, f, patch_dev)
    for f in range(frames):
        query = qkv_ref[0, f].astype(F32)
        keys = qkv_ref[1, f].astype(F32)
        vals = qkv_ref[2, f].astype(F32)
        heads = []
        for h in range(d_s // HEAD_DIM):
            k_h = rows_of(keys, h).astype(BF16)
            v_h = rows_of(vals, h).astype(BF16)
            q_h = rows_of(query, h).astype(BF16)
            parts = []
            for s in range(0, total, step):
                probs = probs_of(k_h.T, q_h[:, s : s + step], None)
                probs_ref[f, h, :, s : s + step] = probs
                parts.append(mm(v_h, probs.astype(BF16)))
            heads.append(parts[0] if len(parts) == 1 else jnp.concatenate(parts, axis=1))
        out = jnp.concatenate(heads, axis=0).astype(BF16)
        for k in range(n_s):
            outs[k][:, f * patch_dev : (f + 1) * patch_dev] = out[
                :, k * patch_dev : (k + 1) * patch_dev
            ]


def lane_block(rows):
    return lax.broadcasted_iota(jnp.int32, (rows, 128), 1) // (2 * RANK)


def fold(token_rows):
    block = lane_block(8)
    result = token_rows[0:8]
    for k in range(1, 4):
        result = jnp.where(block == k, token_rows[8 * k : 8 * k + 8], result)
    return result


def unfold(folded):
    pieces = [folded]
    for k in range(1, 4):
        pieces.append(pltpu.roll(folded, 128 - 2 * RANK * k, 1))
    return jnp.concatenate(pieces, axis=0)


def hidden_kernel(n_t, n_s, *refs):
    pieces, refs = refs[:n_s][::-1], refs[n_s:]
    p_ref, at_ref, hidden_ref = refs[:3]
    sends = refs[3 : 3 + n_t]
    out_buf, codes_buf = refs[3 + n_t :]
    _, frames, patch_dev, width = p_ref.shape
    tokens = frames * patch_dev
    sub = patch_dev // n_t
    for k in range(n_s):
        out_buf[peer("space", k)] = pieces[k][...]
    out = out_buf[...].reshape(width, tokens).T
    hidden = (p_ref[0].reshape(tokens, width).astype(F32) + out.astype(F32)).astype(BF16)
    hidden_ref[...] = hidden
    downs = jnp.concatenate([at_ref[2], at_ref[3]] * 4, axis=0)
    codes_buf[...] = mm(hidden, downs, NT).astype(BF16).astype(F32)
    for k in range(n_t):
        rows = [
            codes_buf[pl.ds(pl.multiple_of(f * patch_dev + peer("tm", k) * sub, sub), sub)]
            for f in range(frames)
        ]
        sends[k][...] = fold(jnp.concatenate(rows, axis=0))


def turn_kernel(frames, sub, q_ref, k_ref, v_ref, g_ref, *refs):
    *pieces, out_ref, own_buf, piece_buf, own_sems, sems = refs
    own = []
    start = pl.multiple_of(peer("tm", 0) * sub, sub)
    for index, ref in enumerate((q_ref, k_ref, v_ref, g_ref)):
        for f in range(frames):
            copy = pltpu.make_async_copy(
                ref.at[0, f, pl.ds(start, sub)],
                own_buf.at[index, f * sub : (f + 1) * sub],
                own_sems.at[index * frames + f],
            )
            copy.start()
            own.append(copy)
    copies = load_all(pieces, [piece_buf.at[k] for k in range(len(pieces))], sems)
    for copy in own + copies:
        copy.wait()
    for index in range(4):
        parts = [own_buf[index]] + [piece_buf[k, index] for k in range(len(pieces))]
        out_ref[index] = jnp.concatenate(parts, axis=0).T


def time_kernel(n_t, sub, x_ref, b_ref, *refs):
    codes_refs, refs = refs[:n_t][::-1], refs[n_t:]
    outs, sends, grad_b_ref = refs[:n_t], refs[n_t : 2 * n_t], refs[2 * n_t]
    _, width, tokens = x_ref.shape
    codes = jnp.concatenate([unfold(ref[...]) for ref in codes_refs], axis=0).T
    codes_q = codes[:RANK].astype(BF16)
    codes_v = codes[RANK : 2 * RANK].astype(BF16)
    query = (x_ref[0].astype(F32) + mm(b_ref[2], codes_q, TN)).astype(BF16).astype(F32)
    vals = (x_ref[2].astype(F32) + mm(b_ref[3], codes_v, TN)).astype(BF16).astype(F32)
    keys = x_ref[1].astype(F32)
    grad = x_ref[3].astype(F32)
    row = lax.broadcasted_iota(jnp.int32, (tokens, 2 * tokens), 0)
    col = lax.broadcasted_iota(jnp.int32, (tokens, 2 * tokens), 1)
    mask = lax.rem(row, sub) == lax.rem(col, sub)
    top = lax.broadcasted_iota(jnp.int32, (2 * HEAD_DIM, tokens), 0) < HEAD_DIM

    def spread(pair):
        return jnp.concatenate(
            [jnp.where(top, pair, 0.0), jnp.where(top, 0.0, pair)], axis=1
        ).astype(BF16)

    def pick(wide):
        return jnp.concatenate([wide[:HEAD_DIM, :tokens], wide[HEAD_DIM:, tokens:]], axis=0)

    outs_h, d_query, d_vals = [], [], []
    for h in range(0, width, 2 * HEAD_DIM):
        pair = slice(h, h + 2 * HEAD_DIM)
        k_h, v_h = keys[pair].astype(BF16), vals[pair].astype(BF16)
        g_h = spread(grad[pair])
        probs = probs_of(k_h.T, spread(query[pair]), mask)
        low = probs.astype(BF16)
        dprob = mm(v_h.T, g_h)
        inner = jnp.sum(probs * dprob, axis=0, keepdims=True)
        dscore = (probs * (dprob - inner) * SCALE).astype(BF16)
        outs_h.append(pick(mm(v_h, low)))
        d_vals.append(mm(g_h, low, NT))
        d_query.append(pick(mm(k_h, dscore)))
    d_query = jnp.concatenate(d_query, axis=0).astype(BF16)
    d_vals = jnp.concatenate(d_vals, axis=0).astype(BF16)
    d_codes = jnp.concatenate([mm(b_ref[2], d_query), mm(b_ref[3], d_vals)] * 4, axis=0)
    d_codes = d_codes.astype(BF16).astype(F32).T
    per = tokens // n_t
    for k in range(n_t):
        sends[k][...] = fold(d_codes[k * per : (k + 1) * per])
    out = jnp.concatenate(outs_h, axis=0).astype(BF16).T
    for k in range(n_t):
        rows = [out[k * per : (k + 1) * per], jnp.zeros((8, width), BF16)]
        outs[k][...] = jnp.concatenate(rows, axis=0)
    grad_b_ref[:RANK] = mm(codes_q, d_query, NT)
    grad_b_ref[RANK:] = mm(codes_v, d_vals, NT)


def hidden_grad_kernel(frames, n_s, sub, g_ref, at_ref, *refs):
    *pieces, codes_ref = refs[: -n_s - 2]
    pieces = pieces[::-1]
    outs, (buf, turned_ref) = refs[-n_s - 2 : -2], refs[-2:]
    patch_dev = sub * len(pieces)
    _, d_s, tokens = turned_ref.shape
    for k, piece in enumerate(pieces):
        rows = unfold(piece[...])
        for f in range(frames):
            start = pl.multiple_of(f * patch_dev + peer("tm", k) * sub, sub)
            buf[pl.ds(start, sub)] = rows[f * sub : (f + 1) * sub]
    codes = buf[:, : 2 * RANK].astype(BF16)
    codes_ref[...] = buf[...].T[: 2 * RANK].astype(BF16)
    downs = jnp.concatenate([at_ref[2], at_ref[3]], axis=0)
    grad = g_ref[0].reshape(tokens, n_s * d_s).astype(F32) + mm(codes, downs)
    turned = grad.astype(BF16).T
    for j in range(n_s):
        turned_ref[j] = turned[j * d_s : (j + 1) * d_s]
    for k in range(n_s):
        outs[k][...] = turned_ref[peer("space", k)]


def space_backward_kernel(frames, n_s, qkv_ref, probs_ref, hidden_ref, grad_b_ref, dcodes_ref, here_ref, *refs):
    packed, grads, sends = refs[:n_s], refs[n_s : 2 * n_s][::-1], refs[2 * n_s : 3 * n_s]
    part_ref, cut_buf = refs[3 * n_s :]
    d_s = part_ref.shape[1]
    tokens = hidden_ref.shape[0]
    patch_dev = tokens // frames
    total = n_s * patch_dev
    step = min(total, 256)
    b_here = here_ref[...].T
    grads = [x[...] for x in grads]
    grad_b_q = grad_b_v = None
    codes = [x[3 * d_s :] for x in packed]
    for f in range(frames):
        keys = qkv_ref[1, f].astype(F32)
        vals = qkv_ref[2, f].astype(F32)
        grad = frame_rows(grads, f, patch_dev).astype(F32)
        d_query, d_vals = [], []
        for h in range(d_s // HEAD_DIM):
            k_h = rows_of(keys, h).astype(BF16)
            v_h = rows_of(vals, h).astype(BF16)
            g_h = rows_of(grad, h).astype(BF16)
            dq_parts, dv_sum = [], None
            for s in range(0, total, step):
                probs = probs_ref[f, h, :, s : s + step]
                dq, dv = head_backward(probs, k_h, v_h, g_h[:, s : s + step])
                dq_parts.append(dq)
                dv_sum = dv if dv_sum is None else dv_sum + dv
            d_query.append(
                dq_parts[0] if len(dq_parts) == 1 else jnp.concatenate(dq_parts, axis=1)
            )
            d_vals.append(dv_sum)
        d_query = jnp.concatenate(d_query, axis=0).astype(BF16)
        d_vals = jnp.concatenate(d_vals, axis=0).astype(BF16)
        partial = jnp.concatenate([mm(b_here[:RANK], d_query), mm(b_here[RANK:], d_vals)], axis=0)
        for k in range(n_s):
            place = slice(f * patch_dev, (f + 1) * patch_dev)
            sends[k][:, place] = partial[:, k * patch_dev : (k + 1) * patch_dev].astype(BF16)
        frame_codes = frame_rows(codes, f, patch_dev)
        term_q = mm(frame_codes[:RANK], d_query, NT)
        term_v = mm(frame_codes[RANK:], d_vals, NT)
        grad_b_q = term_q if grad_b_q is None else grad_b_q + term_q
        grad_b_v = term_v if grad_b_v is None else grad_b_v + term_v
    part_ref[:RANK] = grad_b_q
    part_ref[RANK:] = grad_b_v
    grad_a = mm(dcodes_ref[...], hidden_ref[...])
    for j in range(n_s):
        here = slice(j * d_s, (j + 1) * d_s)
        cut_buf[j, :, :d_s] = grad_a[:, here].astype(BF16)
        cut_buf[j, :, d_s:] = grad_b_ref[:, here].astype(BF16)
    for k in range(n_s):
        sends[k][:, tokens:] = cut_buf[peer("space", k)]


def add_up(terms):
    result = None
    for term in terms:
        result = term if result is None else result + term
    return result


def merge_kernel(n_s, n_d, part_ref, patches_ref, *refs):
    recvs, sends, buf = refs[:n_s][::-1], refs[n_s : n_s + n_d], refs[n_s + n_d]
    d_s = part_ref.shape[1]
    tokens = recvs[0].shape[1] - 2 * d_s
    codes = add_up([recv[:, :tokens].astype(F32) for recv in recvs]).astype(BF16)
    full = mm(codes, patches_ref[0].reshape(tokens, n_s * d_s))
    time_a = add_up([recv[:, tokens : tokens + d_s].astype(F32) for recv in recvs])
    time_b = add_up([recv[:, tokens + d_s :].astype(F32) for recv in recvs])
    split = jnp.concatenate([time_a, part_ref[...], time_b], axis=0)
    per, per_full = split.shape[0] // n_d, full.shape[0] // n_d
    for d in range(n_d):
        mine = [split[d * per : (d + 1) * per]]
        rows = full[d * per_full : (d + 1) * per_full]
        mine += [rows[:, j * d_s : (j + 1) * d_s] for j in range(n_s)]
        mine = jnp.concatenate(mine, axis=0)
        half = mine.shape[0] // 2
        buf[d] = jnp.concatenate([mine[:half], mine[half:]], axis=1).astype(BF16)
    for k in range(n_d):
        sends[k][...] = buf[peer("dp", k)]


def total_kernel(*refs):
    terms = [ref[...].astype(F32) for ref in refs[:-1]]
    while len(terms) > 1:
        terms = [terms[i] + terms[i + 1] for i in range(0, len(terms), 2)]
    refs[-1][...] = terms[0].astype(refs[-1].dtype)


def join_kernel(n_full, *refs):
    pieces, (out_ref, buf) = refs[:-2], refs[-2:]
    n_s, d_s = len(pieces), buf.shape[2] // 2
    for k, piece in enumerate(pieces):
        buf[peer("space", k)] = piece[...]
    rows = [
        jnp.concatenate([buf[j, :, :d_s], buf[j, :, d_s:]], axis=0).astype(F32) for j in range(n_s)
    ]
    n_split = rows[0].shape[0] - n_s * n_full
    out_ref[n_full:] = jnp.concatenate([x[:n_split] for x in rows], axis=1).astype(BF16)
    full = add_up([x[n_split:] for x in rows])
    cuts = [full[j * n_full : (j + 1) * n_full] for j in range(n_s)]
    out_ref[:n_full] = jnp.concatenate(cuts, axis=1).astype(BF16)


def final_kernel(factor, n_d, n_full, *refs):
    pieces, (a_ref, b_ref, buf) = refs[:n_d], refs[n_d:]
    for k, piece in enumerate(pieces):
        buf[peer("dp", k)] = piece[...]
    n_split = pieces[0].shape[0] - n_full
    size = math.gcd(n_full, n_split, RANK)
    for d in range(n_d):
        rows = buf[d].astype(F32) * factor
        for r in range(0, n_full + n_split, size):
            row = d * n_full + r if r < n_full else 2 * RANK + d * n_split + r - n_full
            target = a_ref if row < 4 * RANK else b_ref
            row %= 4 * RANK
            target[row // RANK, row % RANK : row % RANK + size] = rows[r : r + size]


def mixed_kernel(frames, hidden_ref, *refs):
    pieces, (mixed_ref, buf) = refs[:-2], refs[-2:]
    n_t = len(pieces)
    tokens, width = hidden_ref.shape
    patch_dev = tokens // frames
    sub = patch_dev // n_t
    for k, piece in enumerate(pieces):
        for f in range(frames):
            start = pl.multiple_of(f * patch_dev + peer("tm", k) * sub, sub)
            buf[pl.ds(start, sub)] = piece[f * sub : (f + 1) * sub]
    total = hidden_ref[...].astype(F32) + buf[...].astype(F32)
    mixed_ref[0] = total.astype(BF16).reshape(frames, patch_dev, width)


def hops(arrays, axis, first):
    size = lax.axis_size(axis)
    return [
        lax.ppermute(array, axis, [(i, i ^ k) for i in range(size)])
        for k, array in enumerate(arrays, first)
    ]


def exchange(pieces, axis):
    return [pieces[0]] + hops(pieces[1:], axis, 1)


def share(array, axis):
    return exchange([array] * lax.axis_size(axis), axis)


def per_device(
    patches, query_s, key_s, value_s, query_t, key_t, value_t, adapters_a, adapters_b, cotangent
):
    _, frames, patch_dev, width = patches.shape
    n_d, n_t, n_s = (lax.axis_size(name) for name in ("dp", "tm", "space"))
    tokens = frames * patch_dev
    sub = patch_dev // n_t
    d_s = width // n_s
    total = n_s * patch_dev
    factor = (tokens * n_d * n_t * n_s) ** (-0.5)
    downs = jnp.swapaxes(adapters_a, 1, 2)
    dma = pltpu.SemaphoreType.DMA

    time_arrays = [far(x) for x in (query_t, key_t, value_t, cotangent)]
    space_arrays = [
        far(x) for x in (patches, downs, adapters_b, query_s, value_s, key_s)
    ]
    packed = call(
        functools.partial(pack_kernel, n_s, n_t, sub),
        [shape((3 * d_s + 2 * RANK, tokens), BF16)] * n_s
        + [shape((d_s, 2 * RANK), BF16)]
        + [shape((4, frames * sub, width), BF16)] * (n_t - 1),
        *space_arrays, *time_arrays,
        scratch=[pltpu.VMEM(x.shape, BF16) for x in space_arrays]
        + [
            pltpu.VMEM((4,) + query_t.shape, BF16),
            pltpu.VMEM((3, n_s, d_s, tokens), BF16),
            pltpu.VMEM((n_s, d_s, 2 * RANK), BF16),
            dma((6,)),
            dma((4,)),
        ],
        hbm=True,
    )
    here, time_pieces = packed[n_s], hops(packed[n_s + 1 :], "tm", 1)
    packed = exchange(packed[:n_s], "space")
    probs_dims = (frames, d_s // HEAD_DIM, total, total)
    qkv, probs, *out_s = call(
        functools.partial(space_forward_kernel, frames, n_s),
        [shape((3, frames, d_s, total), BF16), shape(probs_dims, F32)]
        + [shape((d_s, tokens), BF16)] * n_s,
        *packed,
        after=time_pieces[:1],
    )
    out_s = exchange(out_s, "space")
    hidden, *codes = call(
        functools.partial(hidden_kernel, n_t, n_s),
        [shape((tokens, width), BF16)] + [shape((8, 128), F32)] * n_t,
        *out_s[::-1], patches, downs,
        scratch=[pltpu.VMEM((n_s, d_s, tokens), BF16), pltpu.VMEM((tokens, 128), F32)],
    )
    codes = exchange(codes, "tm")
    turned = call(
        functools.partial(turn_kernel, frames, sub),
        shape((4, width, n_t * frames * sub), BF16),
        *time_arrays, *time_pieces,
        scratch=[
            pltpu.VMEM((4, frames * sub, width), BF16),
            pltpu.VMEM((n_t - 1, 4, frames * sub, width), BF16),
            dma((4 * frames,)),
            dma((n_t - 1,)),
        ],
        hbm=True,
    )
    timed = call(
        functools.partial(time_kernel, n_t, sub),
        [shape((frames * sub + 8, width), BF16)] * n_t
        + [shape((8, 128), F32)] * n_t
        + [shape((2 * RANK, width), F32)],
        turned, adapters_b, *codes[::-1],
    )
    out_t, dcodes, time_grad_b = timed[:n_t], timed[n_t : 2 * n_t], timed[2 * n_t]
    dcodes = exchange(dcodes, "tm")
    out_t[2:] = hops(out_t[2:], "tm", 2)
    dcodes, *grads = call(
        functools.partial(hidden_grad_kernel, frames, n_s, sub),
        [shape((2 * RANK, tokens), BF16)] + [shape((d_s, tokens), BF16)] * n_s,
        cotangent, downs, *dcodes[::-1],
        scratch=[pltpu.VMEM((tokens, 128), F32), pltpu.VMEM((n_s, d_s, tokens), BF16)],
    )
    grads = exchange(grads, "space")
    backward = call(
        functools.partial(space_backward_kernel, frames, n_s),
        [shape((2 * RANK, tokens + 2 * d_s), BF16)] * n_s + [shape((2 * RANK, d_s), F32)],
        qkv, probs, hidden, time_grad_b, dcodes, here, *packed, *grads[::-1],
        scratch=[pltpu.VMEM((n_s, 2 * RANK, 2 * d_s), BF16)],
        carry=out_t[1:2],
    )
    partial, part = backward[:n_s], backward[n_s]
    partial = exchange(partial, "space")
    out_t[1:2] = hops(backward[n_s + 1 :], "tm", 1)
    n_full, n_split = 2 * RANK // n_d, 6 * RANK // n_d
    dims = ((n_s * n_full + n_split) // 2, 2 * d_s)
    sums = call(
        functools.partial(merge_kernel, n_s, n_d),
        [shape(dims, BF16)] * n_d,
        part, patches, *partial[::-1],
        scratch=[pltpu.VMEM((n_d,) + dims, BF16)],
        after=out_t[2:],
    )
    sums = call(total_kernel, shape(dims, BF16), *exchange(sums, "dp"), after=out_t[1:2])
    sums = call(total_kernel, shape(dims, BF16), *share(sums, "tm"))
    sums = call(
        functools.partial(join_kernel, n_full),
        shape((n_full + n_split, width), BF16),
        *share(sums, "space"),
        scratch=[pltpu.VMEM((n_s,) + dims, BF16)],
    )
    grads_a, grads_b = call(
        functools.partial(final_kernel, factor, n_d, n_full),
        [shape((4, RANK, width), F32)] * 2,
        *share(sums, "dp"),
        scratch=[pltpu.VMEM((n_d, n_full + n_split, width), BF16)],
    )
    mixed = call(
        functools.partial(mixed_kernel, frames),
        shape(patches.shape, BF16),
        hidden, *out_t,
        scratch=[pltpu.VMEM((tokens, width), BF16)],
    )
    return (mixed, jnp.swapaxes(grads_a, 1, 2), grads_b)


def solution(mesh):
    token = P("dp", "tm", "space", None)
    return jax.shard_map(
        per_device,
        mesh=mesh,
        in_specs=(token,) * 7 + (P(), P(), token),
        out_specs=(token, P(), P()),
        check_vma=False,
    )
```
